32 devices in a mesh: dp: 8 (over z, y), tensor: 4 (over x, core).
Axes of the slice: x: 2, y: 2, z: 4, core: 2. Of those that a mesh axis runs over, the one named last changes fastest.
Arguments:
- tokens: bfloat16 [8192, 2048], P('dp'), may hold values from -6 to 6
- attention_gain: float32 [2048], replicated, may hold values from 0.5 to 1.5
- query_weight: bfloat16 [2048, 2048], P(None, 'tensor'), may hold values from -0.125 to 0.125
- key_weight: bfloat16 [2048, 1024], P(None, 'tensor'), may hold values from -0.125 to 0.125
- value_weight: bfloat16 [2048, 1024], P(None, 'tensor'), may hold values from -0.125 to 0.125
- query_gain: float32 [128], replicated, may hold values from 0.25 to 1.75
- key_gain: float32 [128], replicated, may hold values from 0.25 to 1.75
- output_weight: bfloat16 [2048, 2048], P('tensor'), may hold values from -1 to 1
- feedforward_gain: float32 [2048], replicated, may hold values from 0.5 to 1.5
- gate_weight: bfloat16 [2048, 6144], P(None, 'tensor'), may hold values from -0.125 to 0.125
- up_weight: bfloat16 [2048, 6144], P(None, 'tensor'), may hold values from -0.125 to 0.125
- down_weight: bfloat16 [6144, 2048], P('tensor'), may hold values from -0.078125 to 0.078125
- segment_numbers: int32 [8192], P('dp'), may hold values from 0 to 3, as said below
- positions: int32 [8192], P('dp'), may hold values from 0 to 2047, as said below
- cotangent: bfloat16 [8192, 2048], P('dp'), may hold values from -6 to 6
Outputs:
- layer_output: bfloat16 [8192, 2048], P('dp')
- tokens_gradient: bfloat16 [8192, 2048], P('dp')
- attention_gain_gradient: float32 [2048], P('dp')
- query_gradient: float32 [2048, 2048], P('dp', 'tensor')
- key_gradient: float32 [2048, 1024], P('dp', 'tensor')
- value_gradient: float32 [2048, 1024], P('dp', 'tensor')
- query_gain_gradient: float32 [128], P('dp')
- key_gain_gradient: float32 [128], P('dp')
- output_gradient: float32 [2048, 2048], P('tensor', 'dp')
- feedforward_gain_gradient: float32 [2048], P('dp')
- gate_gradient: float32 [2048, 6144], P('dp', 'tensor')
- up_gradient: float32 [2048, 6144], P('dp', 'tensor')
- down_gradient: float32 [6144, 2048], P('tensor', 'dp')
The draws below stay inside these ranges and needn't reach their ends.
Inputs may be any that keep to these rules, and one draw needn't show every extreme that they name: `segment_numbers`: each aligned sequence of 1024 tokens holds four documents numbered 0 to 3 in order, never falling, each of 128 tokens or more. `positions`: within a document the position rises by one from token to token; only the first document of a sequence may start at a position above 0, the others start at 0.
All inputs are finite; a program needn't handle non-finite values.
Results may differ from the reference program's by a relative error of at most 0.014.
Values sent between devices are 32-bit elements; how exact they have to be, the bound alone decides.
A program may use at most 256 MiB of HBM per device.

```python
import jax
import jax.numpy as jnp
from jax import lax

D = 2048
HQ = 16
KV = 8
HD = 128
FF = 6144
SEQ_LEN = 1024
TOKENS = 8192


def cut_points(key):
    count = TOKENS // SEQ_LEN
    jitter = jax.random.randint(key, (count, 3), -(SEQ_LEN // 16), SEQ_LEN // 16 + 1)
    base = (jnp.arange(1, 4, dtype=jnp.int32) * (SEQ_LEN // 4))[None, :]
    return base + jitter


def draw_segment_numbers(key, part):
    cuts = cut_points(key)
    index = jnp.arange(SEQ_LEN, dtype=jnp.int32)
    passed = (index[None, :, None] >= cuts[:, None, :]).astype(jnp.int32)
    return jnp.sum(passed, axis=2).reshape(TOKENS)


def draw_positions(key, part):
    cuts = cut_points(key)
    key = jax.random.fold_in(key, 5)
    count = TOKENS // SEQ_LEN
    first_length = cuts[:, 0:1]
    ceiling = 2 * SEQ_LEN - first_length
    offset = jax.random.randint(key, (count, 1), 0, ceiling + 1)
    sequence = jnp.arange(count, dtype=jnp.int32)[:, None]
    offset = jnp.where(sequence == 0, ceiling, offset)
    index = jnp.arange(SEQ_LEN, dtype=jnp.int32)
    starts = jnp.max(jnp.where(index[None, :, None] >= cuts[:, None, :], cuts[:, None, :], 0), axis=2)
    places = index[None, :] - starts + jnp.where(starts == 0, offset, 0)
    return places.reshape(TOKENS)


def raised(values, stream_key, source, target, blocks, factor):
    def block_of(position):
        return (jnp.arange(values.shape[position]) // (values.shape[position] // blocks)).reshape((-1,) + (1,) * (values.ndim - 1 - position))

    one_side = jax.random.permutation(stream_key, blocks)[block_of(target)]
    far = (block_of(target) + blocks // 2) % blocks
    return jnp.where((block_of(source) == one_side) | (block_of(source) == far), factor * values, values)


def shard_levels(own_key, dims, split, low, high):
    factor_of, own = 1.0, jax.random.fold_in(own_key, 6)
    for dim, parts in split:
        heights = jnp.exp(jax.random.uniform(jax.random.fold_in(own, dim), (parts,), jnp.float32, low / len(split), high / len(split)))
        factor_of = factor_of * jnp.repeat(heights, dims[dim] // parts).reshape([-1 if axis == dim else 1 for axis in range(len(dims))])
    return factor_of


def scatter_about(stream_key, dims, width, reach, cuts=(), kind=jnp.bfloat16):
    values = jax.random.normal(stream_key, dims, jnp.float32) * width
    if len(cuts) > 0:
        values = shard_levels(stream_key, dims, cuts, -0.22, 0.18) * values
    return jnp.clip(values, min=-reach, max=reach).astype(kind)


def heavy_noise(key, extent, scale, bound, cuts, heavy, kind=jnp.bfloat16):
    drawn = scale * jax.random.normal(key, extent, jnp.float32)
    if cuts:
        drawn = drawn * shard_levels(key, extent, cuts, -0.22, 0.18)
    return jnp.clip(raised(drawn, jax.random.fold_in(key, 3), *heavy), -bound, bound).astype(kind)


def setup_inputs(seed: int = 0) -> dict:
    key_of = jax.random.split(jax.random.key(seed), 16)
    tokens = heavy_noise(key_of[0], (TOKENS, D), 1.0, 6.0, ((0, 8),), (0, 1, 8, 2.0))
    attention_gain = jnp.clip(1.0 + 0.1 * jax.random.normal(key_of[1], (D,), jnp.float32), 0.5, 1.5)
    query_weight = scatter_about(key_of[2], (D, HQ * HD), D ** -0.5, 0.125, ((1, 4),))
    key_weight = scatter_about(key_of[3], (D, KV * HD), D ** -0.5, 0.125, ((1, 4),))
    value_weight = scatter_about(key_of[4], (D, KV * HD), D ** -0.5, 0.125, ((1, 4),))
    query_gain = jnp.clip(1.0 + 0.15 * jax.random.normal(key_of[5], (HD,), jnp.float32), 0.25, 1.75)
    key_gain = jnp.clip(1.0 + 0.15 * jax.random.normal(key_of[6], (HD,), jnp.float32), 0.25, 1.75)
    output_weight = scatter_about(key_of[7], (HQ * HD, D), (HQ * HD // 64) ** -0.5, 1.0, ((0, 4),))
    feedforward_gain = jnp.clip(1.0 + 0.1 * jax.random.normal(key_of[8], (D,), jnp.float32), 0.5, 1.5)
    gate_weight = scatter_about(key_of[9], (D, FF), D ** -0.5, 0.125, ((1, 4),))
    up_weight = scatter_about(key_of[10], (D, FF), D ** -0.5, 0.125, ((1, 4),))
    down_weight = scatter_about(key_of[11], (FF, D), FF ** -0.5, 0.078125, ((0, 4),))
    segment_numbers = draw_segment_numbers(jax.random.fold_in(key_of[15], 71), 0)
    positions = draw_positions(jax.random.fold_in(key_of[15], 71), 0)
    cotangent = heavy_noise(key_of[14], (TOKENS, D), 1.0, 6.0, ((0, 8),), (0, 1, 8, 2.0))
    return {"tokens": tokens, "attention_gain": attention_gain, "query_weight": query_weight, "key_weight": key_weight, "value_weight": value_weight, "query_gain": query_gain, "key_gain": key_gain, "output_weight": output_weight, "feedforward_gain": feedforward_gain, "gate_weight": gate_weight, "up_weight": up_weight, "down_weight": down_weight, "segment_numbers": segment_numbers, "positions": positions, "cotangent": cotangent}


@jax.custom_vjp
def low(v):
    return lax.optimization_barrier(v.astype(jnp.bfloat16)).astype(jnp.float32)

@jax.custom_vjp
def low_back(v):
    return v

def low_keep(v):
    return (low(v), None)

def low_pass(kept, grad):
    return (grad,)

def back_keep(v):
    return (v, None)

def back_low(kept, grad):
    return (low(grad),)
low.defvjp(low_keep, low_pass)
low_back.defvjp(back_keep, back_low)
epsilon = 1e-06
rope_base = 1000000.0
masked = -1e+30
highest = lax.Precision.HIGHEST

def rms_norm(value, gain):
    return value * lax.rsqrt(lax.optimization_barrier(jnp.mean(value * value, axis=-1, keepdims=True)) + epsilon) * gain

def rotary_tables(positions):
    exponent = jnp.arange(0, HD, 2, dtype=jnp.float32) / HD
    frequency = rope_base ** (-exponent)
    phase = positions.astype(jnp.float32)[:, None] * frequency[None, :]
    phase = jnp.concatenate([phase, phase], axis=-1)
    return (jnp.cos(phase), jnp.sin(phase))

def rotate(value, cosine, sine):
    half = value.shape[-1] // 2
    turned = jnp.concatenate([-value[..., half:], value[..., :half]], axis=-1)
    return value * cosine + turned * sine

def forward(inputs, weights, segments, positions):
    attention_gain, query_weight, key_weight, value_weight, query_gain, key_gain, output_weight, feedforward_gain, gate_weight, up_weight, down_weight = weights
    length = inputs.shape[0]
    group = HQ // KV
    normed = low(rms_norm(inputs, attention_gain))
    query_raw = low_back(jnp.dot(normed, query_weight, precision=highest)).reshape(length, HQ, HD)
    key_raw = low_back(jnp.dot(normed, key_weight, precision=highest)).reshape(length, KV, HD)
    values = low(low_back(jnp.dot(normed, value_weight, precision=highest))).reshape(length, KV, HD)
    cosine, sine = rotary_tables(positions)
    queries = low(rotate(rms_norm(query_raw, query_gain), cosine[:, None], sine[:, None]))
    keys = low(rotate(rms_norm(key_raw, key_gain), cosine[:, None], sine[:, None]))
    grouped = queries.reshape(length, KV, group, HD)
    scores = jnp.einsum('qkgd,tkd->kgqt', grouped, keys, precision=highest) * HD ** (-0.5)
    index = jnp.arange(length, dtype=jnp.int32)
    allowed = (segments[:, None] == segments[None, :]) & (index[:, None] >= index[None, :])
    scores = low_back(jnp.where(allowed[None, None], scores, masked))
    peak = lax.optimization_barrier(jnp.max(scores, axis=-1, keepdims=True))
    expons = jnp.exp(scores - peak)
    chance = low(expons / lax.optimization_barrier(jnp.sum(expons, axis=-1, keepdims=True)))
    mixed = jnp.einsum('kgqt,tkd->qkgd', chance, values, precision=highest).reshape(length, HQ * HD)
    mixed = low(low_back(mixed))
    attention = low_back(jnp.dot(mixed, output_weight, precision=highest))
    hidden = inputs + attention
    second = low(rms_norm(hidden, feedforward_gain))
    gate = low_back(jnp.dot(second, gate_weight, precision=highest))
    upward = low_back(jnp.dot(second, up_weight, precision=highest))
    product = low(jax.nn.silu(gate) * upward)
    feedforward = low_back(jnp.dot(product, down_weight, precision=highest))
    return hidden + feedforward

def reference(tokens, attention_gain, query_weight, key_weight, value_weight, query_gain, key_gain, output_weight, feedforward_gain, gate_weight, up_weight, down_weight, segment_numbers, positions, cotangent):
    weights = tuple((item.astype(jnp.float32) for item in (attention_gain, query_weight, key_weight, value_weight, query_gain, key_gain, output_weight, feedforward_gain, gate_weight, up_weight, down_weight)))
    count = TOKENS // SEQ_LEN
    inputs = tokens.astype(jnp.float32).reshape(count, SEQ_LEN, D)
    upstream = cotangent.astype(jnp.float32).reshape(count, SEQ_LEN, D)
    segments = segment_numbers.reshape(count, SEQ_LEN)
    places = positions.reshape(count, SEQ_LEN)

    def step(carry, item):
        block_inputs, block_segments, block_places, block_upstream = item

        def local(values, params):
            return forward(values, params, block_segments, block_places)
        result, pullback = jax.vjp(local, block_inputs, weights)
        input_grad, weight_grads = pullback(block_upstream)
        carry = jax.tree.map(lambda left, right: left + right, carry, weight_grads)
        return (carry, (result, input_grad))
    zeros = jax.tree.map(jnp.zeros_like, weights)
    totals, (results, input_grads) = lax.scan(step, zeros, (inputs, segments, places, upstream))
    layer_output = results.reshape(TOKENS, D).astype(jnp.bfloat16)
    tokens_gradient = input_grads.reshape(TOKENS, D).astype(jnp.bfloat16)
    return (layer_output, tokens_gradient, totals[0], totals[1], totals[2], totals[3], totals[4], totals[5], totals[6], totals[7], totals[8], totals[9], totals[10])
```

```python
import functools

import jax
import jax.numpy as jnp
from jax import lax
from jax.sharding import PartitionSpec as P

HD = 128
SEQ_LEN = 1024


epsilon = 1e-06
rope_base = 1000000.0
masked = -1e30


def rms_inverse(value):
    return lax.rsqrt(jnp.mean(value * value, axis=-1, keepdims=True) + epsilon)


def norm_back(upstream, value, inverse, gain):
    scaled = upstream * gain
    return inverse * scaled - value * inverse**3 * jnp.mean(scaled * value, axis=-1, keepdims=True)


def rotary_tables(positions):
    exponent = jnp.arange(0, HD, 2, dtype=jnp.float32) / HD
    frequency = rope_base ** (-exponent)
    phase = positions.astype(jnp.float32)[:, None] * frequency[None, :]
    phase = jnp.concatenate([phase, phase], axis=-1)
    return (jnp.cos(phase), jnp.sin(phase))


def rotate(value, cosine, sine):
    half = value.shape[-1] // 2
    turned = jnp.concatenate([-value[..., half:], value[..., :half]], axis=-1)
    return value * cosine + turned * sine


def rotate_back(upstream, cosine, sine):
    half = upstream.shape[-1] // 2
    moved = upstream * sine
    return upstream * cosine + jnp.concatenate([moved[..., half:], -moved[..., :half]], axis=-1)


def block_scores(query_rows, keys, row_segments, segments, begin):
    scores = jnp.einsum(
        "rkgd,tkd->kgrt", query_rows, keys, preferred_element_type=jnp.float32
    ) * HD ** (-0.5)
    rows = begin + lax.iota(jnp.int32, query_rows.shape[0])
    columns = lax.iota(jnp.int32, keys.shape[0])
    allowed = (row_segments[:, None] == segments[None, :]) & (rows[:, None] >= columns[None, :])
    return jnp.where(allowed[None, None], scores, masked)


def attend(item):
    queries, keys, values, segments = item
    length = queries.shape[0]
    width = min(512, length)
    outputs = []
    totals = []
    for begin in range(0, length, width):
        scores = block_scores(
            queries[begin : begin + width], keys, segments[begin : begin + width], segments, begin
        )
        peak = jnp.max(scores, axis=-1, keepdims=True)
        expons = jnp.exp(scores - peak)
        total = jnp.sum(expons, axis=-1, keepdims=True)
        chance_low = (expons / total).astype(jnp.bfloat16)
        outputs.append(
            jnp.einsum("kgrt,tkd->rkgd", chance_low, values, preferred_element_type=jnp.float32)
        )
        totals.append(peak + jnp.log(total))
    return (jnp.concatenate(outputs, axis=0), jnp.concatenate(totals, axis=2))


def attend_back(item):
    queries, keys, values, segments, totals, upstream = item
    length = queries.shape[0]
    width = min(512, length)
    query_parts = []
    key_grad = jnp.zeros(keys.shape, jnp.float32)
    value_grad = jnp.zeros(values.shape, jnp.float32)
    for begin in range(0, length, width):
        rows = queries[begin : begin + width]
        scores = block_scores(rows, keys, segments[begin : begin + width], segments, begin)
        chance = jnp.exp(scores - totals[:, :, begin : begin + width])
        chance_low = chance.astype(jnp.bfloat16)
        incoming = upstream[begin : begin + width]
        value_grad = value_grad + jnp.einsum(
            "kgrt,rkgd->tkd", chance_low, incoming, preferred_element_type=jnp.float32
        )
        along = jnp.einsum("rkgd,tkd->kgrt", incoming, values, preferred_element_type=jnp.float32)
        center = jnp.sum(along * chance, axis=-1, keepdims=True)
        score_grad = (chance * (along - center)).astype(jnp.bfloat16)
        query_parts.append(
            jnp.einsum("kgrt,tkd->rkgd", score_grad, keys, preferred_element_type=jnp.float32)
            * HD ** (-0.5)
        )
        key_grad = key_grad + jnp.einsum(
            "kgrt,rkgd->tkd", score_grad, rows, preferred_element_type=jnp.float32
        ) * HD ** (-0.5)
    return (jnp.concatenate(query_parts, axis=0), key_grad, value_grad)


def dot(left, right):
    return jnp.dot(left, right, preferred_element_type=jnp.float32)


def dot_back(left, right):
    return jnp.einsum("tc,dc->td", left, right, preferred_element_type=jnp.float32)


def dot_tokens(left, right):
    return jnp.einsum("tm,tn->mn", left, right, preferred_element_type=jnp.float32)


def line_pairs(high, step, towards):
    pairs = []
    for place in range(high):
        if towards > 0 and place < step and place + 1 < high:
            pairs.append((place, place + 1))
        if towards < 0 and high - 1 - place < step and place - 1 >= 0:
            pairs.append((place, place - 1))
    return [(2 * a + lane, 2 * b + lane) for a, b in pairs for lane in (0, 1)]


def choose(index, candidates):
    value = candidates[0][1]
    for place, candidate in candidates[1:]:
        value = jnp.where(index == place, candidate, value)
    return value


def swap_core(value):
    return lax.ppermute(value, "tensor", [(i, i ^ 1) for i in range(4)])


def swap_chip(value):
    return lax.ppermute(value, "tensor", [(i, i ^ 2) for i in range(4)])


class Ticks:
    def __init__(self, dp):
        self.arrived = []
        self.tensor = [(i, i ^ 2) for i in range(4)]
        self.lane = [(i, i ^ 1) for i in range(dp)]
        self.pair = [(i, i ^ 2) for i in range(dp)]

    def __call__(self, **sends):
        names = list(sends)
        values = []
        for name in names:
            values.append(sends[name][0])
        held = lax.optimization_barrier((values, self.arrived))[0]
        moved = {}
        for name, value in zip(names, held):
            axis, pairs = sends[name][1:]
            moved[name] = lax.ppermute(value, axis, pairs)
        self.arrived = list(moved.values())
        return moved


def shards(
    dp,
    tokens,
    attention_gain,
    query_weight,
    key_weight,
    value_weight,
    query_gain,
    key_gain,
    output_weight,
    feedforward_gain,
    gate_weight,
    up_weight,
    down_weight,
    segment_numbers,
    positions,
    cotangent,
):
    chunks = 4
    count, depth = tokens.shape
    batch = count // SEQ_LEN
    query_heads = query_weight.shape[1] // HD
    value_heads = key_weight.shape[1] // HD
    group = query_heads // value_heads
    width = depth // dp
    high = dp // 2
    teams = high // 2
    half = count // 2
    size = half // chunks
    place = lax.axis_index("dp") // 2
    lane = lax.axis_index("dp") % 2
    team = place // 2
    side = place % 2
    core = lax.axis_index("tensor") % 2
    tick = Ticks(dp)
    over_x = lambda value: (value, "tensor", tick.tensor)
    over_y = lambda value: (value, "dp", tick.lane)
    over_z = lambda value: (value, "dp", tick.pair)

    def chunk(array, index):
        begin = index * size
        return jnp.concatenate(
            [array[begin : begin + size], array[half + begin : half + begin + size]], axis=0
        )

    def unchunk(parts):
        return jnp.concatenate([p[:size] for p in parts] + [p[size:] for p in parts], axis=0)

    def mine(part):
        rows = part.shape[0] // 2
        return lax.dynamic_slice_in_dim(part, core * rows, rows, 0)

    def theirs(part):
        rows = part.shape[0] // 2
        return lax.dynamic_slice_in_dim(part, (1 - core) * rows, rows, 0)

    def both(own):
        other = swap_core(own)
        return jnp.concatenate(
            [jnp.where(core == 0, own, other), jnp.where(core == 0, other, own)], axis=0
        )

    def cores_sum(part):
        return mine(part) + swap_core(theirs(part))

    upstream_wide = lax.dynamic_slice_in_dim(cotangent, core * half, half, 0).astype(jnp.float32)
    partner_cotangent = [None] * chunks

    def keep_cotangent(moved, first, number):
        pieces = both(moved) + attention_gain * 0.0
        rows = number * size
        for index in range(number):
            partner_cotangent[first + index] = jnp.concatenate(
                [
                    pieces[index * size : (index + 1) * size],
                    pieces[rows + index * size : rows + (index + 1) * size],
                ],
                axis=0,
            ).astype(jnp.bfloat16)

    moved = tick(z=over_z(upstream_wide[: 2 * size]))
    keep_cotangent(moved["z"], 0, 2)

    inputs = tokens.astype(jnp.float32)
    first_inverse = rms_inverse(inputs)
    first_normed = inputs * first_inverse
    normed_low = (first_normed * attention_gain).astype(jnp.bfloat16)
    query_raw = dot(normed_low, query_weight).reshape(count, query_heads, HD)
    key_raw = dot(normed_low, key_weight).reshape(count, value_heads, HD)
    value_low = dot(normed_low, value_weight).astype(jnp.bfloat16)
    cosine, sine = rotary_tables(positions)
    cosine = cosine[:, None]
    sine = sine[:, None]
    query_inverse = rms_inverse(query_raw)
    query_unit = query_raw * query_inverse
    query_low = rotate(query_unit * query_gain, cosine, sine).astype(jnp.bfloat16)
    key_inverse = rms_inverse(key_raw)
    key_unit = key_raw * key_inverse
    key_low = rotate(key_unit * key_gain, cosine, sine).astype(jnp.bfloat16)
    queries = query_low.reshape(batch, SEQ_LEN, value_heads, group, HD)
    keys = key_low.reshape(batch, SEQ_LEN, value_heads, HD)
    values = value_low.reshape(batch, SEQ_LEN, value_heads, HD)
    segments = segment_numbers.reshape(batch, SEQ_LEN)
    mixed, totals = lax.map(attend, (queries, keys, values, segments))
    mixed_low = mixed.reshape(count, query_heads * HD).astype(jnp.bfloat16)

    def attention_part(index):
        return over_x(cores_sum(dot(chunk(mixed_low, index), output_weight)))

    def feed(normed, upstream):
        low = (normed * feedforward_gain).astype(jnp.bfloat16)
        gate = dot(low, gate_weight)
        upward = dot(low, up_weight)
        grad = dot_back(upstream, down_weight)
        sigmoid_gate = jax.nn.sigmoid(gate)
        activated = gate * sigmoid_gate
        product = (activated * upward).astype(jnp.bfloat16)
        gate_grad = (
            grad * upward * sigmoid_gate * (1.0 + gate * (1.0 - sigmoid_gate))
        ).astype(jnp.bfloat16)
        upward_grad = (grad * activated).astype(jnp.bfloat16)
        return (low, product, gate_grad, upward_grad)

    hidden = [None] * chunks
    second_inverse = [None] * chunks
    second_normed = [None] * chunks
    fed = [None] * (2 * chunks)

    def finish_attention(sent, moved, index):
        hidden[index] = chunk(tokens, index).astype(jnp.float32) + both(sent[0] + moved)
        second_inverse[index] = rms_inverse(hidden[index])
        second_normed[index] = hidden[index] * second_inverse[index]
        fed[index] = feed(second_normed[index], chunk(cotangent, index))

    def finish_partner(moved, index):
        fed[chunks + index] = feed(both(moved), partner_cotangent[index])

    second_parts = [None] * chunks

    def second_part(index):
        _, _, gate_grad, upward_grad = fed[index]
        second_parts[index] = dot_back(gate_grad, gate_weight) + dot_back(upward_grad, up_weight)
        return over_x(cores_sum(second_parts[index]))

    hidden_grad = [None] * chunks

    def finish_second(sent, moved, index):
        hidden_grad[index] = chunk(cotangent, index).astype(jnp.float32) + norm_back(
            both(sent[0] + moved), hidden[index], second_inverse[index], feedforward_gain
        )

    att = [attention_part(index) for index in range(chunks)]
    moved = tick(x=att[0], z=over_z(upstream_wide[2 * size : 3 * size]))
    keep_cotangent(moved["z"], 2, 1)
    finish_attention(att[0], moved["x"], 0)
    moved = tick(x=att[1], z=over_z(upstream_wide[3 * size :]))
    keep_cotangent(moved["z"], 3, 1)
    finish_attention(att[1], moved["x"], 1)
    moved = tick(x=att[2], z=over_z(mine(second_normed[0])))
    finish_attention(att[2], moved["x"], 2)
    finish_partner(moved["z"], 0)
    moved = tick(x=att[3], z=over_z(mine(second_normed[1])))
    finish_attention(att[3], moved["x"], 3)
    finish_partner(moved["z"], 1)
    sec = second_part(0)
    moved = tick(x=sec, z=over_z(mine(second_normed[2])))
    finish_second(sec, moved["x"], 0)
    finish_partner(moved["z"], 2)
    sec = second_part(1)
    moved = tick(x=sec, z=over_z(mine(second_normed[3])))
    finish_second(sec, moved["x"], 1)
    finish_partner(moved["z"], 3)

    second_low, product_low, gate_grad_low, upward_grad_low = (
        jnp.concatenate(parts, axis=0) for parts in zip(*fed)
    )
    upstream_low = jnp.concatenate(
        [chunk(cotangent, index) for index in range(chunks)] + partner_cotangent, axis=0
    )

    def column(turn, which):
        return side * (depth // 2) + (2 * ((team + turn) % teams) + which) * width

    def block(kind, turn, which):
        left, right, transposed = {
            "down": (upstream_low, product_low, True),
            "gate": (second_low, gate_grad_low, False),
            "up": (second_low, upward_grad_low, False),
        }[kind]
        piece = lax.dynamic_slice_in_dim(left, column(turn, which), width, 1)
        return dot_tokens(right, piece) if transposed else dot_tokens(piece, right)

    def team_send(value, turn):
        pairs = []
        for place_from in range(high):
            t, s = place_from // 2, place_from % 2
            goal = s * teams + (t + turn) % teams
            pairs += [(2 * place_from + k, 2 * goal + k) for k in (0, 1)]
        return (value, "dp", pairs)

    weights = {"down": None, "gate": None, "up": None}
    order = [(kind, turn) for kind in weights for turn in range(teams)]
    waiting = None
    x_work = [("second", 2), ("second", 3)]
    x_work += [("out", index) for index in range(chunks)]
    layer_parts = [None] * chunks
    for kind, turn in order + [(None, None)]:
        sends = {}
        if kind is not None:
            sends["y"] = over_y(block(kind, turn, 1 - lane))
        if waiting is not None:
            sends["z"] = team_send(waiting[2], waiting[1])
        what = None
        if x_work:
            what, index = x_work.pop(0)
            if what == "second":
                sent = second_part(index)
            else:
                sent = over_x(cores_sum(dot(fed[index][1], down_weight)))
            sends["x"] = sent
        moved = tick(**sends)
        if waiting is not None:
            old = weights[waiting[0]]
            weights[waiting[0]] = moved["z"] if old is None else old + moved["z"]
        if what == "second":
            finish_second(sent, moved["x"], index)
        elif what == "out":
            layer_parts[index] = (hidden[index] + both(sent[0] + moved["x"])).astype(jnp.bfloat16)
        if kind is not None:
            waiting = (kind, turn, block(kind, turn, lane) + moved["y"])

    hidden_low = unchunk([part.astype(jnp.bfloat16) for part in hidden_grad])
    mixed_grad = dot_back(hidden_low, output_weight).astype(jnp.bfloat16)
    upstream = mixed_grad.reshape(batch, SEQ_LEN, value_heads, group, HD)
    query_back, key_back, value_back = lax.map(
        attend_back, (queries, keys, values, segments, totals, upstream)
    )
    query_unit_grad = rotate_back(query_back.reshape(count, query_heads, HD), cosine, sine)
    key_unit_grad = rotate_back(key_back.reshape(count, value_heads, HD), cosine, sine)
    query_gain_part = jnp.sum(query_unit_grad * query_unit, axis=(0, 1))
    key_gain_part = jnp.sum(key_unit_grad * key_unit, axis=(0, 1))
    query_raw_grad = (
        norm_back(query_unit_grad, query_raw, query_inverse, query_gain)
        .reshape(count, query_heads * HD)
        .astype(jnp.bfloat16)
    )
    key_raw_grad = (
        norm_back(key_unit_grad, key_raw, key_inverse, key_gain)
        .reshape(count, value_heads * HD)
        .astype(jnp.bfloat16)
    )
    value_raw_grad = value_back.reshape(count, value_heads * HD).astype(jnp.bfloat16)
    raw_grad = jnp.concatenate([query_raw_grad, key_raw_grad, value_raw_grad], axis=1)

    first_parts = [
        dot_back(chunk(query_raw_grad, index), query_weight)
        + dot_back(chunk(key_raw_grad, index), key_weight)
        + dot_back(chunk(value_raw_grad, index), value_weight)
        for index in range(chunks)
    ]
    second_gain_part = sum(
        jnp.sum(part * normed, axis=0) for part, normed in zip(second_parts, second_normed)
    )
    first_gain_part = sum(
        jnp.sum(part * chunk(first_normed, index), axis=0)
        for index, part in enumerate(first_parts)
    )
    head_width = HD // dp

    def gain_rows(spot):
        lines = jnp.zeros((8, raw_grad.shape[1]), jnp.float32)
        for row, (value, length) in enumerate(
            [
                (second_gain_part, width),
                (first_gain_part, width),
                (query_gain_part, head_width),
                (key_gain_part, head_width),
            ]
        ):
            taken = lax.dynamic_slice_in_dim(value, spot * length, length, 0)
            lines = lines.at[row, :length].set(taken)
        return lines

    def head_block(spot, which):
        begin = (2 * spot + which) * width
        piece = lax.dynamic_slice_in_dim(normed_low, begin, width, 1)
        raw = dot_tokens(piece, raw_grad)
        raw = jnp.concatenate([raw, gain_rows(2 * spot + which)], axis=0)
        piece = lax.dynamic_slice_in_dim(hidden_low, begin, width, 1)
        return (raw, dot_tokens(mixed_low, piece))

    raw_blocks = [None] * high
    out_blocks = [None] * high
    spots = [high - 1 - turn // 2 if turn % 2 == 0 else turn // 2 for turn in range(high)]
    tokens_parts = [None] * chunks
    x_work = list(range(chunks))
    raw_right = raw_left = out_right = out_left = None
    step = 1
    for turn in range(2 * high):
        sends = {}
        if turn < high:
            raw_sent, out_sent = head_block(spots[turn], 1 - lane)
            sends["y"] = over_y(raw_sent)
            sends["y_out"] = over_y(out_sent)
        needed = list(range(high - step, high)) + list(range(step))
        moving = step < high and all(raw_blocks[spot] is not None for spot in needed)
        if moving:
            for name, blocks, carry, towards in (
                ("raw_right", raw_blocks, raw_right, 1),
                ("raw_left", raw_blocks, raw_left, -1),
                ("out_right", out_blocks, out_right, 1),
                ("out_left", out_blocks, out_left, -1),
            ):
                if towards > 0:
                    options = [(p, blocks[p + high - step]) for p in range(step)]
                else:
                    options = [(high - 1 - p, blocks[step - 1 - p]) for p in range(step)]
                value = choose(place, options)
                if carry is not None:
                    value = value + carry
                sends[name] = (value, "dp", line_pairs(high, step, towards))
        if x_work:
            index = x_work.pop(0)
            sent = over_x(cores_sum(first_parts[index]))
            sends["x"] = sent
        else:
            index = None
        if not sends:
            break
        moved = tick(**sends)
        if index is not None:
            tokens_parts[index] = (
                hidden_grad[index]
                + norm_back(
                    both(sent[0] + moved["x"]),
                    chunk(tokens, index).astype(jnp.float32),
                    chunk(first_inverse, index),
                    attention_gain,
                )
            ).astype(jnp.bfloat16)
        if turn < high:
            raw_kept, out_kept = head_block(spots[turn], lane)
            raw_blocks[spots[turn]] = raw_kept + moved["y"]
            out_blocks[spots[turn]] = out_kept + moved["y_out"]
        if moving:
            raw_right, raw_left = moved["raw_right"], moved["raw_left"]
            out_right, out_left = moved["out_right"], moved["out_left"]
            step += 1
    raw_whole = choose(place, list(enumerate(raw_blocks))) + raw_right + raw_left
    output_weight_grad = choose(place, list(enumerate(out_blocks))) + out_right + out_left
    gains = raw_whole[width:, :width]
    gains = gains + swap_core(gains)
    gains = gains + swap_chip(gains)
    columns_query = query_weight.shape[1]
    columns_key = columns_query + key_weight.shape[1]
    return (
        unchunk(layer_parts),
        unchunk(tokens_parts),
        gains[1],
        raw_whole[:width, :columns_query],
        raw_whole[:width, columns_query:columns_key],
        raw_whole[:width, columns_key:],
        gains[2, :head_width],
        gains[3, :head_width],
        output_weight_grad,
        gains[0],
        weights["gate"],
        weights["up"],
        weights["down"],
    )


def solution(mesh):
    return jax.shard_map(
        functools.partial(shards, mesh.shape["dp"]),
        mesh=mesh,
        in_specs=(
            P("dp", None),
            P(),
            P(None, "tensor"),
            P(None, "tensor"),
            P(None, "tensor"),
            P(),
            P(),
            P("tensor", None),
            P(),
            P(None, "tensor"),
            P(None, "tensor"),
            P("tensor", None),
            P("dp"),
            P("dp"),
            P("dp", None),
        ),
        out_specs=(
            P("dp", None),
            P("dp", None),
            P("dp"),
            P("dp", "tensor"),
            P("dp", "tensor"),
            P("dp", "tensor"),
            P("dp"),
            P("dp"),
            P("tensor", "dp"),
            P("dp"),
            P("dp", "tensor"),
            P("dp", "tensor"),
            P("tensor", "dp"),
        ),
        check_vma=False,
    )
```

```python
import functools

import jax
import jax.numpy as jnp
from jax import lax
from jax.experimental import pallas as pl
from jax.experimental.pallas import tpu as pltpu
from jax.sharding import PartitionSpec as P

HD = 128
SEQ_LEN = 1024


epsilon = 1e-06
rope_base = 1000000.0
masked = -1e30


def rms_inverse(value):
    return lax.rsqrt(jnp.mean(value * value, axis=-1, keepdims=True) + epsilon)


def norm_back(upstream, value, inverse, gain):
    scaled = upstream * gain
    return inverse * scaled - value * inverse**3 * jnp.mean(scaled * value, axis=-1, keepdims=True)


def rotary_tables(positions):
    exponent = jnp.arange(0, HD, 2, dtype=jnp.float32) / HD
    frequency = rope_base ** (-exponent)
    phase = positions.astype(jnp.float32)[:, None] * frequency[None, :]
    phase = jnp.concatenate([phase, phase], axis=-1)
    return (jnp.cos(phase), jnp.sin(phase))


def rotate(value, cosine, sine):
    half = value.shape[-1] // 2
    turned = jnp.concatenate([-value[..., half:], value[..., :half]], axis=-1)
    return value * cosine + turned * sine


def rotate_back(upstream, cosine, sine):
    half = upstream.shape[-1] // 2
    moved = upstream * sine
    return upstream * cosine + jnp.concatenate([moved[..., half:], -moved[..., :half]], axis=-1)


def block_scores(query_rows, keys, row_segments, segments, begin):
    scores = jnp.einsum(
        "rkgd,tkd->kgrt", query_rows, keys, preferred_element_type=jnp.float32
    ) * HD ** (-0.5)
    rows = begin + lax.iota(jnp.int32, query_rows.shape[0])
    columns = lax.iota(jnp.int32, keys.shape[0])
    allowed = (row_segments[:, None] == segments[None, :]) & (rows[:, None] >= columns[None, :])
    return jnp.where(allowed[None, None], scores, masked)


def attend(item):
    queries, keys, values, segments = item
    length = queries.shape[0]
    width = min(512, length)
    outputs = []
    totals = []
    for begin in range(0, length, width):
        scores = block_scores(
            queries[begin : begin + width], keys, segments[begin : begin + width], segments, begin
        )
        peak = jnp.max(scores, axis=-1, keepdims=True)
        expons = jnp.exp(scores - peak)
        total = jnp.sum(expons, axis=-1, keepdims=True)
        chance_low = (expons / total).astype(jnp.bfloat16)
        outputs.append(
            jnp.einsum("kgrt,tkd->rkgd", chance_low, values, preferred_element_type=jnp.float32)
        )
        totals.append(peak + jnp.log(total))
    return (jnp.concatenate(outputs, axis=0), jnp.concatenate(totals, axis=2))


def attend_back(item):
    queries, keys, values, segments, totals, upstream = item
    length = queries.shape[0]
    width = min(512, length)
    query_parts = []
    key_grad = jnp.zeros(keys.shape, jnp.float32)
    value_grad = jnp.zeros(values.shape, jnp.float32)
    for begin in range(0, length, width):
        rows = queries[begin : begin + width]
        scores = block_scores(rows, keys, segments[begin : begin + width], segments, begin)
        chance = jnp.exp(scores - totals[:, :, begin : begin + width])
        chance_low = chance.astype(jnp.bfloat16)
        incoming = upstream[begin : begin + width]
        value_grad = value_grad + jnp.einsum(
            "kgrt,rkgd->tkd", chance_low, incoming, preferred_element_type=jnp.float32
        )
        along = jnp.einsum("rkgd,tkd->kgrt", incoming, values, preferred_element_type=jnp.float32)
        center = jnp.sum(along * chance, axis=-1, keepdims=True)
        score_grad = (chance * (along - center)).astype(jnp.bfloat16)
        query_parts.append(
            jnp.einsum("kgrt,tkd->rkgd", score_grad, keys, preferred_element_type=jnp.float32)
            * HD ** (-0.5)
        )
        key_grad = key_grad + jnp.einsum(
            "kgrt,rkgd->tkd", score_grad, rows, preferred_element_type=jnp.float32
        ) * HD ** (-0.5)
    return (jnp.concatenate(query_parts, axis=0), key_grad, value_grad)


def dot(left, right):
    return jnp.dot(left, right, preferred_element_type=jnp.float32)


def dot_back(left, right):
    return jnp.einsum("tc,dc->td", left, right, preferred_element_type=jnp.float32)


def dot_tokens(left, right):
    return jnp.einsum("tm,tn->mn", left, right, preferred_element_type=jnp.float32)


def line_order(high, place):
    steps = {}
    for block in range(high):
        if block > place:
            steps[block] = high - block + place
        elif block < place:
            steps[block] = high - place + block
    return sorted(steps, key=lambda block: (steps[block], block)) + [place]


def swap_core(value):
    return lax.ppermute(value, "tensor", [(i, i ^ 1) for i in range(4)])


def swap_chip(value):
    return lax.ppermute(value, "tensor", [(i, i ^ 2) for i in range(4)])


MESH = pl.DeviceIdType.MESH


def neighbours():
    dp, tensor = lax.axis_index("dp"), lax.axis_index("tensor")
    core = lax.rem(tensor, 2)
    sibling = {"tensor": tensor + 1 - 2 * core}
    facing = {"tensor": lax.rem(tensor + 2, 4)}
    place = dp // 2
    pair = {"dp": dp + 2 * (1 - 2 * lax.rem(place, 2))}
    return core, sibling, facing, pair


def greet(devices):
    barrier = pltpu.get_barrier_semaphore()
    for device in devices:
        pl.semaphore_signal(barrier, inc=1, device_id=device, device_id_type=MESH)
    pl.semaphore_wait(barrier, len(devices))


def loop_rows(count, step, body):
    def run(index, carry):
        body(pl.ds(pl.multiple_of(index * step, step), step))
        return carry

    lax.fori_loop(0, count // step, run, 0)


def front_kernel(
    size,
    mixed_hbm, output_weight_hbm, tokens_hbm, upstream_hbm, upstream_first,
    gain, gate_hbm, up_hbm, down_hbm,
    hidden_out, second_out, low_own, product_own, gate_own, upward_own,
    low_pair, product_pair, gate_pair, upward_pair, upstream_pair,
    n_recv, n_side, u_recv, u_side,
    mixed, output_weight, gate_weight, up_weight, down_weight,
    c_recv, x_send, x_recv, back_recv, tok, hid, z_send, low, rows16, tiles,
    stage, stage16, terms,
    load_sems, c_sems, x_sems, back_sems, n_sems, n_side_sems, u_sems, u_side_sems,
    tok_sems, hid_sems, low_sems, wave_sems, tile_sems, stage_sems, stage16_sems, term_sems,
):
    core, sibling, facing, pair = neighbours()
    depth = gain.shape[1]
    half = 4 * size
    tile = tiles.shape[-1]
    units = gate_weight.shape[1]

    def begin(which, k):
        side = core if which == 0 else 1 - core
        return pl.multiple_of(side * half + k * size, size)

    def remote(source, target, sems, k, device):
        return pltpu.make_async_remote_copy(
            src_ref=source, dst_ref=target, send_sem=sems.at[0, k], recv_sem=sems.at[1, k],
            device_id=device, device_id_type=MESH,
        )

    loads = [
        pltpu.make_async_copy(source, target, load_sems.at[index])
        for index, (source, target) in enumerate(
            [
                (mixed_hbm, mixed),
                (output_weight_hbm, output_weight),
                (gate_hbm, gate_weight),
                (up_hbm, up_weight),
                (down_hbm, down_weight),
            ]
        )
    ]
    for load in loads:
        load.start()
    greet([sibling, facing, pair])

    c_copies = [remote(terms.at[pl.ds(k * size, size)], c_recv.at[k], c_sems, k, sibling) for k in range(4)]
    x_copies = [remote(x_send.at[k], x_recv.at[k], x_sems, k, facing) for k in range(4)]
    back_copies = [remote(x_send.at[k], back_recv.at[k], back_sems, k, sibling) for k in range(4)]
    n_copies = [remote(z_send.at[k % 2], n_recv.at[k], n_sems, k, pair) for k in range(4)]
    n_sides = [remote(n_recv.at[k], n_side.at[k], n_side_sems, k, sibling) for k in range(4)]
    u_copies = [
        None if k < 2 else remote(z_send.at[k % 2], u_recv.at[k], u_sems, k, pair) for k in range(4)
    ]
    u_sources = [
        upstream_first.at[pl.ds(k * size, size)] if k < 2 else u_recv.at[k] for k in range(4)
    ]
    u_sides = [remote(u_sources[k], u_side.at[k], u_side_sems, k, sibling) for k in range(4)]

    def attention_terms(k):
        def run(column):
            x_send[k, :, column] = jnp.dot(
                mixed[pl.ds(begin(0, k), size), :],
                output_weight[:, column],
                preferred_element_type=jnp.float32,
            )
            terms[pl.ds(k * size, size), column] = jnp.dot(
                mixed[pl.ds(begin(1, k), size), :],
                output_weight[:, column],
                preferred_element_type=jnp.float32,
            )

        loop_rows(depth, 512, run)
        c_copies[k].start()

    def attention_cores(k):
        c_copies[k].wait_recv()

        def run(row):
            x_send[k, row, :] = x_send[k, row, :] + c_recv[k, row, :]

        loop_rows(size, 16, run)
        x_copies[k].start()

    def attention_chips(k):
        x_copies[k].wait()

        def run(row):
            x_send[k, row, :] = x_send[k, row, :] + x_recv[k, row, :]

        loop_rows(size, 16, run)
        back_copies[k].start()

    def token_loads(k):
        return [
            pltpu.make_async_copy(
                tokens_hbm.at[pl.ds(begin(which, k), size)],
                tok.at[k % 2, which],
                tok_sems.at[k % 2, which],
            )
            for which in range(2)
        ]

    def hidden_stores(k):
        return [
            pltpu.make_async_copy(
                hid.at[which], hidden_out.at[pl.ds(begin(which, k), size)], hid_sems.at[which]
            )
            for which in range(2)
        ]

    def low_rows(buffer, which, k, row):
        side = core if which == 0 else 1 - core
        return pl.ds(pl.multiple_of((2 * side + k % 2) * size + row.start, 16), row.size)

    def normed(k):
        for load in token_loads(k):
            load.wait()
        back_copies[k].wait_recv()
        if k > 0:
            for store in hidden_stores(k - 1):
                store.wait()
        if k >= 2:
            n_copies[k - 2].wait_send()

        def run(which, source, row):
            value = tok[k % 2, which, row, :].astype(jnp.float32) + source[k, row, :]
            hid[which, row, :] = value
            unit = value * lax.rsqrt(jnp.mean(value * value, axis=-1, keepdims=True) + epsilon)
            if which == 0:
                z_send[k % 2, row, :] = unit
            low[0, low_rows(low, which, k, row), :] = (unit * gain[...]).astype(jnp.bfloat16)

        loop_rows(size, 16, functools.partial(run, 0, x_send))
        n_copies[k].start()
        loop_rows(size, 16, functools.partial(run, 1, back_recv))
        for store in hidden_stores(k):
            store.start()
        if k + 2 < 4:
            for load in token_loads(k + 2):
                load.start()

    def stage_load(source, slot):
        return pltpu.make_async_copy(source, stage.at[slot], stage_sems.at[slot])

    def pair_rows(k):
        n_copies[k].wait_recv()
        n_sides[k].start()
        stage_load(n_recv.at[k], 0).start()
        stage_load(n_recv.at[k], 0).wait()

        def run(which, row):
            low[1, low_rows(low, which, k, row), :] = (stage[which, row, :] * gain[...]).astype(
                jnp.bfloat16
            )

        loop_rows(size, 16, functools.partial(run, 0))
        n_sides[k].wait_recv()
        stage_load(n_side.at[k], 1).start()
        stage_load(n_side.at[k], 1).wait()
        loop_rows(size, 16, functools.partial(run, 1))

    def upstream_send(k):
        load = pltpu.make_async_copy(
            upstream_hbm.at[pl.ds(begin(0, k), size)], stage16.at[0], stage16_sems.at[0]
        )
        load.start()
        load.wait()

        def run(row):
            z_send[k % 2, row, :] = stage16[0, row, :].astype(jnp.float32)

        loop_rows(size, 16, run)
        u_copies[k].start()

    def upstream_rows(k):
        if k >= 2:
            u_copies[k].wait_recv()
        u_sides[k].start()
        for which in range(2):
            if which == 1:
                u_sides[k].wait_recv()
            source = u_sources[k] if which == 0 else u_side.at[k]
            stage_load(source, which).start()
            stage_load(source, which).wait()

            def run(row):
                stage16[which, row, :] = stage[which, row, :].astype(jnp.bfloat16)

            loop_rows(size, 16, run)
            store = pltpu.make_async_copy(
                stage16.at[which],
                upstream_pair.at[pl.ds(begin(which, k), size)],
                stage16_sems.at[which],
            )
            store.start()
            store.wait()

    def wave_rows(wave, part):
        return pl.ds(part * half + wave * 2 * size, 2 * size)

    def term_stores(wave):
        return [
            pltpu.make_async_copy(
                terms.at[pl.ds(part * 2 * size, 2 * size)],
                second_out.at[wave_rows(wave, part)],
                term_sems.at[part],
            )
            for part in range(2)
        ]

    def feed(wave, index):
        source = upstream_pair if index else upstream_hbm
        low_out, *outs = (
            (low_pair, product_pair, gate_pair, upward_pair)
            if index
            else (low_own, product_own, gate_own, upward_own)
        )
        fetches = [
            pltpu.make_async_copy(
                source.at[wave_rows(wave, part)],
                rows16.at[pl.ds(part * 2 * size, 2 * size)],
                wave_sems.at[part],
            )
            for part in range(2)
        ]
        low_stores = [
            pltpu.make_async_copy(
                low.at[index, pl.ds(part * 2 * size, 2 * size)],
                low_out.at[wave_rows(wave, part)],
                low_sems.at[part],
            )
            for part in range(2)
        ]
        for copy in fetches + low_stores:
            copy.start()
        if index == 0 and wave > 0:
            for copy in term_stores(wave - 1):
                copy.wait()
        for copy in fetches:
            copy.wait()

        def stores(j, slot):
            return [
                pltpu.make_async_copy(
                    tiles.at[slot, which, pl.ds(part * 2 * size, 2 * size)],
                    outs[which].at[
                        wave_rows(wave, part), pl.ds(pl.multiple_of(j * tile, tile), tile)
                    ],
                    tile_sems.at[slot, which, part],
                )
                for which in range(3)
                for part in range(2)
            ]

        def run(j, carry):
            slot = lax.rem(j, 2)
            column = pl.ds(pl.multiple_of(j * tile, tile), tile)
            gate = jnp.dot(
                low[index], gate_weight[:, column], preferred_element_type=jnp.float32
            )
            upward = jnp.dot(
                low[index], up_weight[:, column], preferred_element_type=jnp.float32
            )
            grad = lax.dot_general(
                rows16[...],
                down_weight[column, :],
                (((1,), (1,)), ((), ())),
                preferred_element_type=jnp.float32,
            )
            sigmoid_gate = jax.nn.sigmoid(gate)
            activated = gate * sigmoid_gate

            @pl.when(j >= 2)
            def _():
                for store in stores(j - 2, slot):
                    store.wait()

            tiles[slot, 0] = (activated * upward).astype(jnp.bfloat16)
            gate_grad = (
                grad * upward * sigmoid_gate * (1.0 + gate * (1.0 - sigmoid_gate))
            ).astype(jnp.bfloat16)
            upward_grad = (grad * activated).astype(jnp.bfloat16)
            tiles[slot, 1] = gate_grad
            tiles[slot, 2] = upward_grad
            for store in stores(j, slot):
                store.start()
            if index == 0:
                across_last = (((1,), (1,)), ((), ()))
                for first in range(0, depth, depth // 4):
                    part = pl.ds(first, depth // 4)
                    term = lax.dot_general(
                        gate_grad,
                        gate_weight[part, column],
                        across_last,
                        preferred_element_type=jnp.float32,
                    ) + lax.dot_general(
                        upward_grad,
                        up_weight[part, column],
                        across_last,
                        preferred_element_type=jnp.float32,
                    )

                    @pl.when(j == 0)
                    def _():
                        terms[:, part] = term

                    @pl.when(j > 0)
                    def _():
                        terms[:, part] += term

            return carry

        number = units // tile
        lax.fori_loop(0, number, run, 0)
        for j in range(max(0, number - 2), number):
            for store in stores(j, j % 2):
                store.wait()
        for copy in low_stores:
            copy.wait()
        if index == 0:
            for copy in term_stores(wave):
                copy.start()

    for k in range(2):
        for load in token_loads(k):
            load.start()
    loads[0].wait()
    loads[1].wait()
    attention_terms(0)
    attention_terms(1)
    attention_cores(0)
    attention_terms(2)
    attention_cores(1)
    attention_terms(3)
    attention_cores(2)
    attention_cores(3)
    upstream_send(2)
    upstream_send(3)
    upstream_rows(0)
    upstream_rows(1)
    attention_chips(0)
    u_copies[2].wait_send()
    normed(0)
    attention_chips(1)
    u_copies[3].wait_send()
    normed(1)
    for load in loads[2:]:
        load.wait()
    upstream_rows(2)
    for k in range(4):
        c_copies[k].wait_send()
    feed(0, 0)
    attention_chips(2)
    normed(2)
    upstream_rows(3)
    pair_rows(0)
    attention_chips(3)
    normed(3)
    pair_rows(1)
    feed(0, 1)
    feed(1, 0)
    pair_rows(2)
    pair_rows(3)
    feed(1, 1)

    for k in range(4):
        back_copies[k].wait_send()
        n_sides[k].wait_send()
        u_sides[k].wait_send()
        if k >= 2:
            n_copies[k].wait_send()
    for store in hidden_stores(3):
        store.wait()
    for copy in term_stores(1):
        copy.wait()


def front(mixed, output_weight, tokens, upstream, upstream_first, gain, gate_weight, up_weight, down_weight):
    rows, depth = tokens.shape
    inner, units = mixed.shape[1], gate_weight.shape[1]
    size = rows // 8
    tile = 256
    f32, b16 = jnp.float32, jnp.bfloat16
    any_space = pl.BlockSpec(memory_space=pl.ANY)
    shape = jax.ShapeDtypeStruct
    outs = [shape((rows, depth), f32)] * 2
    outs += ([shape((rows, depth), b16)] + [shape((rows, units), b16)] * 3) * 2
    outs += [shape((rows, depth), b16)] + [shape((4, size, depth), f32)] * 4
    dma = pltpu.SemaphoreType.DMA
    return pl.pallas_call(
        functools.partial(front_kernel, size),
        out_shape=outs,
        in_specs=[any_space] * 5 + [pl.BlockSpec(memory_space=pltpu.VMEM)] + [any_space] * 3,
        out_specs=[any_space] * len(outs),
        scratch_shapes=[
            pltpu.VMEM((rows, inner), b16),
            pltpu.VMEM((inner, depth), b16),
            pltpu.VMEM((depth, units), b16),
            pltpu.VMEM((depth, units), b16),
            pltpu.VMEM((units, depth), b16),
            pltpu.VMEM((4, size, depth), f32),
            pltpu.VMEM((4, size, depth), f32),
            pltpu.VMEM((4, size, depth), f32),
            pltpu.VMEM((4, size, depth), f32),
            pltpu.VMEM((2, 2, size, depth), b16),
            pltpu.VMEM((2, size, depth), f32),
            pltpu.VMEM((2, size, depth), f32),
            pltpu.VMEM((2, 4 * size, depth), b16),
            pltpu.VMEM((4 * size, depth), b16),
            pltpu.VMEM((2, 3, 4 * size, tile), b16),
            pltpu.VMEM((2, size, depth), f32),
            pltpu.VMEM((2, size, depth), b16),
            pltpu.VMEM((4 * size, depth), f32),
            dma((5,)),
            dma((2, 4)),
            dma((2, 4)),
            dma((2, 4)),
            dma((2, 4)),
            dma((2, 4)),
            dma((2, 4)),
            dma((2, 4)),
            dma((2, 2)),
            dma((2,)),
            dma((2,)),
            dma((2,)),
            dma((2, 3, 2)),
            dma((2,)),
            dma((2,)),
            dma((2,)),
        ],
        compiler_params=pltpu.CompilerParams(
            collective_id=1, has_side_effects=True, vmem_limit_bytes=62 * 1024 * 1024
        ),
        cost_estimate=pl.CostEstimate(
            flops=12 * rows * depth * units, bytes_accessed=6 * depth * units, transcendentals=0
        ),
    )(mixed, output_weight, tokens, upstream, upstream_first, gain[None], gate_weight, up_weight, down_weight)


def sequence_rows(size, core, which, k):
    side = core if which == 0 else 1 - core
    return pl.multiple_of(side * 4 * size + k * size, size)


def remote(source, target, sems, k, device):
    return pltpu.make_async_remote_copy(
        src_ref=source, dst_ref=target, send_sem=sems.at[0, k], recv_sem=sems.at[1, k],
        device_id=device, device_id_type=MESH,
    )


def grid_neighbours():
    dp = lax.axis_index("dp")
    place, lane = dp // 2, lax.rem(dp, 2)
    towards = 1 - 2 * (place // 2)
    across = {"dp": dp + 1 - 2 * lane}
    inward, outward = {"dp": dp + 2 * towards}, {"dp": dp - 2 * towards}
    team = place // 2
    side = lax.rem(place, 2)
    inner = lax.rem(team + side, 2)
    return place, lane, team, side, inner, across, inward, outward


def greet_grid(always, inner, outward):
    barrier = pltpu.get_barrier_semaphore()
    for device in always:
        pl.semaphore_signal(barrier, inc=1, device_id=device, device_id_type=MESH)

    @pl.when(inner == 1)
    def _():
        pl.semaphore_signal(barrier, inc=1, device_id=outward, device_id_type=MESH)

    pl.semaphore_wait(barrier, len(always) + inner)


def middle_kernel(
    size,
    second_hbm, hidden_hbm, upstream_hbm, upstream_pair, product_own, product_pair, gain, down_hbm,
    grad_out, grad_low_out, out_part, weight_out,
    products, down_weight, columns, c_recv, x_send, x_recv, back_recv,
    y_send, y_recv, kept, in_recv, mid_recv, out_recv,
    hid, tok, grad, grad_low, out_stage,
    load_sems, c_sems, x_sems, back_sems, y_sems, z_sems, column_sems,
    x_load_sems, hid_sems, tok_sems, grad_sems, low_sems, out_sems, weight_sems,
):
    core, sibling, facing, _ = neighbours()
    place, lane, team, side, inner, across, inward, outward = grid_neighbours()
    depth = gain.shape[1]
    units = down_weight.shape[0]
    width = columns.shape[-1]
    begin = functools.partial(sequence_rows, size, core)
    loads = [
        pltpu.make_async_copy(source, target, load_sems.at[index])
        for index, (source, target) in enumerate(
            [(product_own, products.at[0]), (product_pair, products.at[1]), (down_hbm, down_weight)]
        )
    ]
    turns = [(0, 1), (1, 1), (0, 0), (1, 0)]

    def column_loads(index):
        turn, other = turns[index]
        spot = lax.rem(1 - team + turn, 2)
        which = 1 - lane if other else lane
        start = pl.multiple_of((side * 4 + 2 * spot + which) * width, width)
        return [
            pltpu.make_async_copy(
                source.at[:, pl.ds(start, width)],
                columns.at[index % 2, part],
                column_sems.at[index % 2, part],
            )
            for part, source in enumerate((upstream_hbm, upstream_pair))
        ]

    x_loads = [
        pltpu.make_async_copy(
            second_hbm.at[pl.ds(begin(0, k), size)], x_send.at[k], x_load_sems.at[k]
        )
        for k in range(4)
    ]
    for copy in column_loads(0) + x_loads[:1] + loads[:2] + column_loads(1) + x_loads[1:] + loads[2:]:
        copy.start()
    greet_grid([sibling, facing, across, inward], inner, outward)
    c_copies = [
        remote(second_hbm.at[pl.ds(begin(1, k), size)], c_recv.at[k], c_sems, k, sibling)
        for k in range(4)
    ]
    x_copies = [remote(x_send.at[k], x_recv.at[k], x_sems, k, facing) for k in range(4)]
    back_copies = [remote(x_send.at[k], back_recv.at[k], back_sems, k, sibling) for k in range(4)]
    y_copies = [remote(y_send.at[k], y_recv.at[k], y_sems, k, across) for k in range(2)]
    in_copy = remote(kept.at[0], in_recv, z_sems, 0, inward)
    mid_copies = [remote(kept.at[k], mid_recv.at[k], z_sems, 1 + k, inward) for k in range(2)]
    out_copy = remote(mid_recv.at[0], out_recv, z_sems, 3, outward)
    for copy in c_copies:
        copy.start()

    def cores(k):
        x_loads[k].wait()
        c_copies[k].wait_recv()

        def run(row):
            x_send[k, row, :] = x_send[k, row, :] + c_recv[k, row, :]

        loop_rows(size, 16, run)
        x_copies[k].start()

    def chips(k):
        x_copies[k].wait()

        def run(row):
            x_send[k, row, :] = x_send[k, row, :] + x_recv[k, row, :]

        loop_rows(size, 16, run)
        back_copies[k].start()

    def block(index, target):
        for copy in column_loads(index):
            copy.wait()

        def run(rows):
            total = None
            for part in range(2):
                term = lax.dot_general(
                    products[part, :, rows],
                    columns[index % 2, part],
                    (((0,), (0,)), ((), ())),
                    preferred_element_type=jnp.float32,
                )
                total = term if total is None else total + term
            target[rows, :] = total

        loop_rows(units, 512, run)
        if index + 2 < 4:
            for copy in column_loads(index + 2):
                copy.start()

    def chunk_loads(k):
        return [
            pltpu.make_async_copy(
                source.at[pl.ds(begin(which, k), size)], target.at[which], sems.at[which]
            )
            for which in range(2)
            for source, target, sems in ((hidden_hbm, hid, hid_sems), (upstream_hbm, tok, tok_sems))
        ]

    def grad_stores(k):
        return [
            pltpu.make_async_copy(
                source.at[which], target.at[pl.ds(begin(which, k), size)], sems.at[which]
            )
            for which in range(2)
            for source, target, sems in (
                (grad, grad_out, grad_sems),
                (grad_low, grad_low_out, low_sems),
            )
        ]

    def finish(k):
        for copy in chunk_loads(k):
            copy.wait()
        if k > 0:
            for copy in grad_stores(k - 1):
                copy.wait()
        back_copies[k].wait_recv()

        def run(which, source, row):
            value = hid[which, row, :]
            inverse = lax.rsqrt(jnp.mean(value * value, axis=-1, keepdims=True) + epsilon)
            total = tok[which, row, :].astype(jnp.float32) + norm_back(
                source[k, row, :], value, inverse, gain[...]
            )
            grad[which, row, :] = total
            grad_low[which, row, :] = total.astype(jnp.bfloat16)

        for which, source in enumerate((x_send, back_recv)):
            loop_rows(size, 16, functools.partial(run, which, source))
        for copy in grad_stores(k):
            copy.start()
        if k < 3:
            for copy in chunk_loads(k + 1):
                copy.start()

    def out_store(k):
        rows = 2 * size
        return pltpu.make_async_copy(
            out_stage, out_part.at[pl.ds(k * rows, rows)], out_sems.at[0]
        )

    def out_terms(k):
        if k > 0:
            out_store(k - 1).wait()
        rows = pl.ds(k * 2 * size, 2 * size)

        def run(column):
            out_stage[:, column] = jnp.dot(
                products[0, rows, :], down_weight[:, column], preferred_element_type=jnp.float32
            )

        loop_rows(depth, 512, run)
        out_store(k).start()

    def take(k):
        y_copies[k].wait_recv()

        def run(row):
            kept[k, row, :] = kept[k, row, :] + y_recv[k, row, :]

        loop_rows(units, 64, run)

    cores(0)
    for copy in loads[:2]:
        copy.wait()
    block(0, y_send.at[0])
    y_copies[0].start()
    for copy in chunk_loads(0):
        copy.start()
    cores(1)
    cores(2)
    cores(3)
    block(1, y_send.at[1])
    y_copies[1].start()
    block(2, kept.at[0])
    chips(0)
    loads[2].wait()
    out_terms(0)
    finish(0)
    take(0)

    @pl.when(inner == 1)
    def _():
        mid_copies[0].start()

    @pl.when(inner == 0)
    def _():
        in_copy.start()

    block(3, kept.at[1])
    chips(1)
    out_terms(1)
    finish(1)
    chips(2)
    out_terms(2)
    take(1)

    @pl.when(inner == 1)
    def _():
        mid_copies[1].start()
        mid_copies[0].wait_recv()
        out_copy.start()

    finish(2)
    out_terms(3)
    chips(3)
    finish(3)

    @pl.when(inner == 1)
    def _():
        in_copy.wait_recv()
        mid_copies[1].wait_recv()
        mid_copies[0].wait_send()
        mid_copies[1].wait_send()
        out_copy.wait_send()

        def run(row):
            kept[0, row, :] = in_recv[row, :] + mid_recv[1, row, :]

        loop_rows(units, 64, run)

    @pl.when(inner == 0)
    def _():
        in_copy.wait_send()
        out_copy.wait_recv()

        def run(row):
            kept[0, row, :] = kept[1, row, :] + out_recv[row, :]

        loop_rows(units, 64, run)

    store = pltpu.make_async_copy(kept.at[0], weight_out, weight_sems.at[0])
    store.start()
    for k in range(4):
        back_copies[k].wait_send()
        c_copies[k].wait_send()
    for k in range(2):
        y_copies[k].wait_send()
    for copy in grad_stores(3):
        copy.wait()
    out_store(3).wait()
    store.wait()


def middle(second, hidden, upstream, upstream_pair, product_own, product_pair, gain, down_weight):
    rows, depth = hidden.shape
    units = down_weight.shape[0]
    size = rows // 8
    width = depth // 8
    f32, b16 = jnp.float32, jnp.bfloat16
    any_space = pl.BlockSpec(memory_space=pl.ANY)
    shape = jax.ShapeDtypeStruct
    dma = pltpu.SemaphoreType.DMA
    vmem = pltpu.VMEM
    return pl.pallas_call(
        functools.partial(middle_kernel, size),
        out_shape=[
            shape((rows, depth), f32),
            shape((rows, depth), b16),
            shape((rows, depth), f32),
            shape((units, width), f32),
        ],
        in_specs=[any_space] * 6 + [pl.BlockSpec(memory_space=pltpu.VMEM), any_space],
        out_specs=[any_space] * 4,
        scratch_shapes=[
            vmem((2, rows, units), b16),
            vmem((units, depth), b16),
            vmem((2, 2, rows, width), b16),
            vmem((4, size, depth), f32),
            vmem((4, size, depth), f32),
            vmem((4, size, depth), f32),
            vmem((4, size, depth), f32),
            vmem((2, units, width), f32),
            vmem((2, units, width), f32),
            vmem((2, units, width), f32),
            vmem((units, width), f32),
            vmem((2, units, width), f32),
            vmem((units, width), f32),
            vmem((2, size, depth), f32),
            vmem((2, size, depth), b16),
            vmem((2, size, depth), f32),
            vmem((2, size, depth), b16),
            vmem((2 * size, depth), f32),
            dma((3,)),
            dma((2, 4)),
            dma((2, 4)),
            dma((2, 4)),
            dma((2, 2)),
            dma((2, 4)),
            dma((2, 2)),
            dma((4,)),
            dma((2,)),
            dma((2,)),
            dma((2,)),
            dma((2,)),
            dma((1,)),
            dma((1,)),
        ],
        compiler_params=pltpu.CompilerParams(
            collective_id=2, has_side_effects=True, vmem_limit_bytes=62 * 1024 * 1024
        ),
        cost_estimate=pl.CostEstimate(
            flops=8 * rows * depth * units, bytes_accessed=6 * depth * units, transcendentals=0
        ),
    )(second, hidden, upstream, upstream_pair, product_own, product_pair, gain[None], down_weight)


class TensorSum:
    def __init__(self, size, own, landed, stage, sems, stage_sems, devices):
        self.size, self.own, self.landed, self.stage = size, own, landed, stage
        self.stage_sems = stage_sems
        c_sems, x_sems, back_sems = sems
        self.sibling, facing = devices
        self.c_sems = c_sems
        self.x_copies = [remote(own.at[k], landed[1].at[k], x_sems, k, facing) for k in range(4)]
        self.back_copies = [
            remote(own.at[k], landed[2].at[k], back_sems, k, self.sibling) for k in range(4)
        ]
        self.c_copies = [None] * 4

    def give(self, k, source):
        self.c_copies[k] = remote(source, self.landed[0].at[k], self.c_sems, k, self.sibling)
        self.c_copies[k].start()

    def staged(self, which, k):
        copy = pltpu.make_async_copy(self.landed[which].at[k], self.stage.at[0], self.stage_sems.at[0])
        copy.start()
        copy.wait()

    def add_stage(self, k):
        def run(row):
            self.own[k, row, :] = self.own[k, row, :] + self.stage[0, row, :]

        loop_rows(self.size, 16, run)

    def cores(self, k):
        self.c_copies[k].wait_recv()
        self.staged(0, k)
        self.add_stage(k)
        self.x_copies[k].start()

    def chips(self, k):
        self.x_copies[k].wait()
        self.staged(1, k)
        self.add_stage(k)
        self.back_copies[k].start()

    def other(self, k):
        self.back_copies[k].wait_recv()
        self.staged(2, k)


def rear_kernel(
    size, turns,
    gate_ready0, gate_ready1, low_own, low_pair, upward_own, upward_pair,
    normed_hbm, raw_hbm, hidden_low_hbm, mixed_hbm, lines,
    out_hbm, hidden_hbm, grad_hbm, tokens_hbm, query_hbm, key_hbm, value_hbm, gain,
    layer_out, tokens_out, gate_out, up_out, raw_out, head_out,
    o_c, o_x, o_back, d_c, d_x, d_back, gate_landed, up_landed,
    upwards, raw, mixed, query_weight, key_weight, value_weight, columns,
    up_send, up_kept, raw_send, raw_kept, head_send, head_kept, raw_line, head_line,
    own, give, stage, wide, narrow, result,
    load_sems, column_sems, y_up_sems, y_raw_sems, y_head_sems, gate_sems, up_sems,
    raw_line_sems, head_line_sems,
    oc_sems, ox_sems, ob_sems, dc_sems, dx_sems, db_sems,
    own_sems, stage_sems, wide_sems, narrow_sems, result_sems, end_sems,
):
    core, sibling, facing, _ = neighbours()
    place, lane, team, side, inner, across, inward, outward = grid_neighbours()
    high = len(turns)
    depth = gain.shape[1]
    width = columns.shape[-1]
    units = upwards.shape[-1]
    begin = functools.partial(sequence_rows, size, core)
    loads = [
        pltpu.make_async_copy(source, target, load_sems.at[index])
        for index, (source, target) in enumerate(
            [
                (upward_own, upwards.at[0]),
                (upward_pair, upwards.at[1]),
                (raw_hbm, raw),
                (mixed_hbm, mixed),
                (query_hbm, query_weight),
                (key_hbm, key_weight),
                (value_hbm, value_weight),
            ]
        )
    ]
    blocks = [
        ("up", 0, 1), ("up", 1, 1), ("head", 0, 1), ("head", 1, 1), ("up", 0, 0), ("up", 1, 0),
        ("head", 0, 0), ("head", 2, 1), ("head", 1, 0), ("head", 3, 1), ("head", 2, 0), ("head", 3, 0),
    ]

    def spot_of(kind, turn):
        if kind == "up":
            return side * 2 + lax.rem(1 - team + turn, 2)
        spot = jnp.int32(turns[0][turn])
        for p in range(1, high):
            spot = jnp.where(place == p, jnp.int32(turns[p][turn]), spot)
        return spot

    def column_loads(index):
        kind, turn, other = blocks[index]
        which = 1 - lane if other else lane
        start = pl.multiple_of((2 * spot_of(kind, turn) + which) * width, width)
        sources = (low_own, low_pair) if kind == "up" else (normed_hbm, hidden_low_hbm)
        return [
            pltpu.make_async_copy(
                source.at[:, pl.ds(start, width)],
                columns.at[index % 2, part],
                column_sems.at[index % 2, part],
            )
            for part, source in enumerate(sources)
        ]

    own_loads = [
        pltpu.make_async_copy(out_hbm.at[pl.ds(begin(0, k), size)], own.at[k], own_sems.at[k])
        for k in range(4)
    ]
    for copy in column_loads(0) + loads[:2] + column_loads(1) + own_loads + loads[2:]:
        copy.start()
    greet_grid([sibling, facing, across, inward], inner, outward)
    devices = (sibling, facing)
    outs = TensorSum(
        size, own, (o_c, o_x, o_back), stage, (oc_sems, ox_sems, ob_sems), stage_sems, devices
    )
    heads = TensorSum(
        size, own, (d_c, d_x, d_back), stage, (dc_sems, dx_sems, db_sems), stage_sems, devices
    )
    for k in range(4):
        outs.give(k, out_hbm.at[pl.ds(begin(1, k), size)])

    def team_copies(values, landed, sems):
        return (
            remote(values[0], landed.at[0], sems, 0, inward),
            [remote(values[k], landed.at[1 + k], sems, 1 + k, inward) for k in range(2)],
            remote(landed.at[1], landed.at[3], sems, 3, outward),
        )

    gate_copies = team_copies((gate_ready0, gate_ready1), gate_landed, gate_sems)
    up_copies = team_copies((up_kept.at[0], up_kept.at[1]), up_landed, up_sems)

    def team_send(copies, turn):
        @pl.when(inner == 1)
        def _():
            copies[1][turn].start()

        if turn == 0:

            @pl.when(inner == 0)
            def _():
                copies[0].start()

    def team_forward(copies):
        @pl.when(inner == 1)
        def _():
            copies[1][0].wait_recv()
            copies[2].start()

    def team_combine(copies, landed, last, out, sem):
        def fetch(source, slot):
            copy = pltpu.make_async_copy(source, up_send.at[slot], end_sems.at[4 + slot])
            copy.start()
            copy.wait()

        @pl.when(inner == 1)
        def _():
            copies[0].wait_recv()
            copies[1][1].wait_recv()
            fetch(landed.at[0], 0)
            fetch(landed.at[2], 1)
            copies[1][0].wait_send()
            copies[1][1].wait_send()
            copies[2].wait_send()

        @pl.when(inner == 0)
        def _():
            copies[0].wait_send()
            copies[2].wait_recv()
            fetch(landed.at[3], 0)
            fetch(last, 1)

        def run(row):
            up_send[0, row, :] = up_send[0, row, :] + up_send[1, row, :]

        loop_rows(width, 16, run)
        store = pltpu.make_async_copy(up_send.at[0], out, sem)
        store.start()
        store.wait()

    y_up = [remote(up_send.at[k], up_kept.at[k], y_up_sems, k, across) for k in range(2)]
    y_raw = [remote(raw_send.at[k % 2], raw_kept.at[k], y_raw_sems, k, across) for k in range(high)]
    y_head = [
        remote(head_send.at[k % 2], head_kept.at[k], y_head_sems, k, across) for k in range(high)
    ]

    def line_copy(p, turn, towards=None):
        block = turns[p][turn]
        ahead = block > p
        slot = block - 1 if ahead else high - 1 + block
        device = {"dp": lax.axis_index("dp") + (2 if ahead else -2)}
        return slot, [
            remote(kept.at[turn], line.at[slot], sems, slot, device)
            for kept, line, sems in (
                (raw_kept, raw_line, raw_line_sems),
                (head_kept, head_line, head_line_sems),
            )
        ]

    def line_arrived(slot, turn):
        for kept, line, sems in (
            (raw_kept, raw_line, raw_line_sems),
            (head_kept, head_line, head_line_sems),
        ):
            remote(kept.at[turn], line.at[slot], sems, slot, across).wait_recv()

            def run(row):
                kept[turn, row, :] = kept[turn, row, :] + line[slot, row, :]

            loop_rows(kept.shape[1], 8, run)

    def line_step(turn):
        for p in range(high):
            block = turns[p][turn]

            @pl.when(place == p)
            def _():
                slot, copies = line_copy(p, turn)
                if (block > p and p > 0) or (block < p and p < high - 1):
                    line_arrived(slot, turn)
                for copy in copies:
                    copy.start()

    def line_end():
        for p in range(high):

            @pl.when(place == p)
            def _():
                if p > 0:
                    line_arrived(p - 1, high - 1)
                if p < high - 1:
                    line_arrived(high - 1 + p, high - 1)
                for turn in range(high - 1):
                    for copy in line_copy(p, turn)[1]:
                        copy.wait_send()

    def up_block(index, target, added):
        for copy in column_loads(index):
            copy.wait()

        def run(rows):
            total = None
            for part in range(2):
                term = lax.dot_general(
                    columns[index % 2, part],
                    upwards[part, :, rows],
                    (((0,), (0,)), ((), ())),
                    preferred_element_type=jnp.float32,
                )
                total = term if total is None else total + term
            target[:, rows] = target[:, rows] + total if added else total

        loop_rows(units, 512, run)
        if index + 2 < len(blocks):
            for copy in column_loads(index + 2):
                copy.start()

    def head_block(index, raw_target, head_target, added):
        kind, turn, other = blocks[index]
        which = 1 - lane if other else lane
        for copy in column_loads(index):
            copy.wait()
        sums = (((0,), (0,)), ((), ()))

        def run(rows):
            total = lax.dot_general(
                columns[index % 2, 0], raw[:, rows], sums, preferred_element_type=jnp.float32
            )
            line = lines[2 * spot_of(kind, turn) + which, :, rows]
            if added:
                raw_target[:width, rows] = raw_target[:width, rows] + total
                raw_target[width:, rows] = raw_target[width:, rows] + line
            else:
                raw_target[:width, rows] = total
                raw_target[width:, rows] = line

        loop_rows(raw.shape[1], 512, run)
        total = lax.dot_general(
            mixed[...], columns[index % 2, 1], sums, preferred_element_type=jnp.float32
        )
        head_target[...] = head_target[...] + total if added else total
        if index + 2 < len(blocks):
            for copy in column_loads(index + 2):
                copy.start()

    def head_send_block(index):
        turn = blocks[index][1]
        if turn >= 2:
            y_raw[turn - 2].wait_send()
            y_head[turn - 2].wait_send()
        head_block(index, raw_send.at[turn % 2], head_send.at[turn % 2], False)
        y_raw[turn].start()
        y_head[turn].start()

    def head_take(index):
        turn = blocks[index][1]
        y_raw[turn].wait_recv()
        y_head[turn].wait_recv()
        head_block(index, raw_kept.at[turn], head_kept.at[turn], True)

    def head_terms(k):
        outs.back_copies[k].wait_send()
        if k >= 2:
            heads.c_copies[k - 2].wait_send()
        across_last = (((1,), (1,)), ((), ()))
        cuts = (0, query_weight.shape[1], query_weight.shape[1] + key_weight.shape[1], raw.shape[1])

        def run(rows):
            for which in range(2):
                total = None
                for part, weight in enumerate((query_weight, key_weight, value_weight)):
                    term = lax.dot_general(
                        raw[pl.ds(begin(which, k), size), cuts[part] : cuts[part + 1]],
                        weight[rows, :],
                        across_last,
                        preferred_element_type=jnp.float32,
                    )
                    total = term if total is None else total + term
                if which == 0:
                    own[k, :, rows] = total
                else:
                    give[k % 2, :, rows] = total

        loop_rows(depth, 512, run)
        heads.give(k, give.at[k % 2])

    def fetches(what, k):
        pairs = ((hidden_hbm, wide, wide_sems),)
        if what == "tokens":
            pairs = ((grad_hbm, wide, wide_sems), (tokens_hbm, narrow, narrow_sems))
        return [
            pltpu.make_async_copy(
                source.at[pl.ds(begin(which, k), size)], target.at[which], sems.at[which]
            )
            for which in range(2)
            for source, target, sems in pairs
        ]

    def stores(what, k):
        return [
            pltpu.make_async_copy(
                result.at[which],
                (layer_out if what == "layer" else tokens_out).at[pl.ds(begin(which, k), size)],
                result_sems.at[which],
            )
            for which in range(2)
        ]

    sequence = [("layer", k) for k in range(4)] + [("tokens", k) for k in range(4)]

    def finish(what, k):
        number = sequence.index((what, k))
        for copy in fetches(what, k):
            copy.wait()
        if number > 0:
            for copy in stores(*sequence[number - 1]):
                copy.wait()
        (outs if what == "layer" else heads).other(k)

        def run(which, row):
            total = stage[0, row, :] if which else own[k, row, :]
            value = wide[which, row, :]
            if what == "layer":
                total = value + total
            else:
                inputs = narrow[which, row, :].astype(jnp.float32)
                inverse = lax.rsqrt(jnp.mean(inputs * inputs, axis=-1, keepdims=True) + epsilon)
                total = value + norm_back(total, inputs, inverse, gain[...])
            result[which, row, :] = total.astype(jnp.bfloat16)

        for which in range(2):
            loop_rows(size, 16, functools.partial(run, which))
        for copy in stores(what, k):
            copy.start()
        if number + 1 < len(sequence):
            for copy in fetches(*sequence[number + 1]):
                copy.start()

    team_send(gate_copies, 0)
    team_send(gate_copies, 1)
    for copy in fetches("layer", 0):
        copy.start()
    for copy in loads[:2]:
        copy.wait()
    up_block(0, up_send.at[0], False)
    y_up[0].start()
    own_loads[0].wait()
    outs.cores(0)
    up_block(1, up_send.at[1], False)
    y_up[1].start()
    for k in range(1, 4):
        own_loads[k].wait()
        outs.cores(k)
    for copy in loads[2:]:
        copy.wait()
    head_send_block(2)
    head_send_block(3)
    outs.chips(0)
    finish("layer", 0)
    team_forward(gate_copies)
    y_up[0].wait_recv()
    up_block(4, up_kept.at[0], True)
    team_send(up_copies, 0)
    head_terms(0)
    outs.chips(1)
    finish("layer", 1)
    head_terms(1)
    y_up[1].wait_recv()
    up_block(5, up_kept.at[1], True)
    team_send(up_copies, 1)
    outs.chips(2)
    heads.cores(0)
    finish("layer", 2)
    head_terms(2)
    heads.cores(1)
    outs.chips(3)
    heads.cores(2)
    finish("layer", 3)
    head_terms(3)
    heads.cores(3)
    head_take(6)
    line_step(0)
    head_send_block(7)
    heads.chips(0)
    finish("tokens", 0)
    head_take(8)
    line_step(1)
    head_send_block(9)
    team_forward(up_copies)
    heads.chips(1)
    finish("tokens", 1)
    heads.chips(2)
    finish("tokens", 2)
    head_take(10)
    line_step(2)
    for k in range(2):
        y_up[k].wait_send()
    team_combine(gate_copies, gate_landed, gate_ready1, gate_out, end_sems.at[0])
    heads.chips(3)
    finish("tokens", 3)
    team_combine(up_copies, up_landed, up_kept.at[1], up_out, end_sems.at[1])
    head_take(11)
    line_end()
    ends = [
        pltpu.make_async_copy(raw_kept.at[high - 1], raw_out, end_sems.at[2]),
        pltpu.make_async_copy(head_kept.at[high - 1], head_out, end_sems.at[3]),
    ]
    for copy in ends:
        copy.start()
    for k in range(4):
        outs.c_copies[k].wait_send()
        heads.back_copies[k].wait_send()
    for k in range(2, 4):
        heads.c_copies[k].wait_send()
        y_raw[k].wait_send()
        y_head[k].wait_send()
    for copy in stores(*sequence[-1]) + ends:
        copy.wait()


def rear(turns, arrays, lines, places, weights, gain):
    rows, depth = places[0].shape
    units = arrays[0].shape[1]
    heads, inner = arrays[7].shape[1], arrays[9].shape[1]
    size = rows // 8
    width = depth // 8
    high = len(turns)
    f32, b16 = jnp.float32, jnp.bfloat16
    any_space = pl.BlockSpec(memory_space=pl.ANY)
    in_vmem = pl.BlockSpec(memory_space=pltpu.VMEM)
    shape = jax.ShapeDtypeStruct
    dma = pltpu.SemaphoreType.DMA
    vmem = pltpu.VMEM
    slots = 2 * (high - 1)
    return pl.pallas_call(
        functools.partial(rear_kernel, size, turns),
        out_shape=[
            shape((rows, depth), b16),
            shape((rows, depth), b16),
            shape((width, units), f32),
            shape((width, units), f32),
            shape((width + 8, heads), f32),
            shape((inner, width), f32),
        ]
        + [shape((4, size, depth), f32)] * 6
        + [shape((4, width, units), f32)] * 2,
        in_specs=[any_space] * 10 + [in_vmem] + [any_space] * 7 + [in_vmem],
        out_specs=[any_space] * 14,
        scratch_shapes=[
            vmem((2, rows, units), b16),
            vmem((rows, heads), b16),
            vmem((rows, inner), b16),
            *[vmem(weight.shape, b16) for weight in weights],
            vmem((2, 2, rows, width), b16),
            vmem((2, width, units), f32),
            vmem((2, width, units), f32),
            vmem((2, width + 8, heads), f32),
            vmem((high, width + 8, heads), f32),
            vmem((2, inner, width), f32),
            vmem((high, inner, width), f32),
            vmem((slots, width + 8, heads), f32),
            vmem((slots, inner, width), f32),
            vmem((4, size, depth), f32),
            vmem((2, size, depth), f32),
            vmem((1, size, depth), f32),
            vmem((2, size, depth), f32),
            vmem((2, size, depth), b16),
            vmem((2, size, depth), b16),
            dma((7,)),
            dma((2, 2)),
            dma((2, 2)),
            dma((2, high)),
            dma((2, high)),
            dma((2, 4)),
            dma((2, 4)),
            dma((2, slots)),
            dma((2, slots)),
            *[dma((2, 4))] * 6,
            dma((4,)),
            dma((1,)),
            dma((2,)),
            dma((2,)),
            dma((2,)),
            dma((6,)),
        ],
        compiler_params=pltpu.CompilerParams(
            collective_id=3, has_side_effects=True, vmem_limit_bytes=62 * 1024 * 1024
        ),
        cost_estimate=pl.CostEstimate(
            flops=8 * rows * depth * units, bytes_accessed=6 * depth * units, transcendentals=0
        ),
    )(*arrays, lines, *places, *weights, gain[None])


def gradient_kernel(number, transposed, added, extra, column, *refs):
    lefts, rights = refs[:number], refs[number : 2 * number]
    out = refs[-1]
    total = None
    for left, right in zip(lefts, rights):
        first, second = (right, left) if transposed else (left, right)
        term = lax.dot_general(
            first[...], second[...], (((0,), (0,)), ((), ())), preferred_element_type=jnp.float32
        )
        total = term if total is None else total + term
    width = total.shape[0]
    rest = list(refs[2 * number : -1])
    lines = rest.pop(0)[0] if extra else None
    if added:
        total = total + rest[0][:width, :]
        if extra:
            lines = lines + rest[0][width:, :]
    out[:width, :] = total
    if extra:
        out[width:, :] = lines


def gradient(lefts, rights, column, width, transposed, added=None, extra=None):
    rows = lefts[0].shape[0]
    columns = rights[0].shape[1]
    tile = 512
    more = 8 if extra is not None else 0
    if transposed:
        shape, block, place = (columns, width), (tile, width), lambda n, c: (n, 0)
    else:
        shape, block, place = (width + more, columns), (width + more, tile), lambda n, c: (0, n)
    specs = [pl.BlockSpec((rows, width), lambda n, c: (0, c[0]))] * len(lefts)
    specs += [pl.BlockSpec((rows, tile), lambda n, c: (0, n))] * len(rights)
    inputs = list(lefts) + list(rights)
    if extra is not None:
        specs.append(pl.BlockSpec((1, 8, tile), lambda n, c: (c[0], 0, n)))
        inputs.append(extra)
    if added is not None:
        specs.append(pl.BlockSpec(block, place))
        inputs.append(added)
    return pl.pallas_call(
        functools.partial(
            gradient_kernel, len(lefts), transposed, added is not None, extra is not None
        ),
        grid_spec=pltpu.PrefetchScalarGridSpec(
            num_scalar_prefetch=1,
            grid=(columns // tile,),
            in_specs=specs,
            out_specs=pl.BlockSpec(block, place),
        ),
        out_shape=jax.ShapeDtypeStruct(shape, jnp.float32),
        compiler_params=pltpu.CompilerParams(vmem_limit_bytes=32 * 1024 * 1024),
        cost_estimate=pl.CostEstimate(
            flops=2 * len(lefts) * rows * width * columns,
            bytes_accessed=2 * len(lefts) * rows * (width + columns) + 4 * width * columns,
            transcendentals=0,
        ),
    )(column[None], *inputs)


def plain_shards(
    tokens,
    attention_gain,
    query_weight,
    key_weight,
    value_weight,
    query_gain,
    key_gain,
    output_weight,
    feedforward_gain,
    gate_weight,
    up_weight,
    down_weight,
    segment_numbers,
    positions,
    cotangent,
):
    count = tokens.shape[0]
    batch = count // SEQ_LEN
    query_heads = query_weight.shape[1] // HD
    value_heads = key_weight.shape[1] // HD
    group = query_heads // value_heads
    inputs = tokens.astype(jnp.float32)
    first_inverse = rms_inverse(inputs)
    first_normed = inputs * first_inverse
    normed_low = (first_normed * attention_gain).astype(jnp.bfloat16)
    query_raw = jnp.dot(normed_low, query_weight, preferred_element_type=jnp.float32).reshape(
        count, query_heads, HD
    )
    key_raw = jnp.dot(normed_low, key_weight, preferred_element_type=jnp.float32).reshape(
        count, value_heads, HD
    )
    value_low = jnp.dot(normed_low, value_weight, preferred_element_type=jnp.float32).astype(
        jnp.bfloat16
    )
    cosine, sine = rotary_tables(positions)
    cosine = cosine[:, None]
    sine = sine[:, None]
    query_inverse = rms_inverse(query_raw)
    query_unit = query_raw * query_inverse
    query_low = rotate(query_unit * query_gain, cosine, sine).astype(jnp.bfloat16)
    key_inverse = rms_inverse(key_raw)
    key_unit = key_raw * key_inverse
    key_low = rotate(key_unit * key_gain, cosine, sine).astype(jnp.bfloat16)
    queries = query_low.reshape(batch, SEQ_LEN, value_heads, group, HD)
    keys = key_low.reshape(batch, SEQ_LEN, value_heads, HD)
    values = value_low.reshape(batch, SEQ_LEN, value_heads, HD)
    segments = segment_numbers.reshape(batch, SEQ_LEN)
    mixed, totals = lax.map(attend, (queries, keys, values, segments))
    mixed_low = mixed.reshape(count, query_heads * HD).astype(jnp.bfloat16)
    attention = lax.psum(
        jnp.dot(mixed_low, output_weight, preferred_element_type=jnp.float32), "tensor"
    )
    hidden = inputs + attention
    second_inverse = rms_inverse(hidden)
    second_normed = hidden * second_inverse
    second_low = (second_normed * feedforward_gain).astype(jnp.bfloat16)
    gate = jnp.dot(second_low, gate_weight, preferred_element_type=jnp.float32)
    upward = jnp.dot(second_low, up_weight, preferred_element_type=jnp.float32)
    sigmoid_gate = jax.nn.sigmoid(gate)
    activated = gate * sigmoid_gate
    product_low = (activated * upward).astype(jnp.bfloat16)
    feedforward = lax.psum(
        jnp.dot(product_low, down_weight, preferred_element_type=jnp.float32), "tensor"
    )
    layer_output = (hidden + feedforward).astype(jnp.bfloat16)
    down_grad = jnp.einsum("tf,td->fd", product_low, cotangent, preferred_element_type=jnp.float32)
    product_grad = jnp.einsum(
        "td,fd->tf", cotangent, down_weight, preferred_element_type=jnp.float32
    )
    gate_grad_low = (
        product_grad * upward * sigmoid_gate * (1.0 + gate * (1.0 - sigmoid_gate))
    ).astype(jnp.bfloat16)
    upward_grad_low = (product_grad * activated).astype(jnp.bfloat16)
    gate_weight_grad = jnp.einsum(
        "td,tf->df", second_low, gate_grad_low, preferred_element_type=jnp.float32
    )
    upward_weight_grad = jnp.einsum(
        "td,tf->df", second_low, upward_grad_low, preferred_element_type=jnp.float32
    )
    second_part = jnp.einsum(
        "tf,df->td", gate_grad_low, gate_weight, preferred_element_type=jnp.float32
    )
    second_part = second_part + jnp.einsum(
        "tf,df->td", upward_grad_low, up_weight, preferred_element_type=jnp.float32
    )
    second_grad = lax.psum(second_part, "tensor")
    second_gain_grad = jnp.sum(second_grad * second_normed, axis=0)
    hidden_grad = cotangent.astype(jnp.float32) + norm_back(
        second_grad, hidden, second_inverse, feedforward_gain
    )
    hidden_low = hidden_grad.astype(jnp.bfloat16)
    output_weight_grad = jnp.einsum(
        "tc,td->cd", mixed_low, hidden_low, preferred_element_type=jnp.float32
    )
    mixed_grad = jnp.einsum(
        "td,cd->tc", hidden_low, output_weight, preferred_element_type=jnp.float32
    ).astype(jnp.bfloat16)
    upstream = mixed_grad.reshape(batch, SEQ_LEN, value_heads, group, HD)
    query_back, key_back, value_back = lax.map(
        attend_back, (queries, keys, values, segments, totals, upstream)
    )
    query_unit_grad = rotate_back(query_back.reshape(count, query_heads, HD), cosine, sine)
    key_unit_grad = rotate_back(key_back.reshape(count, value_heads, HD), cosine, sine)
    query_gain_part = jnp.sum(query_unit_grad * query_unit, axis=(0, 1))
    key_gain_part = jnp.sum(key_unit_grad * key_unit, axis=(0, 1))
    query_raw_grad = (
        norm_back(query_unit_grad, query_raw, query_inverse, query_gain)
        .reshape(count, query_heads * HD)
        .astype(jnp.bfloat16)
    )
    key_raw_grad = (
        norm_back(key_unit_grad, key_raw, key_inverse, key_gain)
        .reshape(count, value_heads * HD)
        .astype(jnp.bfloat16)
    )
    value_raw_grad = value_back.reshape(count, value_heads * HD).astype(jnp.bfloat16)
    query_weight_grad = jnp.einsum(
        "td,tc->dc", normed_low, query_raw_grad, preferred_element_type=jnp.float32
    )
    key_weight_grad = jnp.einsum(
        "td,tc->dc", normed_low, key_raw_grad, preferred_element_type=jnp.float32
    )
    value_weight_grad = jnp.einsum(
        "td,tc->dc", normed_low, value_raw_grad, preferred_element_type=jnp.float32
    )
    first_part = jnp.einsum(
        "tc,dc->td", query_raw_grad, query_weight, preferred_element_type=jnp.float32
    )
    first_part = first_part + jnp.einsum(
        "tc,dc->td", key_raw_grad, key_weight, preferred_element_type=jnp.float32
    )
    first_part = first_part + jnp.einsum(
        "tc,dc->td", value_raw_grad, value_weight, preferred_element_type=jnp.float32
    )
    first_grad, query_gain_grad, key_gain_grad = lax.psum(
        (first_part, query_gain_part, key_gain_part), "tensor"
    )
    first_gain_grad = jnp.sum(first_grad * first_normed, axis=0)
    tokens_gradient = (
        hidden_grad + norm_back(first_grad, inputs, first_inverse, attention_gain)
    ).astype(jnp.bfloat16)
    summed = (
        lax.psum_scatter(first_gain_grad, "dp", scatter_dimension=0, tiled=True),
        lax.psum_scatter(query_weight_grad, "dp", scatter_dimension=0, tiled=True),
        lax.psum_scatter(key_weight_grad, "dp", scatter_dimension=0, tiled=True),
        lax.psum_scatter(value_weight_grad, "dp", scatter_dimension=0, tiled=True),
        lax.psum_scatter(query_gain_grad, "dp", scatter_dimension=0, tiled=True),
        lax.psum_scatter(key_gain_grad, "dp", scatter_dimension=0, tiled=True),
        lax.psum_scatter(output_weight_grad, "dp", scatter_dimension=1, tiled=True),
        lax.psum_scatter(second_gain_grad, "dp", scatter_dimension=0, tiled=True),
        lax.psum_scatter(gate_weight_grad, "dp", scatter_dimension=0, tiled=True),
        lax.psum_scatter(upward_weight_grad, "dp", scatter_dimension=0, tiled=True),
        lax.psum_scatter(down_grad, "dp", scatter_dimension=1, tiled=True),
    )
    return (
        layer_output,
        tokens_gradient,
        summed[0],
        summed[1],
        summed[2],
        summed[3],
        summed[4],
        summed[5],
        summed[6],
        summed[7],
        summed[8],
        summed[9],
        summed[10],
    )


def shards(
    dp,
    tokens,
    attention_gain,
    query_weight,
    key_weight,
    value_weight,
    query_gain,
    key_gain,
    output_weight,
    feedforward_gain,
    gate_weight,
    up_weight,
    down_weight,
    segment_numbers,
    positions,
    cotangent,
):
    count, depth = tokens.shape
    query_heads = query_weight.shape[1] // HD
    value_heads = key_weight.shape[1] // HD
    group = query_heads // value_heads
    width = depth // dp
    high = dp // 2
    place = lax.axis_index("dp") // 2
    lane = lax.axis_index("dp") % 2
    core = lax.axis_index("tensor") % 2
    upstream_first = lax.ppermute(
        lax.dynamic_slice_in_dim(cotangent, core * (count // 2), count // 4, 0).astype(jnp.float32),
        "dp",
        [(i, i ^ 2) for i in range(dp)],
    )

    inputs = tokens.astype(jnp.float32)
    first_inverse = rms_inverse(inputs)
    normed_low = (inputs * first_inverse * attention_gain).astype(jnp.bfloat16)
    query_raw = dot(normed_low, query_weight).reshape(count, query_heads, HD)
    key_raw = dot(normed_low, key_weight).reshape(count, value_heads, HD)
    value_low = dot(normed_low, value_weight).astype(jnp.bfloat16)
    cosine, sine = rotary_tables(positions)
    cosine = cosine[:, None]
    sine = sine[:, None]
    query_inverse = rms_inverse(query_raw)
    query_unit = query_raw * query_inverse
    query_low = rotate(query_unit * query_gain, cosine, sine).astype(jnp.bfloat16)
    key_inverse = rms_inverse(key_raw)
    key_unit = key_raw * key_inverse
    key_low = rotate(key_unit * key_gain, cosine, sine).astype(jnp.bfloat16)
    queries = query_low.reshape(1, count, value_heads, group, HD)
    keys = key_low.reshape(1, count, value_heads, HD)
    values = value_low.reshape(1, count, value_heads, HD)
    segments = segment_numbers.reshape(1, count)
    mixed, totals = lax.map(attend, (queries, keys, values, segments))
    mixed_low = mixed.reshape(count, query_heads * HD).astype(jnp.bfloat16)

    (
        hidden,
        second_part,
        low_own,
        product_own,
        gate_own,
        upward_own,
        low_pair,
        product_pair,
        gate_pair,
        upward_pair,
        upstream_pair,
    ) = front(
        mixed_low,
        output_weight,
        tokens,
        cotangent,
        upstream_first,
        feedforward_gain,
        gate_weight,
        up_weight,
        down_weight,
    )[:11]
    hidden_grad, hidden_low, out_part, down_weight_grad = middle(
        second_part,
        hidden,
        cotangent,
        upstream_pair,
        product_own,
        product_pair,
        feedforward_gain,
        down_weight,
    )

    def gate_block(turn, which, added=None):
        spot = (1 - place // 2 + turn) % 2
        column = place % 2 * (dp // 2) + 2 * spot + which
        return gradient([low_own, low_pair], [gate_own, gate_pair], column, width, False, added)

    gate_moved = [
        lax.ppermute(gate_block(turn, 1 - lane), "dp", [(i, i ^ 1) for i in range(dp)])
        for turn in range(2)
    ]
    mixed_grad = dot_back(hidden_low, output_weight).astype(jnp.bfloat16)
    upstream = mixed_grad.reshape(1, count, value_heads, group, HD)
    query_back, key_back, value_back = lax.map(
        attend_back, (queries, keys, values, segments, totals, upstream)
    )
    query_unit_grad = rotate_back(query_back.reshape(count, query_heads, HD), cosine, sine)
    key_unit_grad = rotate_back(key_back.reshape(count, value_heads, HD), cosine, sine)
    query_gain_part = jnp.sum(query_unit_grad * query_unit, axis=(0, 1))
    key_gain_part = jnp.sum(key_unit_grad * key_unit, axis=(0, 1))
    query_raw_grad = (
        norm_back(query_unit_grad, query_raw, query_inverse, query_gain)
        .reshape(count, query_heads * HD)
        .astype(jnp.bfloat16)
    )
    key_raw_grad = (
        norm_back(key_unit_grad, key_raw, key_inverse, key_gain)
        .reshape(count, value_heads * HD)
        .astype(jnp.bfloat16)
    )
    value_raw_grad = value_back.reshape(count, value_heads * HD).astype(jnp.bfloat16)
    raw_grad = jnp.concatenate([query_raw_grad, key_raw_grad, value_raw_grad], axis=1)

    head_width = HD // dp

    lines = [
        jnp.pad(value.reshape(dp, -1), ((0, 0), (0, raw_grad.shape[1] - value.size // dp)))
        for value in (query_gain_part, key_gain_part)
    ]
    gain_lines = jnp.pad(jnp.stack(lines, axis=1), ((0, 0), (0, 6), (0, 0)))

    gate_ready = [gate_block(turn, lane, gate_moved[turn]) for turn in range(2)]
    layer_output, tokens_gradient, gate_weight_grad, up_weight_grad, raw_whole, output_weight_grad = (
        rear(
            [line_order(high, p) for p in range(high)],
            gate_ready
            + [low_own, low_pair, upward_own, upward_pair]
            + [normed_low, raw_grad, hidden_low, mixed_low],
            gain_lines,
            [out_part, hidden, hidden_grad, tokens],
            [query_weight, key_weight, value_weight],
            attention_gain,
        )[:6]
    )
    place_rows = (lax.axis_index("dp") * width, width, 0)
    raw_weight = jnp.concatenate(
        [
            lax.dynamic_slice_in_dim(value, *place_rows)
            for value in (query_weight, key_weight, value_weight)
        ],
        axis=1,
    )
    first_gain = jnp.sum(raw_weight * raw_whole[:width], axis=1) / lax.dynamic_slice_in_dim(
        attention_gain, *place_rows
    )
    second_gain = sum(
        jnp.sum(lax.dynamic_slice_in_dim(value, *place_rows) * gradient, axis=1)
        for gradient, value in ((gate_weight_grad, gate_weight), (up_weight_grad, up_weight))
    ) / lax.dynamic_slice_in_dim(feedforward_gain, *place_rows)
    gains = jnp.concatenate(
        [first_gain[None], second_gain[None], raw_whole[width : width + 2, :width]], axis=0
    )
    gains = gains + swap_core(gains)
    gains = gains + swap_chip(gains)
    columns_query = query_weight.shape[1]
    columns_key = columns_query + key_weight.shape[1]
    return (
        layer_output,
        tokens_gradient,
        gains[0],
        raw_whole[:width, :columns_query],
        raw_whole[:width, columns_query:columns_key],
        raw_whole[:width, columns_key:],
        gains[2, :head_width],
        gains[3, :head_width],
        output_weight_grad,
        gains[1],
        gate_weight_grad,
        up_weight_grad,
        down_weight_grad,
    )


def solution(mesh):
    dp, tensor = mesh.shape["dp"], mesh.shape["tensor"]

    def program(*args):
        if dp == 8 and tensor == 4 and args[0].shape[0] == SEQ_LEN:
            return shards(dp, *args)
        return plain_shards(*args)

    return jax.shard_map(
        program,
        mesh=mesh,
        in_specs=(
            P("dp", None),
            P(),
            P(None, "tensor"),
            P(None, "tensor"),
            P(None, "tensor"),
            P(),
            P(),
            P("tensor", None),
            P(),
            P(None, "tensor"),
            P(None, "tensor"),
            P("tensor", None),
            P("dp"),
            P("dp"),
            P("dp", None),
        ),
        out_specs=(
            P("dp", None),
            P("dp", None),
            P("dp"),
            P("dp", "tensor"),
            P("dp", "tensor"),
            P("dp", "tensor"),
            P("dp"),
            P("dp"),
            P("tensor", "dp"),
            P("dp"),
            P("dp", "tensor"),
            P("dp", "tensor"),
            P("tensor", "dp"),
        ),
        check_vma=False,
    )
```

```python
import functools

import jax
import jax.numpy as jnp
from jax import lax
from jax.experimental import pallas as pl
from jax.experimental.pallas import tpu as pltpu
from jax.sharding import PartitionSpec as P

HD = 128
SEQ_LEN = 1024


epsilon = 1e-06
rope_base = 1000000.0
masked = -1e30


def rms_inverse(value):
    return lax.rsqrt(jnp.mean(value * value, axis=-1, keepdims=True) + epsilon)


def norm_back(upstream, value, inverse, gain):
    scaled = upstream * gain
    return inverse * scaled - value * inverse**3 * jnp.mean(scaled * value, axis=-1, keepdims=True)


def rotary_tables(positions):
    exponent = jnp.arange(0, HD, 2, dtype=jnp.float32) / HD
    frequency = rope_base ** (-exponent)
    phase = positions.astype(jnp.float32)[:, None] * frequency[None, :]
    phase = jnp.concatenate([phase, phase], axis=-1)
    return (jnp.cos(phase), jnp.sin(phase))


def rotate(value, cosine, sine):
    half = value.shape[-1] // 2
    turned = jnp.concatenate([-value[..., half:], value[..., :half]], axis=-1)
    return value * cosine + turned * sine


def rotate_back(upstream, cosine, sine):
    half = upstream.shape[-1] // 2
    moved = upstream * sine
    return upstream * cosine + jnp.concatenate([moved[..., half:], -moved[..., :half]], axis=-1)


def block_scores(query_rows, keys, row_segments, segments, begin):
    scores = jnp.einsum(
        "rkgd,tkd->kgrt", query_rows, keys, preferred_element_type=jnp.float32
    ) * HD ** (-0.5)
    rows = begin + lax.iota(jnp.int32, query_rows.shape[0])
    columns = lax.iota(jnp.int32, keys.shape[0])
    allowed = (row_segments[:, None] == segments[None, :]) & (rows[:, None] >= columns[None, :])
    return jnp.where(allowed[None, None], scores, masked)


def attend(item):
    queries, keys, values, segments = item
    length = queries.shape[0]
    width = min(512, length)
    outputs = []
    totals = []
    for begin in range(0, length, width):
        scores = block_scores(
            queries[begin : begin + width], keys, segments[begin : begin + width], segments, begin
        )
        peak = jnp.max(scores, axis=-1, keepdims=True)
        expons = jnp.exp(scores - peak)
        total = jnp.sum(expons, axis=-1, keepdims=True)
        chance_low = (expons / total).astype(jnp.bfloat16)
        outputs.append(
            jnp.einsum("kgrt,tkd->rkgd", chance_low, values, preferred_element_type=jnp.float32)
        )
        totals.append(peak + jnp.log(total))
    return (jnp.concatenate(outputs, axis=0), jnp.concatenate(totals, axis=2))


def attend_back(item):
    queries, keys, values, segments, totals, upstream = item
    length = queries.shape[0]
    width = min(512, length)
    query_parts = []
    key_grad = jnp.zeros(keys.shape, jnp.float32)
    value_grad = jnp.zeros(values.shape, jnp.float32)
    for begin in range(0, length, width):
        rows = queries[begin : begin + width]
        scores = block_scores(rows, keys, segments[begin : begin + width], segments, begin)
        chance = jnp.exp(scores - totals[:, :, begin : begin + width])
        chance_low = chance.astype(jnp.bfloat16)
        incoming = upstream[begin : begin + width]
        value_grad = value_grad + jnp.einsum(
            "kgrt,rkgd->tkd", chance_low, incoming, preferred_element_type=jnp.float32
        )
        along = jnp.einsum("rkgd,tkd->kgrt", incoming, values, preferred_element_type=jnp.float32)
        center = jnp.sum(along * chance, axis=-1, keepdims=True)
        score_grad = (chance * (along - center)).astype(jnp.bfloat16)
        query_parts.append(
            jnp.einsum("kgrt,tkd->rkgd", score_grad, keys, preferred_element_type=jnp.float32)
            * HD ** (-0.5)
        )
        key_grad = key_grad + jnp.einsum(
            "kgrt,rkgd->tkd", score_grad, rows, preferred_element_type=jnp.float32
        ) * HD ** (-0.5)
    return (jnp.concatenate(query_parts, axis=0), key_grad, value_grad)


def dot(left, right):
    return jnp.dot(left, right, preferred_element_type=jnp.float32)


def dot_back(left, right):
    return jnp.einsum("tc,dc->td", left, right, preferred_element_type=jnp.float32)


def dot_tokens(left, right):
    return jnp.einsum("tm,tn->mn", left, right, preferred_element_type=jnp.float32)


def line_order(high, place):
    steps = {}
    for block in range(high):
        if block > place:
            steps[block] = high - block + place
        elif block < place:
            steps[block] = high - place + block
    return sorted(steps, key=lambda block: (steps[block], block)) + [place]


def swap_core(value):
    return lax.ppermute(value, "tensor", [(i, i ^ 1) for i in range(4)])


def swap_chip(value):
    return lax.ppermute(value, "tensor", [(i, i ^ 2) for i in range(4)])


MESH = pl.DeviceIdType.MESH


def neighbours():
    dp, tensor = lax.axis_index("dp"), lax.axis_index("tensor")
    core = lax.rem(tensor, 2)
    sibling = {"tensor": tensor + 1 - 2 * core}
    facing = {"tensor": lax.rem(tensor + 2, 4)}
    place = dp // 2
    pair = {"dp": dp + 2 * (1 - 2 * lax.rem(place, 2))}
    return core, sibling, facing, pair


def greet(devices):
    barrier = pltpu.get_barrier_semaphore()
    for device in devices:
        pl.semaphore_signal(barrier, inc=1, device_id=device, device_id_type=MESH)
    pl.semaphore_wait(barrier, len(devices))


def loop_rows(count, step, body):
    def run(index, carry):
        body(pl.ds(pl.multiple_of(index * step, step), step))
        return carry

    lax.fori_loop(0, count // step, run, 0)


def front_kernel(
    size,
    mixed_hbm, output_weight_hbm, tokens_hbm, upstream_hbm, upstream_first,
    gain, gate_hbm, up_hbm, down_hbm,
    hidden_out, second_out, low_own, product_own, gate_own, upward_own,
    low_pair, product_pair, gate_pair, upward_pair, upstream_pair,
    n_recv, n_side, u_recv, u_side,
    mixed, output_weight, gate_weight, up_weight, down_weight,
    c_recv, x_send, x_recv, back_recv, tok, hid, z_send, low, rows16, tiles,
    stage, stage16, terms,
    load_sems, c_sems, x_sems, back_sems, n_sems, n_side_sems, u_sems, u_side_sems,
    tok_sems, hid_sems, low_sems, wave_sems, tile_sems, stage_sems, stage16_sems, term_sems,
):
    core, sibling, facing, pair = neighbours()
    depth = gain.shape[1]
    half = 4 * size
    tile = tiles.shape[-1]
    units = gate_weight.shape[1]

    def begin(which, k):
        side = core if which == 0 else 1 - core
        return pl.multiple_of(side * half + k * size, size)

    def remote(source, target, sems, k, device):
        return pltpu.make_async_remote_copy(
            src_ref=source, dst_ref=target, send_sem=sems.at[0, k], recv_sem=sems.at[1, k],
            device_id=device, device_id_type=MESH,
        )

    loads = [
        pltpu.make_async_copy(source, target, load_sems.at[index])
        for index, (source, target) in enumerate(
            [
                (mixed_hbm, mixed),
                (output_weight_hbm, output_weight),
                (gate_hbm, gate_weight),
                (up_hbm, up_weight),
                (down_hbm, down_weight),
            ]
        )
    ]
    for load in loads:
        load.start()
    greet([sibling, facing, pair])

    c_copies = [remote(terms.at[pl.ds(k * size, size)], c_recv.at[k], c_sems, k, sibling) for k in range(4)]
    x_copies = [remote(x_send.at[k], x_recv.at[k], x_sems, k, facing) for k in range(4)]
    back_copies = [remote(x_send.at[k], back_recv.at[k], back_sems, k, sibling) for k in range(4)]
    n_copies = [remote(z_send.at[k % 2], n_recv.at[k], n_sems, k, pair) for k in range(4)]
    n_sides = [remote(n_recv.at[k], n_side.at[k], n_side_sems, k, sibling) for k in range(4)]
    u_copies = [
        None if k < 2 else remote(z_send.at[k % 2], u_recv.at[k], u_sems, k, pair) for k in range(4)
    ]
    u_sources = [
        upstream_first.at[pl.ds(k * size, size)] if k < 2 else u_recv.at[k] for k in range(4)
    ]
    u_sides = [remote(u_sources[k], u_side.at[k], u_side_sems, k, sibling) for k in range(4)]

    def attention_terms(k):
        def run(column):
            x_send[k, :, column] = jnp.dot(
                mixed[pl.ds(begin(0, k), size), :],
                output_weight[:, column],
                preferred_element_type=jnp.float32,
            )
            terms[pl.ds(k * size, size), column] = jnp.dot(
                mixed[pl.ds(begin(1, k), size), :],
                output_weight[:, column],
                preferred_element_type=jnp.float32,
            )

        loop_rows(depth, 512, run)
        c_copies[k].start()

    def attention_cores(k):
        c_copies[k].wait_recv()

        def run(row):
            x_send[k, row, :] = x_send[k, row, :] + c_recv[k, row, :]

        loop_rows(size, 16, run)
        x_copies[k].start()

    def attention_chips(k):
        x_copies[k].wait()

        def run(row):
            x_send[k, row, :] = x_send[k, row, :] + x_recv[k, row, :]

        loop_rows(size, 16, run)
        back_copies[k].start()

    def token_loads(k):
        return [
            pltpu.make_async_copy(
                tokens_hbm.at[pl.ds(begin(which, k), size)],
                tok.at[k % 2, which],
                tok_sems.at[k % 2, which],
            )
            for which in range(2)
        ]

    def hidden_stores(k):
        return [
            pltpu.make_async_copy(
                hid.at[which], hidden_out.at[pl.ds(begin(which, k), size)], hid_sems.at[which]
            )
            for which in range(2)
        ]

    def low_rows(buffer, which, k, row):
        side = core if which == 0 else 1 - core
        return pl.ds(pl.multiple_of((2 * side + k % 2) * size + row.start, 16), row.size)

    def normed(k):
        for load in token_loads(k):
            load.wait()
        back_copies[k].wait_recv()
        if k > 0:
            for store in hidden_stores(k - 1):
                store.wait()
        if k >= 2:
            n_copies[k - 2].wait_send()

        def run(which, source, row):
            value = tok[k % 2, which, row, :].astype(jnp.float32) + source[k, row, :]
            hid[which, row, :] = value
            unit = value * lax.rsqrt(jnp.mean(value * value, axis=-1, keepdims=True) + epsilon)
            if which == 0:
                z_send[k % 2, row, :] = unit
            low[0, low_rows(low, which, k, row), :] = (unit * gain[...]).astype(jnp.bfloat16)

        loop_rows(size, 16, functools.partial(run, 0, x_send))
        n_copies[k].start()
        loop_rows(size, 16, functools.partial(run, 1, back_recv))
        for store in hidden_stores(k):
            store.start()
        if k + 2 < 4:
            for load in token_loads(k + 2):
                load.start()

    def stage_load(source, slot):
        return pltpu.make_async_copy(source, stage.at[slot], stage_sems.at[slot])

    def pair_rows(k):
        n_copies[k].wait_recv()
        n_sides[k].start()
        stage_load(n_recv.at[k], 0).start()
        stage_load(n_recv.at[k], 0).wait()

        def run(which, row):
            low[1, low_rows(low, which, k, row), :] = (stage[which, row, :] * gain[...]).astype(
                jnp.bfloat16
            )

        loop_rows(size, 16, functools.partial(run, 0))
        n_sides[k].wait_recv()
        stage_load(n_side.at[k], 1).start()
        stage_load(n_side.at[k], 1).wait()
        loop_rows(size, 16, functools.partial(run, 1))

    def upstream_send(k):
        load = pltpu.make_async_copy(
            upstream_hbm.at[pl.ds(begin(0, k), size)], stage16.at[0], stage16_sems.at[0]
        )
        load.start()
        load.wait()

        def run(row):
            z_send[k % 2, row, :] = stage16[0, row, :].astype(jnp.float32)

        loop_rows(size, 16, run)
        u_copies[k].start()

    def upstream_rows(k):
        if k >= 2:
            u_copies[k].wait_recv()
        u_sides[k].start()
        for which in range(2):
            if which == 1:
                u_sides[k].wait_recv()
            source = u_sources[k] if which == 0 else u_side.at[k]
            stage_load(source, which).start()
            stage_load(source, which).wait()

            def run(row):
                stage16[which, row, :] = stage[which, row, :].astype(jnp.bfloat16)

            loop_rows(size, 16, run)
            store = pltpu.make_async_copy(
                stage16.at[which],
                upstream_pair.at[pl.ds(begin(which, k), size)],
                stage16_sems.at[which],
            )
            store.start()
            store.wait()

    def wave_rows(wave, part):
        return pl.ds(part * half + wave * 2 * size, 2 * size)

    def term_stores(wave):
        return [
            pltpu.make_async_copy(
                terms.at[pl.ds(part * 2 * size, 2 * size)],
                second_out.at[wave_rows(wave, part)],
                term_sems.at[part],
            )
            for part in range(2)
        ]

    def feed(wave, index):
        source = upstream_pair if index else upstream_hbm
        low_out, *outs = (
            (low_pair, product_pair, gate_pair, upward_pair)
            if index
            else (low_own, product_own, gate_own, upward_own)
        )
        fetches = [
            pltpu.make_async_copy(
                source.at[wave_rows(wave, part)],
                rows16.at[pl.ds(part * 2 * size, 2 * size)],
                wave_sems.at[part],
            )
            for part in range(2)
        ]
        low_stores = [
            pltpu.make_async_copy(
                low.at[index, pl.ds(part * 2 * size, 2 * size)],
                low_out.at[wave_rows(wave, part)],
                low_sems.at[part],
            )
            for part in range(2)
        ]
        for copy in fetches + low_stores:
            copy.start()
        if index == 0 and wave > 0:
            for copy in term_stores(wave - 1):
                copy.wait()
        for copy in fetches:
            copy.wait()

        def stores(j, slot):
            return [
                pltpu.make_async_copy(
                    tiles.at[slot, which, pl.ds(part * 2 * size, 2 * size)],
                    outs[which].at[
                        wave_rows(wave, part), pl.ds(pl.multiple_of(j * tile, tile), tile)
                    ],
                    tile_sems.at[slot, which, part],
                )
                for which in range(3)
                for part in range(2)
            ]

        def run(j, carry):
            slot = lax.rem(j, 2)
            column = pl.ds(pl.multiple_of(j * tile, tile), tile)
            gate = jnp.dot(
                low[index], gate_weight[:, column], preferred_element_type=jnp.float32
            )
            upward = jnp.dot(
                low[index], up_weight[:, column], preferred_element_type=jnp.float32
            )
            grad = lax.dot_general(
                rows16[...],
                down_weight[column, :],
                (((1,), (1,)), ((), ())),
                preferred_element_type=jnp.float32,
            )
            sigmoid_gate = jax.nn.sigmoid(gate)
            activated = gate * sigmoid_gate

            @pl.when(j >= 2)
            def _():
                for store in stores(j - 2, slot):
                    store.wait()

            tiles[slot, 0] = (activated * upward).astype(jnp.bfloat16)
            gate_grad = (
                grad * upward * sigmoid_gate * (1.0 + gate * (1.0 - sigmoid_gate))
            ).astype(jnp.bfloat16)
            upward_grad = (grad * activated).astype(jnp.bfloat16)
            tiles[slot, 1] = gate_grad
            tiles[slot, 2] = upward_grad
            for store in stores(j, slot):
                store.start()
            if index == 0:
                across_last = (((1,), (1,)), ((), ()))
                for first in range(0, depth, depth // 4):
                    part = pl.ds(first, depth // 4)
                    term = lax.dot_general(
                        gate_grad,
                        gate_weight[part, column],
                        across_last,
                        preferred_element_type=jnp.float32,
                    ) + lax.dot_general(
                        upward_grad,
                        up_weight[part, column],
                        across_last,
                        preferred_element_type=jnp.float32,
                    )

                    @pl.when(j == 0)
                    def _():
                        terms[:, part] = term

                    @pl.when(j > 0)
                    def _():
                        terms[:, part] += term

            return carry

        number = units // tile
        lax.fori_loop(0, number, run, 0)
        for j in range(max(0, number - 2), number):
            for store in stores(j, j % 2):
                store.wait()
        for copy in low_stores:
            copy.wait()
        if index == 0:
            for copy in term_stores(wave):
                copy.start()

    for k in range(2):
        for load in token_loads(k):
            load.start()
    loads[0].wait()
    loads[1].wait()
    attention_terms(0)
    attention_terms(1)
    attention_cores(0)
    attention_terms(2)
    attention_cores(1)
    attention_terms(3)
    attention_cores(2)
    attention_cores(3)
    upstream_send(2)
    upstream_send(3)
    upstream_rows(0)
    upstream_rows(1)
    attention_chips(0)
    u_copies[2].wait_send()
    normed(0)
    attention_chips(1)
    u_copies[3].wait_send()
    normed(1)
    for load in loads[2:]:
        load.wait()
    upstream_rows(2)
    for k in range(4):
        c_copies[k].wait_send()
    feed(0, 0)
    attention_chips(2)
    normed(2)
    upstream_rows(3)
    pair_rows(0)
    attention_chips(3)
    normed(3)
    pair_rows(1)
    feed(0, 1)
    feed(1, 0)
    pair_rows(2)
    pair_rows(3)
    feed(1, 1)

    for k in range(4):
        back_copies[k].wait_send()
        n_sides[k].wait_send()
        u_sides[k].wait_send()
        if k >= 2:
            n_copies[k].wait_send()
    for store in hidden_stores(3):
        store.wait()
    for copy in term_stores(1):
        copy.wait()


def front(mixed, output_weight, tokens, upstream, upstream_first, gain, gate_weight, up_weight, down_weight):
    rows, depth = tokens.shape
    inner, units = mixed.shape[1], gate_weight.shape[1]
    size = rows // 8
    tile = 256
    f32, b16 = jnp.float32, jnp.bfloat16
    any_space = pl.BlockSpec(memory_space=pl.ANY)
    shape = jax.ShapeDtypeStruct
    outs = [shape((rows, depth), f32)] * 2
    outs += ([shape((rows, depth), b16)] + [shape((rows, units), b16)] * 3) * 2
    outs += [shape((rows, depth), b16)] + [shape((4, size, depth), f32)] * 4
    dma = pltpu.SemaphoreType.DMA
    return pl.pallas_call(
        functools.partial(front_kernel, size),
        out_shape=outs,
        in_specs=[any_space] * 5 + [pl.BlockSpec(memory_space=pltpu.VMEM)] + [any_space] * 3,
        out_specs=[any_space] * len(outs),
        scratch_shapes=[
            pltpu.VMEM((rows, inner), b16),
            pltpu.VMEM((inner, depth), b16),
            pltpu.VMEM((depth, units), b16),
            pltpu.VMEM((depth, units), b16),
            pltpu.VMEM((units, depth), b16),
            pltpu.VMEM((4, size, depth), f32),
            pltpu.VMEM((4, size, depth), f32),
            pltpu.VMEM((4, size, depth), f32),
            pltpu.VMEM((4, size, depth), f32),
            pltpu.VMEM((2, 2, size, depth), b16),
            pltpu.VMEM((2, size, depth), f32),
            pltpu.VMEM((2, size, depth), f32),
            pltpu.VMEM((2, 4 * size, depth), b16),
            pltpu.VMEM((4 * size, depth), b16),
            pltpu.VMEM((2, 3, 4 * size, tile), b16),
            pltpu.VMEM((2, size, depth), f32),
            pltpu.VMEM((2, size, depth), b16),
            pltpu.VMEM((4 * size, depth), f32),
            dma((5,)),
            dma((2, 4)),
            dma((2, 4)),
            dma((2, 4)),
            dma((2, 4)),
            dma((2, 4)),
            dma((2, 4)),
            dma((2, 4)),
            dma((2, 2)),
            dma((2,)),
            dma((2,)),
            dma((2,)),
            dma((2, 3, 2)),
            dma((2,)),
            dma((2,)),
            dma((2,)),
        ],
        compiler_params=pltpu.CompilerParams(
            collective_id=1, has_side_effects=True, vmem_limit_bytes=62 * 1024 * 1024
        ),
        cost_estimate=pl.CostEstimate(
            flops=12 * rows * depth * units, bytes_accessed=6 * depth * units, transcendentals=0
        ),
    )(mixed, output_weight, tokens, upstream, upstream_first, gain[None], gate_weight, up_weight, down_weight)


def sequence_rows(size, core, which, k):
    side = core if which == 0 else 1 - core
    return pl.multiple_of(side * 4 * size + k * size, size)


def remote(source, target, sems, k, device):
    return pltpu.make_async_remote_copy(
        src_ref=source, dst_ref=target, send_sem=sems.at[0, k], recv_sem=sems.at[1, k],
        device_id=device, device_id_type=MESH,
    )


def grid_neighbours():
    dp = lax.axis_index("dp")
    place, lane = dp // 2, lax.rem(dp, 2)
    towards = 1 - 2 * (place // 2)
    across = {"dp": dp + 1 - 2 * lane}
    inward, outward = {"dp": dp + 2 * towards}, {"dp": dp - 2 * towards}
    team = place // 2
    side = lax.rem(place, 2)
    inner = lax.rem(team + side, 2)
    return place, lane, team, side, inner, across, inward, outward


def greet_grid(always, inner, outward):
    barrier = pltpu.get_barrier_semaphore()
    for device in always:
        pl.semaphore_signal(barrier, inc=1, device_id=device, device_id_type=MESH)

    @pl.when(inner == 1)
    def _():
        pl.semaphore_signal(barrier, inc=1, device_id=outward, device_id_type=MESH)

    pl.semaphore_wait(barrier, len(always) + inner)


def middle_kernel(
    size,
    second_hbm, hidden_hbm, upstream_hbm, upstream_pair, product_own, product_pair,
    gate_own, gate_pair, low_own, low_pair, gain, down_hbm,
    grad_out, grad_low_out, out_part, weight_out, gate_ready, gate_given, gate_own_block,
    products, down_weight, columns, c_recv, x_send, x_recv, back_recv,
    y_send, y_recv, kept, in_recv, mid_recv, out_recv,
    hid, tok, grad, grad_low, out_stage, gate_send, gate_kept, gate_stage,
    load_sems, gate_load_sems, gate_sems, c_sems, x_sems, back_sems, y_sems, z_sems, column_sems,
    x_load_sems, hid_sems, tok_sems, grad_sems, low_sems, out_sems, weight_sems,
):
    core, sibling, facing, _ = neighbours()
    place, lane, team, side, inner, across, inward, outward = grid_neighbours()
    depth = gain.shape[1]
    units = down_weight.shape[0]
    width = columns.shape[-1]
    begin = functools.partial(sequence_rows, size, core)
    loads = [
        pltpu.make_async_copy(source, target, load_sems.at[index])
        for index, (source, target) in enumerate(
            [(product_own, products.at[0]), (product_pair, products.at[1]), (down_hbm, down_weight)]
        )
    ]
    gate_loads = [
        pltpu.make_async_copy(source, products.at[index], gate_load_sems.at[index])
        for index, source in enumerate((gate_own, gate_pair))
    ]
    turns = [(0, 1), (1, 1), (0, 0), (1, 0)]
    turns += [(0, 1), (1, 1), (1, 0), (0, 0)]

    def column_loads(index):
        turn, other = turns[index]
        spot = lax.rem(1 - team + turn, 2)
        which = 1 - lane if other else lane
        start = pl.multiple_of((side * 4 + 2 * spot + which) * width, width)
        return [
            pltpu.make_async_copy(
                source.at[:, pl.ds(start, width)],
                columns.at[index % 2, part],
                column_sems.at[index % 2, part],
            )
            for part, source in enumerate(
                (upstream_hbm, upstream_pair) if index < 4 else (low_own, low_pair)
            )
        ]

    x_loads = [
        pltpu.make_async_copy(
            second_hbm.at[pl.ds(begin(0, k), size)], x_send.at[k], x_load_sems.at[k]
        )
        for k in range(4)
    ]
    for copy in column_loads(0) + x_loads[:1] + loads[:2] + column_loads(1) + x_loads[1:] + loads[2:]:
        copy.start()
    greet_grid([sibling, facing, across, inward], inner, outward)
    c_copies = [
        remote(second_hbm.at[pl.ds(begin(1, k), size)], c_recv.at[k], c_sems, k, sibling)
        for k in range(4)
    ]
    x_copies = [remote(x_send.at[k], x_recv.at[k], x_sems, k, facing) for k in range(4)]
    back_copies = [remote(x_send.at[k], back_recv.at[k], back_sems, k, sibling) for k in range(4)]
    y_copies = [remote(y_send.at[k], y_recv.at[k], y_sems, k, across) for k in range(2)]
    in_copy = remote(kept.at[0], in_recv, z_sems, 0, inward)
    mid_copies = [remote(kept.at[k], mid_recv.at[k], z_sems, 1 + k, inward) for k in range(2)]
    out_copy = remote(mid_recv.at[0], out_recv, z_sems, 3, outward)
    for copy in c_copies:
        copy.start()

    def cores(k):
        x_loads[k].wait()
        c_copies[k].wait_recv()

        def run(row):
            x_send[k, row, :] = x_send[k, row, :] + c_recv[k, row, :]

        loop_rows(size, 16, run)
        x_copies[k].start()

    def chips(k):
        x_copies[k].wait()

        def run(row):
            x_send[k, row, :] = x_send[k, row, :] + x_recv[k, row, :]

        loop_rows(size, 16, run)
        back_copies[k].start()

    def block(index, target):
        for copy in column_loads(index):
            copy.wait()

        def run(rows):
            total = None
            for part in range(2):
                term = lax.dot_general(
                    products[part, :, rows],
                    columns[index % 2, part],
                    (((0,), (0,)), ((), ())),
                    preferred_element_type=jnp.float32,
                )
                total = term if total is None else total + term
            target[rows, :] = total

        loop_rows(units, 512, run)
        for copy in column_loads(index + 2):
            copy.start()

    gate_copy = remote(gate_send, gate_kept, gate_sems, 0, across)

    def gate_block(index, target, added):
        for copy in column_loads(index):
            copy.wait()

        def run(rows):
            total = None
            for part in range(2):
                term = lax.dot_general(
                    columns[index % 2, part],
                    products[part, :, rows],
                    (((0,), (0,)), ((), ())),
                    preferred_element_type=jnp.float32,
                )
                total = term if total is None else total + term
            target[:, rows] = target[:, rows] + total if added else total

        loop_rows(units, 512, run)
        if index + 2 < len(turns):
            for copy in column_loads(index + 2):
                copy.start()

    def gate_store(source, target, index):
        return pltpu.make_async_copy(source, target, gate_load_sems.at[2 + index])

    def chunk_loads(k):
        return [
            pltpu.make_async_copy(
                source.at[pl.ds(begin(which, k), size)], target.at[which], sems.at[which]
            )
            for which in range(2)
            for source, target, sems in ((hidden_hbm, hid, hid_sems), (upstream_hbm, tok, tok_sems))
        ]

    def grad_stores(k):
        return [
            pltpu.make_async_copy(
                source.at[which], target.at[pl.ds(begin(which, k), size)], sems.at[which]
            )
            for which in range(2)
            for source, target, sems in (
                (grad, grad_out, grad_sems),
                (grad_low, grad_low_out, low_sems),
            )
        ]

    def finish(k):
        for copy in chunk_loads(k):
            copy.wait()
        if k > 0:
            for copy in grad_stores(k - 1):
                copy.wait()
        back_copies[k].wait_recv()

        def run(which, source, row):
            value = hid[which, row, :]
            inverse = lax.rsqrt(jnp.mean(value * value, axis=-1, keepdims=True) + epsilon)
            total = tok[which, row, :].astype(jnp.float32) + norm_back(
                source[k, row, :], value, inverse, gain[...]
            )
            grad[which, row, :] = total
            grad_low[which, row, :] = total.astype(jnp.bfloat16)

        for which, source in enumerate((x_send, back_recv)):
            loop_rows(size, 16, functools.partial(run, which, source))
        for copy in grad_stores(k):
            copy.start()
        if k < 3:
            for copy in chunk_loads(k + 1):
                copy.start()

    def out_store(k):
        rows = 2 * size
        return pltpu.make_async_copy(
            out_stage, out_part.at[pl.ds(k * rows, rows)], out_sems.at[0]
        )

    def out_terms(k):
        if k > 0:
            out_store(k - 1).wait()
        rows = pl.ds(k * 2 * size, 2 * size)

        def run(column):
            out_stage[:, column] = jnp.dot(
                products[0, rows, :], down_weight[:, column], preferred_element_type=jnp.float32
            )

        loop_rows(depth, 512, run)
        out_store(k).start()

    def take(k):
        y_copies[k].wait_recv()

        def run(row):
            kept[k, row, :] = kept[k, row, :] + y_recv[k, row, :]

        loop_rows(units, 64, run)

    cores(0)
    for copy in loads[:2]:
        copy.wait()
    block(0, y_send.at[0])
    y_copies[0].start()
    for copy in chunk_loads(0):
        copy.start()
    cores(1)
    cores(2)
    cores(3)
    block(1, y_send.at[1])
    y_copies[1].start()
    block(2, kept.at[0])
    loads[2].wait()
    out_terms(0)
    chips(0)
    out_terms(1)
    block(3, kept.at[1])
    finish(0)
    out_terms(2)
    take(0)

    @pl.when(inner == 1)
    def _():
        mid_copies[0].start()

    @pl.when(inner == 0)
    def _():
        in_copy.start()

    out_terms(3)
    for copy in gate_loads:
        copy.start()
    chips(1)
    for copy in gate_loads:
        copy.wait()
    gate_block(4, gate_send, False)
    gate_copy.start()
    finish(1)
    gate_block(5, gate_stage, False)
    gate_store(gate_stage, gate_given, 0).start()
    chips(2)
    take(1)

    @pl.when(inner == 1)
    def _():
        mid_copies[1].start()
        mid_copies[0].wait_recv()
        out_copy.start()

    finish(2)
    gate_store(gate_stage, gate_given, 0).wait()
    gate_block(6, gate_stage, False)
    gate_store(gate_stage, gate_own_block, 1).start()
    chips(3)
    finish(3)
    gate_copy.wait()
    gate_block(7, gate_kept, True)
    gate_store(gate_kept, gate_ready, 2).start()

    @pl.when(inner == 1)
    def _():
        in_copy.wait_recv()
        mid_copies[1].wait_recv()
        mid_copies[0].wait_send()
        mid_copies[1].wait_send()
        out_copy.wait_send()

        def run(row):
            kept[0, row, :] = in_recv[row, :] + mid_recv[1, row, :]

        loop_rows(units, 64, run)

    @pl.when(inner == 0)
    def _():
        in_copy.wait_send()
        out_copy.wait_recv()

        def run(row):
            kept[0, row, :] = kept[1, row, :] + out_recv[row, :]

        loop_rows(units, 64, run)

    store = pltpu.make_async_copy(kept.at[0], weight_out, weight_sems.at[0])
    store.start()
    for k in range(4):
        back_copies[k].wait_send()
        c_copies[k].wait_send()
    for k in range(2):
        y_copies[k].wait_send()
    for copy in grad_stores(3):
        copy.wait()
    gate_store(gate_stage, gate_own_block, 1).wait()
    gate_store(gate_kept, gate_ready, 2).wait()
    out_store(3).wait()
    store.wait()


def middle(
    second, hidden, upstream, upstream_pair, product_own, product_pair,
    gate_own, gate_pair, low_own, low_pair, gain, down_weight,
):
    rows, depth = hidden.shape
    units = down_weight.shape[0]
    size = rows // 8
    width = depth // 8
    f32, b16 = jnp.float32, jnp.bfloat16
    any_space = pl.BlockSpec(memory_space=pl.ANY)
    shape = jax.ShapeDtypeStruct
    dma = pltpu.SemaphoreType.DMA
    vmem = pltpu.VMEM
    return pl.pallas_call(
        functools.partial(middle_kernel, size),
        out_shape=[
            shape((rows, depth), f32),
            shape((rows, depth), b16),
            shape((rows, depth), f32),
            shape((units, width), f32),
        ]
        + [shape((width, units), f32)] * 3,
        in_specs=[any_space] * 10 + [pl.BlockSpec(memory_space=pltpu.VMEM), any_space],
        out_specs=[any_space] * 7,
        scratch_shapes=[
            vmem((2, rows, units), b16),
            vmem((units, depth), b16),
            vmem((2, 2, rows, width), b16),
            vmem((4, size, depth), f32),
            vmem((4, size, depth), f32),
            vmem((4, size, depth), f32),
            vmem((4, size, depth), f32),
            vmem((2, units, width), f32),
            vmem((2, units, width), f32),
            vmem((2, units, width), f32),
            vmem((units, width), f32),
            vmem((2, units, width), f32),
            vmem((units, width), f32),
            vmem((2, size, depth), f32),
            vmem((2, size, depth), b16),
            vmem((2, size, depth), f32),
            vmem((2, size, depth), b16),
            vmem((2 * size, depth), f32),
            vmem((width, units), f32),
            vmem((width, units), f32),
            vmem((width, units), f32),
            dma((3,)),
            dma((5,)),
            dma((2, 1)),
            dma((2, 4)),
            dma((2, 4)),
            dma((2, 4)),
            dma((2, 2)),
            dma((2, 4)),
            dma((2, 2)),
            dma((4,)),
            dma((2,)),
            dma((2,)),
            dma((2,)),
            dma((2,)),
            dma((1,)),
            dma((1,)),
        ],
        compiler_params=pltpu.CompilerParams(
            collective_id=2, has_side_effects=True, vmem_limit_bytes=62 * 1024 * 1024
        ),
        cost_estimate=pl.CostEstimate(
            flops=8 * rows * depth * units, bytes_accessed=6 * depth * units, transcendentals=0
        ),
    )(
        second, hidden, upstream, upstream_pair, product_own, product_pair,
        gate_own, gate_pair, low_own, low_pair, gain[None], down_weight,
    )


class TensorSum:
    def __init__(self, size, own, landed, stage, sems, stage_sems, devices):
        self.size, self.own, self.landed, self.stage = size, own, landed, stage
        self.stage_sems = stage_sems
        c_sems, x_sems, back_sems = sems
        self.sibling, facing = devices
        self.c_sems = c_sems
        self.x_copies = [remote(own.at[k], landed[1].at[k], x_sems, k, facing) for k in range(4)]
        self.back_copies = [
            remote(own.at[k], landed[2].at[k], back_sems, k, self.sibling) for k in range(4)
        ]
        self.c_copies = [None] * 4

    def give(self, k, source):
        self.c_copies[k] = remote(source, self.landed[0].at[k], self.c_sems, k, self.sibling)
        self.c_copies[k].start()

    def staged(self, which, k):
        copy = pltpu.make_async_copy(self.landed[which].at[k], self.stage.at[0], self.stage_sems.at[0])
        copy.start()
        copy.wait()

    def add_stage(self, k):
        def run(row):
            self.own[k, row, :] = self.own[k, row, :] + self.stage[0, row, :]

        loop_rows(self.size, 16, run)

    def cores(self, k):
        self.c_copies[k].wait_recv()
        self.staged(0, k)
        self.add_stage(k)
        self.x_copies[k].start()

    def chips(self, k):
        self.x_copies[k].wait()
        self.staged(1, k)
        self.add_stage(k)
        self.back_copies[k].start()

    def other(self, k):
        self.back_copies[k].wait_recv()
        self.staged(2, k)


def rear_kernel(
    size, turns,
    gate_ready0, gate_ready1, low_own, low_pair, upward_own, upward_pair,
    normed_hbm, raw_hbm, hidden_low_hbm, mixed_hbm, lines,
    out_hbm, hidden_hbm, grad_hbm, tokens_hbm, query_hbm, key_hbm, value_hbm, gain,
    layer_out, tokens_out, gate_out, up_out, raw_out, head_out,
    o_c, o_x, o_back, d_c, d_x, d_back, gate_landed, up_landed,
    upwards, raw, mixed, query_weight, key_weight, value_weight, columns,
    up_send, up_kept, raw_send, raw_kept, head_send, head_kept, raw_line, head_line,
    own, give, stage, wide, narrow, result,
    load_sems, column_sems, y_up_sems, y_raw_sems, y_head_sems, gate_sems, up_sems,
    raw_line_sems, head_line_sems,
    oc_sems, ox_sems, ob_sems, dc_sems, dx_sems, db_sems,
    own_sems, stage_sems, wide_sems, narrow_sems, result_sems, end_sems,
):
    core, sibling, facing, _ = neighbours()
    place, lane, team, side, inner, across, inward, outward = grid_neighbours()
    high = len(turns)
    depth = gain.shape[1]
    width = columns.shape[-1]
    units = upwards.shape[-1]
    begin = functools.partial(sequence_rows, size, core)
    loads = [
        pltpu.make_async_copy(source, target, load_sems.at[index])
        for index, (source, target) in enumerate(
            [
                (upward_own, upwards.at[0]),
                (upward_pair, upwards.at[1]),
                (raw_hbm, raw),
                (mixed_hbm, mixed),
                (query_hbm, query_weight),
                (key_hbm, key_weight),
                (value_hbm, value_weight),
            ]
        )
    ]
    blocks = [
        ("up", 0, 1), ("up", 1, 1), ("head", 0, 1), ("head", 1, 1), ("head", 2, 1), ("head", 3, 1),
        ("up", 0, 0), ("up", 1, 0), ("head", 0, 0), ("head", 1, 0), ("head", 2, 0), ("head", 3, 0),
    ]

    def spot_of(kind, turn):
        if kind == "up":
            return side * 2 + lax.rem(1 - team + turn, 2)
        spot = jnp.int32(turns[0][turn])
        for p in range(1, high):
            spot = jnp.where(place == p, jnp.int32(turns[p][turn]), spot)
        return spot

    def column_loads(index):
        kind, turn, other = blocks[index]
        which = 1 - lane if other else lane
        start = pl.multiple_of((2 * spot_of(kind, turn) + which) * width, width)
        sources = (low_own, low_pair) if kind == "up" else (normed_hbm, hidden_low_hbm)
        return [
            pltpu.make_async_copy(
                source.at[:, pl.ds(start, width)],
                columns.at[index % 2, part],
                column_sems.at[index % 2, part],
            )
            for part, source in enumerate(sources)
        ]

    own_loads = [
        pltpu.make_async_copy(out_hbm.at[pl.ds(begin(0, k), size)], own.at[k], own_sems.at[k])
        for k in range(4)
    ]
    for copy in column_loads(0) + loads[:2] + column_loads(1) + own_loads + loads[2:]:
        copy.start()
    greet_grid([sibling, facing, across, inward], inner, outward)
    devices = (sibling, facing)
    outs = TensorSum(
        size, own, (o_c, o_x, o_back), stage, (oc_sems, ox_sems, ob_sems), stage_sems, devices
    )
    heads = TensorSum(
        size, own, (d_c, d_x, d_back), stage, (dc_sems, dx_sems, db_sems), stage_sems, devices
    )
    for k in range(4):
        outs.give(k, out_hbm.at[pl.ds(begin(1, k), size)])

    def team_copies(values, landed, sems):
        return (
            remote(values[0], landed.at[0], sems, 0, inward),
            [remote(values[k], landed.at[1 + k], sems, 1 + k, inward) for k in range(2)],
            remote(landed.at[1], landed.at[3], sems, 3, outward),
        )

    gate_copies = team_copies((gate_ready0, gate_ready1), gate_landed, gate_sems)
    up_copies = team_copies((up_kept.at[0], up_kept.at[1]), up_landed, up_sems)

    def team_send(copies, turn):
        @pl.when(inner == 1)
        def _():
            copies[1][turn].start()

        if turn == 0:

            @pl.when(inner == 0)
            def _():
                copies[0].start()

    def team_forward(copies):
        @pl.when(inner == 1)
        def _():
            copies[1][0].wait_recv()
            copies[2].start()

    def team_combine(copies, landed, last, out, sem):
        def fetch(source, slot):
            copy = pltpu.make_async_copy(source, up_send.at[slot], end_sems.at[4 + slot])
            copy.start()
            copy.wait()

        @pl.when(inner == 1)
        def _():
            copies[0].wait_recv()
            copies[1][1].wait_recv()
            fetch(landed.at[0], 0)
            fetch(landed.at[2], 1)
            copies[1][0].wait_send()
            copies[1][1].wait_send()
            copies[2].wait_send()

        @pl.when(inner == 0)
        def _():
            copies[0].wait_send()
            copies[2].wait_recv()
            fetch(landed.at[3], 0)
            fetch(last, 1)

        def run(row):
            up_send[0, row, :] = up_send[0, row, :] + up_send[1, row, :]

        loop_rows(width, 16, run)
        store = pltpu.make_async_copy(up_send.at[0], out, sem)
        store.start()
        store.wait()

    y_up = [remote(up_send.at[k], up_kept.at[k], y_up_sems, k, across) for k in range(2)]
    y_raw = [remote(raw_send.at[k], raw_kept.at[k], y_raw_sems, k, across) for k in range(high)]
    y_head = [
        remote(head_send.at[k], head_kept.at[k], y_head_sems, k, across) for k in range(high)
    ]

    def line_copy(p, turn, towards=None):
        block = turns[p][turn]
        ahead = block > p
        slot = block - 1 if ahead else high - 1 + block
        device = {"dp": lax.axis_index("dp") + (2 if ahead else -2)}
        return slot, [
            remote(kept.at[turn], line.at[slot], sems, slot, device)
            for kept, line, sems in (
                (raw_kept, raw_line, raw_line_sems),
                (head_kept, head_line, head_line_sems),
            )
        ]

    def line_arrived(slot, turn):
        for kept, line, sems in (
            (raw_kept, raw_line, raw_line_sems),
            (head_kept, head_line, head_line_sems),
        ):
            remote(kept.at[turn], line.at[slot], sems, slot, across).wait_recv()

            def run(row):
                kept[turn, row, :] = kept[turn, row, :] + line[slot, row, :]

            loop_rows(kept.shape[1], 8, run)

    def line_step(turn):
        for p in range(high):
            block = turns[p][turn]

            @pl.when(place == p)
            def _():
                slot, copies = line_copy(p, turn)
                if (block > p and p > 0) or (block < p and p < high - 1):
                    line_arrived(slot, turn)
                for copy in copies:
                    copy.start()

    def line_end():
        for p in range(high):

            @pl.when(place == p)
            def _():
                if p > 0:
                    line_arrived(p - 1, high - 1)
                if p < high - 1:
                    line_arrived(high - 1 + p, high - 1)
                for turn in range(high - 1):
                    for copy in line_copy(p, turn)[1]:
                        copy.wait_send()

    def up_block(index, target, added):
        for copy in column_loads(index):
            copy.wait()

        def run(rows):
            total = None
            for part in range(2):
                term = lax.dot_general(
                    columns[index % 2, part],
                    upwards[part, :, rows],
                    (((0,), (0,)), ((), ())),
                    preferred_element_type=jnp.float32,
                )
                total = term if total is None else total + term
            target[:, rows] = target[:, rows] + total if added else total

        loop_rows(units, 512, run)
        if index + 2 < len(blocks):
            for copy in column_loads(index + 2):
                copy.start()

    def head_block(index, raw_target, head_target, added):
        kind, turn, other = blocks[index]
        which = 1 - lane if other else lane
        for copy in column_loads(index):
            copy.wait()
        sums = (((0,), (0,)), ((), ()))

        def run(rows):
            total = lax.dot_general(
                columns[index % 2, 0], raw[:, rows], sums, preferred_element_type=jnp.float32
            )
            line = lines[2 * spot_of(kind, turn) + which, :, rows]
            if added:
                raw_target[:width, rows] = raw_target[:width, rows] + total
                raw_target[width:, rows] = raw_target[width:, rows] + line
            else:
                raw_target[:width, rows] = total
                raw_target[width:, rows] = line

        loop_rows(raw.shape[1], 512, run)
        total = lax.dot_general(
            mixed[...], columns[index % 2, 1], sums, preferred_element_type=jnp.float32
        )
        head_target[...] = head_target[...] + total if added else total
        if index + 2 < len(blocks):
            for copy in column_loads(index + 2):
                copy.start()

    def head_send_block(index):
        turn = blocks[index][1]
        head_block(index, raw_send.at[turn], head_send.at[turn], False)
        y_raw[turn].start()
        y_head[turn].start()

    def head_take(index):
        turn = blocks[index][1]
        y_raw[turn].wait_recv()
        y_head[turn].wait_recv()
        head_block(index, raw_kept.at[turn], head_kept.at[turn], True)

    def head_terms(k):
        outs.back_copies[k].wait_send()
        if k >= 2:
            heads.c_copies[k - 2].wait_send()
        across_last = (((1,), (1,)), ((), ()))
        cuts = (0, query_weight.shape[1], query_weight.shape[1] + key_weight.shape[1], raw.shape[1])

        def run(rows):
            for which in range(2):
                total = None
                for part, weight in enumerate((query_weight, key_weight, value_weight)):
                    term = lax.dot_general(
                        raw[pl.ds(begin(which, k), size), cuts[part] : cuts[part + 1]],
                        weight[rows, :],
                        across_last,
                        preferred_element_type=jnp.float32,
                    )
                    total = term if total is None else total + term
                if which == 0:
                    own[k, :, rows] = total
                else:
                    give[k % 2, :, rows] = total

        loop_rows(depth, 512, run)
        heads.give(k, give.at[k % 2])

    def fetches(what, k):
        pairs = ((hidden_hbm, wide, wide_sems),)
        if what == "tokens":
            pairs = ((grad_hbm, wide, wide_sems), (tokens_hbm, narrow, narrow_sems))
        return [
            pltpu.make_async_copy(
                source.at[pl.ds(begin(which, k), size)], target.at[which], sems.at[which]
            )
            for which in range(2)
            for source, target, sems in pairs
        ]

    def stores(what, k):
        return [
            pltpu.make_async_copy(
                result.at[which],
                (layer_out if what == "layer" else tokens_out).at[pl.ds(begin(which, k), size)],
                result_sems.at[which],
            )
            for which in range(2)
        ]

    sequence = [("layer", k) for k in range(4)] + [("tokens", k) for k in range(4)]

    def finish(what, k):
        number = sequence.index((what, k))
        for copy in fetches(what, k):
            copy.wait()
        if number > 0:
            for copy in stores(*sequence[number - 1]):
                copy.wait()
        (outs if what == "layer" else heads).other(k)

        def run(which, row):
            total = stage[0, row, :] if which else own[k, row, :]
            value = wide[which, row, :]
            if what == "layer":
                total = value + total
            else:
                inputs = narrow[which, row, :].astype(jnp.float32)
                inverse = lax.rsqrt(jnp.mean(inputs * inputs, axis=-1, keepdims=True) + epsilon)
                total = value + norm_back(total, inputs, inverse, gain[...])
            result[which, row, :] = total.astype(jnp.bfloat16)

        for which in range(2):
            loop_rows(size, 16, functools.partial(run, which))
        for copy in stores(what, k):
            copy.start()
        if number + 1 < len(sequence):
            for copy in fetches(*sequence[number + 1]):
                copy.start()

    team_send(gate_copies, 0)
    team_send(gate_copies, 1)
    for copy in fetches("layer", 0):
        copy.start()
    for copy in loads[:2]:
        copy.wait()
    up_block(0, up_send.at[0], False)
    y_up[0].start()
    own_loads[0].wait()
    outs.cores(0)
    up_block(1, up_send.at[1], False)
    y_up[1].start()
    for k in range(1, 4):
        own_loads[k].wait()
        outs.cores(k)
    for copy in loads[2:]:
        copy.wait()
    head_send_block(2)
    head_send_block(3)
    outs.chips(0)
    head_send_block(4)
    finish("layer", 0)
    team_forward(gate_copies)
    y_up[0].wait_recv()
    head_send_block(5)
    up_block(6, up_kept.at[0], True)
    team_send(up_copies, 0)
    head_terms(0)
    outs.chips(1)
    finish("layer", 1)
    head_terms(1)
    y_up[1].wait_recv()
    up_block(7, up_kept.at[1], True)
    team_send(up_copies, 1)
    outs.chips(2)
    heads.cores(0)
    finish("layer", 2)
    head_terms(2)
    heads.cores(1)
    outs.chips(3)
    heads.cores(2)
    finish("layer", 3)
    head_terms(3)
    heads.cores(3)
    head_take(8)
    line_step(0)
    heads.chips(0)
    finish("tokens", 0)
    team_forward(up_copies)
    head_take(9)
    line_step(1)
    heads.chips(1)
    finish("tokens", 1)
    heads.chips(2)
    finish("tokens", 2)
    head_take(10)
    line_step(2)
    for k in range(2):
        y_up[k].wait_send()
    team_combine(gate_copies, gate_landed, gate_ready1, gate_out, end_sems.at[0])
    heads.chips(3)
    finish("tokens", 3)
    team_combine(up_copies, up_landed, up_kept.at[1], up_out, end_sems.at[1])
    head_take(11)
    line_end()
    ends = [
        pltpu.make_async_copy(raw_kept.at[high - 1], raw_out, end_sems.at[2]),
        pltpu.make_async_copy(head_kept.at[high - 1], head_out, end_sems.at[3]),
    ]
    for copy in ends:
        copy.start()
    for k in range(4):
        outs.c_copies[k].wait_send()
        heads.back_copies[k].wait_send()
    for k in range(2, 4):
        heads.c_copies[k].wait_send()
    for k in range(high):
        y_raw[k].wait_send()
        y_head[k].wait_send()
    for copy in stores(*sequence[-1]) + ends:
        copy.wait()


def rear(turns, arrays, lines, places, weights, gain):
    rows, depth = places[0].shape
    units = arrays[0].shape[1]
    heads, inner = arrays[7].shape[1], arrays[9].shape[1]
    size = rows // 8
    width = depth // 8
    high = len(turns)
    f32, b16 = jnp.float32, jnp.bfloat16
    any_space = pl.BlockSpec(memory_space=pl.ANY)
    in_vmem = pl.BlockSpec(memory_space=pltpu.VMEM)
    shape = jax.ShapeDtypeStruct
    dma = pltpu.SemaphoreType.DMA
    vmem = pltpu.VMEM
    slots = 2 * (high - 1)
    return pl.pallas_call(
        functools.partial(rear_kernel, size, turns),
        out_shape=[
            shape((rows, depth), b16),
            shape((rows, depth), b16),
            shape((width, units), f32),
            shape((width, units), f32),
            shape((width + 8, heads), f32),
            shape((inner, width), f32),
        ]
        + [shape((4, size, depth), f32)] * 6
        + [shape((4, width, units), f32)] * 2,
        in_specs=[any_space] * 10 + [in_vmem] + [any_space] * 7 + [in_vmem],
        out_specs=[any_space] * 14,
        scratch_shapes=[
            vmem((2, rows, units), b16),
            vmem((rows, heads), b16),
            vmem((rows, inner), b16),
            *[vmem(weight.shape, b16) for weight in weights],
            vmem((2, 2, rows, width), b16),
            vmem((2, width, units), f32),
            vmem((2, width, units), f32),
            vmem((high, width + 8, heads), f32),
            vmem((high, width + 8, heads), f32),
            vmem((high, inner, width), f32),
            vmem((high, inner, width), f32),
            vmem((slots, width + 8, heads), f32),
            vmem((slots, inner, width), f32),
            vmem((4, size, depth), f32),
            vmem((2, size, depth), f32),
            vmem((1, size, depth), f32),
            vmem((2, size, depth), f32),
            vmem((2, size, depth), b16),
            vmem((2, size, depth), b16),
            dma((7,)),
            dma((2, 2)),
            dma((2, 2)),
            dma((2, high)),
            dma((2, high)),
            dma((2, 4)),
            dma((2, 4)),
            dma((2, slots)),
            dma((2, slots)),
            *[dma((2, 4))] * 6,
            dma((4,)),
            dma((1,)),
            dma((2,)),
            dma((2,)),
            dma((2,)),
            dma((6,)),
        ],
        compiler_params=pltpu.CompilerParams(
            collective_id=3, has_side_effects=True, vmem_limit_bytes=62 * 1024 * 1024
        ),
        cost_estimate=pl.CostEstimate(
            flops=8 * rows * depth * units, bytes_accessed=6 * depth * units, transcendentals=0
        ),
    )(*arrays, lines, *places, *weights, gain[None])


def block_mask(segment_column, segment_row, begin, rows, columns):
    row = begin + lax.broadcasted_iota(jnp.int32, (rows, columns), 0)
    column = lax.broadcasted_iota(jnp.int32, (rows, columns), 1)
    same = segment_column[pl.ds(begin, rows), :] == segment_row[:, :columns]
    return same & (row >= column)


def head_columns(index):
    return pl.ds(pl.multiple_of(index * HD, HD), HD)


def attention_kernel(
    step,
    tokens, gain, query_weight, key_weight, value_weight, query_gain, key_gain, cosine, sine,
    segment_column, segment_row,
    normed_out, query_raw, key_raw, query_out, key_out, value_out, mixed_out, total_out,
):
    count = tokens.shape[0]
    query_heads = query_weight.shape[1] // HD
    value_heads = key_weight.shape[1] // HD
    group = query_heads // value_heads

    def normalize(rows):
        value = tokens[rows, :].astype(jnp.float32)
        normed_out[rows, :] = (value * rms_inverse(value) * gain[...]).astype(jnp.bfloat16)

    loop_rows(count, 32, normalize)

    def project(rows):
        low = normed_out[rows, :]
        value_out[rows, :] = jnp.dot(
            low, value_weight[...], preferred_element_type=jnp.float32
        ).astype(jnp.bfloat16)
        for weight, raw, out, head_gain, heads in (
            (query_weight, query_raw, query_out, query_gain, query_heads),
            (key_weight, key_raw, key_out, key_gain, value_heads),
        ):
            product = jnp.dot(low, weight[...], preferred_element_type=jnp.float32)
            raw[rows, :] = product
            for head in range(heads):
                part = product[:, head * HD : (head + 1) * HD]
                unit = part * rms_inverse(part) * head_gain[...]
                turned = unit * cosine[rows, :] + pltpu.roll(unit, HD // 2, 1) * sine[rows, :]
                out[rows, head * HD : (head + 1) * HD] = turned.astype(jnp.bfloat16)

    loop_rows(count, step, project)

    def head_step(head, carry):
        own = head_columns(head)
        shared = head_columns(head // group)
        for begin in range(0, count, step):
            reach = begin + step
            scores = lax.dot_general(
                query_out[pl.ds(begin, step), own],
                key_out[pl.ds(0, reach), shared],
                (((1,), (1,)), ((), ())),
                preferred_element_type=jnp.float32,
            ) * HD ** (-0.5)
            allowed = block_mask(segment_column, segment_row, begin, step, reach)
            scores = jnp.where(allowed, scores, masked)
            peak = jnp.max(scores, axis=-1, keepdims=True)
            expons = jnp.exp(scores - peak)
            total = jnp.sum(expons, axis=-1, keepdims=True)
            chance = (expons * (1.0 / total)).astype(jnp.bfloat16)
            mixed_out[pl.ds(begin, step), own] = jnp.dot(
                chance, value_out[pl.ds(0, reach), shared], preferred_element_type=jnp.float32
            ).astype(jnp.bfloat16)
            total_out[head, pl.ds(begin, step), :] = jnp.broadcast_to(
                peak + jnp.log(total), (step, HD)
            )
        return carry

    lax.fori_loop(0, query_heads, head_step, 0)


def attention(tokens, gain, weights, query_gain, key_gain, cosine, sine, segment_column, segment_row):
    count, depth = tokens.shape
    queries, keys = weights[0].shape[1], weights[1].shape[1]
    f32, b16 = jnp.float32, jnp.bfloat16
    shape = jax.ShapeDtypeStruct
    return pl.pallas_call(
        functools.partial(attention_kernel, 256),
        out_shape=[
            shape((count, depth), b16),
            shape((count, queries), f32),
            shape((count, keys), f32),
            shape((count, queries), b16),
            shape((count, keys), b16),
            shape((count, keys), b16),
            shape((count, queries), b16),
            shape((queries // HD, count, HD), f32),
        ],
        compiler_params=pltpu.CompilerParams(vmem_limit_bytes=56 * 1024 * 1024),
        cost_estimate=pl.CostEstimate(
            flops=2 * count * depth * (queries + 2 * keys) + 4 * count * count * queries,
            bytes_accessed=32 * 1024 * 1024,
            transcendentals=count * count * queries // HD,
        ),
    )(tokens, gain[None], *weights, query_gain[None], key_gain[None], cosine, sine, segment_column, segment_row)


def attention_back_kernel(
    step,
    hidden_low, output_weight, queries, keys, values, totals, query_raw, key_raw,
    query_gain, key_gain, cosine, sine, segment_column, segment_row,
    raw_out, query_gain_out, key_gain_out,
    upstream, query_grad, key_grad, value_grad,
):
    count = hidden_low.shape[0]
    query_heads = queries.shape[1] // HD
    value_heads = keys.shape[1] // HD
    group = query_heads // value_heads
    across_last = (((1,), (1,)), ((), ()))
    down_first = (((0,), (0,)), ((), ()))

    def project(rows):
        upstream[rows, :] = lax.dot_general(
            hidden_low[rows, :],
            output_weight[...],
            across_last,
            preferred_element_type=jnp.float32,
        ).astype(jnp.bfloat16)

    loop_rows(count, step, project)
    key_grad[...] = jnp.zeros_like(key_grad)
    value_grad[...] = jnp.zeros_like(value_grad)

    def head_step(head, carry):
        own = head_columns(head)
        shared = head_columns(head // group)
        for begin in range(0, count, step):
            reach = begin + step
            rows, before = pl.ds(begin, step), pl.ds(0, reach)
            scores = lax.dot_general(
                queries[rows, own],
                keys[before, shared],
                across_last,
                preferred_element_type=jnp.float32,
            ) * HD ** (-0.5)
            allowed = block_mask(segment_column, segment_row, begin, step, reach)
            chance = jnp.exp(jnp.where(allowed, scores, masked) - totals[head, rows, :][:, :1])
            incoming = upstream[rows, own]
            value_grad[before, shared] += lax.dot_general(
                chance.astype(jnp.bfloat16),
                incoming,
                down_first,
                preferred_element_type=jnp.float32,
            )
            along = lax.dot_general(
                incoming, values[before, shared], across_last, preferred_element_type=jnp.float32
            )
            center = jnp.sum(along * chance, axis=-1, keepdims=True)
            score_grad = (chance * (along - center)).astype(jnp.bfloat16)
            query_grad[rows, own] = jnp.dot(
                score_grad, keys[before, shared], preferred_element_type=jnp.float32
            ) * HD ** (-0.5)
            key_grad[before, shared] += lax.dot_general(
                score_grad, queries[rows, own], down_first, preferred_element_type=jnp.float32
            ) * HD ** (-0.5)
        return carry

    lax.fori_loop(0, query_heads, head_step, 0)
    query_gain_out[...] = jnp.zeros_like(query_gain_out)
    key_gain_out[...] = jnp.zeros_like(key_gain_out)

    def finish(rows):
        for grad, raw, head_gain, gain_out, heads, place in (
            (query_grad, query_raw, query_gain, query_gain_out, query_heads, 0),
            (key_grad, key_raw, key_gain, key_gain_out, value_heads, query_heads),
        ):
            for head in range(heads):
                columns = slice(head * HD, (head + 1) * HD)
                upward = grad[rows, columns]
                unit_grad = upward * cosine[rows, :] - pltpu.roll(upward, HD // 2, 1) * sine[rows, :]
                value = raw[rows, columns]
                inverse = rms_inverse(value)
                product = unit_grad * (value * inverse)
                gain_out[...] += jnp.sum(product.reshape(-1, 8, HD), axis=0)
                begin = (place + head) * HD
                raw_out[rows, begin : begin + HD] = norm_back(
                    unit_grad, value, inverse, head_gain[...]
                ).astype(jnp.bfloat16)
        begin = (query_heads + value_heads) * HD
        raw_out[rows, begin:] = value_grad[rows, :].astype(jnp.bfloat16)

    loop_rows(count, 64, finish)


def attention_back(
    hidden_low, output_weight, queries, keys, values, totals, query_raw, key_raw,
    query_gain, key_gain, cosine, sine, segment_column, segment_row,
):
    count = hidden_low.shape[0]
    query_columns, key_columns = queries.shape[1], keys.shape[1]
    f32, b16 = jnp.float32, jnp.bfloat16
    shape = jax.ShapeDtypeStruct
    return pl.pallas_call(
        functools.partial(attention_back_kernel, 256),
        out_shape=[
            shape((count, query_columns + 2 * key_columns), b16),
            shape((8, HD), f32),
            shape((8, HD), f32),
        ],
        scratch_shapes=[
            pltpu.VMEM((count, query_columns), b16),
            pltpu.VMEM((count, query_columns), f32),
            pltpu.VMEM((count, key_columns), f32),
            pltpu.VMEM((count, key_columns), f32),
        ],
        compiler_params=pltpu.CompilerParams(vmem_limit_bytes=56 * 1024 * 1024),
        cost_estimate=pl.CostEstimate(
            flops=2 * count * hidden_low.shape[1] * query_columns + 10 * count * count * query_columns,
            bytes_accessed=24 * 1024 * 1024,
            transcendentals=count * count * query_columns // HD,
        ),
    )(
        hidden_low, output_weight, queries, keys, values, totals, query_raw, key_raw,
        query_gain[None], key_gain[None], cosine, sine, segment_column, segment_row,
    )


def plain_shards(
    tokens,
    attention_gain,
    query_weight,
    key_weight,
    value_weight,
    query_gain,
    key_gain,
    output_weight,
    feedforward_gain,
    gate_weight,
    up_weight,
    down_weight,
    segment_numbers,
    positions,
    cotangent,
):
    count = tokens.shape[0]
    batch = count // SEQ_LEN
    query_heads = query_weight.shape[1] // HD
    value_heads = key_weight.shape[1] // HD
    group = query_heads // value_heads
    inputs = tokens.astype(jnp.float32)
    first_inverse = rms_inverse(inputs)
    first_normed = inputs * first_inverse
    normed_low = (first_normed * attention_gain).astype(jnp.bfloat16)
    query_raw = jnp.dot(normed_low, query_weight, preferred_element_type=jnp.float32).reshape(
        count, query_heads, HD
    )
    key_raw = jnp.dot(normed_low, key_weight, preferred_element_type=jnp.float32).reshape(
        count, value_heads, HD
    )
    value_low = jnp.dot(normed_low, value_weight, preferred_element_type=jnp.float32).astype(
        jnp.bfloat16
    )
    cosine, sine = rotary_tables(positions)
    cosine = cosine[:, None]
    sine = sine[:, None]
    query_inverse = rms_inverse(query_raw)
    query_unit = query_raw * query_inverse
    query_low = rotate(query_unit * query_gain, cosine, sine).astype(jnp.bfloat16)
    key_inverse = rms_inverse(key_raw)
    key_unit = key_raw * key_inverse
    key_low = rotate(key_unit * key_gain, cosine, sine).astype(jnp.bfloat16)
    queries = query_low.reshape(batch, SEQ_LEN, value_heads, group, HD)
    keys = key_low.reshape(batch, SEQ_LEN, value_heads, HD)
    values = value_low.reshape(batch, SEQ_LEN, value_heads, HD)
    segments = segment_numbers.reshape(batch, SEQ_LEN)
    mixed, totals = lax.map(attend, (queries, keys, values, segments))
    mixed_low = mixed.reshape(count, query_heads * HD).astype(jnp.bfloat16)
    attention = lax.psum(
        jnp.dot(mixed_low, output_weight, preferred_element_type=jnp.float32), "tensor"
    )
    hidden = inputs + attention
    second_inverse = rms_inverse(hidden)
    second_normed = hidden * second_inverse
    second_low = (second_normed * feedforward_gain).astype(jnp.bfloat16)
    gate = jnp.dot(second_low, gate_weight, preferred_element_type=jnp.float32)
    upward = jnp.dot(second_low, up_weight, preferred_element_type=jnp.float32)
    sigmoid_gate = jax.nn.sigmoid(gate)
    activated = gate * sigmoid_gate
    product_low = (activated * upward).astype(jnp.bfloat16)
    feedforward = lax.psum(
        jnp.dot(product_low, down_weight, preferred_element_type=jnp.float32), "tensor"
    )
    layer_output = (hidden + feedforward).astype(jnp.bfloat16)
    down_grad = jnp.einsum("tf,td->fd", product_low, cotangent, preferred_element_type=jnp.float32)
    product_grad = jnp.einsum(
        "td,fd->tf", cotangent, down_weight, preferred_element_type=jnp.float32
    )
    gate_grad_low = (
        product_grad * upward * sigmoid_gate * (1.0 + gate * (1.0 - sigmoid_gate))
    ).astype(jnp.bfloat16)
    upward_grad_low = (product_grad * activated).astype(jnp.bfloat16)
    gate_weight_grad = jnp.einsum(
        "td,tf->df", second_low, gate_grad_low, preferred_element_type=jnp.float32
    )
    upward_weight_grad = jnp.einsum(
        "td,tf->df", second_low, upward_grad_low, preferred_element_type=jnp.float32
    )
    second_part = jnp.einsum(
        "tf,df->td", gate_grad_low, gate_weight, preferred_element_type=jnp.float32
    )
    second_part = second_part + jnp.einsum(
        "tf,df->td", upward_grad_low, up_weight, preferred_element_type=jnp.float32
    )
    second_grad = lax.psum(second_part, "tensor")
    second_gain_grad = jnp.sum(second_grad * second_normed, axis=0)
    hidden_grad = cotangent.astype(jnp.float32) + norm_back(
        second_grad, hidden, second_inverse, feedforward_gain
    )
    hidden_low = hidden_grad.astype(jnp.bfloat16)
    output_weight_grad = jnp.einsum(
        "tc,td->cd", mixed_low, hidden_low, preferred_element_type=jnp.float32
    )
    mixed_grad = jnp.einsum(
        "td,cd->tc", hidden_low, output_weight, preferred_element_type=jnp.float32
    ).astype(jnp.bfloat16)
    upstream = mixed_grad.reshape(batch, SEQ_LEN, value_heads, group, HD)
    query_back, key_back, value_back = lax.map(
        attend_back, (queries, keys, values, segments, totals, upstream)
    )
    query_unit_grad = rotate_back(query_back.reshape(count, query_heads, HD), cosine, sine)
    key_unit_grad = rotate_back(key_back.reshape(count, value_heads, HD), cosine, sine)
    query_gain_part = jnp.sum(query_unit_grad * query_unit, axis=(0, 1))
    key_gain_part = jnp.sum(key_unit_grad * key_unit, axis=(0, 1))
    query_raw_grad = (
        norm_back(query_unit_grad, query_raw, query_inverse, query_gain)
        .reshape(count, query_heads * HD)
        .astype(jnp.bfloat16)
    )
    key_raw_grad = (
        norm_back(key_unit_grad, key_raw, key_inverse, key_gain)
        .reshape(count, value_heads * HD)
        .astype(jnp.bfloat16)
    )
    value_raw_grad = value_back.reshape(count, value_heads * HD).astype(jnp.bfloat16)
    query_weight_grad = jnp.einsum(
        "td,tc->dc", normed_low, query_raw_grad, preferred_element_type=jnp.float32
    )
    key_weight_grad = jnp.einsum(
        "td,tc->dc", normed_low, key_raw_grad, preferred_element_type=jnp.float32
    )
    value_weight_grad = jnp.einsum(
        "td,tc->dc", normed_low, value_raw_grad, preferred_element_type=jnp.float32
    )
    first_part = jnp.einsum(
        "tc,dc->td", query_raw_grad, query_weight, preferred_element_type=jnp.float32
    )
    first_part = first_part + jnp.einsum(
        "tc,dc->td", key_raw_grad, key_weight, preferred_element_type=jnp.float32
    )
    first_part = first_part + jnp.einsum(
        "tc,dc->td", value_raw_grad, value_weight, preferred_element_type=jnp.float32
    )
    first_grad, query_gain_grad, key_gain_grad = lax.psum(
        (first_part, query_gain_part, key_gain_part), "tensor"
    )
    first_gain_grad = jnp.sum(first_grad * first_normed, axis=0)
    tokens_gradient = (
        hidden_grad + norm_back(first_grad, inputs, first_inverse, attention_gain)
    ).astype(jnp.bfloat16)
    summed = (
        lax.psum_scatter(first_gain_grad, "dp", scatter_dimension=0, tiled=True),
        lax.psum_scatter(query_weight_grad, "dp", scatter_dimension=0, tiled=True),
        lax.psum_scatter(key_weight_grad, "dp", scatter_dimension=0, tiled=True),
        lax.psum_scatter(value_weight_grad, "dp", scatter_dimension=0, tiled=True),
        lax.psum_scatter(query_gain_grad, "dp", scatter_dimension=0, tiled=True),
        lax.psum_scatter(key_gain_grad, "dp", scatter_dimension=0, tiled=True),
        lax.psum_scatter(output_weight_grad, "dp", scatter_dimension=1, tiled=True),
        lax.psum_scatter(second_gain_grad, "dp", scatter_dimension=0, tiled=True),
        lax.psum_scatter(gate_weight_grad, "dp", scatter_dimension=0, tiled=True),
        lax.psum_scatter(upward_weight_grad, "dp", scatter_dimension=0, tiled=True),
        lax.psum_scatter(down_grad, "dp", scatter_dimension=1, tiled=True),
    )
    return (
        layer_output,
        tokens_gradient,
        summed[0],
        summed[1],
        summed[2],
        summed[3],
        summed[4],
        summed[5],
        summed[6],
        summed[7],
        summed[8],
        summed[9],
        summed[10],
    )


def shards(
    dp,
    tokens,
    attention_gain,
    query_weight,
    key_weight,
    value_weight,
    query_gain,
    key_gain,
    output_weight,
    feedforward_gain,
    gate_weight,
    up_weight,
    down_weight,
    segment_numbers,
    positions,
    cotangent,
):
    count, depth = tokens.shape
    width = depth // dp
    high = dp // 2
    core = lax.axis_index("tensor") % 2
    upstream_first = lax.ppermute(
        lax.dynamic_slice_in_dim(cotangent, core * (count // 2), count // 4, 0).astype(jnp.float32),
        "dp",
        [(i, i ^ 2) for i in range(dp)],
    )

    cosine, sine = rotary_tables(positions)
    sine = jnp.concatenate([-sine[:, : HD // 2], sine[:, HD // 2 :]], axis=1)
    tables = (cosine, sine, segment_numbers[:, None], segment_numbers[None])
    normed_low, query_raw, key_raw, queries, keys, values, mixed_low, totals = attention(
        tokens,
        attention_gain,
        (query_weight, key_weight, value_weight),
        query_gain,
        key_gain,
        *tables,
    )
    (
        hidden,
        second_part,
        low_own,
        product_own,
        gate_own,
        upward_own,
        low_pair,
        product_pair,
        gate_pair,
        upward_pair,
        upstream_pair,
    ) = front(
        mixed_low,
        output_weight,
        tokens,
        cotangent,
        upstream_first,
        feedforward_gain,
        gate_weight,
        up_weight,
        down_weight,
    )[:11]
    hidden_grad, hidden_low, out_part, down_weight_grad, gate_ready, gate_given, gate_kept = middle(
        second_part,
        hidden,
        cotangent,
        upstream_pair,
        product_own,
        product_pair,
        gate_own,
        gate_pair,
        low_own,
        low_pair,
        feedforward_gain,
        down_weight,
    )
    gate_moved = lax.ppermute(gate_given, "dp", [(i, i ^ 1) for i in range(dp)])
    raw_grad, query_gain_part, key_gain_part = attention_back(
        hidden_low,
        output_weight,
        queries,
        keys,
        values,
        totals,
        query_raw,
        key_raw,
        query_gain,
        key_gain,
        *tables,
    )
    head_width = HD // dp

    lines = [
        jnp.pad(value.reshape(dp, -1), ((0, 0), (0, raw_grad.shape[1] - value.size // dp)))
        for value in (jnp.sum(query_gain_part, axis=0), jnp.sum(key_gain_part, axis=0))
    ]
    gain_lines = jnp.pad(jnp.stack(lines, axis=1), ((0, 0), (0, 6), (0, 0)))

    layer_output, tokens_gradient, gate_weight_grad, up_weight_grad, raw_whole, output_weight_grad = (
        rear(
            [line_order(high, p) for p in range(high)],
            [gate_ready, gate_kept + gate_moved]
            + [low_own, low_pair, upward_own, upward_pair]
            + [normed_low, raw_grad, hidden_low, mixed_low],
            gain_lines,
            [out_part, hidden, hidden_grad, tokens],
            [query_weight, key_weight, value_weight],
            attention_gain,
        )[:6]
    )
    place_rows = (lax.axis_index("dp") * width, width, 0)
    raw_weight = jnp.concatenate(
        [
            lax.dynamic_slice_in_dim(value, *place_rows)
            for value in (query_weight, key_weight, value_weight)
        ],
        axis=1,
    )
    first_gain = jnp.sum(raw_weight * raw_whole[:width], axis=1) / lax.dynamic_slice_in_dim(
        attention_gain, *place_rows
    )
    second_gain = sum(
        jnp.sum(lax.dynamic_slice_in_dim(value, *place_rows) * gradient, axis=1)
        for gradient, value in ((gate_weight_grad, gate_weight), (up_weight_grad, up_weight))
    ) / lax.dynamic_slice_in_dim(feedforward_gain, *place_rows)
    gains = jnp.concatenate(
        [first_gain[None], second_gain[None], raw_whole[width : width + 2, :width]], axis=0
    )
    gains = gains + swap_core(gains)
    gains = gains + swap_chip(gains)
    columns_query = query_weight.shape[1]
    columns_key = columns_query + key_weight.shape[1]
    return (
        layer_output,
        tokens_gradient,
        gains[0],
        raw_whole[:width, :columns_query],
        raw_whole[:width, columns_query:columns_key],
        raw_whole[:width, columns_key:],
        gains[2, :head_width],
        gains[3, :head_width],
        output_weight_grad,
        gains[1],
        gate_weight_grad,
        up_weight_grad,
        down_weight_grad,
    )


def solution(mesh):
    dp, tensor = mesh.shape["dp"], mesh.shape["tensor"]

    def program(*args):
        if dp == 8 and tensor == 4 and args[0].shape[0] == SEQ_LEN:
            return shards(dp, *args)
        return plain_shards(*args)

    return jax.shard_map(
        program,
        mesh=mesh,
        in_specs=(
            P("dp", None),
            P(),
            P(None, "tensor"),
            P(None, "tensor"),
            P(None, "tensor"),
            P(),
            P(),
            P("tensor", None),
            P(),
            P(None, "tensor"),
            P(None, "tensor"),
            P("tensor", None),
            P("dp"),
            P("dp"),
            P("dp", None),
        ),
        out_specs=(
            P("dp", None),
            P("dp", None),
            P("dp"),
            P("dp", "tensor"),
            P("dp", "tensor"),
            P("dp", "tensor"),
            P("dp"),
            P("dp"),
            P("tensor", "dp"),
            P("dp"),
            P("dp", "tensor"),
            P("dp", "tensor"),
            P("tensor", "dp"),
        ),
        check_vma=False,
    )
```

```python
import functools

import jax
import jax.numpy as jnp
from jax import lax
from jax.experimental import pallas as pl
from jax.experimental.pallas import tpu as pltpu
from jax.sharding import PartitionSpec as P

HD = 128
SEQ_LEN = 1024


epsilon = 1e-06
rope_base = 1000000.0
masked = -1e30


def rms_inverse(value):
    return lax.rsqrt(jnp.mean(value * value, axis=-1, keepdims=True) + epsilon)


def norm_back(upstream, value, inverse, gain):
    scaled = upstream * gain
    return inverse * scaled - value * inverse**3 * jnp.mean(scaled * value, axis=-1, keepdims=True)


def rotary_tables(positions):
    exponent = jnp.arange(0, HD, 2, dtype=jnp.float32) / HD
    frequency = rope_base ** (-exponent)
    phase = positions.astype(jnp.float32)[:, None] * frequency[None, :]
    phase = jnp.concatenate([phase, phase], axis=-1)
    return (jnp.cos(phase), jnp.sin(phase))


def rotate(value, cosine, sine):
    half = value.shape[-1] // 2
    turned = jnp.concatenate([-value[..., half:], value[..., :half]], axis=-1)
    return value * cosine + turned * sine


def rotate_back(upstream, cosine, sine):
    half = upstream.shape[-1] // 2
    moved = upstream * sine
    return upstream * cosine + jnp.concatenate([moved[..., half:], -moved[..., :half]], axis=-1)


def block_scores(query_rows, keys, row_segments, segments, begin):
    scores = jnp.einsum(
        "rkgd,tkd->kgrt", query_rows, keys, preferred_element_type=jnp.float32
    ) * HD ** (-0.5)
    rows = begin + lax.iota(jnp.int32, query_rows.shape[0])
    columns = lax.iota(jnp.int32, keys.shape[0])
    allowed = (row_segments[:, None] == segments[None, :]) & (rows[:, None] >= columns[None, :])
    return jnp.where(allowed[None, None], scores, masked)


def attend(item):
    queries, keys, values, segments = item
    length = queries.shape[0]
    width = min(512, length)
    outputs = []
    totals = []
    for begin in range(0, length, width):
        scores = block_scores(
            queries[begin : begin + width], keys, segments[begin : begin + width], segments, begin
        )
        peak = jnp.max(scores, axis=-1, keepdims=True)
        expons = jnp.exp(scores - peak)
        total = jnp.sum(expons, axis=-1, keepdims=True)
        chance_low = (expons / total).astype(jnp.bfloat16)
        outputs.append(
            jnp.einsum("kgrt,tkd->rkgd", chance_low, values, preferred_element_type=jnp.float32)
        )
        totals.append(peak + jnp.log(total))
    return (jnp.concatenate(outputs, axis=0), jnp.concatenate(totals, axis=2))


def attend_back(item):
    queries, keys, values, segments, totals, upstream = item
    length = queries.shape[0]
    width = min(512, length)
    query_parts = []
    key_grad = jnp.zeros(keys.shape, jnp.float32)
    value_grad = jnp.zeros(values.shape, jnp.float32)
    for begin in range(0, length, width):
        rows = queries[begin : begin + width]
        scores = block_scores(rows, keys, segments[begin : begin + width], segments, begin)
        chance = jnp.exp(scores - totals[:, :, begin : begin + width])
        chance_low = chance.astype(jnp.bfloat16)
        incoming = upstream[begin : begin + width]
        value_grad = value_grad + jnp.einsum(
            "kgrt,rkgd->tkd", chance_low, incoming, preferred_element_type=jnp.float32
        )
        along = jnp.einsum("rkgd,tkd->kgrt", incoming, values, preferred_element_type=jnp.float32)
        center = jnp.sum(along * chance, axis=-1, keepdims=True)
        score_grad = (chance * (along - center)).astype(jnp.bfloat16)
        query_parts.append(
            jnp.einsum("kgrt,tkd->rkgd", score_grad, keys, preferred_element_type=jnp.float32)
            * HD ** (-0.5)
        )
        key_grad = key_grad + jnp.einsum(
            "kgrt,rkgd->tkd", score_grad, rows, preferred_element_type=jnp.float32
        ) * HD ** (-0.5)
    return (jnp.concatenate(query_parts, axis=0), key_grad, value_grad)


def dot(left, right):
    return jnp.dot(left, right, preferred_element_type=jnp.float32)


def dot_back(left, right):
    return jnp.einsum("tc,dc->td", left, right, preferred_element_type=jnp.float32)


def dot_tokens(left, right):
    return jnp.einsum("tm,tn->mn", left, right, preferred_element_type=jnp.float32)


def line_order(high, place):
    steps = {}
    for block in range(high):
        if block > place:
            steps[block] = high - block + place
        elif block < place:
            steps[block] = high - place + block
    return sorted(steps, key=lambda block: (steps[block], block)) + [place]


MESH = pl.DeviceIdType.MESH


def neighbours():
    dp, tensor = lax.axis_index("dp"), lax.axis_index("tensor")
    core = lax.rem(tensor, 2)
    sibling = {"tensor": tensor + 1 - 2 * core}
    facing = {"tensor": lax.rem(tensor + 2, 4)}
    place = dp // 2
    pair = {"dp": dp + 2 * (1 - 2 * lax.rem(place, 2))}
    return core, sibling, facing, pair


def greet(devices):
    barrier = pltpu.get_barrier_semaphore()
    for device in devices:
        pl.semaphore_signal(barrier, inc=1, device_id=device, device_id_type=MESH)
    pl.semaphore_wait(barrier, len(devices))


def loop_rows(count, step, body):
    def run(index, carry):
        body(pl.ds(pl.multiple_of(index * step, step), step))
        return carry

    lax.fori_loop(0, count // step, run, 0)


def sequence_rows(size, core, which, k):
    side = core if which == 0 else 1 - core
    return pl.multiple_of(side * 4 * size + k * size, size)


def remote(source, target, sems, k, device):
    return pltpu.make_async_remote_copy(
        src_ref=source, dst_ref=target, send_sem=sems.at[0, k], recv_sem=sems.at[1, k],
        device_id=device, device_id_type=MESH,
    )


def front_kernel(
    size, first,
    mixed_hbm, output_weight_hbm, tokens_hbm, upstream_hbm, upstream_first,
    gain, gate_hbm, up_hbm, down_hbm,
    hidden_out, second_out, low_own, product_own, gate_own, upward_own,
    low_pair, product_pair, gate_pair, upward_pair, upstream_pair,
    c_landed, n_recv, n_side, u_recv, u_side,
    mixed, output_weight, gate_weight, up_weight, down_weight,
    x_send, x_recv, back_recv, tok, hid, z_send, low, rows16, tiles, stage, terms,
    load_sems, c_sems, x_sems, back_sems, n_sems, n_side_sems, u_sems, u_side_sems,
    tok_sems, hid_sems, low_sems, wave_sems, tile_sems, stage_sems, term_sems,
):
    core, sibling, facing, pair = neighbours()
    depth = gain.shape[1]
    half = 4 * size
    units = gate_weight.shape[1]
    begin = functools.partial(sequence_rows, size, core)
    across_last = (((1,), (1,)), ((), ()))
    rest = half - first
    loads = [
        pltpu.make_async_copy(source, target, load_sems.at[index])
        for index, (source, target) in enumerate(
            [
                (
                    upstream_hbm.at[pl.ds(pl.multiple_of(core * half + first, 16), rest)],
                    rows16.at[pl.ds(0, rest)],
                ),
                (mixed_hbm, mixed),
                (output_weight_hbm, output_weight),
                (gate_hbm, gate_weight),
                (up_hbm, up_weight),
                (down_hbm, down_weight),
            ]
        )
    ]
    for load in loads:
        load.start()
    greet([sibling, facing, pair])

    c_copies = [
        remote(terms.at[pl.ds(k * size, size)], c_landed.at[k], c_sems, k, sibling) for k in range(4)
    ]
    x_copies = [remote(x_send.at[k], x_recv.at[k], x_sems, k, facing) for k in range(4)]
    back_copies = [remote(x_send.at[k], back_recv.at[k], back_sems, k, sibling) for k in range(4)]
    n_copies = [remote(z_send.at[k % 2], n_recv.at[k], n_sems, k, pair) for k in range(4)]
    n_sides = [remote(n_recv.at[k], n_side.at[k], n_side_sems, k, sibling) for k in range(4)]
    u_rows = [(0, rest - 2 * size), (rest - 2 * size, size), (rest - size, size)]
    u_buffers = [hid.at[0, pl.ds(0, u_rows[0][1])], z_send.at[0], z_send.at[1]]
    u_copies = [
        remote(u_buffers[j], u_recv.at[pl.ds(start, number)], u_sems, j, pair)
        for j, (start, number) in enumerate(u_rows)
    ]
    u_sides = [remote(upstream_first, u_side.at[pl.ds(0, first)], u_side_sems, 0, sibling)] + [
        remote(
            u_recv.at[pl.ds(start, number)],
            u_side.at[pl.ds(first + start, number)],
            u_side_sems,
            1 + j,
            sibling,
        )
        for j, (start, number) in enumerate(u_rows)
    ]

    def stage_load(source, slot, number):
        return pltpu.make_async_copy(source, stage.at[slot, pl.ds(0, number)], stage_sems.at[slot])

    def upstream_send(j):
        start, number = u_rows[j]

        def run(row):
            u_buffers[j][row, :] = rows16[
                pl.ds(pl.multiple_of(start + row.start, 16), row.size), :
            ].astype(jnp.float32)

        loop_rows(number, 16, run)
        u_copies[j].start()

    def upstream_forward(j):
        u_copies[j].wait_recv()
        u_sides[1 + j].start()

    def attention_terms(k):
        rows = jnp.concatenate(
            [mixed[pl.ds(begin(which, k), size), :] for which in range(2)], axis=0
        )

        def run(column):
            both = jnp.dot(rows, output_weight[:, column], preferred_element_type=jnp.float32)
            x_send[k, :, column] = both[:size]
            terms[pl.ds(k * size, size), column] = both[size:]

        loop_rows(depth, 1024, run)
        c_copies[k].start()

    def attention_cores(k):
        c_copies[k].wait_recv()
        stage_load(c_landed.at[k], k % 2, size).start()
        stage_load(c_landed.at[k], k % 2, size).wait()

        def run(row):
            x_send[k, row, :] = x_send[k, row, :] + stage[k % 2, row, :]

        loop_rows(size, 16, run)
        x_copies[k].start()

    def attention_chips(k):
        x_copies[k].wait()

        def run(row):
            x_send[k, row, :] = x_send[k, row, :] + x_recv[k, row, :]

        loop_rows(size, 16, run)
        back_copies[k].start()

    def token_loads(k):
        return [
            pltpu.make_async_copy(
                tokens_hbm.at[pl.ds(begin(which, k), size)], tok.at[which], tok_sems.at[which]
            )
            for which in range(2)
        ]

    def hidden_stores(k):
        return [
            pltpu.make_async_copy(
                hid.at[which], hidden_out.at[pl.ds(begin(which, k), size)], hid_sems.at[which]
            )
            for which in range(2)
        ]

    def low_rows(which, k, row):
        side = core if which == 0 else 1 - core
        return pl.ds(pl.multiple_of((side + k % 2 * 2) * size + row.start, 16), row.size)

    def normed(k):
        for load in token_loads(k):
            load.wait()
        if k > 0:
            for store in hidden_stores(k - 1):
                store.wait()
        if k < 2:
            u_copies[1 + k].wait_send()
        else:
            n_copies[k - 2].wait_send()

        def run(which, source, row):
            value = tok[which, row, :].astype(jnp.float32) + source[k, row, :]
            hid[which, row, :] = value
            unit = value * lax.rsqrt(jnp.mean(value * value, axis=-1, keepdims=True) + epsilon)
            if which == 0:
                z_send[k % 2, row, :] = unit
            low[0, low_rows(which, k, row), :] = (unit * gain[...]).astype(jnp.bfloat16)

        loop_rows(size, 16, functools.partial(run, 0, x_send))
        n_copies[k].start()
        back_copies[k].wait_recv()
        loop_rows(size, 16, functools.partial(run, 1, back_recv))
        for store in hidden_stores(k):
            store.start()
        if k < 3:
            for load in token_loads(k + 1):
                load.start()

    def pipeline(pieces):
        def bring(index):
            before, source, number, _ = pieces[index]
            if before is not None:
                before.wait_recv()
            stage_load(source, index % 2, number).start()

        bring(0)
        for index, (_, source, number, consume) in enumerate(pieces):
            if index + 1 < len(pieces):
                bring(index + 1)
            stage_load(source, index % 2, number).wait()
            loop_rows(number, 16, functools.partial(consume, index % 2))

    def pair_forward(k):
        n_copies[k].wait_recv()
        n_sides[k].start()

    def pair_rows(chunks):
        def consume(k, which, slot, row):
            low[1, low_rows(which, k, row), :] = (stage[slot, row, :] * gain[...]).astype(
                jnp.bfloat16
            )

        pipeline(
            [
                (
                    n_sides[k] if which else None,
                    (n_side if which else n_recv).at[k],
                    size,
                    functools.partial(consume, k, which),
                )
                for which in range(2)
                for k in chunks
            ]
        )

    def wave_copies(local, distant, sems, wave, inwards=False):
        copies = []
        for part in range(4):
            here = local.at[pl.ds(part * size, size)]
            there = distant.at[pl.ds(part % 2 * half + (2 * wave + part // 2) * size, size)]
            source, target = (there, here) if inwards else (here, there)
            copies.append(pltpu.make_async_copy(source, target, sems.at[part]))
        return copies

    def pair_stores(wave):
        return wave_copies(rows16, upstream_pair, wave_sems.at[1], wave)

    def upstream_wave(wave):
        def consume(which, start, slot, row):
            side = core if which == 0 else 1 - core
            chunk, within = start // size, start % size
            place = pl.multiple_of((2 * chunk + side) * size + within + row.start, 16)
            rows16[pl.ds(place, row.size), :] = stage[slot, row, :].astype(jnp.bfloat16)

        if wave == 0:
            own = [
                (upstream_first.at[pl.ds(0, size)], size, 0),
                (upstream_first.at[pl.ds(size, first - size)], first - size, size),
                (u_recv.at[pl.ds(0, u_rows[0][1])], u_rows[0][1], first),
            ]
            waits = [u_sides[0], u_sides[1]]
        else:
            own = [(u_recv.at[pl.ds(u_rows[j][0], size)], size, (j - 1) * size) for j in (1, 2)]
            waits = [u_sides[2], u_sides[3]]
        pieces = [
            (None, source, number, functools.partial(consume, 0, start))
            for source, number, start in own
        ]
        if wave == 0:
            waits[0].wait_recv()
            waits[1].wait_recv()
            waits = [None, None]
        pieces += [
            (
                waits[j],
                u_side.at[pl.ds((2 * wave + j) * size, size)],
                size,
                functools.partial(consume, 1, j * size),
            )
            for j in range(2)
        ]
        pipeline(pieces)
        for copy in pair_stores(wave):
            copy.start()

    def term_stores(wave):
        return wave_copies(terms, second_out, term_sems, wave)

    def low_stores(wave, index):
        return wave_copies(low.at[index], low_pair if index else low_own, low_sems.at[index], wave)

    def tile_stores(wave, index):
        outs = (
            (product_pair, gate_pair, upward_pair) if index else (product_own, gate_own, upward_own)
        )
        return [
            copy
            for which in range(3)
            for copy in wave_copies(tiles.at[which], outs[which], tile_sems.at[which], wave)
        ]

    feeds = [(0, 0), (0, 1), (1, 0), (1, 1)]

    def fetches(wave):
        return wave_copies(rows16, upstream_hbm, wave_sems.at[0], wave, True)

    def feed(wave, index, part=None):
        number = feeds.index((wave, index))
        rows = slice(None) if part is None else pl.ds(part * 2 * size, 2 * size)
        if not part:
            if number > 0:
                for copy in tile_stores(*feeds[number - 1]):
                    copy.wait()
        if index == 0:
            for copy in fetches(wave):
                copy.wait()

        def run(column):
            gate = jnp.dot(
                low[index, rows], gate_weight[:, column], preferred_element_type=jnp.float32
            )
            upward = jnp.dot(
                low[index, rows], up_weight[:, column], preferred_element_type=jnp.float32
            )
            grad = lax.dot_general(
                rows16[rows],
                down_weight[column, :],
                across_last,
                preferred_element_type=jnp.float32,
            )
            sigmoid_gate = jax.nn.sigmoid(gate)
            activated = gate * sigmoid_gate
            tiles[0, rows, column] = (activated * upward).astype(jnp.bfloat16)
            tiles[1, rows, column] = (
                grad * upward * sigmoid_gate * (1.0 + gate * (1.0 - sigmoid_gate))
            ).astype(jnp.bfloat16)
            tiles[2, rows, column] = (grad * activated).astype(jnp.bfloat16)

        loop_rows(units, 512, run)
        copies = tile_stores(wave, index) + low_stores(wave, index)
        for number, copy in enumerate(copies):
            if part is None or number % 4 // 2 == part:
                copy.start()
        if index == 0:
            if wave > 0:
                for copy in term_stores(wave - 1):
                    copy.wait()

            def second(column):
                terms[:, column] = lax.dot_general(
                    tiles[1],
                    gate_weight[column, :],
                    across_last,
                    preferred_element_type=jnp.float32,
                ) + lax.dot_general(
                    tiles[2],
                    up_weight[column, :],
                    across_last,
                    preferred_element_type=jnp.float32,
                )

            loop_rows(depth, 512, second)
            for copy in term_stores(wave):
                copy.start()

    for load in token_loads(0):
        load.start()
    loads[0].wait()
    for j in range(3):
        upstream_send(j)
    u_sides[0].start()
    loads[1].wait()
    loads[2].wait()
    attention_terms(0)
    attention_terms(1)
    attention_cores(0)
    attention_terms(2)
    attention_cores(1)
    attention_terms(3)
    attention_cores(2)
    attention_cores(3)
    for copy in fetches(0):
        copy.start()
    upstream_forward(0)
    attention_chips(0)
    u_copies[0].wait_send()
    upstream_forward(1)
    normed(0)
    for load in loads[3:]:
        load.wait()
    attention_chips(1)
    normed(1)
    upstream_forward(2)
    for k in range(4):
        c_copies[k].wait_send()
    feed(0, 0)
    attention_chips(2)
    for copy in low_stores(0, 0):
        copy.wait()
    normed(2)
    pair_forward(0)
    upstream_wave(0)
    attention_chips(3)
    normed(3)
    pair_forward(1)
    pair_rows((0, 1))
    feed(0, 1)
    for copy in pair_stores(0):
        copy.wait()
    for copy in fetches(1):
        copy.start()
    pair_forward(2)
    feed(1, 0)
    upstream_wave(1)
    for copy in low_stores(0, 1):
        copy.wait()
    pair_rows((2,))
    feed(1, 1, 0)
    pair_forward(3)
    pair_rows((3,))
    feed(1, 1, 1)

    for k in range(4):
        back_copies[k].wait_send()
        n_sides[k].wait_send()
        u_sides[k].wait_send()
        if k >= 2:
            n_copies[k].wait_send()
    ends = hidden_stores(3) + term_stores(1) + low_stores(1, 0) + low_stores(1, 1)
    for copy in ends + pair_stores(1) + tile_stores(1, 1):
        copy.wait()


def front(mixed, output_weight, tokens, upstream, upstream_first, gain, gate_weight, up_weight, down_weight):
    rows, depth = tokens.shape
    inner, units = mixed.shape[1], gate_weight.shape[1]
    first = upstream_first.shape[0]
    size = rows // 8
    f32, b16 = jnp.float32, jnp.bfloat16
    any_space = pl.BlockSpec(memory_space=pl.ANY)
    shape = jax.ShapeDtypeStruct
    outs = [shape((rows, depth), f32)] * 2
    outs += ([shape((rows, depth), b16)] + [shape((rows, units), b16)] * 3) * 2
    outs += [shape((rows, depth), b16)] + [shape((4, size, depth), f32)] * 3
    outs += [shape((4 * size - first, depth), f32), shape((4 * size, depth), f32)]
    dma = pltpu.SemaphoreType.DMA
    vmem = pltpu.VMEM
    return pl.pallas_call(
        functools.partial(front_kernel, size, first),
        out_shape=outs,
        in_specs=[any_space] * 5 + [pl.BlockSpec(memory_space=pltpu.VMEM)] + [any_space] * 3,
        out_specs=[any_space] * len(outs),
        scratch_shapes=[
            vmem((rows, inner), b16),
            vmem((inner, depth), b16),
            vmem((depth, units), b16),
            vmem((depth, units), b16),
            vmem((units, depth), b16),
            vmem((4, size, depth), f32),
            vmem((4, size, depth), f32),
            vmem((4, size, depth), f32),
            vmem((2, size, depth), b16),
            vmem((2, size, depth), f32),
            vmem((2, size, depth), f32),
            vmem((2, 4 * size, depth), b16),
            vmem((4 * size, depth), b16),
            vmem((3, 4 * size, units), b16),
            vmem((2, size, depth), f32),
            vmem((4 * size, depth), f32),
            dma((6,)),
            *[dma((2, 4))] * 5,
            dma((2, 3)),
            dma((2, 4)),
            dma((2,)),
            dma((2,)),
            dma((2, 4)),
            dma((2, 4)),
            dma((3, 4)),
            dma((2,)),
            dma((4,)),
        ],
        compiler_params=pltpu.CompilerParams(
            collective_id=1, has_side_effects=True, vmem_limit_bytes=63 * 1024 * 1024
        ),
        cost_estimate=pl.CostEstimate(
            flops=12 * rows * depth * units, bytes_accessed=6 * depth * units, transcendentals=0
        ),
    )(mixed, output_weight, tokens, upstream, upstream_first, gain[None], gate_weight, up_weight, down_weight)


def grid_neighbours():
    dp = lax.axis_index("dp")
    place, lane = dp // 2, lax.rem(dp, 2)
    towards = 1 - 2 * (place // 2)
    across = {"dp": dp + 1 - 2 * lane}
    inward, outward = {"dp": dp + 2 * towards}, {"dp": dp - 2 * towards}
    team = place // 2
    side = lax.rem(place, 2)
    inner = lax.rem(team + side, 2)
    return place, lane, team, side, inner, across, inward, outward


def greet_grid(always, inner, outward):
    barrier = pltpu.get_barrier_semaphore()
    for device in always:
        pl.semaphore_signal(barrier, inc=1, device_id=device, device_id_type=MESH)

    @pl.when(inner == 1)
    def _():
        pl.semaphore_signal(barrier, inc=1, device_id=outward, device_id_type=MESH)

    pl.semaphore_wait(barrier, len(always) + inner)


def middle_kernel(
    size,
    second_hbm, hidden_hbm, upstream_hbm, upstream_pair, product_own, product_pair,
    gate_own, gate_pair, low_own, low_pair, gain, down_hbm,
    grad_out, grad_low_out, out_part, weight_out, gate_ready, gate_given, gate_own_block,
    products, down_weight, columns, c_recv, x_send, x_recv, back_recv,
    y_send, y_recv, kept, in_recv, mid_recv, out_recv,
    hid, tok, grad, grad_low, out_stage, gate_send, gate_kept, gate_stage,
    load_sems, gate_load_sems, gate_sems, c_sems, x_sems, back_sems, y_sems, z_sems, column_sems,
    x_load_sems, hid_sems, tok_sems, grad_sems, low_sems, out_sems, weight_sems,
):
    core, sibling, facing, _ = neighbours()
    place, lane, team, side, inner, across, inward, outward = grid_neighbours()
    depth = gain.shape[1]
    units = down_weight.shape[0]
    width = columns.shape[-1]
    begin = functools.partial(sequence_rows, size, core)
    rows_in = 8 * size
    down_first = (((0,), (0,)), ((), ()))
    loads = [
        pltpu.make_async_copy(source, target, load_sems.at[index])
        for index, (source, target) in enumerate(
            [
                (product_own, products.at[pl.ds(0, rows_in)]),
                (product_pair, products.at[pl.ds(rows_in, rows_in)]),
                (down_hbm, down_weight),
            ]
        )
    ]
    gate_loads = [
        pltpu.make_async_copy(
            source, products.at[pl.ds(index * rows_in, rows_in)], gate_load_sems.at[index]
        )
        for index, source in enumerate((gate_own, gate_pair))
    ]
    turns = [(0, 1), (1, 1), (0, 0), (1, 0)]
    turns += [(0, 1), (1, 1), (1, 0), (0, 0)]

    def column_loads(index):
        turn, other = turns[index]
        spot = lax.rem(1 - team + turn, 2)
        which = 1 - lane if other else lane
        start = pl.multiple_of((side * 4 + 2 * spot + which) * width, width)
        return [
            pltpu.make_async_copy(
                source.at[:, pl.ds(start, width)],
                columns.at[index % 2, pl.ds(part * rows_in, rows_in)],
                column_sems.at[index % 2, part],
            )
            for part, source in enumerate(
                (upstream_hbm, upstream_pair) if index < 4 else (low_own, low_pair)
            )
        ]

    x_loads = [
        pltpu.make_async_copy(
            second_hbm.at[pl.ds(begin(0, k), size)], x_send.at[k], x_load_sems.at[k]
        )
        for k in range(4)
    ]
    for copy in column_loads(0) + x_loads[:1] + loads[:2] + column_loads(1) + x_loads[1:] + loads[2:]:
        copy.start()
    greet_grid([sibling, facing, across, inward], inner, outward)
    c_copies = [
        remote(second_hbm.at[pl.ds(begin(1, k), size)], c_recv.at[k], c_sems, k, sibling)
        for k in range(4)
    ]
    x_copies = [remote(x_send.at[k], x_recv.at[k], x_sems, k, facing) for k in range(4)]
    back_copies = [remote(x_send.at[k], back_recv.at[k], back_sems, k, sibling) for k in range(4)]
    y_copies = [remote(y_send.at[k], y_recv.at[k], y_sems, k, across) for k in range(2)]
    in_copy = remote(kept.at[0], in_recv, z_sems, 0, inward)
    mid_copies = [remote(kept.at[k], mid_recv.at[k], z_sems, 1 + k, inward) for k in range(2)]
    out_copy = remote(mid_recv.at[0], out_recv, z_sems, 3, outward)
    for copy in c_copies:
        copy.start()

    def cores(k):
        x_loads[k].wait()
        c_copies[k].wait_recv()

        def run(row):
            x_send[k, row, :] = x_send[k, row, :] + c_recv[k, row, :]

        loop_rows(size, 16, run)
        x_copies[k].start()

    def chips(k):
        x_copies[k].wait()

        def run(row):
            x_send[k, row, :] = x_send[k, row, :] + x_recv[k, row, :]

        loop_rows(size, 16, run)
        back_copies[k].start()

    def block(index, target):
        for copy in column_loads(index):
            copy.wait()

        target[...] = lax.dot_general(
            products[...], columns[index % 2], down_first, preferred_element_type=jnp.float32
        )
        for copy in column_loads(index + 2):
            copy.start()

    gate_copy = remote(gate_send, gate_kept, gate_sems, 0, across)

    def gate_block(index, target):
        for copy in column_loads(index):
            copy.wait()
        target[...] = lax.dot_general(
            columns[index % 2], products[...], down_first, preferred_element_type=jnp.float32
        )
        if index + 2 < len(turns):
            for copy in column_loads(index + 2):
                copy.start()

    def gate_store(source, target, index):
        return pltpu.make_async_copy(source, target, gate_load_sems.at[2 + index])

    def chunk_loads(k):
        return [
            pltpu.make_async_copy(
                source.at[pl.ds(begin(which, k), size)], target.at[which], sems.at[which]
            )
            for which in range(2)
            for source, target, sems in ((hidden_hbm, hid, hid_sems), (upstream_hbm, tok, tok_sems))
        ]

    def grad_stores(k):
        return [
            pltpu.make_async_copy(
                source.at[which], target.at[pl.ds(begin(which, k), size)], sems.at[which]
            )
            for which in range(2)
            for source, target, sems in (
                (grad, grad_out, grad_sems),
                (grad_low, grad_low_out, low_sems),
            )
        ]

    def finish(k):
        for copy in chunk_loads(k):
            copy.wait()
        if k > 0:
            for copy in grad_stores(k - 1):
                copy.wait()
        back_copies[k].wait_recv()

        def run(which, source, row):
            value = hid[which, row, :]
            inverse = lax.rsqrt(jnp.mean(value * value, axis=-1, keepdims=True) + epsilon)
            total = tok[which, row, :].astype(jnp.float32) + norm_back(
                source[k, row, :], value, inverse, gain[...]
            )
            grad[which, row, :] = total
            grad_low[which, row, :] = total.astype(jnp.bfloat16)

        for which, source in enumerate((x_send, back_recv)):
            loop_rows(size, 16, functools.partial(run, which, source))
        for copy in grad_stores(k):
            copy.start()
        if k < 3:
            for copy in chunk_loads(k + 1):
                copy.start()

    def out_store(k):
        rows = 2 * size
        return pltpu.make_async_copy(
            out_stage, out_part.at[pl.ds(k * rows, rows)], out_sems.at[0]
        )

    def out_terms(k):
        if k > 0:
            out_store(k - 1).wait()
        rows = pl.ds(k * 2 * size, 2 * size)

        def run(column):
            out_stage[:, column] = jnp.dot(
                products[rows, :], down_weight[:, column], preferred_element_type=jnp.float32
            )

        loop_rows(depth, 1024, run)
        out_store(k).start()

    def take(k):
        y_copies[k].wait_recv()

        def run(row):
            kept[k, row, :] = kept[k, row, :] + y_recv[k, row, :]

        loop_rows(units, 64, run)

    for copy in loads[:2]:
        copy.wait()
    block(0, y_send.at[0])
    y_copies[0].start()
    cores(0)
    for copy in chunk_loads(0):
        copy.start()
    cores(1)
    cores(2)
    cores(3)
    block(1, y_send.at[1])
    y_copies[1].start()
    block(2, kept.at[0])
    loads[2].wait()
    out_terms(0)
    chips(0)
    out_terms(1)
    block(3, kept.at[1])
    finish(0)
    out_terms(2)
    take(0)

    @pl.when(inner == 1)
    def _():
        mid_copies[0].start()

    @pl.when(inner == 0)
    def _():
        in_copy.start()

    out_terms(3)
    for copy in gate_loads:
        copy.start()
    chips(1)
    for copy in gate_loads:
        copy.wait()
    gate_block(4, gate_send)
    gate_copy.start()
    finish(1)
    gate_block(5, gate_stage)
    gate_store(gate_stage, gate_given, 0).start()
    chips(2)
    take(1)

    @pl.when(inner == 1)
    def _():
        mid_copies[1].start()
        mid_copies[0].wait_recv()
        out_copy.start()

    finish(2)
    gate_store(gate_stage, gate_given, 0).wait()
    gate_block(6, gate_stage)
    gate_store(gate_stage, gate_own_block, 1).start()
    gate_store(gate_stage, gate_own_block, 1).wait()
    gate_block(7, gate_stage)
    chips(3)
    finish(3)
    gate_copy.wait()

    def run_gate(row):
        gate_kept[row, :] = gate_kept[row, :] + gate_stage[row, :]

    loop_rows(width, 16, run_gate)
    gate_store(gate_kept, gate_ready, 2).start()

    @pl.when(inner == 1)
    def _():
        in_copy.wait_recv()
        mid_copies[1].wait_recv()
        mid_copies[0].wait_send()
        mid_copies[1].wait_send()
        out_copy.wait_send()

        def run(row):
            kept[0, row, :] = in_recv[row, :] + mid_recv[1, row, :]

        loop_rows(units, 64, run)

    @pl.when(inner == 0)
    def _():
        in_copy.wait_send()
        out_copy.wait_recv()

        def run(row):
            kept[0, row, :] = kept[1, row, :] + out_recv[row, :]

        loop_rows(units, 64, run)

    store = pltpu.make_async_copy(kept.at[0], weight_out, weight_sems.at[0])
    store.start()
    for k in range(4):
        back_copies[k].wait_send()
        c_copies[k].wait_send()
    for k in range(2):
        y_copies[k].wait_send()
    for copy in grad_stores(3):
        copy.wait()
    gate_store(gate_kept, gate_ready, 2).wait()
    out_store(3).wait()
    store.wait()


def middle(
    second, hidden, upstream, upstream_pair, product_own, product_pair,
    gate_own, gate_pair, low_own, low_pair, gain, down_weight,
):
    rows, depth = hidden.shape
    units = down_weight.shape[0]
    size = rows // 8
    width = depth // 8
    f32, b16 = jnp.float32, jnp.bfloat16
    any_space = pl.BlockSpec(memory_space=pl.ANY)
    shape = jax.ShapeDtypeStruct
    dma = pltpu.SemaphoreType.DMA
    vmem = pltpu.VMEM
    return pl.pallas_call(
        functools.partial(middle_kernel, size),
        out_shape=[
            shape((rows, depth), f32),
            shape((rows, depth), b16),
            shape((rows, depth), f32),
            shape((units, width), f32),
        ]
        + [shape((width, units), f32)] * 3,
        in_specs=[any_space] * 10 + [pl.BlockSpec(memory_space=pltpu.VMEM), any_space],
        out_specs=[any_space] * 7,
        scratch_shapes=[
            vmem((2 * rows, units), b16),
            vmem((units, depth), b16),
            vmem((2, 2 * rows, width), b16),
            vmem((4, size, depth), f32),
            vmem((4, size, depth), f32),
            vmem((4, size, depth), f32),
            vmem((4, size, depth), f32),
            vmem((2, units, width), f32),
            vmem((2, units, width), f32),
            vmem((2, units, width), f32),
            vmem((units, width), f32),
            vmem((2, units, width), f32),
            vmem((units, width), f32),
            vmem((2, size, depth), f32),
            vmem((2, size, depth), b16),
            vmem((2, size, depth), f32),
            vmem((2, size, depth), b16),
            vmem((2 * size, depth), f32),
            vmem((width, units), f32),
            vmem((width, units), f32),
            vmem((width, units), f32),
            dma((3,)),
            dma((5,)),
            dma((2, 1)),
            dma((2, 4)),
            dma((2, 4)),
            dma((2, 4)),
            dma((2, 2)),
            dma((2, 4)),
            dma((2, 2)),
            dma((4,)),
            dma((2,)),
            dma((2,)),
            dma((2,)),
            dma((2,)),
            dma((1,)),
            dma((1,)),
        ],
        compiler_params=pltpu.CompilerParams(
            collective_id=2, has_side_effects=True, vmem_limit_bytes=62 * 1024 * 1024
        ),
        cost_estimate=pl.CostEstimate(
            flops=8 * rows * depth * units, bytes_accessed=6 * depth * units, transcendentals=0
        ),
    )(
        second, hidden, upstream, upstream_pair, product_own, product_pair,
        gate_own, gate_pair, low_own, low_pair, gain[None], down_weight,
    )


class TensorSum:
    def __init__(self, size, own, landed, stage, sems, stage_sems, devices):
        self.size, self.own, self.landed, self.stage = size, own, landed, stage
        self.stage_sems = stage_sems
        c_sems, x_sems, back_sems = sems
        self.sibling, facing = devices
        self.c_sems = c_sems
        self.x_copies = [remote(own.at[k], landed[1].at[k], x_sems, k, facing) for k in range(4)]
        self.back_copies = [
            remote(own.at[k], landed[2].at[k], back_sems, k, self.sibling) for k in range(4)
        ]
        self.c_copies = [None] * 4

    def give(self, k, source):
        self.c_copies[k] = remote(source, self.landed[0].at[k], self.c_sems, k, self.sibling)
        self.c_copies[k].start()

    def staged(self, which, k):
        copy = pltpu.make_async_copy(self.landed[which].at[k], self.stage.at[0], self.stage_sems.at[0])
        copy.start()
        copy.wait()

    def add_stage(self, k):
        def run(row):
            self.own[k, row, :] = self.own[k, row, :] + self.stage[0, row, :]

        loop_rows(self.size, 16, run)

    def cores(self, k):
        self.c_copies[k].wait_recv()
        self.staged(0, k)
        self.add_stage(k)
        self.x_copies[k].start()

    def chips(self, k):
        self.x_copies[k].wait()
        self.staged(1, k)
        self.add_stage(k)
        self.back_copies[k].start()

    def other(self, k):
        self.back_copies[k].wait_recv()
        self.staged(2, k)


def rear_kernel(
    size, turns,
    gate_middle, gate_inward, gate_ready, low_own, low_pair, upward_own, upward_pair,
    normed_hbm, raw_hbm, hidden_low_hbm, mixed_hbm, lines,
    out_hbm, hidden_hbm, grad_hbm, tokens_hbm,
    query_hbm, key_hbm, value_hbm, gate_hbm, up_hbm, gain, feed_gain,
    layer_out, tokens_out, gate_out, up_out, raw_out, head_out, gains_out,
    o_c, o_x, o_back, d_c, d_x, d_back, gate_landed, up_landed,
    upwards, raw, mixed, head_weights, feed_rows, gains, gain_rows, gains_in, columns,
    up_send, up_kept, raw_send, raw_kept, head_send, head_kept, raw_line, head_line,
    own, give, stage, wide, narrow, result,
    load_sems, column_sems, y_up_sems, y_raw_sems, y_head_sems, gate_sems, up_sems,
    raw_line_sems, head_line_sems,
    oc_sems, ox_sems, ob_sems, dc_sems, dx_sems, db_sems,
    own_sems, stage_sems, wide_sems, narrow_sems, result_sems, end_sems, gain_sems,
):
    core, sibling, facing, _ = neighbours()
    place, lane, team, side, inner, across, inward, outward = grid_neighbours()
    high = len(turns)
    depth = gain.shape[1]
    width = columns.shape[-1]
    units = upwards.shape[-1]
    begin = functools.partial(sequence_rows, size, core)
    rows_in = 8 * size
    down_first = (((0,), (0,)), ((), ()))
    cuts = (query_hbm.shape[1], key_hbm.shape[1])
    own_rows = pl.ds(pl.multiple_of(lax.axis_index("dp") * width, width), width)
    loads = [
        pltpu.make_async_copy(source, target, load_sems.at[index])
        for index, (source, target) in enumerate(
            [
                (raw_hbm, raw),
                (mixed_hbm, mixed),
                (upward_own, upwards.at[pl.ds(0, rows_in)]),
                (upward_pair, upwards.at[pl.ds(rows_in, rows_in)]),
                (query_hbm, head_weights.at[:, pl.ds(0, cuts[0])]),
                (key_hbm, head_weights.at[:, pl.ds(cuts[0], cuts[1])]),
                (value_hbm, head_weights.at[:, pl.ds(cuts[0] + cuts[1], cuts[1])]),
                (gate_hbm.at[own_rows], feed_rows.at[0]),
                (up_hbm.at[own_rows], feed_rows.at[1]),
            ]
        )
    ]
    blocks = [
        ("head", 0, 1), ("up", 0, 1), ("up", 1, 1), ("head", 1, 1), ("head", 2, 1), ("head", 3, 1),
        ("head", 0, 0), ("up", 0, 0), ("up", 1, 0), ("head", 1, 0), ("head", 2, 0), ("head", 3, 0),
    ]

    def spot_of(kind, turn):
        if kind == "up":
            return side * 2 + lax.rem(1 - team + turn, 2)
        spot = jnp.int32(turns[0][turn])
        for p in range(1, high):
            spot = jnp.where(place == p, jnp.int32(turns[p][turn]), spot)
        return spot

    def column_loads(index):
        kind, turn, other = blocks[index]
        which = 1 - lane if other else lane
        start = pl.multiple_of((2 * spot_of(kind, turn) + which) * width, width)
        sources = (low_own, low_pair) if kind == "up" else (normed_hbm, hidden_low_hbm)
        return [
            pltpu.make_async_copy(
                source.at[:, pl.ds(start, width)],
                columns.at[index % 2, pl.ds(part * rows_in, rows_in)],
                column_sems.at[index % 2, part],
            )
            for part, source in enumerate(sources)
        ]

    own_loads = [
        pltpu.make_async_copy(out_hbm.at[pl.ds(begin(0, k), size)], own.at[k], own_sems.at[k])
        for k in range(4)
    ]
    for copy in column_loads(0) + loads[:2] + column_loads(1) + own_loads + loads[2:]:
        copy.start()
    greet_grid([sibling, facing, across, inward], inner, outward)
    devices = (sibling, facing)
    outs = TensorSum(
        size, own, (o_c, o_x, o_back), stage, (oc_sems, ox_sems, ob_sems), stage_sems, devices
    )
    heads = TensorSum(
        size, own, (d_c, d_x, d_back), stage, (dc_sems, dx_sems, db_sems), stage_sems, devices
    )
    for k in range(4):
        outs.give(k, out_hbm.at[pl.ds(begin(1, k), size)])

    def team_copies(values, landed, sems):
        return (
            remote(values[0], landed.at[0], sems, 0, inward),
            [remote(values[k], landed.at[1 + k], sems, 1 + k, inward) for k in range(2)],
            remote(landed.at[1], landed.at[3], sems, 3, outward),
        )

    gate_copies = (
        None,
        [None, remote(gate_ready, gate_landed.at[0], gate_sems, 0, inward)],
        remote(gate_middle, gate_landed.at[1], gate_sems, 1, outward),
    )
    up_copies = team_copies((up_kept.at[0], up_kept.at[1]), up_landed, up_sems)

    def team_send(copies, turn):
        @pl.when(inner == 1)
        def _():
            copies[1][turn].start()

        if turn == 0:

            @pl.when(inner == 0)
            def _():
                copies[0].start()

    def team_forward(copies):
        @pl.when(inner == 1)
        def _():
            copies[1][0].wait_recv()
            copies[2].start()

    def add_gain(lane_index, row, value, weight):
        total = jnp.sum(value * weight.astype(jnp.float32), axis=-1, keepdims=True)
        lanes = lax.broadcasted_iota(jnp.int32, (total.shape[0], gains.shape[1]), 1)
        gains[row, :] = gains[row, :] + jnp.where(lanes == lane_index, total, 0.0)

    def team_combine(copies, first, second, outward_landed, last, out, sem, which):
        def fetch(source, slot):
            copy = pltpu.make_async_copy(source, up_send.at[slot], end_sems.at[4 + slot])
            copy.start()
            copy.wait()

        @pl.when(inner == 1)
        def _():
            if copies[0] is not None:
                copies[0].wait_recv()
                copies[1][0].wait_send()
            copies[1][1].wait_recv()
            fetch(first, 0)
            fetch(second, 1)
            copies[1][1].wait_send()
            copies[2].wait_send()

        @pl.when(inner == 0)
        def _():
            if copies[0] is not None:
                copies[0].wait_send()
            copies[2].wait_recv()
            fetch(outward_landed, 0)
            fetch(last, 1)

        def run(row):
            total = up_send[0, row, :] + up_send[1, row, :]
            up_send[0, row, :] = total
            add_gain(1, row, total, feed_rows[which, row, :])

        loop_rows(width, 16, run)
        store = pltpu.make_async_copy(up_send.at[0], out, sem)
        store.start()
        store.wait()

    y_up = [remote(up_send.at[k], up_kept.at[k], y_up_sems, k, across) for k in range(2)]
    y_raw = [remote(raw_send.at[k], raw_kept.at[k], y_raw_sems, k, across) for k in range(high)]
    y_head = [
        remote(head_send.at[k], head_kept.at[k], y_head_sems, k, across) for k in range(high)
    ]

    def line_copy(p, turn, towards=None):
        block = turns[p][turn]
        ahead = block > p
        slot = block - 1 if ahead else high - 1 + block
        device = {"dp": lax.axis_index("dp") + (2 if ahead else -2)}
        return slot, [
            remote(kept.at[turn], line.at[slot], sems, slot, device)
            for kept, line, sems in (
                (raw_kept, raw_line, raw_line_sems),
                (head_kept, head_line, head_line_sems),
            )
        ]

    def line_arrived(slot, turn):
        for kept, line, sems in (
            (raw_kept, raw_line, raw_line_sems),
            (head_kept, head_line, head_line_sems),
        ):
            remote(kept.at[turn], line.at[slot], sems, slot, across).wait_recv()

            def run(row):
                kept[turn, row, :] = kept[turn, row, :] + line[slot, row, :]

            loop_rows(kept.shape[1], 8, run)

    def line_step(turn):
        for p in range(high):
            block = turns[p][turn]

            @pl.when(place == p)
            def _():
                slot, copies = line_copy(p, turn)
                if (block > p and p > 0) or (block < p and p < high - 1):
                    line_arrived(slot, turn)
                for copy in copies:
                    copy.start()

    def line_end():
        for p in range(high):

            @pl.when(place == p)
            def _():
                if p > 0:
                    line_arrived(p - 1, high - 1)
                if p < high - 1:
                    line_arrived(high - 1 + p, high - 1)
                for turn in range(high - 1):
                    for copy in line_copy(p, turn)[1]:
                        copy.wait_send()

    def up_block(index, target, added):
        for copy in column_loads(index):
            copy.wait()

        total = lax.dot_general(
            columns[index % 2], upwards[...], down_first, preferred_element_type=jnp.float32
        )
        target[...] = target[...] + total if added else total
        if index + 2 < len(blocks):
            for copy in column_loads(index + 2):
                copy.start()

    def head_block(index, raw_target, head_target, added):
        kind, turn, other = blocks[index]
        which = 1 - lane if other else lane
        for copy in column_loads(index):
            copy.wait()
        slot = index % 2
        total = lax.dot_general(
            columns[slot, :rows_in], raw[...], down_first, preferred_element_type=jnp.float32
        )
        line = lines[2 * spot_of(kind, turn) + which]
        raw_target[:width, :] = raw_target[:width, :] + total if added else total
        raw_target[width:, :] = raw_target[width:, :] + line if added else line
        total = lax.dot_general(
            mixed[...], columns[slot, rows_in:], down_first, preferred_element_type=jnp.float32
        )
        head_target[...] = head_target[...] + total if added else total
        if index + 2 < len(blocks):
            for copy in column_loads(index + 2):
                copy.start()

    def head_send_block(index):
        turn = blocks[index][1]
        head_block(index, raw_send.at[turn], head_send.at[turn], False)
        y_raw[turn].start()
        y_head[turn].start()

    def head_take(index):
        turn = blocks[index][1]
        y_raw[turn].wait_recv()
        y_head[turn].wait_recv()
        head_block(index, raw_kept.at[turn], head_kept.at[turn], True)

    def head_terms(k):
        outs.back_copies[k].wait_send()
        if k >= 2:
            heads.c_copies[k - 2].wait_send()
        rows = jnp.concatenate(
            [raw[pl.ds(begin(which, k), size), :] for which in range(2)], axis=0
        )

        def run(column):
            total = lax.dot_general(
                rows,
                head_weights[column, :],
                (((1,), (1,)), ((), ())),
                preferred_element_type=jnp.float32,
            )
            own[k, :, column] = total[:size]
            give[k % 2, :, column] = total[size:]

        loop_rows(depth, 1024, run)
        heads.give(k, give.at[k % 2])

    def fetches(what, k):
        pairs = ((hidden_hbm, wide, wide_sems),)
        if what == "tokens":
            pairs = ((grad_hbm, wide, wide_sems), (tokens_hbm, narrow, narrow_sems))
        return [
            pltpu.make_async_copy(
                source.at[pl.ds(begin(which, k), size)], target.at[which], sems.at[which]
            )
            for which in range(2)
            for source, target, sems in pairs
        ]

    def stores(what, k):
        return [
            pltpu.make_async_copy(
                result.at[which],
                (layer_out if what == "layer" else tokens_out).at[pl.ds(begin(which, k), size)],
                result_sems.at[which],
            )
            for which in range(2)
        ]

    sequence = [("layer", k) for k in range(4)] + [("tokens", k) for k in range(4)]

    def finish(what, k):
        number = sequence.index((what, k))
        for copy in fetches(what, k):
            copy.wait()
        if number > 0:
            for copy in stores(*sequence[number - 1]):
                copy.wait()
        (outs if what == "layer" else heads).other(k)

        def run(which, row):
            total = stage[0, row, :] if which else own[k, row, :]
            value = wide[which, row, :]
            if what == "layer":
                total = value + total
            else:
                inputs = narrow[which, row, :].astype(jnp.float32)
                inverse = lax.rsqrt(jnp.mean(inputs * inputs, axis=-1, keepdims=True) + epsilon)
                total = value + norm_back(total, inputs, inverse, gain[...])
            result[which, row, :] = total.astype(jnp.bfloat16)

        for which in range(2):
            loop_rows(size, 16, functools.partial(run, which))
        for copy in stores(what, k):
            copy.start()
        if number + 1 < len(sequence):
            for copy in fetches(*sequence[number + 1]):
                copy.start()

    team_send(gate_copies, 1)

    @pl.when(inner == 1)
    def _():
        gate_copies[2].start()

    gains[...] = jnp.zeros_like(gains)
    for copy in fetches("layer", 0):
        copy.start()
    for copy in loads[:2]:
        copy.wait()
    head_send_block(0)
    own_loads[0].wait()
    outs.cores(0)
    for copy in loads[2:]:
        copy.wait()
    up_block(1, up_send.at[0], False)
    y_up[0].start()
    for k in range(1, 4):
        own_loads[k].wait()
        outs.cores(k)
    up_block(2, up_send.at[1], False)
    y_up[1].start()
    for index in range(3, 6):
        head_send_block(index)
    outs.chips(0)
    finish("layer", 0)
    head_take(6)
    line_step(0)
    head_terms(0)
    outs.chips(1)
    finish("layer", 1)
    head_terms(1)
    heads.cores(0)
    y_up[0].wait_recv()
    up_block(7, up_kept.at[0], True)
    team_send(up_copies, 0)
    outs.chips(2)
    finish("layer", 2)
    head_terms(2)
    heads.cores(1)
    outs.chips(3)
    heads.cores(2)
    finish("layer", 3)
    head_terms(3)
    heads.cores(3)
    y_up[1].wait_recv()
    up_block(8, up_kept.at[1], True)
    team_send(up_copies, 1)
    team_forward(up_copies)
    heads.chips(0)
    finish("tokens", 0)
    for k in range(2):
        y_up[k].wait_send()
    team_combine(
        gate_copies, gate_inward, gate_landed.at[0], gate_landed.at[1], gate_ready,
        gate_out, end_sems.at[0], 0,
    )
    head_take(9)
    line_step(1)
    heads.chips(1)
    finish("tokens", 1)
    y_raw[0].wait_send()
    y_head[0].wait_send()
    heads.chips(2)
    finish("tokens", 2)
    head_take(10)
    line_step(2)
    head_block(11, raw_send.at[0], head_send.at[0], False)
    team_combine(
        up_copies, up_landed.at[0], up_landed.at[2], up_landed.at[3], up_kept.at[1],
        up_out, end_sems.at[1], 1,
    )
    heads.chips(3)
    finish("tokens", 3)
    y_raw[high - 1].wait_recv()
    y_head[high - 1].wait_recv()
    for kept, sent, step in ((raw_kept, raw_send, 8), (head_kept, head_send, 16)):

        def run_last(row):
            kept[high - 1, row, :] = kept[high - 1, row, :] + sent[0, row, :]

        loop_rows(kept.shape[1], step, run_last)
    line_end()
    ends = [
        pltpu.make_async_copy(raw_kept.at[high - 1], raw_out, end_sems.at[2]),
        pltpu.make_async_copy(head_kept.at[high - 1], head_out, end_sems.at[3]),
    ]
    for copy in ends:
        copy.start()

    def run_gain(row):
        place_row = pl.ds(pl.multiple_of(own_rows.start + row.start, 16), row.size)
        add_gain(0, row, raw_kept[high - 1, row, :], head_weights[place_row, :])

    loop_rows(width, 16, run_gain)
    own_columns = pl.ds(pl.multiple_of(own_rows.start, 128), width)
    turned = jnp.transpose(gains[...])[:8]
    scale = jnp.concatenate([gain[:, own_columns], feed_gain[:, own_columns]], axis=0)
    gain_rows[:8, :] = turned
    gain_rows[:2, :] = turned[:2] / scale
    gain_rows[8:, :] = raw_kept[high - 1, width:, :width]
    gain_copies = [
        remote(gain_rows, gains_in.at[k], gain_sems, k, device)
        for k, device in enumerate((sibling, facing))
    ]
    for k in range(2):
        gain_copies[k].start()
        gain_copies[k].wait()
        gain_rows[...] = gain_rows[...] + gains_in[k]
    gain_store = pltpu.make_async_copy(gain_rows, gains_out, own_sems.at[0])
    gain_store.start()
    gain_store.wait()
    for k in range(4):
        outs.c_copies[k].wait_send()
        heads.back_copies[k].wait_send()
    for k in range(2, 4):
        heads.c_copies[k].wait_send()
    for k in range(1, high):
        y_raw[k].wait_send()
        y_head[k].wait_send()
    for copy in stores(*sequence[-1]) + ends:
        copy.wait()


def rear(turns, arrays, lines, places, weights, gain, feed_gain):
    rows, depth = places[0].shape
    units = arrays[0].shape[1]
    heads, inner = arrays[8].shape[1], arrays[10].shape[1]
    size = rows // 8
    width = depth // 8
    high = len(turns)
    f32, b16 = jnp.float32, jnp.bfloat16
    any_space = pl.BlockSpec(memory_space=pl.ANY)
    in_vmem = pl.BlockSpec(memory_space=pltpu.VMEM)
    shape = jax.ShapeDtypeStruct
    dma = pltpu.SemaphoreType.DMA
    vmem = pltpu.VMEM
    slots = 2 * (high - 1)
    return pl.pallas_call(
        functools.partial(rear_kernel, size, turns),
        out_shape=[
            shape((rows, depth), b16),
            shape((rows, depth), b16),
            shape((width, units), f32),
            shape((width, units), f32),
            shape((width + 8, heads), f32),
            shape((inner, width), f32),
            shape((16, width), f32),
        ]
        + [shape((4, size, depth), f32)] * 6
        + [shape((2, width, units), f32), shape((4, width, units), f32)],
        in_specs=[any_space] * 11 + [in_vmem] + [any_space] * 9 + [in_vmem] * 2,
        out_specs=[any_space] * 15,
        scratch_shapes=[
            vmem((2 * rows, units), b16),
            vmem((rows, heads), b16),
            vmem((rows, inner), b16),
            vmem((depth, heads), b16),
            vmem((2, width, units), b16),
            vmem((width, HD), f32),
            vmem((16, width), f32),
            vmem((2, 16, width), f32),
            vmem((2, 2 * rows, width), b16),
            vmem((2, width, units), f32),
            vmem((2, width, units), f32),
            vmem((high, width + 8, heads), f32),
            vmem((high, width + 8, heads), f32),
            vmem((high, inner, width), f32),
            vmem((high, inner, width), f32),
            vmem((slots, width + 8, heads), f32),
            vmem((slots, inner, width), f32),
            vmem((4, size, depth), f32),
            vmem((2, size, depth), f32),
            vmem((1, size, depth), f32),
            vmem((2, size, depth), f32),
            vmem((2, size, depth), b16),
            vmem((2, size, depth), b16),
            dma((9,)),
            dma((2, 2)),
            dma((2, 2)),
            dma((2, high)),
            dma((2, high)),
            dma((2, 4)),
            dma((2, 4)),
            dma((2, slots)),
            dma((2, slots)),
            *[dma((2, 4))] * 6,
            dma((4,)),
            dma((1,)),
            dma((2,)),
            dma((2,)),
            dma((2,)),
            dma((6,)),
            dma((2, 2)),
        ],
        compiler_params=pltpu.CompilerParams(
            collective_id=3, has_side_effects=True, vmem_limit_bytes=62 * 1024 * 1024
        ),
        cost_estimate=pl.CostEstimate(
            flops=8 * rows * depth * units, bytes_accessed=6 * depth * units, transcendentals=0
        ),
    )(*arrays, lines, *places, *weights, gain[None], feed_gain[None])


def block_mask(segment_column, segment_row, begin, rows, columns):
    row = begin + lax.broadcasted_iota(jnp.int32, (rows, columns), 0)
    column = lax.broadcasted_iota(jnp.int32, (rows, columns), 1)
    same = segment_column[pl.ds(begin, rows), :] == segment_row[:, :columns]
    return same & (row >= column)


def head_columns(index):
    return pl.ds(pl.multiple_of(index * HD, HD), HD)


def attention_kernel(
    step,
    tokens, gain, query_weight, key_weight, value_weight, query_gain, key_gain, cosine, sine,
    segment_column, segment_row,
    normed_out, query_raw, key_raw, query_out, key_out, value_out, mixed_out, total_out,
):
    count = tokens.shape[0]
    query_heads = query_weight.shape[1] // HD
    value_heads = key_weight.shape[1] // HD
    group = query_heads // value_heads

    def normalize(rows):
        value = tokens[rows, :].astype(jnp.float32)
        normed_out[rows, :] = (value * rms_inverse(value) * gain[...]).astype(jnp.bfloat16)

    loop_rows(count, 32, normalize)

    def project(rows):
        low = normed_out[rows, :]
        value_out[rows, :] = jnp.dot(
            low, value_weight[...], preferred_element_type=jnp.float32
        ).astype(jnp.bfloat16)
        for weight, raw, out, head_gain, heads in (
            (query_weight, query_raw, query_out, query_gain, query_heads),
            (key_weight, key_raw, key_out, key_gain, value_heads),
        ):
            product = jnp.dot(low, weight[...], preferred_element_type=jnp.float32)
            raw[rows, :] = product
            for head in range(heads):
                part = product[:, head * HD : (head + 1) * HD]
                unit = part * rms_inverse(part) * head_gain[...]
                turned = unit * cosine[rows, :] + pltpu.roll(unit, HD // 2, 1) * sine[rows, :]
                out[rows, head * HD : (head + 1) * HD] = turned.astype(jnp.bfloat16)

    loop_rows(count, step, project)

    def head_step(head, carry):
        own = head_columns(head)
        shared = head_columns(head // group)
        for begin in range(0, count, step):
            reach = begin + step
            scores = lax.dot_general(
                query_out[pl.ds(begin, step), own],
                key_out[pl.ds(0, reach), shared],
                (((1,), (1,)), ((), ())),
                preferred_element_type=jnp.float32,
            ) * HD ** (-0.5)
            allowed = block_mask(segment_column, segment_row, begin, step, reach)
            scores = jnp.where(allowed, scores, masked)
            peak = jnp.max(scores, axis=-1, keepdims=True)
            expons = jnp.exp(scores - peak)
            total = jnp.sum(expons, axis=-1, keepdims=True)
            chance = (expons * (1.0 / total)).astype(jnp.bfloat16)
            mixed_out[pl.ds(begin, step), own] = jnp.dot(
                chance, value_out[pl.ds(0, reach), shared], preferred_element_type=jnp.float32
            ).astype(jnp.bfloat16)
            total_out[head, pl.ds(begin, step), :] = jnp.broadcast_to(
                peak + jnp.log(total), (step, HD)
            )
        return carry

    lax.fori_loop(0, query_heads, head_step, 0)


def attention(tokens, gain, weights, query_gain, key_gain, cosine, sine, segment_column, segment_row):
    count, depth = tokens.shape
    queries, keys = weights[0].shape[1], weights[1].shape[1]
    f32, b16 = jnp.float32, jnp.bfloat16
    shape = jax.ShapeDtypeStruct
    return pl.pallas_call(
        functools.partial(attention_kernel, 256),
        out_shape=[
            shape((count, depth), b16),
            shape((count, queries), f32),
            shape((count, keys), f32),
            shape((count, queries), b16),
            shape((count, keys), b16),
            shape((count, keys), b16),
            shape((count, queries), b16),
            shape((queries // HD, count, HD), f32),
        ],
        compiler_params=pltpu.CompilerParams(vmem_limit_bytes=56 * 1024 * 1024),
        cost_estimate=pl.CostEstimate(
            flops=2 * count * depth * (queries + 2 * keys) + 4 * count * count * queries,
            bytes_accessed=32 * 1024 * 1024,
            transcendentals=count * count * queries // HD,
        ),
    )(tokens, gain[None], *weights, query_gain[None], key_gain[None], cosine, sine, segment_column, segment_row)


def attention_back_kernel(
    step,
    hidden_low, output_weight, queries, keys, values, totals, query_raw, key_raw,
    query_gain, key_gain, cosine, sine, segment_column, segment_row,
    raw_out, query_gain_out, key_gain_out,
    upstream, query_grad, key_grad, value_grad,
):
    count = hidden_low.shape[0]
    query_heads = queries.shape[1] // HD
    value_heads = keys.shape[1] // HD
    group = query_heads // value_heads
    across_last = (((1,), (1,)), ((), ()))
    down_first = (((0,), (0,)), ((), ()))

    def project(rows):
        upstream[rows, :] = lax.dot_general(
            hidden_low[rows, :],
            output_weight[...],
            across_last,
            preferred_element_type=jnp.float32,
        ).astype(jnp.bfloat16)

    loop_rows(count, step, project)
    key_grad[...] = jnp.zeros_like(key_grad)
    value_grad[...] = jnp.zeros_like(value_grad)

    def head_step(head, carry):
        own = head_columns(head)
        shared = head_columns(head // group)
        for begin in range(0, count, step):
            reach = begin + step
            rows, before = pl.ds(begin, step), pl.ds(0, reach)
            scores = lax.dot_general(
                queries[rows, own],
                keys[before, shared],
                across_last,
                preferred_element_type=jnp.float32,
            ) * HD ** (-0.5)
            allowed = block_mask(segment_column, segment_row, begin, step, reach)
            chance = jnp.exp(jnp.where(allowed, scores, masked) - totals[head, rows, :][:, :1])
            incoming = upstream[rows, own]
            value_grad[before, shared] += lax.dot_general(
                chance.astype(jnp.bfloat16),
                incoming,
                down_first,
                preferred_element_type=jnp.float32,
            )
            along = lax.dot_general(
                incoming, values[before, shared], across_last, preferred_element_type=jnp.float32
            )
            center = jnp.sum(along * chance, axis=-1, keepdims=True)
            score_grad = (chance * (along - center)).astype(jnp.bfloat16)
            query_grad[rows, own] = jnp.dot(
                score_grad, keys[before, shared], preferred_element_type=jnp.float32
            ) * HD ** (-0.5)
            key_grad[before, shared] += lax.dot_general(
                score_grad, queries[rows, own], down_first, preferred_element_type=jnp.float32
            ) * HD ** (-0.5)
        return carry

    lax.fori_loop(0, query_heads, head_step, 0)
    query_gain_out[...] = jnp.zeros_like(query_gain_out)
    key_gain_out[...] = jnp.zeros_like(key_gain_out)

    def finish(rows):
        for grad, raw, head_gain, gain_out, heads, place in (
            (query_grad, query_raw, query_gain, query_gain_out, query_heads, 0),
            (key_grad, key_raw, key_gain, key_gain_out, value_heads, query_heads),
        ):
            for head in range(heads):
                columns = slice(head * HD, (head + 1) * HD)
                upward = grad[rows, columns]
                unit_grad = upward * cosine[rows, :] - pltpu.roll(upward, HD // 2, 1) * sine[rows, :]
                value = raw[rows, columns]
                inverse = rms_inverse(value)
                product = unit_grad * (value * inverse)
                gain_out[...] += jnp.sum(product.reshape(-1, 8, HD), axis=0)
                begin = (place + head) * HD
                raw_out[rows, begin : begin + HD] = norm_back(
                    unit_grad, value, inverse, head_gain[...]
                ).astype(jnp.bfloat16)
        begin = (query_heads + value_heads) * HD
        raw_out[rows, begin:] = value_grad[rows, :].astype(jnp.bfloat16)

    loop_rows(count, 64, finish)


def attention_back(
    hidden_low, output_weight, queries, keys, values, totals, query_raw, key_raw,
    query_gain, key_gain, cosine, sine, segment_column, segment_row,
):
    count = hidden_low.shape[0]
    query_columns, key_columns = queries.shape[1], keys.shape[1]
    f32, b16 = jnp.float32, jnp.bfloat16
    shape = jax.ShapeDtypeStruct
    return pl.pallas_call(
        functools.partial(attention_back_kernel, 256),
        out_shape=[
            shape((count, query_columns + 2 * key_columns), b16),
            shape((8, HD), f32),
            shape((8, HD), f32),
        ],
        scratch_shapes=[
            pltpu.VMEM((count, query_columns), b16),
            pltpu.VMEM((count, query_columns), f32),
            pltpu.VMEM((count, key_columns), f32),
            pltpu.VMEM((count, key_columns), f32),
        ],
        compiler_params=pltpu.CompilerParams(vmem_limit_bytes=56 * 1024 * 1024),
        cost_estimate=pl.CostEstimate(
            flops=2 * count * hidden_low.shape[1] * query_columns + 10 * count * count * query_columns,
            bytes_accessed=24 * 1024 * 1024,
            transcendentals=count * count * query_columns // HD,
        ),
    )(
        hidden_low, output_weight, queries, keys, values, totals, query_raw, key_raw,
        query_gain[None], key_gain[None], cosine, sine, segment_column, segment_row,
    )


def finish_kernel(columns, number, *refs):
    inputs, gains = refs[:number], refs[number]
    outs, held = refs[number + 1 : -number - 2], refs[-number - 2 : -2]
    in_sems, out_sems = refs[-2:]
    rows = outs[number - 1].shape[0]
    fetches = [
        pltpu.make_async_copy(source, target, in_sems.at[index])
        for index, (source, target) in enumerate(zip(inputs, held))
    ]
    for copy in fetches:
        copy.start()
    stores = [[pltpu.make_async_copy(held[k], outs[k], out_sems.at[k])] for k in range(number - 1)]
    begin, last = 0, []
    for k, count in enumerate(columns):
        last.append(
            pltpu.make_async_copy(
                held[-1].at[pl.ds(0, rows), pl.ds(begin, count)],
                outs[number - 1 + k],
                out_sems.at[number - 1 + k],
            )
        )
        begin += count
    stores.append(last)
    for row, out in zip((0, 1, 8, 9), outs[number + 2 :]):
        out[...] = gains[row : row + 1, : out.shape[1]]
    for fetch, group in zip(fetches, stores):
        fetch.wait()
        for copy in group:
            copy.start()
    for group in stores:
        for copy in group:
            copy.wait()


def finish(columns, head_width, arrays, raw, gains):
    shape = jax.ShapeDtypeStruct
    any_space = pl.BlockSpec(memory_space=pl.ANY)
    in_vmem = pl.BlockSpec(memory_space=pltpu.VMEM)
    width = raw.shape[0] - 8
    number = len(arrays) + 1
    outs = [shape(value.shape, value.dtype) for value in arrays]
    outs += [shape((width, count), jnp.float32) for count in columns]
    outs += [shape((1, count), jnp.float32) for count in (width, width, head_width, head_width)]
    return pl.pallas_call(
        functools.partial(finish_kernel, columns, number),
        out_shape=outs,
        in_specs=[any_space] * number + [in_vmem],
        out_specs=[any_space] * (number + 2) + [in_vmem] * 4,
        scratch_shapes=[pltpu.VMEM(value.shape, value.dtype) for value in (*arrays, raw)]
        + [pltpu.SemaphoreType.DMA((number,)), pltpu.SemaphoreType.DMA((number + 2,))],
        compiler_params=pltpu.CompilerParams(vmem_limit_bytes=60 * 1024 * 1024),
    )(*arrays, raw, gains)


def plain_shards(
    tokens,
    attention_gain,
    query_weight,
    key_weight,
    value_weight,
    query_gain,
    key_gain,
    output_weight,
    feedforward_gain,
    gate_weight,
    up_weight,
    down_weight,
    segment_numbers,
    positions,
    cotangent,
):
    count = tokens.shape[0]
    batch = count // SEQ_LEN
    query_heads = query_weight.shape[1] // HD
    value_heads = key_weight.shape[1] // HD
    group = query_heads // value_heads
    inputs = tokens.astype(jnp.float32)
    first_inverse = rms_inverse(inputs)
    first_normed = inputs * first_inverse
    normed_low = (first_normed * attention_gain).astype(jnp.bfloat16)
    query_raw = jnp.dot(normed_low, query_weight, preferred_element_type=jnp.float32).reshape(
        count, query_heads, HD
    )
    key_raw = jnp.dot(normed_low, key_weight, preferred_element_type=jnp.float32).reshape(
        count, value_heads, HD
    )
    value_low = jnp.dot(normed_low, value_weight, preferred_element_type=jnp.float32).astype(
        jnp.bfloat16
    )
    cosine, sine = rotary_tables(positions)
    cosine = cosine[:, None]
    sine = sine[:, None]
    query_inverse = rms_inverse(query_raw)
    query_unit = query_raw * query_inverse
    query_low = rotate(query_unit * query_gain, cosine, sine).astype(jnp.bfloat16)
    key_inverse = rms_inverse(key_raw)
    key_unit = key_raw * key_inverse
    key_low = rotate(key_unit * key_gain, cosine, sine).astype(jnp.bfloat16)
    queries = query_low.reshape(batch, SEQ_LEN, value_heads, group, HD)
    keys = key_low.reshape(batch, SEQ_LEN, value_heads, HD)
    values = value_low.reshape(batch, SEQ_LEN, value_heads, HD)
    segments = segment_numbers.reshape(batch, SEQ_LEN)
    mixed, totals = lax.map(attend, (queries, keys, values, segments))
    mixed_low = mixed.reshape(count, query_heads * HD).astype(jnp.bfloat16)
    attention = lax.psum(
        jnp.dot(mixed_low, output_weight, preferred_element_type=jnp.float32), "tensor"
    )
    hidden = inputs + attention
    second_inverse = rms_inverse(hidden)
    second_normed = hidden * second_inverse
    second_low = (second_normed * feedforward_gain).astype(jnp.bfloat16)
    gate = jnp.dot(second_low, gate_weight, preferred_element_type=jnp.float32)
    upward = jnp.dot(second_low, up_weight, preferred_element_type=jnp.float32)
    sigmoid_gate = jax.nn.sigmoid(gate)
    activated = gate * sigmoid_gate
    product_low = (activated * upward).astype(jnp.bfloat16)
    feedforward = lax.psum(
        jnp.dot(product_low, down_weight, preferred_element_type=jnp.float32), "tensor"
    )
    layer_output = (hidden + feedforward).astype(jnp.bfloat16)
    down_grad = jnp.einsum("tf,td->fd", product_low, cotangent, preferred_element_type=jnp.float32)
    product_grad = jnp.einsum(
        "td,fd->tf", cotangent, down_weight, preferred_element_type=jnp.float32
    )
    gate_grad_low = (
        product_grad * upward * sigmoid_gate * (1.0 + gate * (1.0 - sigmoid_gate))
    ).astype(jnp.bfloat16)
    upward_grad_low = (product_grad * activated).astype(jnp.bfloat16)
    gate_weight_grad = jnp.einsum(
        "td,tf->df", second_low, gate_grad_low, preferred_element_type=jnp.float32
    )
    upward_weight_grad = jnp.einsum(
        "td,tf->df", second_low, upward_grad_low, preferred_element_type=jnp.float32
    )
    second_part = jnp.einsum(
        "tf,df->td", gate_grad_low, gate_weight, preferred_element_type=jnp.float32
    )
    second_part = second_part + jnp.einsum(
        "tf,df->td", upward_grad_low, up_weight, preferred_element_type=jnp.float32
    )
    second_grad = lax.psum(second_part, "tensor")
    second_gain_grad = jnp.sum(second_grad * second_normed, axis=0)
    hidden_grad = cotangent.astype(jnp.float32) + norm_back(
        second_grad, hidden, second_inverse, feedforward_gain
    )
    hidden_low = hidden_grad.astype(jnp.bfloat16)
    output_weight_grad = jnp.einsum(
        "tc,td->cd", mixed_low, hidden_low, preferred_element_type=jnp.float32
    )
    mixed_grad = jnp.einsum(
        "td,cd->tc", hidden_low, output_weight, preferred_element_type=jnp.float32
    ).astype(jnp.bfloat16)
    upstream = mixed_grad.reshape(batch, SEQ_LEN, value_heads, group, HD)
    query_back, key_back, value_back = lax.map(
        attend_back, (queries, keys, values, segments, totals, upstream)
    )
    query_unit_grad = rotate_back(query_back.reshape(count, query_heads, HD), cosine, sine)
    key_unit_grad = rotate_back(key_back.reshape(count, value_heads, HD), cosine, sine)
    query_gain_part = jnp.sum(query_unit_grad * query_unit, axis=(0, 1))
    key_gain_part = jnp.sum(key_unit_grad * key_unit, axis=(0, 1))
    query_raw_grad = (
        norm_back(query_unit_grad, query_raw, query_inverse, query_gain)
        .reshape(count, query_heads * HD)
        .astype(jnp.bfloat16)
    )
    key_raw_grad = (
        norm_back(key_unit_grad, key_raw, key_inverse, key_gain)
        .reshape(count, value_heads * HD)
        .astype(jnp.bfloat16)
    )
    value_raw_grad = value_back.reshape(count, value_heads * HD).astype(jnp.bfloat16)
    query_weight_grad = jnp.einsum(
        "td,tc->dc", normed_low, query_raw_grad, preferred_element_type=jnp.float32
    )
    key_weight_grad = jnp.einsum(
        "td,tc->dc", normed_low, key_raw_grad, preferred_element_type=jnp.float32
    )
    value_weight_grad = jnp.einsum(
        "td,tc->dc", normed_low, value_raw_grad, preferred_element_type=jnp.float32
    )
    first_part = jnp.einsum(
        "tc,dc->td", query_raw_grad, query_weight, preferred_element_type=jnp.float32
    )
    first_part = first_part + jnp.einsum(
        "tc,dc->td", key_raw_grad, key_weight, preferred_element_type=jnp.float32
    )
    first_part = first_part + jnp.einsum(
        "tc,dc->td", value_raw_grad, value_weight, preferred_element_type=jnp.float32
    )
    first_grad, query_gain_grad, key_gain_grad = lax.psum(
        (first_part, query_gain_part, key_gain_part), "tensor"
    )
    first_gain_grad = jnp.sum(first_grad * first_normed, axis=0)
    tokens_gradient = (
        hidden_grad + norm_back(first_grad, inputs, first_inverse, attention_gain)
    ).astype(jnp.bfloat16)
    summed = (
        lax.psum_scatter(first_gain_grad, "dp", scatter_dimension=0, tiled=True),
        lax.psum_scatter(query_weight_grad, "dp", scatter_dimension=0, tiled=True),
        lax.psum_scatter(key_weight_grad, "dp", scatter_dimension=0, tiled=True),
        lax.psum_scatter(value_weight_grad, "dp", scatter_dimension=0, tiled=True),
        lax.psum_scatter(query_gain_grad, "dp", scatter_dimension=0, tiled=True),
        lax.psum_scatter(key_gain_grad, "dp", scatter_dimension=0, tiled=True),
        lax.psum_scatter(output_weight_grad, "dp", scatter_dimension=1, tiled=True),
        lax.psum_scatter(second_gain_grad, "dp", scatter_dimension=0, tiled=True),
        lax.psum_scatter(gate_weight_grad, "dp", scatter_dimension=0, tiled=True),
        lax.psum_scatter(upward_weight_grad, "dp", scatter_dimension=0, tiled=True),
        lax.psum_scatter(down_grad, "dp", scatter_dimension=1, tiled=True),
    )
    return (
        layer_output,
        tokens_gradient,
        summed[0],
        summed[1],
        summed[2],
        summed[3],
        summed[4],
        summed[5],
        summed[6],
        summed[7],
        summed[8],
        summed[9],
        summed[10],
    )


def shards(
    dp,
    tokens,
    attention_gain,
    query_weight,
    key_weight,
    value_weight,
    query_gain,
    key_gain,
    output_weight,
    feedforward_gain,
    gate_weight,
    up_weight,
    down_weight,
    segment_numbers,
    positions,
    cotangent,
):
    count, depth = tokens.shape
    width = depth // dp
    high = dp // 2
    core = lax.axis_index("tensor") % 2
    upstream_first = lax.ppermute(
        lax.dynamic_slice_in_dim(cotangent, core * (count // 2), 3 * count // 16, 0).astype(jnp.float32),
        "dp",
        [(i, i ^ 2) for i in range(dp)],
    )

    cosine, sine = rotary_tables(positions)
    sine = jnp.concatenate([-sine[:, : HD // 2], sine[:, HD // 2 :]], axis=1)
    tables = (cosine, sine, segment_numbers[:, None], segment_numbers[None])
    normed_low, query_raw, key_raw, queries, keys, values, mixed_low, totals = attention(
        tokens,
        attention_gain,
        (query_weight, key_weight, value_weight),
        query_gain,
        key_gain,
        *tables,
    )
    (
        hidden,
        second_part,
        low_own,
        product_own,
        gate_own,
        upward_own,
        low_pair,
        product_pair,
        gate_pair,
        upward_pair,
        upstream_pair,
    ) = front(
        mixed_low,
        output_weight,
        tokens,
        cotangent,
        upstream_first,
        feedforward_gain,
        gate_weight,
        up_weight,
        down_weight,
    )[:11]
    hidden_grad, hidden_low, out_part, down_weight_grad, gate_ready, gate_given, gate_kept = middle(
        second_part,
        hidden,
        cotangent,
        upstream_pair,
        product_own,
        product_pair,
        gate_own,
        gate_pair,
        low_own,
        low_pair,
        feedforward_gain,
        down_weight,
    )
    gate_middle, gate_inward = (
        lax.ppermute(gate_ready, "dp", [(2 * a + k, 2 * b + k) for a, b in pairs for k in (0, 1)])
        for pairs in (((1, 2), (2, 1)), ((0, 1), (3, 2)))
    )
    gate_moved = lax.ppermute(gate_given, "dp", [(i, i ^ 1) for i in range(dp)])
    raw_grad, query_gain_part, key_gain_part = attention_back(
        hidden_low,
        output_weight,
        queries,
        keys,
        values,
        totals,
        query_raw,
        key_raw,
        query_gain,
        key_gain,
        *tables,
    )

    lines = [
        jnp.pad(value.reshape(dp, -1), ((0, 0), (0, raw_grad.shape[1] - value.size // dp)))
        for value in (jnp.sum(query_gain_part, axis=0), jnp.sum(key_gain_part, axis=0))
    ]
    gain_lines = jnp.pad(jnp.stack(lines, axis=1), ((0, 0), (0, 6), (0, 0)))

    (
        layer_output,
        tokens_gradient,
        gate_weight_grad,
        up_weight_grad,
        raw_whole,
        output_weight_grad,
        gains,
    ) = (
        rear(
            [line_order(high, p) for p in range(high)],
            [gate_middle, gate_inward, gate_kept + gate_moved]
            + [low_own, low_pair, upward_own, upward_pair]
            + [normed_low, raw_grad, hidden_low, mixed_low],
            gain_lines,
            [out_part, hidden, hidden_grad, tokens],
            [query_weight, key_weight, value_weight, gate_weight, up_weight],
            attention_gain,
            feedforward_gain,
        )[:7]
    )
    (
        layer_output,
        tokens_gradient,
        gate_weight_grad,
        up_weight_grad,
        output_weight_grad,
        down_weight_grad,
        query_weight_grad,
        key_weight_grad,
        value_weight_grad,
        attention_gain_grad,
        feedforward_gain_grad,
        query_gain_grad,
        key_gain_grad,
    ) = finish(
        (query_weight.shape[1], key_weight.shape[1], value_weight.shape[1]),
        HD // dp,
        [
            layer_output,
            tokens_gradient,
            gate_weight_grad,
            up_weight_grad,
            output_weight_grad,
            down_weight_grad,
        ],
        raw_whole,
        gains,
    )
    return (
        layer_output,
        tokens_gradient,
        attention_gain_grad[0],
        query_weight_grad,
        key_weight_grad,
        value_weight_grad,
        query_gain_grad[0],
        key_gain_grad[0],
        output_weight_grad,
        feedforward_gain_grad[0],
        gate_weight_grad,
        up_weight_grad,
        down_weight_grad,
    )


def solution(mesh):
    dp, tensor = mesh.shape["dp"], mesh.shape["tensor"]

    def program(*args):
        if dp == 8 and tensor == 4 and args[0].shape[0] == SEQ_LEN:
            return shards(dp, *args)
        return plain_shards(*args)

    return jax.shard_map(
        program,
        mesh=mesh,
        in_specs=(
            P("dp", None),
            P(),
            P(None, "tensor"),
            P(None, "tensor"),
            P(None, "tensor"),
            P(),
            P(),
            P("tensor", None),
            P(),
            P(None, "tensor"),
            P(None, "tensor"),
            P("tensor", None),
            P("dp"),
            P("dp"),
            P("dp", None),
        ),
        out_specs=(
            P("dp", None),
            P("dp", None),
            P("dp"),
            P("dp", "tensor"),
            P("dp", "tensor"),
            P("dp", "tensor"),
            P("dp"),
            P("dp"),
            P("tensor", "dp"),
            P("dp"),
            P("dp", "tensor"),
            P("dp", "tensor"),
            P("tensor", "dp"),
        ),
        check_vma=False,
    )
```

```python
import functools

import jax
import jax.numpy as jnp
from jax import lax
from jax.experimental import pallas as pl
from jax.experimental.pallas import tpu as pltpu
from jax.sharding import PartitionSpec as P

HD = 128
SEQ_LEN = 1024


epsilon = 1e-06
rope_base = 1000000.0
masked = -1e30


def rms_inverse(value):
    return lax.rsqrt(jnp.mean(value * value, axis=-1, keepdims=True) + epsilon)


def norm_back(upstream, value, inverse, gain):
    scaled = upstream * gain
    return inverse * scaled - value * inverse**3 * jnp.mean(scaled * value, axis=-1, keepdims=True)


def rotary_tables(positions):
    exponent = jnp.arange(0, HD, 2, dtype=jnp.float32) / HD
    frequency = rope_base ** (-exponent)
    phase = positions.astype(jnp.float32)[:, None] * frequency[None, :]
    phase = jnp.concatenate([phase, phase], axis=-1)
    return (jnp.cos(phase), jnp.sin(phase))


def rotate(value, cosine, sine):
    half = value.shape[-1] // 2
    turned = jnp.concatenate([-value[..., half:], value[..., :half]], axis=-1)
    return value * cosine + turned * sine


def rotate_back(upstream, cosine, sine):
    half = upstream.shape[-1] // 2
    moved = upstream * sine
    return upstream * cosine + jnp.concatenate([moved[..., half:], -moved[..., :half]], axis=-1)


def block_scores(query_rows, keys, row_segments, segments, begin):
    scores = jnp.einsum(
        "rkgd,tkd->kgrt", query_rows, keys, preferred_element_type=jnp.float32
    ) * HD ** (-0.5)
    rows = begin + lax.iota(jnp.int32, query_rows.shape[0])
    columns = lax.iota(jnp.int32, keys.shape[0])
    allowed = (row_segments[:, None] == segments[None, :]) & (rows[:, None] >= columns[None, :])
    return jnp.where(allowed[None, None], scores, masked)


def attend(item):
    queries, keys, values, segments = item
    length = queries.shape[0]
    width = min(512, length)
    outputs = []
    totals = []
    for begin in range(0, length, width):
        scores = block_scores(
            queries[begin : begin + width], keys, segments[begin : begin + width], segments, begin
        )
        peak = jnp.max(scores, axis=-1, keepdims=True)
        expons = jnp.exp(scores - peak)
        total = jnp.sum(expons, axis=-1, keepdims=True)
        chance_low = (expons / total).astype(jnp.bfloat16)
        outputs.append(
            jnp.einsum("kgrt,tkd->rkgd", chance_low, values, preferred_element_type=jnp.float32)
        )
        totals.append(peak + jnp.log(total))
    return (jnp.concatenate(outputs, axis=0), jnp.concatenate(totals, axis=2))


def attend_back(item):
    queries, keys, values, segments, totals, upstream = item
    length = queries.shape[0]
    width = min(512, length)
    query_parts = []
    key_grad = jnp.zeros(keys.shape, jnp.float32)
    value_grad = jnp.zeros(values.shape, jnp.float32)
    for begin in range(0, length, width):
        rows = queries[begin : begin + width]
        scores = block_scores(rows, keys, segments[begin : begin + width], segments, begin)
        chance = jnp.exp(scores - totals[:, :, begin : begin + width])
        chance_low = chance.astype(jnp.bfloat16)
        incoming = upstream[begin : begin + width]
        value_grad = value_grad + jnp.einsum(
            "kgrt,rkgd->tkd", chance_low, incoming, preferred_element_type=jnp.float32
        )
        along = jnp.einsum("rkgd,tkd->kgrt", incoming, values, preferred_element_type=jnp.float32)
        center = jnp.sum(along * chance, axis=-1, keepdims=True)
        score_grad = (chance * (along - center)).astype(jnp.bfloat16)
        query_parts.append(
            jnp.einsum("kgrt,tkd->rkgd", score_grad, keys, preferred_element_type=jnp.float32)
            * HD ** (-0.5)
        )
        key_grad = key_grad + jnp.einsum(
            "kgrt,rkgd->tkd", score_grad, rows, preferred_element_type=jnp.float32
        ) * HD ** (-0.5)
    return (jnp.concatenate(query_parts, axis=0), key_grad, value_grad)


def dot(left, right):
    return jnp.dot(left, right, preferred_element_type=jnp.float32)


def dot_back(left, right):
    return jnp.einsum("tc,dc->td", left, right, preferred_element_type=jnp.float32)


def dot_tokens(left, right):
    return jnp.einsum("tm,tn->mn", left, right, preferred_element_type=jnp.float32)


def line_order(high, place):
    steps = {}
    for block in range(high):
        if block > place:
            steps[block] = high - block + place
        elif block < place:
            steps[block] = high - place + block
    return sorted(steps, key=lambda block: (steps[block], block)) + [place]


MESH = pl.DeviceIdType.MESH


def neighbours():
    dp, tensor = lax.axis_index("dp"), lax.axis_index("tensor")
    core = lax.rem(tensor, 2)
    sibling = {"tensor": tensor + 1 - 2 * core}
    facing = {"tensor": lax.rem(tensor + 2, 4)}
    place = dp // 2
    pair = {"dp": dp + 2 * (1 - 2 * lax.rem(place, 2))}
    return core, sibling, facing, pair


def greet(devices):
    barrier = pltpu.get_barrier_semaphore()
    for device in devices:
        pl.semaphore_signal(barrier, inc=1, device_id=device, device_id_type=MESH)
    pl.semaphore_wait(barrier, len(devices))


def loop_rows(count, step, body):
    def run(index, carry):
        body(pl.ds(pl.multiple_of(index * step, step), step))
        return carry

    lax.fori_loop(0, count // step, run, 0)


def sequence_rows(size, core, which, k):
    side = core if which == 0 else 1 - core
    return pl.multiple_of(side * 4 * size + k * size, size)


def remote(source, target, sems, k, device):
    return pltpu.make_async_remote_copy(
        src_ref=source, dst_ref=target, send_sem=sems.at[0, k], recv_sem=sems.at[1, k],
        device_id=device, device_id_type=MESH,
    )


def front_kernel(
    size, first,
    mixed_hbm, output_weight_hbm, tokens_hbm, upstream_hbm, upstream_first,
    gain, gate_hbm, up_hbm, down_hbm,
    hidden_out, second_out, low_own, product_own, gate_own, upward_own,
    low_pair, product_pair, gate_pair, upward_pair, upstream_pair,
    c_landed, n_recv, n_side, u_recv, u_side,
    mixed, output_weight, gate_weight, up_weight, down_weight,
    x_send, x_recv, back_recv, tok, hid, z_send, low, rows16, tiles, stage, terms,
    load_sems, c_sems, x_sems, back_sems, n_sems, n_side_sems, u_sems, u_side_sems,
    tok_sems, hid_sems, low_sems, wave_sems, tile_sems, stage_sems, term_sems,
):
    core, sibling, facing, pair = neighbours()
    depth = gain.shape[1]
    half = 4 * size
    units = gate_weight.shape[1]
    begin = functools.partial(sequence_rows, size, core)
    across_last = (((1,), (1,)), ((), ()))
    rest = half - first
    loads = [
        pltpu.make_async_copy(source, target, load_sems.at[index])
        for index, (source, target) in enumerate(
            [
                (
                    upstream_hbm.at[pl.ds(pl.multiple_of(core * half + first, 16), rest)],
                    rows16.at[pl.ds(0, rest)],
                ),
                (mixed_hbm, mixed),
                (output_weight_hbm, output_weight),
                (gate_hbm, gate_weight),
                (up_hbm, up_weight),
                (down_hbm, down_weight),
            ]
        )
    ]
    for load in loads:
        load.start()
    greet([sibling, facing, pair])

    c_copies = [
        remote(terms.at[pl.ds(k * size, size)], c_landed.at[k], c_sems, k, sibling) for k in range(4)
    ]
    x_copies = [remote(x_send.at[k], x_recv.at[k], x_sems, k, facing) for k in range(4)]
    back_copies = [remote(x_send.at[k], back_recv.at[k], back_sems, k, sibling) for k in range(4)]
    n_copies = [remote(z_send.at[k % 2], n_recv.at[k], n_sems, k, pair) for k in range(4)]
    n_sides = [remote(n_recv.at[k], n_side.at[k], n_side_sems, k, sibling) for k in range(4)]
    u_rows = [(0, rest - 2 * size), (rest - 2 * size, size), (rest - size, size)]
    u_buffers = [hid.at[0, pl.ds(0, u_rows[0][1])], z_send.at[0], z_send.at[1]]
    u_copies = [
        remote(u_buffers[j], u_recv.at[pl.ds(start, number)], u_sems, j, pair)
        for j, (start, number) in enumerate(u_rows)
    ]
    u_sides = [remote(upstream_first, u_side.at[pl.ds(0, first)], u_side_sems, 0, sibling)] + [
        remote(
            u_recv.at[pl.ds(start, number)],
            u_side.at[pl.ds(first + start, number)],
            u_side_sems,
            1 + j,
            sibling,
        )
        for j, (start, number) in enumerate(u_rows)
    ]

    def stage_load(source, slot, number):
        return pltpu.make_async_copy(source, stage.at[slot, pl.ds(0, number)], stage_sems.at[slot])

    def upstream_send(j):
        start, number = u_rows[j]

        def run(row):
            u_buffers[j][row, :] = rows16[
                pl.ds(pl.multiple_of(start + row.start, 16), row.size), :
            ].astype(jnp.float32)

        loop_rows(number, 16, run)
        u_copies[j].start()

    def upstream_forward(j):
        u_copies[j].wait_recv()
        u_sides[1 + j].start()

    def attention_terms(k):
        rows = jnp.concatenate(
            [mixed[pl.ds(begin(which, k), size), :] for which in range(2)], axis=0
        )

        def run(column):
            both = jnp.dot(rows, output_weight[:, column], preferred_element_type=jnp.float32)
            x_send[k, :, column] = both[:size]
            terms[pl.ds(k * size, size), column] = both[size:]

        loop_rows(depth, 1024, run)
        c_copies[k].start()

    def attention_cores(k):
        c_copies[k].wait_recv()
        stage_load(c_landed.at[k], k % 2, size).start()
        stage_load(c_landed.at[k], k % 2, size).wait()

        def run(row):
            x_send[k, row, :] = x_send[k, row, :] + stage[k % 2, row, :]

        loop_rows(size, 16, run)
        x_copies[k].start()

    def attention_chips(k):
        x_copies[k].wait()

        def run(row):
            x_send[k, row, :] = x_send[k, row, :] + x_recv[k, row, :]

        loop_rows(size, 16, run)
        back_copies[k].start()

    def token_loads(k):
        return [
            pltpu.make_async_copy(
                tokens_hbm.at[pl.ds(begin(which, k), size)], tok.at[which], tok_sems.at[which]
            )
            for which in range(2)
        ]

    def hidden_stores(k):
        return [
            pltpu.make_async_copy(
                hid.at[which], hidden_out.at[pl.ds(begin(which, k), size)], hid_sems.at[which]
            )
            for which in range(2)
        ]

    def low_rows(which, k, row):
        side = core if which == 0 else 1 - core
        return pl.ds(pl.multiple_of((side + k % 2 * 2) * size + row.start, 16), row.size)

    def normed(k):
        for load in token_loads(k):
            load.wait()
        if k > 0:
            for store in hidden_stores(k - 1):
                store.wait()
        if k < 2:
            u_copies[1 + k].wait_send()
        else:
            n_copies[k - 2].wait_send()

        def run(which, source, row):
            value = tok[which, row, :].astype(jnp.float32) + source[k, row, :]
            hid[which, row, :] = value
            unit = value * lax.rsqrt(jnp.mean(value * value, axis=-1, keepdims=True) + epsilon)
            if which == 0:
                z_send[k % 2, row, :] = unit
            low[0, low_rows(which, k, row), :] = (unit * gain[...]).astype(jnp.bfloat16)

        loop_rows(size, 16, functools.partial(run, 0, x_send))
        n_copies[k].start()
        back_copies[k].wait_recv()
        loop_rows(size, 16, functools.partial(run, 1, back_recv))
        for store in hidden_stores(k):
            store.start()
        if k < 3:
            for load in token_loads(k + 1):
                load.start()

    def pipeline(pieces):
        def bring(index):
            before, source, number, _ = pieces[index]
            if before is not None:
                before.wait_recv()
            stage_load(source, index % 2, number).start()

        bring(0)
        for index, (_, source, number, consume) in enumerate(pieces):
            if index + 1 < len(pieces):
                bring(index + 1)
            stage_load(source, index % 2, number).wait()
            loop_rows(number, 16, functools.partial(consume, index % 2))

    def pair_forward(k):
        n_copies[k].wait_recv()
        n_sides[k].start()

    def pair_rows(chunks):
        def consume(k, which, slot, row):
            low[1, low_rows(which, k, row), :] = (stage[slot, row, :] * gain[...]).astype(
                jnp.bfloat16
            )

        pipeline(
            [
                (
                    n_sides[k] if which else None,
                    (n_side if which else n_recv).at[k],
                    size,
                    functools.partial(consume, k, which),
                )
                for which in range(2)
                for k in chunks
            ]
        )

    def wave_copies(local, distant, sems, wave, inwards=False):
        copies = []
        for part in range(4):
            here = local.at[pl.ds(part * size, size)]
            there = distant.at[pl.ds(part % 2 * half + (2 * wave + part // 2) * size, size)]
            source, target = (there, here) if inwards else (here, there)
            copies.append(pltpu.make_async_copy(source, target, sems.at[part]))
        return copies

    def pair_stores(wave):
        return wave_copies(rows16, upstream_pair, wave_sems.at[1], wave)

    def upstream_wave(wave):
        def consume(which, start, slot, row):
            side = core if which == 0 else 1 - core
            chunk, within = start // size, start % size
            place = pl.multiple_of((2 * chunk + side) * size + within + row.start, 16)
            rows16[pl.ds(place, row.size), :] = stage[slot, row, :].astype(jnp.bfloat16)

        if wave == 0:
            own = [
                (upstream_first.at[pl.ds(0, size)], size, 0),
                (upstream_first.at[pl.ds(size, first - size)], first - size, size),
                (u_recv.at[pl.ds(0, u_rows[0][1])], u_rows[0][1], first),
            ]
            waits = [u_sides[0], u_sides[1]]
        else:
            own = [(u_recv.at[pl.ds(u_rows[j][0], size)], size, (j - 1) * size) for j in (1, 2)]
            waits = [u_sides[2], u_sides[3]]
        pieces = [
            (None, source, number, functools.partial(consume, 0, start))
            for source, number, start in own
        ]
        if wave == 0:
            waits[0].wait_recv()
            waits[1].wait_recv()
            waits = [None, None]
        pieces += [
            (
                waits[j],
                u_side.at[pl.ds((2 * wave + j) * size, size)],
                size,
                functools.partial(consume, 1, j * size),
            )
            for j in range(2)
        ]
        pipeline(pieces)
        for copy in pair_stores(wave):
            copy.start()

    def term_stores(wave):
        return wave_copies(terms, second_out, term_sems, wave)

    def low_stores(wave, index):
        return wave_copies(low.at[index], low_pair if index else low_own, low_sems.at[index], wave)

    def tile_stores(wave, index):
        outs = (
            (product_pair, gate_pair, upward_pair) if index else (product_own, gate_own, upward_own)
        )
        return [
            copy
            for which in range(3)
            for copy in wave_copies(tiles.at[which], outs[which], tile_sems.at[which], wave)
        ]

    feeds = [(0, 0), (1, 0), (0, 1), (1, 1)]

    def fetches(wave):
        return wave_copies(rows16, upstream_hbm, wave_sems.at[0], wave, True)

    def feed(wave, index, part=None):
        number = feeds.index((wave, index))
        rows = slice(None) if part is None else pl.ds(part * 2 * size, 2 * size)
        if not part:
            if number > 0:
                for copy in tile_stores(*feeds[number - 1]):
                    copy.wait()
        if index == 0 and not part:
            for copy in fetches(wave):
                copy.wait()

        def run(column):
            gate = jnp.dot(
                low[index, rows], gate_weight[:, column], preferred_element_type=jnp.float32
            )
            upward = jnp.dot(
                low[index, rows], up_weight[:, column], preferred_element_type=jnp.float32
            )
            grad = lax.dot_general(
                rows16[rows],
                down_weight[column, :],
                across_last,
                preferred_element_type=jnp.float32,
            )
            sigmoid_gate = jax.nn.sigmoid(gate)
            activated = gate * sigmoid_gate
            tiles[0, rows, column] = (activated * upward).astype(jnp.bfloat16)
            tiles[1, rows, column] = (
                grad * upward * sigmoid_gate * (1.0 + gate * (1.0 - sigmoid_gate))
            ).astype(jnp.bfloat16)
            tiles[2, rows, column] = (grad * activated).astype(jnp.bfloat16)

        loop_rows(units, 512, run)
        copies = tile_stores(wave, index) + low_stores(wave, index)
        for number, copy in enumerate(copies):
            if part is None or number % 4 // 2 == part:
                copy.start()
        if index == 0:
            if wave > 0 and not part:
                for copy in term_stores(wave - 1):
                    copy.wait()

            def second(column):
                terms[rows, column] = lax.dot_general(
                    tiles[1, rows],
                    gate_weight[column, :],
                    across_last,
                    preferred_element_type=jnp.float32,
                ) + lax.dot_general(
                    tiles[2, rows],
                    up_weight[column, :],
                    across_last,
                    preferred_element_type=jnp.float32,
                )

            loop_rows(depth, 1024 if part is not None else 512, second)
            for number, copy in enumerate(term_stores(wave)):
                if part is None or number // 2 == part:
                    copy.start()

    for load in token_loads(0):
        load.start()
    loads[0].wait()
    for j in range(3):
        upstream_send(j)
    u_sides[0].start()
    loads[1].wait()
    loads[2].wait()
    attention_terms(0)
    attention_terms(1)
    attention_cores(0)
    attention_terms(2)
    attention_cores(1)
    attention_terms(3)
    attention_cores(2)
    attention_cores(3)
    for copy in fetches(0):
        copy.start()
    upstream_forward(0)
    attention_chips(0)
    u_copies[0].wait_send()
    upstream_forward(1)
    normed(0)
    for load in loads[3:]:
        load.wait()
    for k in range(4):
        c_copies[k].wait_send()
    feed(0, 0, 0)
    attention_chips(1)
    normed(1)
    upstream_forward(2)
    feed(0, 0, 1)
    attention_chips(2)
    for copy in low_stores(0, 0):
        copy.wait()
    normed(2)
    pair_forward(0)
    for copy in fetches(1):
        copy.start()
    feed(1, 0, 0)
    attention_chips(3)
    normed(3)
    feed(1, 0, 1)
    pair_forward(1)
    upstream_wave(0)
    pair_rows((0, 1))
    feed(0, 1)
    for copy in pair_stores(0):
        copy.wait()
    pair_forward(2)
    upstream_wave(1)
    for copy in low_stores(0, 1):
        copy.wait()
    pair_rows((2,))
    feed(1, 1, 0)
    pair_forward(3)
    pair_rows((3,))
    feed(1, 1, 1)

    for k in range(4):
        back_copies[k].wait_send()
        n_sides[k].wait_send()
        u_sides[k].wait_send()
        if k >= 2:
            n_copies[k].wait_send()
    ends = hidden_stores(3) + term_stores(1) + low_stores(1, 0) + low_stores(1, 1)
    for copy in ends + pair_stores(1) + tile_stores(1, 1):
        copy.wait()


def front(mixed, output_weight, tokens, upstream, upstream_first, gain, gate_weight, up_weight, down_weight):
    rows, depth = tokens.shape
    inner, units = mixed.shape[1], gate_weight.shape[1]
    first = upstream_first.shape[0]
    size = rows // 8
    f32, b16 = jnp.float32, jnp.bfloat16
    any_space = pl.BlockSpec(memory_space=pl.ANY)
    shape = jax.ShapeDtypeStruct
    outs = [shape((rows, depth), f32)] * 2
    outs += ([shape((rows, depth), b16)] + [shape((rows, units), b16)] * 3) * 2
    outs += [shape((rows, depth), b16)] + [shape((4, size, depth), f32)] * 3
    outs += [shape((4 * size - first, depth), f32), shape((4 * size, depth), f32)]
    dma = pltpu.SemaphoreType.DMA
    vmem = pltpu.VMEM
    return pl.pallas_call(
        functools.partial(front_kernel, size, first),
        out_shape=outs,
        in_specs=[any_space] * 5 + [pl.BlockSpec(memory_space=pltpu.VMEM)] + [any_space] * 3,
        out_specs=[any_space] * len(outs),
        scratch_shapes=[
            vmem((rows, inner), b16),
            vmem((inner, depth), b16),
            vmem((depth, units), b16),
            vmem((depth, units), b16),
            vmem((units, depth), b16),
            vmem((4, size, depth), f32),
            vmem((4, size, depth), f32),
            vmem((4, size, depth), f32),
            vmem((2, size, depth), b16),
            vmem((2, size, depth), f32),
            vmem((2, size, depth), f32),
            vmem((2, 4 * size, depth), b16),
            vmem((4 * size, depth), b16),
            vmem((3, 4 * size, units), b16),
            vmem((2, size, depth), f32),
            vmem((4 * size, depth), f32),
            dma((6,)),
            *[dma((2, 4))] * 5,
            dma((2, 3)),
            dma((2, 4)),
            dma((2,)),
            dma((2,)),
            dma((2, 4)),
            dma((2, 4)),
            dma((3, 4)),
            dma((2,)),
            dma((4,)),
        ],
        compiler_params=pltpu.CompilerParams(
            collective_id=1, has_side_effects=True, vmem_limit_bytes=63 * 1024 * 1024
        ),
        cost_estimate=pl.CostEstimate(
            flops=12 * rows * depth * units, bytes_accessed=6 * depth * units, transcendentals=0
        ),
    )(mixed, output_weight, tokens, upstream, upstream_first, gain[None], gate_weight, up_weight, down_weight)


def grid_neighbours():
    dp = lax.axis_index("dp")
    place, lane = dp // 2, lax.rem(dp, 2)
    towards = 1 - 2 * (place // 2)
    across = {"dp": dp + 1 - 2 * lane}
    inward, outward = {"dp": dp + 2 * towards}, {"dp": dp - 2 * towards}
    team = place // 2
    side = lax.rem(place, 2)
    inner = lax.rem(team + side, 2)
    return place, lane, team, side, inner, across, inward, outward


def greet_grid(always, inner, outward):
    barrier = pltpu.get_barrier_semaphore()
    for device in always:
        pl.semaphore_signal(barrier, inc=1, device_id=device, device_id_type=MESH)

    @pl.when(inner == 1)
    def _():
        pl.semaphore_signal(barrier, inc=1, device_id=outward, device_id_type=MESH)

    pl.semaphore_wait(barrier, len(always) + inner)


def middle_kernel(
    size,
    second_hbm, hidden_hbm, upstream_hbm, upstream_pair, product_own, product_pair,
    gate_own, gate_pair, low_own, low_pair, gain, down_hbm,
    grad_out, grad_low_out, out_part, weight_out, gate_ready, gate_given, gate_own_block,
    products, down_weight, columns, c_recv, x_send, x_recv, back_recv,
    y_send, y_recv, kept, in_recv, mid_recv, out_recv,
    hid, tok, grad, grad_low, out_stage, gate_send, gate_kept, gate_stage,
    load_sems, gate_load_sems, gate_sems, c_sems, x_sems, back_sems, y_sems, z_sems, column_sems,
    x_load_sems, hid_sems, tok_sems, grad_sems, low_sems, out_sems, weight_sems,
):
    core, sibling, facing, _ = neighbours()
    place, lane, team, side, inner, across, inward, outward = grid_neighbours()
    depth = gain.shape[1]
    units = down_weight.shape[0]
    width = columns.shape[-1]
    begin = functools.partial(sequence_rows, size, core)
    rows_in = 8 * size
    down_first = (((0,), (0,)), ((), ()))
    loads = [
        pltpu.make_async_copy(source, target, load_sems.at[index])
        for index, (source, target) in enumerate(
            [
                (product_own, products.at[pl.ds(0, rows_in)]),
                (product_pair, products.at[pl.ds(rows_in, rows_in)]),
                (down_hbm, down_weight),
            ]
        )
    ]
    gate_loads = [
        pltpu.make_async_copy(
            source, products.at[pl.ds(index * rows_in, rows_in)], gate_load_sems.at[index]
        )
        for index, source in enumerate((gate_own, gate_pair))
    ]
    turns = [(0, 1), (1, 1), (0, 0), (1, 0)]
    turns += [(0, 1), (1, 1), (1, 0), (0, 0)]

    def column_loads(index):
        turn, other = turns[index]
        spot = lax.rem(1 - team + turn, 2)
        which = 1 - lane if other else lane
        start = pl.multiple_of((side * 4 + 2 * spot + which) * width, width)
        return [
            pltpu.make_async_copy(
                source.at[:, pl.ds(start, width)],
                columns.at[index % 2, pl.ds(part * rows_in, rows_in)],
                column_sems.at[index % 2, part],
            )
            for part, source in enumerate(
                (upstream_hbm, upstream_pair) if index < 4 else (low_own, low_pair)
            )
        ]

    x_loads = [
        pltpu.make_async_copy(
            second_hbm.at[pl.ds(begin(0, k), size)], x_send.at[k], x_load_sems.at[k]
        )
        for k in range(4)
    ]
    for copy in column_loads(0) + x_loads[:1] + loads[:2] + column_loads(1) + x_loads[1:] + loads[2:]:
        copy.start()
    greet_grid([sibling, facing, across, inward], inner, outward)
    c_copies = [
        remote(second_hbm.at[pl.ds(begin(1, k), size)], c_recv.at[k], c_sems, k, sibling)
        for k in range(4)
    ]
    x_copies = [remote(x_send.at[k], x_recv.at[k], x_sems, k, facing) for k in range(4)]
    back_copies = [remote(x_send.at[k], back_recv.at[k], back_sems, k, sibling) for k in range(4)]
    y_copies = [remote(y_send.at[k], y_recv.at[k], y_sems, k, across) for k in range(2)]
    in_copy = remote(kept.at[0], in_recv, z_sems, 0, inward)
    mid_copies = [remote(kept.at[k], mid_recv.at[k], z_sems, 1 + k, inward) for k in range(2)]
    out_copy = remote(mid_recv.at[0], out_recv, z_sems, 3, outward)
    for copy in c_copies:
        copy.start()

    def cores(k):
        x_loads[k].wait()
        c_copies[k].wait_recv()

        def run(row):
            x_send[k, row, :] = x_send[k, row, :] + c_recv[k, row, :]

        loop_rows(size, 16, run)
        x_copies[k].start()

    def chips(k):
        x_copies[k].wait()

        def run(row):
            x_send[k, row, :] = x_send[k, row, :] + x_recv[k, row, :]

        loop_rows(size, 16, run)
        back_copies[k].start()

    def block(index, target):
        for copy in column_loads(index):
            copy.wait()

        target[...] = lax.dot_general(
            products[...], columns[index % 2], down_first, preferred_element_type=jnp.float32
        )
        for copy in column_loads(index + 2):
            copy.start()

    gate_copy = remote(gate_send, gate_kept, gate_sems, 0, across)

    def gate_block(index, target):
        for copy in column_loads(index):
            copy.wait()
        target[...] = lax.dot_general(
            columns[index % 2], products[...], down_first, preferred_element_type=jnp.float32
        )
        if index + 2 < len(turns):
            for copy in column_loads(index + 2):
                copy.start()

    def gate_store(source, target, index):
        return pltpu.make_async_copy(source, target, gate_load_sems.at[2 + index])

    def chunk_loads(k):
        return [
            pltpu.make_async_copy(
                source.at[pl.ds(begin(which, k), size)], target.at[which], sems.at[which]
            )
            for which in range(2)
            for source, target, sems in ((hidden_hbm, hid, hid_sems), (upstream_hbm, tok, tok_sems))
        ]

    def grad_stores(k):
        return [
            pltpu.make_async_copy(
                source.at[which], target.at[pl.ds(begin(which, k), size)], sems.at[which]
            )
            for which in range(2)
            for source, target, sems in (
                (grad, grad_out, grad_sems),
                (grad_low, grad_low_out, low_sems),
            )
        ]

    def finish(k):
        for copy in chunk_loads(k):
            copy.wait()
        if k > 0:
            for copy in grad_stores(k - 1):
                copy.wait()
        back_copies[k].wait_recv()

        def run(which, source, row):
            value = hid[which, row, :]
            inverse = lax.rsqrt(jnp.mean(value * value, axis=-1, keepdims=True) + epsilon)
            total = tok[which, row, :].astype(jnp.float32) + norm_back(
                source[k, row, :], value, inverse, gain[...]
            )
            grad[which, row, :] = total
            grad_low[which, row, :] = total.astype(jnp.bfloat16)

        for which, source in enumerate((x_send, back_recv)):
            loop_rows(size, 16, functools.partial(run, which, source))
        for copy in grad_stores(k):
            copy.start()
        if k < 3:
            for copy in chunk_loads(k + 1):
                copy.start()

    def out_store(k):
        rows = 2 * size
        return pltpu.make_async_copy(
            out_stage, out_part.at[pl.ds(k * rows, rows)], out_sems.at[0]
        )

    def out_terms(k):
        if k > 0:
            out_store(k - 1).wait()
        rows = pl.ds(k * 2 * size, 2 * size)

        def run(column):
            out_stage[:, column] = jnp.dot(
                products[rows, :], down_weight[:, column], preferred_element_type=jnp.float32
            )

        loop_rows(depth, 1024, run)
        out_store(k).start()

    def take(k):
        y_copies[k].wait_recv()

        def run(row):
            kept[k, row, :] = kept[k, row, :] + y_recv[k, row, :]

        loop_rows(units, 64, run)

    for copy in loads[:2]:
        copy.wait()
    block(0, y_send.at[0])
    y_copies[0].start()
    cores(0)
    for copy in chunk_loads(0):
        copy.start()
    cores(1)
    cores(2)
    cores(3)
    block(1, y_send.at[1])
    y_copies[1].start()
    block(2, kept.at[0])
    loads[2].wait()
    out_terms(0)
    chips(0)
    out_terms(1)
    block(3, kept.at[1])
    finish(0)
    out_terms(2)
    take(0)

    @pl.when(inner == 1)
    def _():
        mid_copies[0].start()

    @pl.when(inner == 0)
    def _():
        in_copy.start()

    out_terms(3)
    for copy in gate_loads:
        copy.start()
    chips(1)
    for copy in gate_loads:
        copy.wait()
    gate_block(4, gate_send)
    gate_copy.start()
    finish(1)
    gate_block(5, gate_stage)
    gate_store(gate_stage, gate_given, 0).start()
    chips(2)
    take(1)

    @pl.when(inner == 1)
    def _():
        mid_copies[1].start()
        mid_copies[0].wait_recv()
        out_copy.start()

    finish(2)
    gate_store(gate_stage, gate_given, 0).wait()
    gate_block(6, gate_stage)
    gate_store(gate_stage, gate_own_block, 1).start()
    gate_store(gate_stage, gate_own_block, 1).wait()
    gate_block(7, gate_stage)
    chips(3)
    finish(3)
    gate_copy.wait()

    def run_gate(row):
        gate_kept[row, :] = gate_kept[row, :] + gate_stage[row, :]

    loop_rows(width, 16, run_gate)
    gate_store(gate_kept, gate_ready, 2).start()

    @pl.when(inner == 1)
    def _():
        in_copy.wait_recv()
        mid_copies[1].wait_recv()
        mid_copies[0].wait_send()
        mid_copies[1].wait_send()
        out_copy.wait_send()

        def run(row):
            kept[0, row, :] = in_recv[row, :] + mid_recv[1, row, :]

        loop_rows(units, 64, run)

    @pl.when(inner == 0)
    def _():
        in_copy.wait_send()
        out_copy.wait_recv()

        def run(row):
            kept[0, row, :] = kept[1, row, :] + out_recv[row, :]

        loop_rows(units, 64, run)

    store = pltpu.make_async_copy(kept.at[0], weight_out, weight_sems.at[0])
    store.start()
    for k in range(4):
        back_copies[k].wait_send()
        c_copies[k].wait_send()
    for k in range(2):
        y_copies[k].wait_send()
    for copy in grad_stores(3):
        copy.wait()
    gate_store(gate_kept, gate_ready, 2).wait()
    out_store(3).wait()
    store.wait()


def middle(
    second, hidden, upstream, upstream_pair, product_own, product_pair,
    gate_own, gate_pair, low_own, low_pair, gain, down_weight,
):
    rows, depth = hidden.shape
    units = down_weight.shape[0]
    size = rows // 8
    width = depth // 8
    f32, b16 = jnp.float32, jnp.bfloat16
    any_space = pl.BlockSpec(memory_space=pl.ANY)
    shape = jax.ShapeDtypeStruct
    dma = pltpu.SemaphoreType.DMA
    vmem = pltpu.VMEM
    return pl.pallas_call(
        functools.partial(middle_kernel, size),
        out_shape=[
            shape((rows, depth), f32),
            shape((rows, depth), b16),
            shape((rows, depth), f32),
            shape((units, width), f32),
        ]
        + [shape((width, units), f32)] * 3,
        in_specs=[any_space] * 10 + [pl.BlockSpec(memory_space=pltpu.VMEM), any_space],
        out_specs=[any_space] * 7,
        scratch_shapes=[
            vmem((2 * rows, units), b16),
            vmem((units, depth), b16),
            vmem((2, 2 * rows, width), b16),
            vmem((4, size, depth), f32),
            vmem((4, size, depth), f32),
            vmem((4, size, depth), f32),
            vmem((4, size, depth), f32),
            vmem((2, units, width), f32),
            vmem((2, units, width), f32),
            vmem((2, units, width), f32),
            vmem((units, width), f32),
            vmem((2, units, width), f32),
            vmem((units, width), f32),
            vmem((2, size, depth), f32),
            vmem((2, size, depth), b16),
            vmem((2, size, depth), f32),
            vmem((2, size, depth), b16),
            vmem((2 * size, depth), f32),
            vmem((width, units), f32),
            vmem((width, units), f32),
            vmem((width, units), f32),
            dma((3,)),
            dma((5,)),
            dma((2, 1)),
            dma((2, 4)),
            dma((2, 4)),
            dma((2, 4)),
            dma((2, 2)),
            dma((2, 4)),
            dma((2, 2)),
            dma((4,)),
            dma((2,)),
            dma((2,)),
            dma((2,)),
            dma((2,)),
            dma((1,)),
            dma((1,)),
        ],
        compiler_params=pltpu.CompilerParams(
            collective_id=2, has_side_effects=True, vmem_limit_bytes=62 * 1024 * 1024
        ),
        cost_estimate=pl.CostEstimate(
            flops=8 * rows * depth * units, bytes_accessed=6 * depth * units, transcendentals=0
        ),
    )(
        second, hidden, upstream, upstream_pair, product_own, product_pair,
        gate_own, gate_pair, low_own, low_pair, gain[None], down_weight,
    )


class TensorSum:
    def __init__(self, size, own, landed, stage, sems, stage_sems, devices):
        self.size, self.own, self.landed, self.stage = size, own, landed, stage
        self.stage_sems = stage_sems
        c_sems, x_sems, back_sems = sems
        self.sibling, facing = devices
        self.c_sems = c_sems
        self.x_copies = [remote(own.at[k], landed[1].at[k], x_sems, k, facing) for k in range(4)]
        self.back_copies = [
            remote(own.at[k], landed[2].at[k], back_sems, k, self.sibling) for k in range(4)
        ]
        self.c_copies = [None] * 4

    def give(self, k, source):
        self.c_copies[k] = remote(source, self.landed[0].at[k], self.c_sems, k, self.sibling)
        self.c_copies[k].start()

    def staged(self, which, k):
        copy = pltpu.make_async_copy(self.landed[which].at[k], self.stage.at[0], self.stage_sems.at[0])
        copy.start()
        copy.wait()

    def add_stage(self, k):
        def run(row):
            self.own[k, row, :] = self.own[k, row, :] + self.stage[0, row, :]

        loop_rows(self.size, 16, run)

    def cores(self, k):
        self.c_copies[k].wait_recv()
        self.staged(0, k)
        self.add_stage(k)
        self.x_copies[k].start()

    def chips(self, k):
        self.x_copies[k].wait()
        self.staged(1, k)
        self.add_stage(k)
        self.back_copies[k].start()

    def other(self, k):
        self.back_copies[k].wait_recv()
        self.staged(2, k)


def rear_kernel(
    size, turns,
    gate_middle, gate_inward, gate_ready, low_own, low_pair, upward_own, upward_pair,
    normed_hbm, raw_hbm, hidden_low_hbm, mixed_hbm, lines,
    out_hbm, hidden_hbm, grad_hbm, tokens_hbm,
    query_hbm, key_hbm, value_hbm, gate_hbm, up_hbm, gain, feed_gain,
    layer_out, tokens_out, gate_out, up_out, raw_out, head_out, gains_out,
    o_c, o_x, o_back, d_c, d_x, d_back, gate_landed, up_landed,
    upwards, raw, mixed, head_weights, feed_rows, gains, gain_rows, gains_in, columns,
    up_send, up_kept, raw_send, raw_kept, head_send, head_kept, raw_line, head_line,
    own, give, stage, wide, narrow, result,
    load_sems, column_sems, y_up_sems, y_raw_sems, y_head_sems, gate_sems, up_sems,
    raw_line_sems, head_line_sems,
    oc_sems, ox_sems, ob_sems, dc_sems, dx_sems, db_sems,
    own_sems, stage_sems, wide_sems, narrow_sems, result_sems, end_sems, gain_sems,
):
    core, sibling, facing, _ = neighbours()
    place, lane, team, side, inner, across, inward, outward = grid_neighbours()
    high = len(turns)
    depth = gain.shape[1]
    width = columns.shape[-1]
    units = upwards.shape[-1]
    begin = functools.partial(sequence_rows, size, core)
    rows_in = 8 * size
    down_first = (((0,), (0,)), ((), ()))
    cuts = (query_hbm.shape[1], key_hbm.shape[1])
    own_rows = pl.ds(pl.multiple_of(lax.axis_index("dp") * width, width), width)
    loads = [
        pltpu.make_async_copy(source, target, load_sems.at[index])
        for index, (source, target) in enumerate(
            [
                (raw_hbm, raw),
                (mixed_hbm, mixed),
                (upward_own, upwards.at[pl.ds(0, rows_in)]),
                (upward_pair, upwards.at[pl.ds(rows_in, rows_in)]),
                (query_hbm, head_weights.at[:, pl.ds(0, cuts[0])]),
                (key_hbm, head_weights.at[:, pl.ds(cuts[0], cuts[1])]),
                (value_hbm, head_weights.at[:, pl.ds(cuts[0] + cuts[1], cuts[1])]),
                (gate_hbm.at[own_rows], feed_rows.at[0]),
                (up_hbm.at[own_rows], feed_rows.at[1]),
            ]
        )
    ]
    blocks = [
        ("head", 0, 1), ("up", 0, 1), ("up", 1, 1), ("head", 1, 1), ("head", 2, 1), ("head", 3, 1),
        ("head", 0, 0), ("up", 0, 0), ("up", 1, 0), ("head", 1, 0), ("head", 2, 0), ("head", 3, 0),
    ]

    def spot_of(kind, turn):
        if kind == "up":
            return side * 2 + lax.rem(1 - team + turn, 2)
        spot = jnp.int32(turns[0][turn])
        for p in range(1, high):
            spot = jnp.where(place == p, jnp.int32(turns[p][turn]), spot)
        return spot

    def column_loads(index):
        kind, turn, other = blocks[index]
        which = 1 - lane if other else lane
        start = pl.multiple_of((2 * spot_of(kind, turn) + which) * width, width)
        sources = (low_own, low_pair) if kind == "up" else (normed_hbm, hidden_low_hbm)
        return [
            pltpu.make_async_copy(
                source.at[:, pl.ds(start, width)],
                columns.at[index % 2, pl.ds(part * rows_in, rows_in)],
                column_sems.at[index % 2, part],
            )
            for part, source in enumerate(sources)
        ]

    own_loads = [
        pltpu.make_async_copy(out_hbm.at[pl.ds(begin(0, k), size)], own.at[k], own_sems.at[k])
        for k in range(4)
    ]
    for copy in column_loads(0) + loads[:2] + column_loads(1) + own_loads + loads[2:]:
        copy.start()
    greet_grid([sibling, facing, across, inward], inner, outward)
    devices = (sibling, facing)
    outs = TensorSum(
        size, own, (o_c, o_x, o_back), stage, (oc_sems, ox_sems, ob_sems), stage_sems, devices
    )
    heads = TensorSum(
        size, own, (d_c, d_x, d_back), stage, (dc_sems, dx_sems, db_sems), stage_sems, devices
    )
    for k in range(4):
        outs.give(k, out_hbm.at[pl.ds(begin(1, k), size)])

    def team_copies(values, landed, sems):
        return (
            remote(values[0], landed.at[0], sems, 0, inward),
            [remote(values[k], landed.at[1 + k], sems, 1 + k, inward) for k in range(2)],
            remote(landed.at[1], landed.at[3], sems, 3, outward),
        )

    gate_copies = (
        None,
        [None, remote(gate_ready, gate_landed.at[0], gate_sems, 0, inward)],
        remote(gate_middle, gate_landed.at[1], gate_sems, 1, outward),
    )
    up_copies = team_copies((up_kept.at[0], up_kept.at[1]), up_landed, up_sems)

    def team_send(copies, turn):
        @pl.when(inner == 1)
        def _():
            copies[1][turn].start()

        if turn == 0:

            @pl.when(inner == 0)
            def _():
                copies[0].start()

    def team_forward(copies):
        @pl.when(inner == 1)
        def _():
            copies[1][0].wait_recv()
            copies[2].start()

    def add_gain(lane_index, row, value, weight):
        total = jnp.sum(value * weight.astype(jnp.float32), axis=-1, keepdims=True)
        lanes = lax.broadcasted_iota(jnp.int32, (total.shape[0], gains.shape[1]), 1)
        gains[row, :] = gains[row, :] + jnp.where(lanes == lane_index, total, 0.0)

    def team_combine(copies, first, second, outward_landed, last, out, sem, which):
        def fetch(source, slot):
            copy = pltpu.make_async_copy(source, up_send.at[slot], end_sems.at[4 + slot])
            copy.start()
            copy.wait()

        @pl.when(inner == 1)
        def _():
            if copies[0] is not None:
                copies[0].wait_recv()
                copies[1][0].wait_send()
            copies[1][1].wait_recv()
            fetch(first, 0)
            fetch(second, 1)
            copies[1][1].wait_send()
            copies[2].wait_send()

        @pl.when(inner == 0)
        def _():
            if copies[0] is not None:
                copies[0].wait_send()
            copies[2].wait_recv()
            fetch(outward_landed, 0)
            fetch(last, 1)

        def run(row):
            total = up_send[0, row, :] + up_send[1, row, :]
            up_send[0, row, :] = total
            add_gain(1, row, total, feed_rows[which, row, :])

        loop_rows(width, 16, run)
        store = pltpu.make_async_copy(up_send.at[0], out, sem)
        store.start()
        store.wait()

    y_up = [remote(up_send.at[k], up_kept.at[k], y_up_sems, k, across) for k in range(2)]
    y_raw = [remote(raw_send.at[k], raw_kept.at[k], y_raw_sems, k, across) for k in range(high)]
    y_head = [
        remote(head_send.at[k], head_kept.at[k], y_head_sems, k, across) for k in range(high)
    ]

    def line_copy(p, turn, towards=None):
        block = turns[p][turn]
        ahead = block > p
        slot = block - 1 if ahead else high - 1 + block
        device = {"dp": lax.axis_index("dp") + (2 if ahead else -2)}
        return slot, [
            remote(kept.at[turn], line.at[slot], sems, slot, device)
            for kept, line, sems in (
                (raw_kept, raw_line, raw_line_sems),
                (head_kept, head_line, head_line_sems),
            )
        ]

    def line_arrived(slot, turn):
        for kept, line, sems in (
            (raw_kept, raw_line, raw_line_sems),
            (head_kept, head_line, head_line_sems),
        ):
            remote(kept.at[turn], line.at[slot], sems, slot, across).wait_recv()

            def run(row):
                kept[turn, row, :] = kept[turn, row, :] + line[slot, row, :]

            loop_rows(kept.shape[1], 8, run)

    def line_step(turn):
        for p in range(high):
            block = turns[p][turn]

            @pl.when(place == p)
            def _():
                slot, copies = line_copy(p, turn)
                if (block > p and p > 0) or (block < p and p < high - 1):
                    line_arrived(slot, turn)
                for copy in copies:
                    copy.start()

    def line_end():
        for p in range(high):

            @pl.when(place == p)
            def _():
                if p > 0:
                    line_arrived(p - 1, high - 1)
                if p < high - 1:
                    line_arrived(high - 1 + p, high - 1)
                for turn in range(high - 1):
                    for copy in line_copy(p, turn)[1]:
                        copy.wait_send()

    def up_block(index, target, added):
        for copy in column_loads(index):
            copy.wait()

        total = lax.dot_general(
            columns[index % 2], upwards[...], down_first, preferred_element_type=jnp.float32
        )
        target[...] = target[...] + total if added else total
        if index + 2 < len(blocks):
            for copy in column_loads(index + 2):
                copy.start()

    def head_block(index, raw_target, head_target, added):
        kind, turn, other = blocks[index]
        which = 1 - lane if other else lane
        for copy in column_loads(index):
            copy.wait()
        slot = index % 2
        total = lax.dot_general(
            columns[slot, :rows_in], raw[...], down_first, preferred_element_type=jnp.float32
        )
        line = lines[2 * spot_of(kind, turn) + which]
        raw_target[:width, :] = raw_target[:width, :] + total if added else total
        raw_target[width:, :] = raw_target[width:, :] + line if added else line
        total = lax.dot_general(
            mixed[...], columns[slot, rows_in:], down_first, preferred_element_type=jnp.float32
        )
        head_target[...] = head_target[...] + total if added else total
        if index + 2 < len(blocks):
            for copy in column_loads(index + 2):
                copy.start()

    def head_send_block(index):
        turn = blocks[index][1]
        head_block(index, raw_send.at[turn], head_send.at[turn], False)
        y_raw[turn].start()
        y_head[turn].start()

    def head_take(index):
        turn = blocks[index][1]
        y_raw[turn].wait_recv()
        y_head[turn].wait_recv()
        head_block(index, raw_kept.at[turn], head_kept.at[turn], True)

    def head_terms(k):
        outs.back_copies[k].wait_send()
        if k >= 2:
            heads.c_copies[k - 2].wait_send()
        rows = jnp.concatenate(
            [raw[pl.ds(begin(which, k), size), :] for which in range(2)], axis=0
        )

        def run(column):
            total = lax.dot_general(
                rows,
                head_weights[column, :],
                (((1,), (1,)), ((), ())),
                preferred_element_type=jnp.float32,
            )
            own[k, :, column] = total[:size]
            give[k % 2, :, column] = total[size:]

        loop_rows(depth, 1024, run)
        heads.give(k, give.at[k % 2])

    def fetches(what, k):
        pairs = ((hidden_hbm, wide, wide_sems),)
        if what == "tokens":
            pairs = ((grad_hbm, wide, wide_sems), (tokens_hbm, narrow, narrow_sems))
        return [
            pltpu.make_async_copy(
                source.at[pl.ds(begin(which, k), size)], target.at[which], sems.at[which]
            )
            for which in range(2)
            for source, target, sems in pairs
        ]

    def stores(what, k):
        return [
            pltpu.make_async_copy(
                result.at[which],
                (layer_out if what == "layer" else tokens_out).at[pl.ds(begin(which, k), size)],
                result_sems.at[which],
            )
            for which in range(2)
        ]

    sequence = [("layer", k) for k in range(4)] + [("tokens", k) for k in range(4)]

    def finish(what, k):
        number = sequence.index((what, k))
        for copy in fetches(what, k):
            copy.wait()
        if number > 0:
            for copy in stores(*sequence[number - 1]):
                copy.wait()
        (outs if what == "layer" else heads).other(k)

        def run(which, row):
            total = stage[0, row, :] if which else own[k, row, :]
            value = wide[which, row, :]
            if what == "layer":
                total = value + total
            else:
                inputs = narrow[which, row, :].astype(jnp.float32)
                inverse = lax.rsqrt(jnp.mean(inputs * inputs, axis=-1, keepdims=True) + epsilon)
                total = value + norm_back(total, inputs, inverse, gain[...])
            result[which, row, :] = total.astype(jnp.bfloat16)

        for which in range(2):
            loop_rows(size, 16, functools.partial(run, which))
        for copy in stores(what, k):
            copy.start()
        if number + 1 < len(sequence):
            for copy in fetches(*sequence[number + 1]):
                copy.start()

    team_send(gate_copies, 1)

    @pl.when(inner == 1)
    def _():
        gate_copies[2].start()

    gains[...] = jnp.zeros_like(gains)
    for copy in fetches("layer", 0):
        copy.start()
    for copy in loads[:2]:
        copy.wait()
    head_send_block(0)
    own_loads[0].wait()
    outs.cores(0)
    for copy in loads[2:]:
        copy.wait()
    up_block(1, up_send.at[0], False)
    y_up[0].start()
    for k in range(1, 4):
        own_loads[k].wait()
        outs.cores(k)
    up_block(2, up_send.at[1], False)
    y_up[1].start()
    for index in range(3, 6):
        head_send_block(index)
    outs.chips(0)
    finish("layer", 0)
    head_take(6)
    line_step(0)
    head_terms(0)
    outs.chips(1)
    finish("layer", 1)
    head_terms(1)
    heads.cores(0)
    y_up[0].wait_recv()
    up_block(7, up_kept.at[0], True)
    team_send(up_copies, 0)
    outs.chips(2)
    finish("layer", 2)
    head_terms(2)
    heads.cores(1)
    outs.chips(3)
    heads.cores(2)
    finish("layer", 3)
    head_terms(3)
    heads.cores(3)
    y_up[1].wait_recv()
    up_block(8, up_kept.at[1], True)
    team_send(up_copies, 1)
    team_forward(up_copies)
    heads.chips(0)
    finish("tokens", 0)
    for k in range(2):
        y_up[k].wait_send()
    team_combine(
        gate_copies, gate_inward, gate_landed.at[0], gate_landed.at[1], gate_ready,
        gate_out, end_sems.at[0], 0,
    )
    head_take(9)
    line_step(1)
    heads.chips(1)
    finish("tokens", 1)
    y_raw[0].wait_send()
    y_head[0].wait_send()
    heads.chips(2)
    finish("tokens", 2)
    head_take(10)
    line_step(2)
    head_block(11, raw_send.at[0], head_send.at[0], False)
    team_combine(
        up_copies, up_landed.at[0], up_landed.at[2], up_landed.at[3], up_kept.at[1],
        up_out, end_sems.at[1], 1,
    )
    heads.chips(3)
    finish("tokens", 3)
    y_raw[high - 1].wait_recv()
    y_head[high - 1].wait_recv()
    for kept, sent, step in ((raw_kept, raw_send, 8), (head_kept, head_send, 16)):

        def run_last(row):
            kept[high - 1, row, :] = kept[high - 1, row, :] + sent[0, row, :]

        loop_rows(kept.shape[1], step, run_last)
    line_end()
    ends = [
        pltpu.make_async_copy(raw_kept.at[high - 1], raw_out, end_sems.at[2]),
        pltpu.make_async_copy(head_kept.at[high - 1], head_out, end_sems.at[3]),
    ]
    for copy in ends:
        copy.start()

    def run_gain(row):
        place_row = pl.ds(pl.multiple_of(own_rows.start + row.start, 16), row.size)
        add_gain(0, row, raw_kept[high - 1, row, :], head_weights[place_row, :])

    loop_rows(width, 16, run_gain)
    own_columns = pl.ds(pl.multiple_of(own_rows.start, 128), width)
    turned = jnp.transpose(gains[...])[:8]
    scale = jnp.concatenate([gain[:, own_columns], feed_gain[:, own_columns]], axis=0)
    gain_rows[:8, :] = turned
    gain_rows[:2, :] = turned[:2] / scale
    gain_rows[8:, :] = raw_kept[high - 1, width:, :width]
    gain_copies = [
        remote(gain_rows, gains_in.at[k], gain_sems, k, device)
        for k, device in enumerate((sibling, facing))
    ]
    for k in range(2):
        gain_copies[k].start()
        gain_copies[k].wait()
        gain_rows[...] = gain_rows[...] + gains_in[k]
    gain_store = pltpu.make_async_copy(gain_rows, gains_out, own_sems.at[0])
    gain_store.start()
    gain_store.wait()
    for k in range(4):
        outs.c_copies[k].wait_send()
        heads.back_copies[k].wait_send()
    for k in range(2, 4):
        heads.c_copies[k].wait_send()
    for k in range(1, high):
        y_raw[k].wait_send()
        y_head[k].wait_send()
    for copy in stores(*sequence[-1]) + ends:
        copy.wait()


def rear(turns, arrays, lines, places, weights, gain, feed_gain):
    rows, depth = places[0].shape
    units = arrays[0].shape[1]
    heads, inner = arrays[8].shape[1], arrays[10].shape[1]
    size = rows // 8
    width = depth // 8
    high = len(turns)
    f32, b16 = jnp.float32, jnp.bfloat16
    any_space = pl.BlockSpec(memory_space=pl.ANY)
    in_vmem = pl.BlockSpec(memory_space=pltpu.VMEM)
    shape = jax.ShapeDtypeStruct
    dma = pltpu.SemaphoreType.DMA
    vmem = pltpu.VMEM
    slots = 2 * (high - 1)
    return pl.pallas_call(
        functools.partial(rear_kernel, size, turns),
        out_shape=[
            shape((rows, depth), b16),
            shape((rows, depth), b16),
            shape((width, units), f32),
            shape((width, units), f32),
            shape((width + 8, heads), f32),
            shape((inner, width), f32),
            shape((16, width), f32),
        ]
        + [shape((4, size, depth), f32)] * 6
        + [shape((2, width, units), f32), shape((4, width, units), f32)],
        in_specs=[any_space] * 11 + [in_vmem] + [any_space] * 9 + [in_vmem] * 2,
        out_specs=[any_space] * 15,
        scratch_shapes=[
            vmem((2 * rows, units), b16),
            vmem((rows, heads), b16),
            vmem((rows, inner), b16),
            vmem((depth, heads), b16),
            vmem((2, width, units), b16),
            vmem((width, HD), f32),
            vmem((16, width), f32),
            vmem((2, 16, width), f32),
            vmem((2, 2 * rows, width), b16),
            vmem((2, width, units), f32),
            vmem((2, width, units), f32),
            vmem((high, width + 8, heads), f32),
            vmem((high, width + 8, heads), f32),
            vmem((high, inner, width), f32),
            vmem((high, inner, width), f32),
            vmem((slots, width + 8, heads), f32),
            vmem((slots, inner, width), f32),
            vmem((4, size, depth), f32),
            vmem((2, size, depth), f32),
            vmem((1, size, depth), f32),
            vmem((2, size, depth), f32),
            vmem((2, size, depth), b16),
            vmem((2, size, depth), b16),
            dma((9,)),
            dma((2, 2)),
            dma((2, 2)),
            dma((2, high)),
            dma((2, high)),
            dma((2, 4)),
            dma((2, 4)),
            dma((2, slots)),
            dma((2, slots)),
            *[dma((2, 4))] * 6,
            dma((4,)),
            dma((1,)),
            dma((2,)),
            dma((2,)),
            dma((2,)),
            dma((6,)),
            dma((2, 2)),
        ],
        compiler_params=pltpu.CompilerParams(
            collective_id=3, has_side_effects=True, vmem_limit_bytes=62 * 1024 * 1024
        ),
        cost_estimate=pl.CostEstimate(
            flops=8 * rows * depth * units, bytes_accessed=6 * depth * units, transcendentals=0
        ),
    )(*arrays, lines, *places, *weights, gain[None], feed_gain[None])


def block_mask(segment_column, segment_row, begin, rows, columns):
    row = begin + lax.broadcasted_iota(jnp.int32, (rows, columns), 0)
    column = lax.broadcasted_iota(jnp.int32, (rows, columns), 1)
    same = segment_column[pl.ds(begin, rows), :] == segment_row[:, :columns]
    return same & (row >= column)


def head_columns(index):
    return pl.ds(pl.multiple_of(index * HD, HD), HD)


def attention_kernel(
    step,
    tokens, gain, query_weight, key_weight, value_weight, query_gain, key_gain, cosine, sine,
    segment_column, segment_row,
    normed_out, query_raw, key_raw, query_out, key_out, value_out, mixed_out, total_out,
):
    count = tokens.shape[0]
    query_heads = query_weight.shape[1] // HD
    value_heads = key_weight.shape[1] // HD
    group = query_heads // value_heads

    def normalize(rows):
        value = tokens[rows, :].astype(jnp.float32)
        normed_out[rows, :] = (value * rms_inverse(value) * gain[...]).astype(jnp.bfloat16)

    loop_rows(count, 32, normalize)

    def project(rows):
        low = normed_out[rows, :]
        value_out[rows, :] = jnp.dot(
            low, value_weight[...], preferred_element_type=jnp.float32
        ).astype(jnp.bfloat16)
        for weight, raw, out, head_gain, heads in (
            (query_weight, query_raw, query_out, query_gain, query_heads),
            (key_weight, key_raw, key_out, key_gain, value_heads),
        ):
            product = jnp.dot(low, weight[...], preferred_element_type=jnp.float32)
            raw[rows, :] = product
            for head in range(heads):
                part = product[:, head * HD : (head + 1) * HD]
                unit = part * rms_inverse(part) * head_gain[...]
                turned = unit * cosine[rows, :] + pltpu.roll(unit, HD // 2, 1) * sine[rows, :]
                out[rows, head * HD : (head + 1) * HD] = turned.astype(jnp.bfloat16)

    loop_rows(count, step, project)

    def head_step(head, carry):
        own = head_columns(head)
        shared = head_columns(head // group)
        for begin in range(0, count, step):
            reach = begin + step
            scores = lax.dot_general(
                query_out[pl.ds(begin, step), own],
                key_out[pl.ds(0, reach), shared],
                (((1,), (1,)), ((), ())),
                preferred_element_type=jnp.float32,
            ) * HD ** (-0.5)
            allowed = block_mask(segment_column, segment_row, begin, step, reach)
            scores = jnp.where(allowed, scores, masked)
            peak = jnp.max(scores, axis=-1, keepdims=True)
            expons = jnp.exp(scores - peak)
            total = jnp.sum(expons, axis=-1, keepdims=True)
            chance = (expons * (1.0 / total)).astype(jnp.bfloat16)
            mixed_out[pl.ds(begin, step), own] = jnp.dot(
                chance, value_out[pl.ds(0, reach), shared], preferred_element_type=jnp.float32
            ).astype(jnp.bfloat16)
            total_out[head, pl.ds(begin, step), :] = jnp.broadcast_to(
                peak + jnp.log(total), (step, HD)
            )
        return carry

    lax.fori_loop(0, query_heads, head_step, 0)


def attention(tokens, gain, weights, query_gain, key_gain, cosine, sine, segment_column, segment_row):
    count, depth = tokens.shape
    queries, keys = weights[0].shape[1], weights[1].shape[1]
    f32, b16 = jnp.float32, jnp.bfloat16
    shape = jax.ShapeDtypeStruct
    return pl.pallas_call(
        functools.partial(attention_kernel, 256),
        out_shape=[
            shape((count, depth), b16),
            shape((count, queries), f32),
            shape((count, keys), f32),
            shape((count, queries), b16),
            shape((count, keys), b16),
            shape((count, keys), b16),
            shape((count, queries), b16),
            shape((queries // HD, count, HD), f32),
        ],
        compiler_params=pltpu.CompilerParams(vmem_limit_bytes=56 * 1024 * 1024),
        cost_estimate=pl.CostEstimate(
            flops=2 * count * depth * (queries + 2 * keys) + 4 * count * count * queries,
            bytes_accessed=32 * 1024 * 1024,
            transcendentals=count * count * queries // HD,
        ),
    )(tokens, gain[None], *weights, query_gain[None], key_gain[None], cosine, sine, segment_column, segment_row)


def attention_back_kernel(
    step,
    hidden_low, output_weight, queries, keys, values, totals, query_raw, key_raw,
    query_gain, key_gain, cosine, sine, segment_column, segment_row,
    raw_out, query_gain_out, key_gain_out,
    upstream, query_grad, key_grad, value_grad,
):
    count = hidden_low.shape[0]
    query_heads = queries.shape[1] // HD
    value_heads = keys.shape[1] // HD
    group = query_heads // value_heads
    across_last = (((1,), (1,)), ((), ()))
    down_first = (((0,), (0,)), ((), ()))

    def project(rows):
        upstream[rows, :] = lax.dot_general(
            hidden_low[rows, :],
            output_weight[...],
            across_last,
            preferred_element_type=jnp.float32,
        ).astype(jnp.bfloat16)

    loop_rows(count, step, project)
    key_grad[...] = jnp.zeros_like(key_grad)
    value_grad[...] = jnp.zeros_like(value_grad)

    def head_step(head, carry):
        own = head_columns(head)
        shared = head_columns(head // group)
        for begin in range(0, count, step):
            reach = begin + step
            rows, before = pl.ds(begin, step), pl.ds(0, reach)
            scores = lax.dot_general(
                queries[rows, own],
                keys[before, shared],
                across_last,
                preferred_element_type=jnp.float32,
            ) * HD ** (-0.5)
            allowed = block_mask(segment_column, segment_row, begin, step, reach)
            chance = jnp.exp(jnp.where(allowed, scores, masked) - totals[head, rows, :][:, :1])
            incoming = upstream[rows, own]
            value_grad[before, shared] += lax.dot_general(
                chance.astype(jnp.bfloat16),
                incoming,
                down_first,
                preferred_element_type=jnp.float32,
            )
            along = lax.dot_general(
                incoming, values[before, shared], across_last, preferred_element_type=jnp.float32
            )
            center = jnp.sum(along * chance, axis=-1, keepdims=True)
            score_grad = (chance * (along - center)).astype(jnp.bfloat16)
            query_grad[rows, own] = jnp.dot(
                score_grad, keys[before, shared], preferred_element_type=jnp.float32
            ) * HD ** (-0.5)
            key_grad[before, shared] += lax.dot_general(
                score_grad, queries[rows, own], down_first, preferred_element_type=jnp.float32
            ) * HD ** (-0.5)
        return carry

    lax.fori_loop(0, query_heads, head_step, 0)
    query_gain_out[...] = jnp.zeros_like(query_gain_out)
    key_gain_out[...] = jnp.zeros_like(key_gain_out)

    def finish(rows):
        for grad, raw, head_gain, gain_out, heads, place in (
            (query_grad, query_raw, query_gain, query_gain_out, query_heads, 0),
            (key_grad, key_raw, key_gain, key_gain_out, value_heads, query_heads),
        ):
            for head in range(heads):
                columns = slice(head * HD, (head + 1) * HD)
                upward = grad[rows, columns]
                unit_grad = upward * cosine[rows, :] - pltpu.roll(upward, HD // 2, 1) * sine[rows, :]
                value = raw[rows, columns]
                inverse = rms_inverse(value)
                product = unit_grad * (value * inverse)
                gain_out[...] += jnp.sum(product.reshape(-1, 8, HD), axis=0)
                begin = (place + head) * HD
                raw_out[rows, begin : begin + HD] = norm_back(
                    unit_grad, value, inverse, head_gain[...]
                ).astype(jnp.bfloat16)
        begin = (query_heads + value_heads) * HD
        raw_out[rows, begin:] = value_grad[rows, :].astype(jnp.bfloat16)

    loop_rows(count, 64, finish)


def attention_back(
    hidden_low, output_weight, queries, keys, values, totals, query_raw, key_raw,
    query_gain, key_gain, cosine, sine, segment_column, segment_row,
):
    count = hidden_low.shape[0]
    query_columns, key_columns = queries.shape[1], keys.shape[1]
    f32, b16 = jnp.float32, jnp.bfloat16
    shape = jax.ShapeDtypeStruct
    return pl.pallas_call(
        functools.partial(attention_back_kernel, 256),
        out_shape=[
            shape((count, query_columns + 2 * key_columns), b16),
            shape((8, HD), f32),
            shape((8, HD), f32),
        ],
        scratch_shapes=[
            pltpu.VMEM((count, query_columns), b16),
            pltpu.VMEM((count, query_columns), f32),
            pltpu.VMEM((count, key_columns), f32),
            pltpu.VMEM((count, key_columns), f32),
        ],
        compiler_params=pltpu.CompilerParams(vmem_limit_bytes=56 * 1024 * 1024),
        cost_estimate=pl.CostEstimate(
            flops=2 * count * hidden_low.shape[1] * query_columns + 10 * count * count * query_columns,
            bytes_accessed=24 * 1024 * 1024,
            transcendentals=count * count * query_columns // HD,
        ),
    )(
        hidden_low, output_weight, queries, keys, values, totals, query_raw, key_raw,
        query_gain[None], key_gain[None], cosine, sine, segment_column, segment_row,
    )


def finish_kernel(columns, number, *refs):
    inputs, gains = refs[:number], refs[number]
    outs, held = refs[number + 1 : -number - 2], refs[-number - 2 : -2]
    in_sems, out_sems = refs[-2:]
    rows = outs[number - 1].shape[0]
    fetches = [
        pltpu.make_async_copy(source, target, in_sems.at[index])
        for index, (source, target) in enumerate(zip(inputs, held))
    ]
    for copy in fetches:
        copy.start()
    stores = [[pltpu.make_async_copy(held[k], outs[k], out_sems.at[k])] for k in range(number - 1)]
    begin, last = 0, []
    for k, count in enumerate(columns):
        last.append(
            pltpu.make_async_copy(
                held[-1].at[pl.ds(0, rows), pl.ds(begin, count)],
                outs[number - 1 + k],
                out_sems.at[number - 1 + k],
            )
        )
        begin += count
    stores.append(last)
    for row, out in zip((0, 1, 8, 9), outs[number + 2 :]):
        out[...] = gains[row : row + 1, : out.shape[1]]
    for fetch, group in zip(fetches, stores):
        fetch.wait()
        for copy in group:
            copy.start()
    for group in stores:
        for copy in group:
            copy.wait()


def finish(columns, head_width, arrays, raw, gains):
    shape = jax.ShapeDtypeStruct
    any_space = pl.BlockSpec(memory_space=pl.ANY)
    in_vmem = pl.BlockSpec(memory_space=pltpu.VMEM)
    width = raw.shape[0] - 8
    number = len(arrays) + 1
    outs = [shape(value.shape, value.dtype) for value in arrays]
    outs += [shape((width, count), jnp.float32) for count in columns]
    outs += [shape((1, count), jnp.float32) for count in (width, width, head_width, head_width)]
    return pl.pallas_call(
        functools.partial(finish_kernel, columns, number),
        out_shape=outs,
        in_specs=[any_space] * number + [in_vmem],
        out_specs=[any_space] * (number + 2) + [in_vmem] * 4,
        scratch_shapes=[pltpu.VMEM(value.shape, value.dtype) for value in (*arrays, raw)]
        + [pltpu.SemaphoreType.DMA((number,)), pltpu.SemaphoreType.DMA((number + 2,))],
        compiler_params=pltpu.CompilerParams(vmem_limit_bytes=60 * 1024 * 1024),
    )(*arrays, raw, gains)


def plain_shards(
    tokens,
    attention_gain,
    query_weight,
    key_weight,
    value_weight,
    query_gain,
    key_gain,
    output_weight,
    feedforward_gain,
    gate_weight,
    up_weight,
    down_weight,
    segment_numbers,
    positions,
    cotangent,
):
    count = tokens.shape[0]
    batch = count // SEQ_LEN
    query_heads = query_weight.shape[1] // HD
    value_heads = key_weight.shape[1] // HD
    group = query_heads // value_heads
    inputs = tokens.astype(jnp.float32)
    first_inverse = rms_inverse(inputs)
    first_normed = inputs * first_inverse
    normed_low = (first_normed * attention_gain).astype(jnp.bfloat16)
    query_raw = jnp.dot(normed_low, query_weight, preferred_element_type=jnp.float32).reshape(
        count, query_heads, HD
    )
    key_raw = jnp.dot(normed_low, key_weight, preferred_element_type=jnp.float32).reshape(
        count, value_heads, HD
    )
    value_low = jnp.dot(normed_low, value_weight, preferred_element_type=jnp.float32).astype(
        jnp.bfloat16
    )
    cosine, sine = rotary_tables(positions)
    cosine = cosine[:, None]
    sine = sine[:, None]
    query_inverse = rms_inverse(query_raw)
    query_unit = query_raw * query_inverse
    query_low = rotate(query_unit * query_gain, cosine, sine).astype(jnp.bfloat16)
    key_inverse = rms_inverse(key_raw)
    key_unit = key_raw * key_inverse
    key_low = rotate(key_unit * key_gain, cosine, sine).astype(jnp.bfloat16)
    queries = query_low.reshape(batch, SEQ_LEN, value_heads, group, HD)
    keys = key_low.reshape(batch, SEQ_LEN, value_heads, HD)
    values = value_low.reshape(batch, SEQ_LEN, value_heads, HD)
    segments = segment_numbers.reshape(batch, SEQ_LEN)
    mixed, totals = lax.map(attend, (queries, keys, values, segments))
    mixed_low = mixed.reshape(count, query_heads * HD).astype(jnp.bfloat16)
    attention = lax.psum(
        jnp.dot(mixed_low, output_weight, preferred_element_type=jnp.float32), "tensor"
    )
    hidden = inputs + attention
    second_inverse = rms_inverse(hidden)
    second_normed = hidden * second_inverse
    second_low = (second_normed * feedforward_gain).astype(jnp.bfloat16)
    gate = jnp.dot(second_low, gate_weight, preferred_element_type=jnp.float32)
    upward = jnp.dot(second_low, up_weight, preferred_element_type=jnp.float32)
    sigmoid_gate = jax.nn.sigmoid(gate)
    activated = gate * sigmoid_gate
    product_low = (activated * upward).astype(jnp.bfloat16)
    feedforward = lax.psum(
        jnp.dot(product_low, down_weight, preferred_element_type=jnp.float32), "tensor"
    )
    layer_output = (hidden + feedforward).astype(jnp.bfloat16)
    down_grad = jnp.einsum("tf,td->fd", product_low, cotangent, preferred_element_type=jnp.float32)
    product_grad = jnp.einsum(
        "td,fd->tf", cotangent, down_weight, preferred_element_type=jnp.float32
    )
    gate_grad_low = (
        product_grad * upward * sigmoid_gate * (1.0 + gate * (1.0 - sigmoid_gate))
    ).astype(jnp.bfloat16)
    upward_grad_low = (product_grad * activated).astype(jnp.bfloat16)
    gate_weight_grad = jnp.einsum(
        "td,tf->df", second_low, gate_grad_low, preferred_element_type=jnp.float32
    )
    upward_weight_grad = jnp.einsum(
        "td,tf->df", second_low, upward_grad_low, preferred_element_type=jnp.float32
    )
    second_part = jnp.einsum(
        "tf,df->td", gate_grad_low, gate_weight, preferred_element_type=jnp.float32
    )
    second_part = second_part + jnp.einsum(
        "tf,df->td", upward_grad_low, up_weight, preferred_element_type=jnp.float32
    )
    second_grad = lax.psum(second_part, "tensor")
    second_gain_grad = jnp.sum(second_grad * second_normed, axis=0)
    hidden_grad = cotangent.astype(jnp.float32) + norm_back(
        second_grad, hidden, second_inverse, feedforward_gain
    )
    hidden_low = hidden_grad.astype(jnp.bfloat16)
    output_weight_grad = jnp.einsum(
        "tc,td->cd", mixed_low, hidden_low, preferred_element_type=jnp.float32
    )
    mixed_grad = jnp.einsum(
        "td,cd->tc", hidden_low, output_weight, preferred_element_type=jnp.float32
    ).astype(jnp.bfloat16)
    upstream = mixed_grad.reshape(batch, SEQ_LEN, value_heads, group, HD)
    query_back, key_back, value_back = lax.map(
        attend_back, (queries, keys, values, segments, totals, upstream)
    )
    query_unit_grad = rotate_back(query_back.reshape(count, query_heads, HD), cosine, sine)
    key_unit_grad = rotate_back(key_back.reshape(count, value_heads, HD), cosine, sine)
    query_gain_part = jnp.sum(query_unit_grad * query_unit, axis=(0, 1))
    key_gain_part = jnp.sum(key_unit_grad * key_unit, axis=(0, 1))
    query_raw_grad = (
        norm_back(query_unit_grad, query_raw, query_inverse, query_gain)
        .reshape(count, query_heads * HD)
        .astype(jnp.bfloat16)
    )
    key_raw_grad = (
        norm_back(key_unit_grad, key_raw, key_inverse, key_gain)
        .reshape(count, value_heads * HD)
        .astype(jnp.bfloat16)
    )
    value_raw_grad = value_back.reshape(count, value_heads * HD).astype(jnp.bfloat16)
    query_weight_grad = jnp.einsum(
        "td,tc->dc", normed_low, query_raw_grad, preferred_element_type=jnp.float32
    )
    key_weight_grad = jnp.einsum(
        "td,tc->dc", normed_low, key_raw_grad, preferred_element_type=jnp.float32
    )
    value_weight_grad = jnp.einsum(
        "td,tc->dc", normed_low, value_raw_grad, preferred_element_type=jnp.float32
    )
    first_part = jnp.einsum(
        "tc,dc->td", query_raw_grad, query_weight, preferred_element_type=jnp.float32
    )
    first_part = first_part + jnp.einsum(
        "tc,dc->td", key_raw_grad, key_weight, preferred_element_type=jnp.float32
    )
    first_part = first_part + jnp.einsum(
        "tc,dc->td", value_raw_grad, value_weight, preferred_element_type=jnp.float32
    )
    first_grad, query_gain_grad, key_gain_grad = lax.psum(
        (first_part, query_gain_part, key_gain_part), "tensor"
    )
    first_gain_grad = jnp.sum(first_grad * first_normed, axis=0)
    tokens_gradient = (
        hidden_grad + norm_back(first_grad, inputs, first_inverse, attention_gain)
    ).astype(jnp.bfloat16)
    summed = (
        lax.psum_scatter(first_gain_grad, "dp", scatter_dimension=0, tiled=True),
        lax.psum_scatter(query_weight_grad, "dp", scatter_dimension=0, tiled=True),
        lax.psum_scatter(key_weight_grad, "dp", scatter_dimension=0, tiled=True),
        lax.psum_scatter(value_weight_grad, "dp", scatter_dimension=0, tiled=True),
        lax.psum_scatter(query_gain_grad, "dp", scatter_dimension=0, tiled=True),
        lax.psum_scatter(key_gain_grad, "dp", scatter_dimension=0, tiled=True),
        lax.psum_scatter(output_weight_grad, "dp", scatter_dimension=1, tiled=True),
        lax.psum_scatter(second_gain_grad, "dp", scatter_dimension=0, tiled=True),
        lax.psum_scatter(gate_weight_grad, "dp", scatter_dimension=0, tiled=True),
        lax.psum_scatter(upward_weight_grad, "dp", scatter_dimension=0, tiled=True),
        lax.psum_scatter(down_grad, "dp", scatter_dimension=1, tiled=True),
    )
    return (
        layer_output,
        tokens_gradient,
        summed[0],
        summed[1],
        summed[2],
        summed[3],
        summed[4],
        summed[5],
        summed[6],
        summed[7],
        summed[8],
        summed[9],
        summed[10],
    )


def shards(
    dp,
    tokens,
    attention_gain,
    query_weight,
    key_weight,
    value_weight,
    query_gain,
    key_gain,
    output_weight,
    feedforward_gain,
    gate_weight,
    up_weight,
    down_weight,
    segment_numbers,
    positions,
    cotangent,
):
    count, depth = tokens.shape
    width = depth // dp
    high = dp // 2
    core = lax.axis_index("tensor") % 2
    upstream_first = lax.ppermute(
        lax.dynamic_slice_in_dim(cotangent, core * (count // 2), 3 * count // 16, 0).astype(jnp.float32),
        "dp",
        [(i, i ^ 2) for i in range(dp)],
    )

    cosine, sine = rotary_tables(positions)
    sine = jnp.concatenate([-sine[:, : HD // 2], sine[:, HD // 2 :]], axis=1)
    tables = (cosine, sine, segment_numbers[:, None], segment_numbers[None])
    normed_low, query_raw, key_raw, queries, keys, values, mixed_low, totals = attention(
        tokens,
        attention_gain,
        (query_weight, key_weight, value_weight),
        query_gain,
        key_gain,
        *tables,
    )
    (
        hidden,
        second_part,
        low_own,
        product_own,
        gate_own,
        upward_own,
        low_pair,
        product_pair,
        gate_pair,
        upward_pair,
        upstream_pair,
    ) = front(
        mixed_low,
        output_weight,
        tokens,
        cotangent,
        upstream_first,
        feedforward_gain,
        gate_weight,
        up_weight,
        down_weight,
    )[:11]
    hidden_grad, hidden_low, out_part, down_weight_grad, gate_ready, gate_given, gate_kept = middle(
        second_part,
        hidden,
        cotangent,
        upstream_pair,
        product_own,
        product_pair,
        gate_own,
        gate_pair,
        low_own,
        low_pair,
        feedforward_gain,
        down_weight,
    )
    gate_middle, gate_inward = (
        lax.ppermute(gate_ready, "dp", [(2 * a + k, 2 * b + k) for a, b in pairs for k in (0, 1)])
        for pairs in (((1, 2), (2, 1)), ((0, 1), (3, 2)))
    )
    gate_moved = lax.ppermute(gate_given, "dp", [(i, i ^ 1) for i in range(dp)])
    raw_grad, query_gain_part, key_gain_part = attention_back(
        hidden_low,
        output_weight,
        queries,
        keys,
        values,
        totals,
        query_raw,
        key_raw,
        query_gain,
        key_gain,
        *tables,
    )

    lines = [
        jnp.pad(value.reshape(dp, -1), ((0, 0), (0, raw_grad.shape[1] - value.size // dp)))
        for value in (jnp.sum(query_gain_part, axis=0), jnp.sum(key_gain_part, axis=0))
    ]
    gain_lines = jnp.pad(jnp.stack(lines, axis=1), ((0, 0), (0, 6), (0, 0)))

    (
        layer_output,
        tokens_gradient,
        gate_weight_grad,
        up_weight_grad,
        raw_whole,
        output_weight_grad,
        gains,
    ) = (
        rear(
            [line_order(high, p) for p in range(high)],
            [gate_middle, gate_inward, gate_kept + gate_moved]
            + [low_own, low_pair, upward_own, upward_pair]
            + [normed_low, raw_grad, hidden_low, mixed_low],
            gain_lines,
            [out_part, hidden, hidden_grad, tokens],
            [query_weight, key_weight, value_weight, gate_weight, up_weight],
            attention_gain,
            feedforward_gain,
        )[:7]
    )
    (
        layer_output,
        tokens_gradient,
        gate_weight_grad,
        up_weight_grad,
        output_weight_grad,
        down_weight_grad,
        query_weight_grad,
        key_weight_grad,
        value_weight_grad,
        attention_gain_grad,
        feedforward_gain_grad,
        query_gain_grad,
        key_gain_grad,
    ) = finish(
        (query_weight.shape[1], key_weight.shape[1], value_weight.shape[1]),
        HD // dp,
        [
            layer_output,
            tokens_gradient,
            gate_weight_grad,
            up_weight_grad,
            output_weight_grad,
            down_weight_grad,
        ],
        raw_whole,
        gains,
    )
    return (
        layer_output,
        tokens_gradient,
        attention_gain_grad[0],
        query_weight_grad,
        key_weight_grad,
        value_weight_grad,
        query_gain_grad[0],
        key_gain_grad[0],
        output_weight_grad,
        feedforward_gain_grad[0],
        gate_weight_grad,
        up_weight_grad,
        down_weight_grad,
    )


def solution(mesh):
    dp, tensor = mesh.shape["dp"], mesh.shape["tensor"]

    def program(*args):
        if dp == 8 and tensor == 4 and args[0].shape[0] == SEQ_LEN:
            return shards(dp, *args)
        return plain_shards(*args)

    return jax.shard_map(
        program,
        mesh=mesh,
        in_specs=(
            P("dp", None),
            P(),
            P(None, "tensor"),
            P(None, "tensor"),
            P(None, "tensor"),
            P(),
            P(),
            P("tensor", None),
            P(),
            P(None, "tensor"),
            P(None, "tensor"),
            P("tensor", None),
            P("dp"),
            P("dp"),
            P("dp", None),
        ),
        out_specs=(
            P("dp", None),
            P("dp", None),
            P("dp"),
            P("dp", "tensor"),
            P("dp", "tensor"),
            P("dp", "tensor"),
            P("dp"),
            P("dp"),
            P("tensor", "dp"),
            P("dp"),
            P("dp", "tensor"),
            P("dp", "tensor"),
            P("tensor", "dp"),
        ),
        check_vma=False,
    )
```

```python
import functools

import jax
import jax.numpy as jnp
from jax import lax
from jax.experimental import pallas as pl
from jax.experimental.pallas import tpu as pltpu
from jax.sharding import PartitionSpec as P

HD = 128
SEQ_LEN = 1024


epsilon = 1e-06
rope_base = 1000000.0
masked = -1e30


def rms_inverse(value):
    return lax.rsqrt(jnp.mean(value * value, axis=-1, keepdims=True) + epsilon)


def norm_back(upstream, value, inverse, gain):
    scaled = upstream * gain
    return inverse * scaled - value * inverse**3 * jnp.mean(scaled * value, axis=-1, keepdims=True)


def rotary_tables(positions):
    exponent = jnp.arange(0, HD, 2, dtype=jnp.float32) / HD
    frequency = rope_base ** (-exponent)
    phase = positions.astype(jnp.float32)[:, None] * frequency[None, :]
    phase = jnp.concatenate([phase, phase], axis=-1)
    return (jnp.cos(phase), jnp.sin(phase))


def rotate(value, cosine, sine):
    half = value.shape[-1] // 2
    turned = jnp.concatenate([-value[..., half:], value[..., :half]], axis=-1)
    return value * cosine + turned * sine


def rotate_back(upstream, cosine, sine):
    half = upstream.shape[-1] // 2
    moved = upstream * sine
    return upstream * cosine + jnp.concatenate([moved[..., half:], -moved[..., :half]], axis=-1)


def block_scores(query_rows, keys, row_segments, segments, begin):
    scores = jnp.einsum(
        "rkgd,tkd->kgrt", query_rows, keys, preferred_element_type=jnp.float32
    ) * HD ** (-0.5)
    rows = begin + lax.iota(jnp.int32, query_rows.shape[0])
    columns = lax.iota(jnp.int32, keys.shape[0])
    allowed = (row_segments[:, None] == segments[None, :]) & (rows[:, None] >= columns[None, :])
    return jnp.where(allowed[None, None], scores, masked)


def attend(item):
    queries, keys, values, segments = item
    length = queries.shape[0]
    width = min(512, length)
    outputs = []
    totals = []
    for begin in range(0, length, width):
        scores = block_scores(
            queries[begin : begin + width], keys, segments[begin : begin + width], segments, begin
        )
        peak = jnp.max(scores, axis=-1, keepdims=True)
        expons = jnp.exp(scores - peak)
        total = jnp.sum(expons, axis=-1, keepdims=True)
        chance_low = (expons / total).astype(jnp.bfloat16)
        outputs.append(
            jnp.einsum("kgrt,tkd->rkgd", chance_low, values, preferred_element_type=jnp.float32)
        )
        totals.append(peak + jnp.log(total))
    return (jnp.concatenate(outputs, axis=0), jnp.concatenate(totals, axis=2))


def attend_back(item):
    queries, keys, values, segments, totals, upstream = item
    length = queries.shape[0]
    width = min(512, length)
    query_parts = []
    key_grad = jnp.zeros(keys.shape, jnp.float32)
    value_grad = jnp.zeros(values.shape, jnp.float32)
    for begin in range(0, length, width):
        rows = queries[begin : begin + width]
        scores = block_scores(rows, keys, segments[begin : begin + width], segments, begin)
        chance = jnp.exp(scores - totals[:, :, begin : begin + width])
        chance_low = chance.astype(jnp.bfloat16)
        incoming = upstream[begin : begin + width]
        value_grad = value_grad + jnp.einsum(
            "kgrt,rkgd->tkd", chance_low, incoming, preferred_element_type=jnp.float32
        )
        along = jnp.einsum("rkgd,tkd->kgrt", incoming, values, preferred_element_type=jnp.float32)
        center = jnp.sum(along * chance, axis=-1, keepdims=True)
        score_grad = (chance * (along - center)).astype(jnp.bfloat16)
        query_parts.append(
            jnp.einsum("kgrt,tkd->rkgd", score_grad, keys, preferred_element_type=jnp.float32)
            * HD ** (-0.5)
        )
        key_grad = key_grad + jnp.einsum(
            "kgrt,rkgd->tkd", score_grad, rows, preferred_element_type=jnp.float32
        ) * HD ** (-0.5)
    return (jnp.concatenate(query_parts, axis=0), key_grad, value_grad)


def dot(left, right):
    return jnp.dot(left, right, preferred_element_type=jnp.float32)


def dot_back(left, right):
    return jnp.einsum("tc,dc->td", left, right, preferred_element_type=jnp.float32)


def dot_tokens(left, right):
    return jnp.einsum("tm,tn->mn", left, right, preferred_element_type=jnp.float32)


def line_order(high, place):
    steps = {}
    for block in range(high):
        if block > place:
            steps[block] = high - block + place
        elif block < place:
            steps[block] = high - place + block
    return sorted(steps, key=lambda block: (steps[block], block)) + [place]


MESH = pl.DeviceIdType.MESH


def neighbours():
    dp, tensor = lax.axis_index("dp"), lax.axis_index("tensor")
    core = lax.rem(tensor, 2)
    sibling = {"tensor": tensor + 1 - 2 * core}
    facing = {"tensor": lax.rem(tensor + 2, 4)}
    place = dp // 2
    pair = {"dp": dp + 2 * (1 - 2 * lax.rem(place, 2))}
    return core, sibling, facing, pair


def greet(devices):
    barrier = pltpu.get_barrier_semaphore()
    for device in devices:
        pl.semaphore_signal(barrier, inc=1, device_id=device, device_id_type=MESH)
    pl.semaphore_wait(barrier, len(devices))


def loop_rows(count, step, body):
    def run(index, carry):
        body(pl.ds(pl.multiple_of(index * step, step), step))
        return carry

    lax.fori_loop(0, count // step, run, 0)


def sequence_rows(size, core, which, k):
    side = core if which == 0 else 1 - core
    return pl.multiple_of(side * 4 * size + k * size, size)


def remote(source, target, sems, k, device):
    return pltpu.make_async_remote_copy(
        src_ref=source, dst_ref=target, send_sem=sems.at[0, k], recv_sem=sems.at[1, k],
        device_id=device, device_id_type=MESH,
    )


def front_kernel(
    size, first,
    mixed_hbm, output_weight_hbm, tokens_hbm, upstream_hbm, upstream_first,
    gain, gate_hbm, up_hbm, down_hbm,
    hidden_out, second_out, low_own, product_own, gate_own, upward_own,
    low_pair, product_pair, gate_pair, upward_pair, upstream_pair,
    c_landed, n_recv, n_side, u_recv, u_side,
    mixed, output_weight, gate_weight, up_weight, down_weight,
    x_send, x_recv, back_recv, tok, hid, z_send, low, rows16, pair16, tiles, stage, terms,
    load_sems, c_sems, x_sems, back_sems, n_sems, n_side_sems, u_sems, u_side_sems,
    tok_sems, hid_sems, low_sems, wave_sems, tile_sems, stage_sems, term_sems, join_sems,
):
    core, sibling, facing, pair = neighbours()
    depth = gain.shape[1]
    half = 4 * size
    units = gate_weight.shape[1]
    begin = functools.partial(sequence_rows, size, core)
    across_last = (((1,), (1,)), ((), ()))
    rest = half - first
    loads = [
        pltpu.make_async_copy(source, target, load_sems.at[index])
        for index, (source, target) in enumerate(
            [
                (
                    upstream_hbm.at[pl.ds(pl.multiple_of(core * half + first, 16), rest)],
                    rows16.at[pl.ds(0, rest)],
                ),
                (mixed_hbm, mixed),
                (output_weight_hbm, output_weight),
                (gate_hbm, gate_weight),
                (up_hbm, up_weight),
                (down_hbm, down_weight),
            ]
        )
    ]
    for load in loads:
        load.start()
    greet([sibling, facing, pair])

    c_copies = [
        remote(terms.at[pl.ds(k * size, size)], c_landed.at[k], c_sems, k, sibling) for k in range(4)
    ]
    x_copies = [remote(x_send.at[k], x_recv.at[k], x_sems, k, facing) for k in range(4)]
    back_copies = [remote(x_send.at[k], back_recv.at[k], back_sems, k, sibling) for k in range(4)]
    part = pl.ds(pl.multiple_of(lax.axis_index("tensor") // 2 * (size // 2), 16), size // 2)
    n_copies = [
        remote(z_send.at[k % 2], n_recv.at[k], n_sems, k, pair)
        if k < 2
        else remote(z_send.at[k % 2, part], n_recv.at[k, part], n_sems, k, pair)
        for k in range(4)
    ]
    n_joins = [
        remote(n_recv.at[k, part], n_recv.at[k, part], join_sems, k - 2, facing) for k in (2, 3)
    ]
    n_sides = [remote(n_recv.at[k], n_side.at[k], n_side_sems, k, sibling) for k in range(4)]
    u_rows = [(0, rest - 2 * size), (rest - 2 * size, size), (rest - size, size)]
    u_buffers = [hid.at[0, pl.ds(0, u_rows[0][1])], z_send.at[0], z_send.at[1]]
    u_copies = [
        remote(u_buffers[j], u_recv.at[pl.ds(start, number)], u_sems, j, pair)
        for j, (start, number) in enumerate(u_rows)
    ]
    u_sides = [remote(upstream_first, u_side.at[pl.ds(0, first)], u_side_sems, 0, sibling)] + [
        remote(
            u_recv.at[pl.ds(start, number)],
            u_side.at[pl.ds(first + start, number)],
            u_side_sems,
            1 + j,
            sibling,
        )
        for j, (start, number) in enumerate(u_rows)
    ]

    def stage_load(source, slot, number):
        return pltpu.make_async_copy(source, stage.at[slot, pl.ds(0, number)], stage_sems.at[slot])

    def upstream_send(j):
        start, number = u_rows[j]

        def run(row):
            u_buffers[j][row, :] = rows16[
                pl.ds(pl.multiple_of(start + row.start, 16), row.size), :
            ].astype(jnp.float32)

        loop_rows(number, 16, run)
        u_copies[j].start()

    def upstream_forward(j):
        u_copies[j].wait_recv()
        u_sides[1 + j].start()

    def attention_terms(k):
        rows = jnp.concatenate(
            [mixed[pl.ds(begin(which, k), size), :] for which in range(2)], axis=0
        )

        def run(column):
            both = jnp.dot(rows, output_weight[:, column], preferred_element_type=jnp.float32)
            x_send[k, :, column] = both[:size]
            terms[pl.ds(k * size, size), column] = both[size:]

        loop_rows(depth, 1024, run)
        c_copies[k].start()

    def attention_cores(k):
        c_copies[k].wait_recv()
        stage_load(c_landed.at[k], k % 2, size).start()
        stage_load(c_landed.at[k], k % 2, size).wait()

        def run(row):
            x_send[k, row, :] = x_send[k, row, :] + stage[k % 2, row, :]

        loop_rows(size, 16, run)
        x_copies[k].start()

    def attention_chips(k):
        x_copies[k].wait()

        def run(row):
            x_send[k, row, :] = x_send[k, row, :] + x_recv[k, row, :]

        loop_rows(size, 16, run)
        back_copies[k].start()

    def token_loads(k):
        return [
            pltpu.make_async_copy(
                tokens_hbm.at[pl.ds(begin(which, k), size)], tok.at[which], tok_sems.at[which]
            )
            for which in range(2)
        ]

    def hidden_stores(k):
        return [
            pltpu.make_async_copy(
                hid.at[which], hidden_out.at[pl.ds(begin(which, k), size)], hid_sems.at[which]
            )
            for which in range(2)
        ]

    def low_rows(which, k, row):
        side = core if which == 0 else 1 - core
        return pl.ds(pl.multiple_of((side + k % 2 * 2) * size + row.start, 16), row.size)

    def normed(k):
        for load in token_loads(k):
            load.wait()
        if k > 0:
            for store in hidden_stores(k - 1):
                store.wait()
        if k < 2:
            u_copies[1 + k].wait_send()
        else:
            n_copies[k - 2].wait_send()

        def run(which, source, row):
            value = tok[which, row, :].astype(jnp.float32) + source[k, row, :]
            hid[which, row, :] = value
            unit = value * lax.rsqrt(jnp.mean(value * value, axis=-1, keepdims=True) + epsilon)
            if which == 0:
                z_send[k % 2, row, :] = unit
            low[0, low_rows(which, k, row), :] = (unit * gain[...]).astype(jnp.bfloat16)

        loop_rows(size, 16, functools.partial(run, 0, x_send))
        n_copies[k].start()
        back_copies[k].wait_recv()
        loop_rows(size, 16, functools.partial(run, 1, back_recv))
        for store in hidden_stores(k):
            store.start()
        if k < 3:
            for load in token_loads(k + 1):
                load.start()

    def pipeline(pieces):
        def bring(index):
            before, source, number, _ = pieces[index]
            if before is not None:
                before.wait_recv()
            stage_load(source, index % 2, number).start()

        bring(0)
        for index, (_, source, number, consume) in enumerate(pieces):
            if index + 1 < len(pieces):
                bring(index + 1)
            stage_load(source, index % 2, number).wait()
            loop_rows(number, 16, functools.partial(consume, index % 2))

    def pair_join(k):
        n_copies[k].wait_recv()
        n_joins[k - 2].start()

    def pair_forward(k):
        if k < 2:
            n_copies[k].wait_recv()
        else:
            n_joins[k - 2].wait_recv()
        n_sides[k].start()

    def pair_rows(chunks):
        def consume(k, which, slot, row):
            low[1, low_rows(which, k, row), :] = (stage[slot, row, :] * gain[...]).astype(
                jnp.bfloat16
            )

        pipeline(
            [
                (
                    n_sides[k] if which else None,
                    (n_side if which else n_recv).at[k],
                    size,
                    functools.partial(consume, k, which),
                )
                for which in range(2)
                for k in chunks
            ]
        )

    def wave_copies(local, distant, sems, wave, inwards=False):
        copies = []
        for part in range(4):
            here = local.at[pl.ds(part * size, size)]
            there = distant.at[pl.ds(part % 2 * half + (2 * wave + part // 2) * size, size)]
            source, target = (there, here) if inwards else (here, there)
            copies.append(pltpu.make_async_copy(source, target, sems.at[part]))
        return copies

    def pair_stores(wave):
        return wave_copies(pair16, upstream_pair, wave_sems.at[1], wave)

    def upstream_wave(wave):
        def consume(which, start, slot, row):
            side = core if which == 0 else 1 - core
            chunk, within = start // size, start % size
            place = pl.multiple_of((2 * chunk + side) * size + within + row.start, 16)
            pair16[pl.ds(place, row.size), :] = stage[slot, row, :].astype(jnp.bfloat16)

        if wave == 0:
            own = [
                (upstream_first.at[pl.ds(0, size)], size, 0),
                (upstream_first.at[pl.ds(size, first - size)], first - size, size),
                (u_recv.at[pl.ds(0, u_rows[0][1])], u_rows[0][1], first),
            ]
            waits = [u_sides[0], u_sides[1]]
        else:
            own = [(u_recv.at[pl.ds(u_rows[j][0], size)], size, (j - 1) * size) for j in (1, 2)]
            waits = [u_sides[2], u_sides[3]]
        pieces = [
            (None, source, number, functools.partial(consume, 0, start))
            for source, number, start in own
        ]
        if wave == 0:
            waits[0].wait_recv()
            waits[1].wait_recv()
            waits = [None, None]
        pieces += [
            (
                waits[j],
                u_side.at[pl.ds((2 * wave + j) * size, size)],
                size,
                functools.partial(consume, 1, j * size),
            )
            for j in range(2)
        ]
        pipeline(pieces)
        for copy in pair_stores(wave):
            copy.start()

    def term_stores(wave):
        return wave_copies(terms, second_out, term_sems, wave)

    def low_stores(wave, index):
        return wave_copies(low.at[index], low_pair if index else low_own, low_sems.at[index], wave)

    def tile_stores(wave, index):
        outs = (
            (product_pair, gate_pair, upward_pair) if index else (product_own, gate_own, upward_own)
        )
        return [
            copy
            for which in range(3)
            for copy in wave_copies(tiles.at[which], outs[which], tile_sems.at[which], wave)
        ]

    feeds = [(0, 0), (1, 0), (0, 1), (1, 1)]

    def fetches(wave):
        return wave_copies(rows16, upstream_hbm, wave_sems.at[0], wave, True)

    def feed(wave, index, part=None):
        number = feeds.index((wave, index))
        rows = slice(None) if part is None else pl.ds(part * 2 * size, 2 * size)
        if not part:
            if number > 0:
                for copy in tile_stores(*feeds[number - 1]):
                    copy.wait()
        if index == 0 and not part:
            for copy in fetches(wave):
                copy.wait()

        def run(column):
            gate = jnp.dot(
                low[index, rows], gate_weight[:, column], preferred_element_type=jnp.float32
            )
            upward = jnp.dot(
                low[index, rows], up_weight[:, column], preferred_element_type=jnp.float32
            )
            grad = lax.dot_general(
                (pair16 if index else rows16)[rows],
                down_weight[column, :],
                across_last,
                preferred_element_type=jnp.float32,
            )
            sigmoid_gate = jax.nn.sigmoid(gate)
            activated = gate * sigmoid_gate
            tiles[0, rows, column] = (activated * upward).astype(jnp.bfloat16)
            tiles[1, rows, column] = (
                grad * upward * sigmoid_gate * (1.0 + gate * (1.0 - sigmoid_gate))
            ).astype(jnp.bfloat16)
            tiles[2, rows, column] = (grad * activated).astype(jnp.bfloat16)

        loop_rows(units, 512, run)
        copies = tile_stores(wave, index) + low_stores(wave, index)
        for number, copy in enumerate(copies):
            if part is None or number % 4 // 2 == part:
                copy.start()
        if index == 0:
            if wave > 0 and not part:
                for copy in term_stores(wave - 1):
                    copy.wait()

            def second(column):
                terms[rows, column] = lax.dot_general(
                    tiles[1, rows],
                    gate_weight[column, :],
                    across_last,
                    preferred_element_type=jnp.float32,
                ) + lax.dot_general(
                    tiles[2, rows],
                    up_weight[column, :],
                    across_last,
                    preferred_element_type=jnp.float32,
                )

            loop_rows(depth, 1024 if part is not None else 512, second)
            for number, copy in enumerate(term_stores(wave)):
                if part is None or number // 2 == part:
                    copy.start()

    for load in token_loads(0):
        load.start()
    loads[0].wait()
    for j in range(3):
        upstream_send(j)
    u_sides[0].start()
    loads[1].wait()
    loads[2].wait()
    attention_terms(0)
    attention_terms(1)
    attention_cores(0)
    attention_terms(2)
    attention_cores(1)
    attention_terms(3)
    attention_cores(2)
    attention_cores(3)
    for copy in fetches(0):
        copy.start()
    upstream_forward(0)
    upstream_wave(0)
    attention_chips(0)
    u_copies[0].wait_send()
    upstream_forward(1)
    normed(0)
    for load in loads[3:]:
        load.wait()
    for k in range(4):
        c_copies[k].wait_send()
    feed(0, 0, 0)
    attention_chips(1)
    normed(1)
    upstream_forward(2)
    feed(0, 0, 1)
    attention_chips(2)
    for copy in low_stores(0, 0):
        copy.wait()
    normed(2)
    pair_forward(0)
    for copy in fetches(1):
        copy.start()
    feed(1, 0, 0)
    attention_chips(3)
    normed(3)
    feed(1, 0, 1)
    pair_forward(1)
    pair_rows((0, 1))
    pair_join(2)
    feed(0, 1)
    for copy in pair_stores(0):
        copy.wait()
    pair_join(3)
    pair_forward(2)
    upstream_wave(1)
    for copy in low_stores(0, 1):
        copy.wait()
    pair_rows((2,))
    feed(1, 1, 0)
    pair_forward(3)
    pair_rows((3,))
    feed(1, 1, 1)

    for k in range(4):
        back_copies[k].wait_send()
        n_sides[k].wait_send()
        u_sides[k].wait_send()
        if k >= 2:
            n_copies[k].wait_send()
            n_joins[k - 2].wait_send()
    ends = hidden_stores(3) + term_stores(1) + low_stores(1, 0) + low_stores(1, 1)
    for copy in ends + pair_stores(1) + tile_stores(1, 1):
        copy.wait()


def front(mixed, output_weight, tokens, upstream, upstream_first, gain, gate_weight, up_weight, down_weight):
    rows, depth = tokens.shape
    inner, units = mixed.shape[1], gate_weight.shape[1]
    first = upstream_first.shape[0]
    size = rows // 8
    f32, b16 = jnp.float32, jnp.bfloat16
    any_space = pl.BlockSpec(memory_space=pl.ANY)
    shape = jax.ShapeDtypeStruct
    outs = [shape((rows, depth), f32)] * 2
    outs += ([shape((rows, depth), b16)] + [shape((rows, units), b16)] * 3) * 2
    outs += [shape((rows, depth), b16)] + [shape((4, size, depth), f32)] * 3
    outs += [shape((4 * size - first, depth), f32), shape((4 * size, depth), f32)]
    dma = pltpu.SemaphoreType.DMA
    vmem = pltpu.VMEM
    return pl.pallas_call(
        functools.partial(front_kernel, size, first),
        out_shape=outs,
        in_specs=[any_space] * 5 + [pl.BlockSpec(memory_space=pltpu.VMEM)] + [any_space] * 3,
        out_specs=[any_space] * len(outs),
        scratch_shapes=[
            vmem((rows, inner), b16),
            vmem((inner, depth), b16),
            vmem((depth, units), b16),
            vmem((depth, units), b16),
            vmem((units, depth), b16),
            vmem((4, size, depth), f32),
            vmem((4, size, depth), f32),
            vmem((4, size, depth), f32),
            vmem((2, size, depth), b16),
            vmem((2, size, depth), f32),
            vmem((2, size, depth), f32),
            vmem((2, 4 * size, depth), b16),
            vmem((4 * size, depth), b16),
            vmem((4 * size, depth), b16),
            vmem((3, 4 * size, units), b16),
            vmem((2, size, depth), f32),
            vmem((4 * size, depth), f32),
            dma((6,)),
            *[dma((2, 4))] * 5,
            dma((2, 3)),
            dma((2, 4)),
            dma((2,)),
            dma((2,)),
            dma((2, 4)),
            dma((2, 4)),
            dma((3, 4)),
            dma((2,)),
            dma((4,)),
            dma((2, 2)),
        ],
        compiler_params=pltpu.CompilerParams(
            collective_id=1, has_side_effects=True, vmem_limit_bytes=63 * 1024 * 1024
        ),
        cost_estimate=pl.CostEstimate(
            flops=12 * rows * depth * units, bytes_accessed=6 * depth * units, transcendentals=0
        ),
    )(mixed, output_weight, tokens, upstream, upstream_first, gain[None], gate_weight, up_weight, down_weight)


def grid_neighbours():
    dp = lax.axis_index("dp")
    place, lane = dp // 2, lax.rem(dp, 2)
    towards = 1 - 2 * (place // 2)
    across = {"dp": dp + 1 - 2 * lane}
    inward, outward = {"dp": dp + 2 * towards}, {"dp": dp - 2 * towards}
    team = place // 2
    side = lax.rem(place, 2)
    inner = lax.rem(team + side, 2)
    return place, lane, team, side, inner, across, inward, outward


def greet_grid(always, inner, outward):
    barrier = pltpu.get_barrier_semaphore()
    for device in always:
        pl.semaphore_signal(barrier, inc=1, device_id=device, device_id_type=MESH)

    @pl.when(inner == 1)
    def _():
        pl.semaphore_signal(barrier, inc=1, device_id=outward, device_id_type=MESH)

    pl.semaphore_wait(barrier, len(always) + inner)


def middle_kernel(
    size,
    second_hbm, hidden_hbm, upstream_hbm, upstream_pair, product_own, product_pair,
    gate_own, gate_pair, low_own, low_pair, gain, down_hbm,
    grad_out, grad_low_out, out_part, weight_out, gate_ready, gate_given, gate_own_block,
    products, down_weight, columns, c_recv, x_send, x_recv, back_recv,
    y_send, y_recv, kept, in_recv, mid_recv, out_recv,
    hid, tok, grad, grad_low, out_stage, gate_send, gate_kept, gate_stage,
    load_sems, gate_load_sems, gate_sems, c_sems, x_sems, back_sems, y_sems, z_sems, column_sems,
    x_load_sems, hid_sems, tok_sems, grad_sems, low_sems, out_sems, weight_sems,
):
    core, sibling, facing, _ = neighbours()
    place, lane, team, side, inner, across, inward, outward = grid_neighbours()
    depth = gain.shape[1]
    units = down_weight.shape[0]
    width = columns.shape[-1]
    begin = functools.partial(sequence_rows, size, core)
    rows_in = 8 * size
    down_first = (((0,), (0,)), ((), ()))
    loads = [
        pltpu.make_async_copy(source, target, load_sems.at[index])
        for index, (source, target) in enumerate(
            [
                (product_own, products.at[pl.ds(0, rows_in)]),
                (product_pair, products.at[pl.ds(rows_in, rows_in)]),
                (down_hbm, down_weight),
            ]
        )
    ]
    gate_loads = [
        pltpu.make_async_copy(
            source, products.at[pl.ds(index * rows_in, rows_in)], gate_load_sems.at[index]
        )
        for index, source in enumerate((gate_own, gate_pair))
    ]
    turns = [(0, 1), (1, 1), (0, 0), (1, 0)]
    turns += [(0, 1), (1, 1), (1, 0), (0, 0)]

    def column_loads(index):
        turn, other = turns[index]
        spot = lax.rem(1 - team + turn, 2)
        which = 1 - lane if other else lane
        start = pl.multiple_of((side * 4 + 2 * spot + which) * width, width)
        return [
            pltpu.make_async_copy(
                source.at[:, pl.ds(start, width)],
                columns.at[index % 2, pl.ds(part * rows_in, rows_in)],
                column_sems.at[index % 2, part],
            )
            for part, source in enumerate(
                (upstream_hbm, upstream_pair) if index < 4 else (low_own, low_pair)
            )
        ]

    x_loads = [
        pltpu.make_async_copy(
            second_hbm.at[pl.ds(begin(0, k), size)], x_send.at[k], x_load_sems.at[k]
        )
        for k in range(4)
    ]
    for copy in column_loads(0) + x_loads[:1] + loads[:2] + column_loads(1) + x_loads[1:] + loads[2:]:
        copy.start()
    greet_grid([sibling, facing, across, inward], inner, outward)
    c_copies = [
        remote(second_hbm.at[pl.ds(begin(1, k), size)], c_recv.at[k], c_sems, k, sibling)
        for k in range(4)
    ]
    x_copies = [remote(x_send.at[k], x_recv.at[k], x_sems, k, facing) for k in range(4)]
    back_copies = [remote(x_send.at[k], back_recv.at[k], back_sems, k, sibling) for k in range(4)]
    y_copies = [remote(y_send.at[k], y_recv.at[k], y_sems, k, across) for k in range(2)]
    in_copy = remote(kept.at[0], in_recv, z_sems, 0, inward)
    mid_copies = [remote(kept.at[k], mid_recv.at[k], z_sems, 1 + k, inward) for k in range(2)]
    out_copy = remote(mid_recv.at[0], out_recv, z_sems, 3, outward)
    for copy in c_copies:
        copy.start()

    def cores(k):
        x_loads[k].wait()
        c_copies[k].wait_recv()

        def run(row):
            x_send[k, row, :] = x_send[k, row, :] + c_recv[k, row, :]

        loop_rows(size, 16, run)
        x_copies[k].start()

    def chips(k):
        x_copies[k].wait()

        def run(row):
            x_send[k, row, :] = x_send[k, row, :] + x_recv[k, row, :]

        loop_rows(size, 16, run)
        back_copies[k].start()

    def block(index, target):
        for copy in column_loads(index):
            copy.wait()

        target[...] = lax.dot_general(
            products[...], columns[index % 2], down_first, preferred_element_type=jnp.float32
        )
        for copy in column_loads(index + 2):
            copy.start()

    gate_copy = remote(gate_send, gate_kept, gate_sems, 0, across)

    def gate_block(index, target):
        for copy in column_loads(index):
            copy.wait()
        target[...] = lax.dot_general(
            columns[index % 2], products[...], down_first, preferred_element_type=jnp.float32
        )
        if index + 2 < len(turns):
            for copy in column_loads(index + 2):
                copy.start()

    def gate_store(source, target, index):
        return pltpu.make_async_copy(source, target, gate_load_sems.at[2 + index])

    def chunk_loads(k):
        return [
            pltpu.make_async_copy(
                source.at[pl.ds(begin(which, k), size)], target.at[which], sems.at[which]
            )
            for which in range(2)
            for source, target, sems in ((hidden_hbm, hid, hid_sems), (upstream_hbm, tok, tok_sems))
        ]

    def grad_stores(k):
        return [
            pltpu.make_async_copy(
                source.at[which], target.at[pl.ds(begin(which, k), size)], sems.at[which]
            )
            for which in range(2)
            for source, target, sems in (
                (grad, grad_out, grad_sems),
                (grad_low, grad_low_out, low_sems),
            )
        ]

    def finish(k):
        for copy in chunk_loads(k):
            copy.wait()
        if k > 0:
            for copy in grad_stores(k - 1):
                copy.wait()
        back_copies[k].wait_recv()

        def run(which, source, row):
            value = hid[which, row, :]
            inverse = lax.rsqrt(jnp.mean(value * value, axis=-1, keepdims=True) + epsilon)
            total = tok[which, row, :].astype(jnp.float32) + norm_back(
                source[k, row, :], value, inverse, gain[...]
            )
            grad[which, row, :] = total
            grad_low[which, row, :] = total.astype(jnp.bfloat16)

        for which, source in enumerate((x_send, back_recv)):
            loop_rows(size, 16, functools.partial(run, which, source))
        for copy in grad_stores(k):
            copy.start()
        if k < 3:
            for copy in chunk_loads(k + 1):
                copy.start()

    def out_store(k):
        rows = 2 * size
        return pltpu.make_async_copy(
            out_stage, out_part.at[pl.ds(k * rows, rows)], out_sems.at[0]
        )

    def out_terms(k):
        if k > 0:
            out_store(k - 1).wait()
        rows = pl.ds(k * 2 * size, 2 * size)

        def run(column):
            out_stage[:, column] = jnp.dot(
                products[rows, :], down_weight[:, column], preferred_element_type=jnp.float32
            )

        loop_rows(depth, 1024, run)
        out_store(k).start()

    def take(k):
        y_copies[k].wait_recv()

        def run(row):
            kept[k, row, :] = kept[k, row, :] + y_recv[k, row, :]

        loop_rows(units, 64, run)

    for copy in loads[:2]:
        copy.wait()
    block(0, y_send.at[0])
    y_copies[0].start()
    cores(0)
    for copy in chunk_loads(0):
        copy.start()
    cores(1)
    cores(2)
    cores(3)
    block(1, y_send.at[1])
    y_copies[1].start()
    block(2, kept.at[0])
    loads[2].wait()
    out_terms(0)
    chips(0)
    out_terms(1)
    block(3, kept.at[1])
    finish(0)
    out_terms(2)
    take(0)

    @pl.when(inner == 1)
    def _():
        mid_copies[0].start()

    @pl.when(inner == 0)
    def _():
        in_copy.start()

    out_terms(3)
    for copy in gate_loads:
        copy.start()
    chips(1)
    for copy in gate_loads:
        copy.wait()
    gate_block(4, gate_send)
    gate_copy.start()
    finish(1)
    gate_block(5, gate_stage)
    gate_store(gate_stage, gate_given, 0).start()
    chips(2)
    take(1)

    @pl.when(inner == 1)
    def _():
        mid_copies[1].start()
        mid_copies[0].wait_recv()
        out_copy.start()

    finish(2)
    gate_store(gate_stage, gate_given, 0).wait()
    gate_block(6, gate_stage)
    gate_store(gate_stage, gate_own_block, 1).start()
    gate_store(gate_stage, gate_own_block, 1).wait()
    gate_block(7, gate_stage)
    chips(3)
    finish(3)
    gate_copy.wait()

    def run_gate(row):
        gate_kept[row, :] = gate_kept[row, :] + gate_stage[row, :]

    loop_rows(width, 16, run_gate)
    gate_store(gate_kept, gate_ready, 2).start()

    @pl.when(inner == 1)
    def _():
        in_copy.wait_recv()
        mid_copies[1].wait_recv()
        mid_copies[0].wait_send()
        mid_copies[1].wait_send()
        out_copy.wait_send()

        def run(row):
            kept[0, row, :] = in_recv[row, :] + mid_recv[1, row, :]

        loop_rows(units, 64, run)

    @pl.when(inner == 0)
    def _():
        in_copy.wait_send()
        out_copy.wait_recv()

        def run(row):
            kept[0, row, :] = kept[1, row, :] + out_recv[row, :]

        loop_rows(units, 64, run)

    store = pltpu.make_async_copy(kept.at[0], weight_out, weight_sems.at[0])
    store.start()
    for k in range(4):
        back_copies[k].wait_send()
        c_copies[k].wait_send()
    for k in range(2):
        y_copies[k].wait_send()
    for copy in grad_stores(3):
        copy.wait()
    gate_store(gate_kept, gate_ready, 2).wait()
    out_store(3).wait()
    store.wait()


def middle(
    second, hidden, upstream, upstream_pair, product_own, product_pair,
    gate_own, gate_pair, low_own, low_pair, gain, down_weight,
):
    rows, depth = hidden.shape
    units = down_weight.shape[0]
    size = rows // 8
    width = depth // 8
    f32, b16 = jnp.float32, jnp.bfloat16
    any_space = pl.BlockSpec(memory_space=pl.ANY)
    shape = jax.ShapeDtypeStruct
    dma = pltpu.SemaphoreType.DMA
    vmem = pltpu.VMEM
    return pl.pallas_call(
        functools.partial(middle_kernel, size),
        out_shape=[
            shape((rows, depth), f32),
            shape((rows, depth), b16),
            shape((rows, depth), f32),
            shape((units, width), f32),
        ]
        + [shape((width, units), f32)] * 3,
        in_specs=[any_space] * 10 + [pl.BlockSpec(memory_space=pltpu.VMEM), any_space],
        out_specs=[any_space] * 7,
        scratch_shapes=[
            vmem((2 * rows, units), b16),
            vmem((units, depth), b16),
            vmem((2, 2 * rows, width), b16),
            vmem((4, size, depth), f32),
            vmem((4, size, depth), f32),
            vmem((4, size, depth), f32),
            vmem((4, size, depth), f32),
            vmem((2, units, width), f32),
            vmem((2, units, width), f32),
            vmem((2, units, width), f32),
            vmem((units, width), f32),
            vmem((2, units, width), f32),
            vmem((units, width), f32),
            vmem((2, size, depth), f32),
            vmem((2, size, depth), b16),
            vmem((2, size, depth), f32),
            vmem((2, size, depth), b16),
            vmem((2 * size, depth), f32),
            vmem((width, units), f32),
            vmem((width, units), f32),
            vmem((width, units), f32),
            dma((3,)),
            dma((5,)),
            dma((2, 1)),
            dma((2, 4)),
            dma((2, 4)),
            dma((2, 4)),
            dma((2, 2)),
            dma((2, 4)),
            dma((2, 2)),
            dma((4,)),
            dma((2,)),
            dma((2,)),
            dma((2,)),
            dma((2,)),
            dma((1,)),
            dma((1,)),
        ],
        compiler_params=pltpu.CompilerParams(
            collective_id=2, has_side_effects=True, vmem_limit_bytes=62 * 1024 * 1024
        ),
        cost_estimate=pl.CostEstimate(
            flops=8 * rows * depth * units, bytes_accessed=6 * depth * units, transcendentals=0
        ),
    )(
        second, hidden, upstream, upstream_pair, product_own, product_pair,
        gate_own, gate_pair, low_own, low_pair, gain[None], down_weight,
    )


class TensorSum:
    def __init__(self, size, own, landed, stage, sems, stage_sems, devices):
        self.size, self.own, self.landed, self.stage = size, own, landed, stage
        self.stage_sems = stage_sems
        c_sems, x_sems, back_sems = sems
        self.sibling, facing = devices
        self.c_sems = c_sems
        self.x_copies = [remote(own.at[k], landed[1].at[k], x_sems, k, facing) for k in range(4)]
        self.back_copies = [
            remote(own.at[k], landed[2].at[k], back_sems, k, self.sibling) for k in range(4)
        ]
        self.c_copies = [None] * 4

    def give(self, k, source):
        self.c_copies[k] = remote(source, self.landed[0].at[k], self.c_sems, k, self.sibling)
        self.c_copies[k].start()

    def staged(self, which, k):
        copy = pltpu.make_async_copy(self.landed[which].at[k], self.stage.at[0], self.stage_sems.at[0])
        copy.start()
        copy.wait()

    def add_stage(self, k):
        def run(row):
            self.own[k, row, :] = self.own[k, row, :] + self.stage[0, row, :]

        loop_rows(self.size, 16, run)

    def cores(self, k):
        self.c_copies[k].wait_recv()
        self.staged(0, k)
        self.add_stage(k)
        self.x_copies[k].start()

    def chips(self, k):
        self.x_copies[k].wait()
        self.staged(1, k)
        self.add_stage(k)
        self.back_copies[k].start()

    def other(self, k):
        self.back_copies[k].wait_recv()
        self.staged(2, k)


def rear_kernel(
    size, turns,
    gate_middle, gate_inward, gate_ready, low_own, low_pair, upward_own, upward_pair,
    normed_hbm, raw_hbm, hidden_low_hbm, mixed_hbm, lines,
    out_hbm, hidden_hbm, grad_hbm, tokens_hbm,
    query_hbm, key_hbm, value_hbm, gate_hbm, up_hbm, gain, feed_gain,
    layer_out, tokens_out, gate_out, up_out, raw_out, head_out, gains_out,
    o_c, o_x, o_back, d_c, d_x, d_back, gate_landed, up_landed,
    upwards, raw, mixed, head_weights, feed_rows, gains, gain_rows, gains_in, columns,
    up_send, up_kept, raw_send, raw_kept, head_send, head_kept, raw_line, head_line,
    own, give, stage, wide, narrow, result,
    load_sems, column_sems, y_up_sems, y_raw_sems, y_head_sems, gate_sems, up_sems,
    raw_line_sems, head_line_sems,
    oc_sems, ox_sems, ob_sems, dc_sems, dx_sems, db_sems,
    own_sems, stage_sems, wide_sems, narrow_sems, result_sems, end_sems, gain_sems,
):
    core, sibling, facing, _ = neighbours()
    place, lane, team, side, inner, across, inward, outward = grid_neighbours()
    high = len(turns)
    depth = gain.shape[1]
    width = columns.shape[-1]
    units = upwards.shape[-1]
    begin = functools.partial(sequence_rows, size, core)
    rows_in = 8 * size
    down_first = (((0,), (0,)), ((), ()))
    cuts = (query_hbm.shape[1], key_hbm.shape[1])
    own_rows = pl.ds(pl.multiple_of(lax.axis_index("dp") * width, width), width)
    loads = [
        pltpu.make_async_copy(source, target, load_sems.at[index])
        for index, (source, target) in enumerate(
            [
                (raw_hbm, raw),
                (mixed_hbm, mixed),
                (upward_own, upwards.at[pl.ds(0, rows_in)]),
                (upward_pair, upwards.at[pl.ds(rows_in, rows_in)]),
                (query_hbm, head_weights.at[:, pl.ds(0, cuts[0])]),
                (key_hbm, head_weights.at[:, pl.ds(cuts[0], cuts[1])]),
                (value_hbm, head_weights.at[:, pl.ds(cuts[0] + cuts[1], cuts[1])]),
                (gate_hbm.at[own_rows], feed_rows.at[0]),
                (up_hbm.at[own_rows], feed_rows.at[1]),
            ]
        )
    ]
    blocks = [
        ("head", 0, 1), ("up", 0, 1), ("up", 1, 1), ("head", 1, 1), ("head", 2, 1), ("head", 3, 1),
        ("head", 0, 0), ("up", 0, 0), ("up", 1, 0), ("head", 1, 0), ("head", 2, 0), ("head", 3, 0),
    ]

    def spot_of(kind, turn):
        if kind == "up":
            return side * 2 + lax.rem(1 - team + turn, 2)
        spot = jnp.int32(turns[0][turn])
        for p in range(1, high):
            spot = jnp.where(place == p, jnp.int32(turns[p][turn]), spot)
        return spot

    def column_loads(index):
        kind, turn, other = blocks[index]
        which = 1 - lane if other else lane
        start = pl.multiple_of((2 * spot_of(kind, turn) + which) * width, width)
        sources = (low_own, low_pair) if kind == "up" else (normed_hbm, hidden_low_hbm)
        return [
            pltpu.make_async_copy(
                source.at[:, pl.ds(start, width)],
                columns.at[index % 2, pl.ds(part * rows_in, rows_in)],
                column_sems.at[index % 2, part],
            )
            for part, source in enumerate(sources)
        ]

    own_loads = [
        pltpu.make_async_copy(out_hbm.at[pl.ds(begin(0, k), size)], own.at[k], own_sems.at[k])
        for k in range(4)
    ]
    for copy in column_loads(0) + loads[:2] + column_loads(1) + own_loads + loads[2:]:
        copy.start()
    greet_grid([sibling, facing, across, inward], inner, outward)
    devices = (sibling, facing)
    outs = TensorSum(
        size, own, (o_c, o_x, o_back), stage, (oc_sems, ox_sems, ob_sems), stage_sems, devices
    )
    heads = TensorSum(
        size, own, (d_c, d_x, d_back), stage, (dc_sems, dx_sems, db_sems), stage_sems, devices
    )
    for k in range(4):
        outs.give(k, out_hbm.at[pl.ds(begin(1, k), size)])

    def team_copies(values, landed, sems):
        return (
            remote(values[0], landed.at[0], sems, 0, inward),
            [remote(values[k], landed.at[1 + k], sems, 1 + k, inward) for k in range(2)],
            remote(landed.at[1], landed.at[3], sems, 3, outward),
        )

    gate_copies = (
        None,
        [None, remote(gate_ready, gate_landed.at[0], gate_sems, 0, inward)],
        remote(gate_middle, gate_landed.at[1], gate_sems, 1, outward),
    )
    up_copies = team_copies((up_kept.at[0], up_kept.at[1]), up_landed, up_sems)

    def team_send(copies, turn):
        @pl.when(inner == 1)
        def _():
            copies[1][turn].start()

        if turn == 0:

            @pl.when(inner == 0)
            def _():
                copies[0].start()

    def team_forward(copies):
        @pl.when(inner == 1)
        def _():
            copies[1][0].wait_recv()
            copies[2].start()

    def add_gain(lane_index, row, value, weight):
        total = jnp.sum(value * weight.astype(jnp.float32), axis=-1, keepdims=True)
        lanes = lax.broadcasted_iota(jnp.int32, (total.shape[0], gains.shape[1]), 1)
        gains[row, :] = gains[row, :] + jnp.where(lanes == lane_index, total, 0.0)

    def team_combine(copies, first, second, outward_landed, last, out, sem, which):
        def fetch(source, slot):
            copy = pltpu.make_async_copy(source, up_send.at[slot], end_sems.at[4 + slot])
            copy.start()
            copy.wait()

        @pl.when(inner == 1)
        def _():
            if copies[0] is not None:
                copies[0].wait_recv()
                copies[1][0].wait_send()
            copies[1][1].wait_recv()
            fetch(first, 0)
            fetch(second, 1)
            copies[1][1].wait_send()
            copies[2].wait_send()

        @pl.when(inner == 0)
        def _():
            if copies[0] is not None:
                copies[0].wait_send()
            copies[2].wait_recv()
            fetch(outward_landed, 0)
            fetch(last, 1)

        def run(row):
            total = up_send[0, row, :] + up_send[1, row, :]
            up_send[0, row, :] = total
            add_gain(1, row, total, feed_rows[which, row, :])

        loop_rows(width, 16, run)
        store = pltpu.make_async_copy(up_send.at[0], out, sem)
        store.start()
        store.wait()

    y_up = [remote(up_send.at[k], up_kept.at[k], y_up_sems, k, across) for k in range(2)]
    y_raw = [remote(raw_send.at[k], raw_kept.at[k], y_raw_sems, k, across) for k in range(high)]
    y_head = [
        remote(head_send.at[k], head_kept.at[k], y_head_sems, k, across) for k in range(high)
    ]

    def line_copy(p, turn, towards=None):
        block = turns[p][turn]
        ahead = block > p
        slot = block - 1 if ahead else high - 1 + block
        device = {"dp": lax.axis_index("dp") + (2 if ahead else -2)}
        return slot, [
            remote(kept.at[turn], line.at[slot], sems, slot, device)
            for kept, line, sems in (
                (raw_kept, raw_line, raw_line_sems),
                (head_kept, head_line, head_line_sems),
            )
        ]

    def line_arrived(slot, turn):
        for kept, line, sems in (
            (raw_kept, raw_line, raw_line_sems),
            (head_kept, head_line, head_line_sems),
        ):
            remote(kept.at[turn], line.at[slot], sems, slot, across).wait_recv()

            def run(row):
                kept[turn, row, :] = kept[turn, row, :] + line[slot, row, :]

            loop_rows(kept.shape[1], 8, run)

    def line_step(turn):
        for p in range(high):
            block = turns[p][turn]

            @pl.when(place == p)
            def _():
                slot, copies = line_copy(p, turn)
                if (block > p and p > 0) or (block < p and p < high - 1):
                    line_arrived(slot, turn)
                for copy in copies:
                    copy.start()

    def line_end():
        for p in range(high):

            @pl.when(place == p)
            def _():
                if p > 0:
                    line_arrived(p - 1, high - 1)
                if p < high - 1:
                    line_arrived(high - 1 + p, high - 1)
                for turn in range(high - 1):
                    for copy in line_copy(p, turn)[1]:
                        copy.wait_send()

    def up_block(index, target, added):
        for copy in column_loads(index):
            copy.wait()

        total = lax.dot_general(
            columns[index % 2], upwards[...], down_first, preferred_element_type=jnp.float32
        )
        target[...] = target[...] + total if added else total
        if index + 2 < len(blocks):
            for copy in column_loads(index + 2):
                copy.start()

    def head_block(index, raw_target, head_target, added):
        kind, turn, other = blocks[index]
        which = 1 - lane if other else lane
        for copy in column_loads(index):
            copy.wait()
        slot = index % 2
        total = lax.dot_general(
            columns[slot, :rows_in], raw[...], down_first, preferred_element_type=jnp.float32
        )
        line = lines[2 * spot_of(kind, turn) + which]
        raw_target[:width, :] = raw_target[:width, :] + total if added else total
        raw_target[width:, :] = raw_target[width:, :] + line if added else line
        total = lax.dot_general(
            mixed[...], columns[slot, rows_in:], down_first, preferred_element_type=jnp.float32
        )
        head_target[...] = head_target[...] + total if added else total
        if index + 2 < len(blocks):
            for copy in column_loads(index + 2):
                copy.start()

    def head_send_block(index):
        turn = blocks[index][1]
        head_block(index, raw_send.at[turn], head_send.at[turn], False)
        y_raw[turn].start()
        y_head[turn].start()

    def head_take(index):
        turn = blocks[index][1]
        y_raw[turn].wait_recv()
        y_head[turn].wait_recv()
        head_block(index, raw_kept.at[turn], head_kept.at[turn], True)

    def head_terms(k):
        outs.back_copies[k].wait_send()
        if k >= 2:
            heads.c_copies[k - 2].wait_send()
        rows = jnp.concatenate(
            [raw[pl.ds(begin(which, k), size), :] for which in range(2)], axis=0
        )

        def run(column):
            total = lax.dot_general(
                rows,
                head_weights[column, :],
                (((1,), (1,)), ((), ())),
                preferred_element_type=jnp.float32,
            )
            own[k, :, column] = total[:size]
            give[k % 2, :, column] = total[size:]

        loop_rows(depth, 1024, run)
        heads.give(k, give.at[k % 2])

    def fetches(what, k):
        pairs = ((hidden_hbm, wide, wide_sems),)
        if what == "tokens":
            pairs = ((grad_hbm, wide, wide_sems), (tokens_hbm, narrow, narrow_sems))
        return [
            pltpu.make_async_copy(
                source.at[pl.ds(begin(which, k), size)], target.at[which], sems.at[which]
            )
            for which in range(2)
            for source, target, sems in pairs
        ]

    def stores(what, k):
        return [
            pltpu.make_async_copy(
                result.at[which],
                (layer_out if what == "layer" else tokens_out).at[pl.ds(begin(which, k), size)],
                result_sems.at[which],
            )
            for which in range(2)
        ]

    sequence = [("layer", k) for k in range(4)] + [("tokens", k) for k in range(4)]

    def finish(what, k):
        number = sequence.index((what, k))
        for copy in fetches(what, k):
            copy.wait()
        if number > 0:
            for copy in stores(*sequence[number - 1]):
                copy.wait()
        (outs if what == "layer" else heads).other(k)

        def run(which, row):
            total = stage[0, row, :] if which else own[k, row, :]
            value = wide[which, row, :]
            if what == "layer":
                total = value + total
            else:
                inputs = narrow[which, row, :].astype(jnp.float32)
                inverse = lax.rsqrt(jnp.mean(inputs * inputs, axis=-1, keepdims=True) + epsilon)
                total = value + norm_back(total, inputs, inverse, gain[...])
            result[which, row, :] = total.astype(jnp.bfloat16)

        for which in range(2):
            loop_rows(size, 16, functools.partial(run, which))
        for copy in stores(what, k):
            copy.start()
        if number + 1 < len(sequence):
            for copy in fetches(*sequence[number + 1]):
                copy.start()

    team_send(gate_copies, 1)

    @pl.when(inner == 1)
    def _():
        gate_copies[2].start()

    gains[...] = jnp.zeros_like(gains)
    for copy in fetches("layer", 0):
        copy.start()
    for copy in loads[:2]:
        copy.wait()
    head_send_block(0)
    own_loads[0].wait()
    outs.cores(0)
    for copy in loads[2:]:
        copy.wait()
    up_block(1, up_send.at[0], False)
    y_up[0].start()
    for k in range(1, 4):
        own_loads[k].wait()
        outs.cores(k)
    up_block(2, up_send.at[1], False)
    y_up[1].start()
    for index in range(3, 6):
        head_send_block(index)
    outs.chips(0)
    finish("layer", 0)
    head_take(6)
    line_step(0)
    head_terms(0)
    outs.chips(1)
    finish("layer", 1)
    head_terms(1)
    heads.cores(0)
    y_up[0].wait_recv()
    up_block(7, up_kept.at[0], True)
    team_send(up_copies, 0)
    outs.chips(2)
    finish("layer", 2)
    head_terms(2)
    heads.cores(1)
    outs.chips(3)
    heads.cores(2)
    finish("layer", 3)
    head_terms(3)
    heads.cores(3)
    y_up[1].wait_recv()
    up_block(8, up_kept.at[1], True)
    team_send(up_copies, 1)
    team_forward(up_copies)
    heads.chips(0)
    finish("tokens", 0)
    for k in range(2):
        y_up[k].wait_send()
    team_combine(
        gate_copies, gate_inward, gate_landed.at[0], gate_landed.at[1], gate_ready,
        gate_out, end_sems.at[0], 0,
    )
    head_take(9)
    line_step(1)
    heads.chips(1)
    finish("tokens", 1)
    y_raw[0].wait_send()
    y_head[0].wait_send()
    heads.chips(2)
    finish("tokens", 2)
    head_take(10)
    line_step(2)
    head_block(11, raw_send.at[0], head_send.at[0], False)
    team_combine(
        up_copies, up_landed.at[0], up_landed.at[2], up_landed.at[3], up_kept.at[1],
        up_out, end_sems.at[1], 1,
    )
    heads.chips(3)
    finish("tokens", 3)
    y_raw[high - 1].wait_recv()
    y_head[high - 1].wait_recv()
    for kept, sent, step in ((raw_kept, raw_send, 8), (head_kept, head_send, 16)):

        def run_last(row):
            kept[high - 1, row, :] = kept[high - 1, row, :] + sent[0, row, :]

        loop_rows(kept.shape[1], step, run_last)
    line_end()
    ends = [
        pltpu.make_async_copy(raw_kept.at[high - 1], raw_out, end_sems.at[2]),
        pltpu.make_async_copy(head_kept.at[high - 1], head_out, end_sems.at[3]),
    ]
    for copy in ends:
        copy.start()

    def run_gain(row):
        place_row = pl.ds(pl.multiple_of(own_rows.start + row.start, 16), row.size)
        add_gain(0, row, raw_kept[high - 1, row, :], head_weights[place_row, :])

    loop_rows(width, 16, run_gain)
    own_columns = pl.ds(pl.multiple_of(own_rows.start, 128), width)
    turned = jnp.transpose(gains[...])[:8]
    scale = jnp.concatenate([gain[:, own_columns], feed_gain[:, own_columns]], axis=0)
    gain_rows[:8, :] = turned
    gain_rows[:2, :] = turned[:2] / scale
    gain_rows[8:, :] = raw_kept[high - 1, width:, :width]
    gain_copies = [
        remote(gain_rows, gains_in.at[k], gain_sems, k, device)
        for k, device in enumerate((sibling, facing))
    ]
    for k in range(2):
        gain_copies[k].start()
        gain_copies[k].wait()
        gain_rows[...] = gain_rows[...] + gains_in[k]
    gain_store = pltpu.make_async_copy(gain_rows, gains_out, own_sems.at[0])
    gain_store.start()
    gain_store.wait()
    for k in range(4):
        outs.c_copies[k].wait_send()
        heads.back_copies[k].wait_send()
    for k in range(2, 4):
        heads.c_copies[k].wait_send()
    for k in range(1, high):
        y_raw[k].wait_send()
        y_head[k].wait_send()
    for copy in stores(*sequence[-1]) + ends:
        copy.wait()


def rear(turns, arrays, lines, places, weights, gain, feed_gain):
    rows, depth = places[0].shape
    units = arrays[0].shape[1]
    heads, inner = arrays[8].shape[1], arrays[10].shape[1]
    size = rows // 8
    width = depth // 8
    high = len(turns)
    f32, b16 = jnp.float32, jnp.bfloat16
    any_space = pl.BlockSpec(memory_space=pl.ANY)
    in_vmem = pl.BlockSpec(memory_space=pltpu.VMEM)
    shape = jax.ShapeDtypeStruct
    dma = pltpu.SemaphoreType.DMA
    vmem = pltpu.VMEM
    slots = 2 * (high - 1)
    return pl.pallas_call(
        functools.partial(rear_kernel, size, turns),
        out_shape=[
            shape((rows, depth), b16),
            shape((rows, depth), b16),
            shape((width, units), f32),
            shape((width, units), f32),
            shape((width + 8, heads), f32),
            shape((inner, width), f32),
            shape((16, width), f32),
        ]
        + [shape((4, size, depth), f32)] * 6
        + [shape((2, width, units), f32), shape((4, width, units), f32)],
        in_specs=[any_space] * 11 + [in_vmem] + [any_space] * 9 + [in_vmem] * 2,
        out_specs=[any_space] * 15,
        scratch_shapes=[
            vmem((2 * rows, units), b16),
            vmem((rows, heads), b16),
            vmem((rows, inner), b16),
            vmem((depth, heads), b16),
            vmem((2, width, units), b16),
            vmem((width, HD), f32),
            vmem((16, width), f32),
            vmem((2, 16, width), f32),
            vmem((2, 2 * rows, width), b16),
            vmem((2, width, units), f32),
            vmem((2, width, units), f32),
            vmem((high, width + 8, heads), f32),
            vmem((high, width + 8, heads), f32),
            vmem((high, inner, width), f32),
            vmem((high, inner, width), f32),
            vmem((slots, width + 8, heads), f32),
            vmem((slots, inner, width), f32),
            vmem((4, size, depth), f32),
            vmem((2, size, depth), f32),
            vmem((1, size, depth), f32),
            vmem((2, size, depth), f32),
            vmem((2, size, depth), b16),
            vmem((2, size, depth), b16),
            dma((9,)),
            dma((2, 2)),
            dma((2, 2)),
            dma((2, high)),
            dma((2, high)),
            dma((2, 4)),
            dma((2, 4)),
            dma((2, slots)),
            dma((2, slots)),
            *[dma((2, 4))] * 6,
            dma((4,)),
            dma((1,)),
            dma((2,)),
            dma((2,)),
            dma((2,)),
            dma((6,)),
            dma((2, 2)),
        ],
        compiler_params=pltpu.CompilerParams(
            collective_id=3, has_side_effects=True, vmem_limit_bytes=62 * 1024 * 1024
        ),
        cost_estimate=pl.CostEstimate(
            flops=8 * rows * depth * units, bytes_accessed=6 * depth * units, transcendentals=0
        ),
    )(*arrays, lines, *places, *weights, gain[None], feed_gain[None])


def block_mask(segment_column, segment_row, begin, rows, columns):
    row = begin + lax.broadcasted_iota(jnp.int32, (rows, columns), 0)
    column = lax.broadcasted_iota(jnp.int32, (rows, columns), 1)
    same = segment_column[pl.ds(begin, rows), :] == segment_row[:, :columns]
    return same & (row >= column)


def head_columns(index):
    return pl.ds(pl.multiple_of(index * HD, HD), HD)


def attention_kernel(
    step,
    tokens, gain, query_weight, key_weight, value_weight, query_gain, key_gain, cosine, sine,
    segment_column, segment_row,
    normed_out, query_raw, key_raw, query_out, key_out, value_out, mixed_out, total_out,
):
    count = tokens.shape[0]
    query_heads = query_weight.shape[1] // HD
    value_heads = key_weight.shape[1] // HD
    group = query_heads // value_heads

    def normalize(rows):
        value = tokens[rows, :].astype(jnp.float32)
        normed_out[rows, :] = (value * rms_inverse(value) * gain[...]).astype(jnp.bfloat16)

    loop_rows(count, 32, normalize)

    def project(rows):
        low = normed_out[rows, :]
        value_out[rows, :] = jnp.dot(
            low, value_weight[...], preferred_element_type=jnp.float32
        ).astype(jnp.bfloat16)
        for weight, raw, out, head_gain, heads in (
            (query_weight, query_raw, query_out, query_gain, query_heads),
            (key_weight, key_raw, key_out, key_gain, value_heads),
        ):
            product = jnp.dot(low, weight[...], preferred_element_type=jnp.float32)
            raw[rows, :] = product
            for head in range(heads):
                part = product[:, head * HD : (head + 1) * HD]
                unit = part * rms_inverse(part) * head_gain[...]
                turned = unit * cosine[rows, :] + pltpu.roll(unit, HD // 2, 1) * sine[rows, :]
                out[rows, head * HD : (head + 1) * HD] = turned.astype(jnp.bfloat16)

    loop_rows(count, step, project)

    def head_step(head, carry):
        own = head_columns(head)
        shared = head_columns(head // group)
        for begin in range(0, count, step):
            reach = begin + step
            scores = lax.dot_general(
                query_out[pl.ds(begin, step), own],
                key_out[pl.ds(0, reach), shared],
                (((1,), (1,)), ((), ())),
                preferred_element_type=jnp.float32,
            ) * HD ** (-0.5)
            allowed = block_mask(segment_column, segment_row, begin, step, reach)
            scores = jnp.where(allowed, scores, masked)
            peak = jnp.max(scores, axis=-1, keepdims=True)
            expons = jnp.exp(scores - peak)
            total = jnp.sum(expons, axis=-1, keepdims=True)
            chance = (expons * (1.0 / total)).astype(jnp.bfloat16)
            mixed_out[pl.ds(begin, step), own] = jnp.dot(
                chance, value_out[pl.ds(0, reach), shared], preferred_element_type=jnp.float32
            ).astype(jnp.bfloat16)
            total_out[head, pl.ds(begin, step), :] = jnp.broadcast_to(
                peak + jnp.log(total), (step, HD)
            )
        return carry

    lax.fori_loop(0, query_heads, head_step, 0)


def attention(tokens, gain, weights, query_gain, key_gain, cosine, sine, segment_column, segment_row):
    count, depth = tokens.shape
    queries, keys = weights[0].shape[1], weights[1].shape[1]
    f32, b16 = jnp.float32, jnp.bfloat16
    shape = jax.ShapeDtypeStruct
    return pl.pallas_call(
        functools.partial(attention_kernel, 256),
        out_shape=[
            shape((count, depth), b16),
            shape((count, queries), f32),
            shape((count, keys), f32),
            shape((count, queries), b16),
            shape((count, keys), b16),
            shape((count, keys), b16),
            shape((count, queries), b16),
            shape((queries // HD, count, HD), f32),
        ],
        compiler_params=pltpu.CompilerParams(vmem_limit_bytes=56 * 1024 * 1024),
        cost_estimate=pl.CostEstimate(
            flops=2 * count * depth * (queries + 2 * keys) + 4 * count * count * queries,
            bytes_accessed=32 * 1024 * 1024,
            transcendentals=count * count * queries // HD,
        ),
    )(tokens, gain[None], *weights, query_gain[None], key_gain[None], cosine, sine, segment_column, segment_row)


def attention_back_kernel(
    step,
    hidden_low, output_weight, queries, keys, values, totals, query_raw, key_raw,
    query_gain, key_gain, cosine, sine, segment_column, segment_row,
    raw_out, query_gain_out, key_gain_out,
    upstream, query_grad, key_grad, value_grad,
):
    count = hidden_low.shape[0]
    query_heads = queries.shape[1] // HD
    value_heads = keys.shape[1] // HD
    group = query_heads // value_heads
    across_last = (((1,), (1,)), ((), ()))
    down_first = (((0,), (0,)), ((), ()))

    def project(rows):
        upstream[rows, :] = lax.dot_general(
            hidden_low[rows, :],
            output_weight[...],
            across_last,
            preferred_element_type=jnp.float32,
        ).astype(jnp.bfloat16)

    loop_rows(count, step, project)
    key_grad[...] = jnp.zeros_like(key_grad)
    value_grad[...] = jnp.zeros_like(value_grad)

    def head_step(head, carry):
        own = head_columns(head)
        shared = head_columns(head // group)
        for begin in range(0, count, step):
            reach = begin + step
            rows, before = pl.ds(begin, step), pl.ds(0, reach)
            scores = lax.dot_general(
                queries[rows, own],
                keys[before, shared],
                across_last,
                preferred_element_type=jnp.float32,
            ) * HD ** (-0.5)
            allowed = block_mask(segment_column, segment_row, begin, step, reach)
            chance = jnp.exp(jnp.where(allowed, scores, masked) - totals[head, rows, :][:, :1])
            incoming = upstream[rows, own]
            value_grad[before, shared] += lax.dot_general(
                chance.astype(jnp.bfloat16),
                incoming,
                down_first,
                preferred_element_type=jnp.float32,
            )
            along = lax.dot_general(
                incoming, values[before, shared], across_last, preferred_element_type=jnp.float32
            )
            center = jnp.sum(along * chance, axis=-1, keepdims=True)
            score_grad = (chance * (along - center)).astype(jnp.bfloat16)
            query_grad[rows, own] = jnp.dot(
                score_grad, keys[before, shared], preferred_element_type=jnp.float32
            ) * HD ** (-0.5)
            key_grad[before, shared] += lax.dot_general(
                score_grad, queries[rows, own], down_first, preferred_element_type=jnp.float32
            ) * HD ** (-0.5)
        return carry

    lax.fori_loop(0, query_heads, head_step, 0)
    query_gain_out[...] = jnp.zeros_like(query_gain_out)
    key_gain_out[...] = jnp.zeros_like(key_gain_out)

    def finish(rows):
        for grad, raw, head_gain, gain_out, heads, place in (
            (query_grad, query_raw, query_gain, query_gain_out, query_heads, 0),
            (key_grad, key_raw, key_gain, key_gain_out, value_heads, query_heads),
        ):
            for head in range(heads):
                columns = slice(head * HD, (head + 1) * HD)
                upward = grad[rows, columns]
                unit_grad = upward * cosine[rows, :] - pltpu.roll(upward, HD // 2, 1) * sine[rows, :]
                value = raw[rows, columns]
                inverse = rms_inverse(value)
                product = unit_grad * (value * inverse)
                gain_out[...] += jnp.sum(product.reshape(-1, 8, HD), axis=0)
                begin = (place + head) * HD
                raw_out[rows, begin : begin + HD] = norm_back(
                    unit_grad, value, inverse, head_gain[...]
                ).astype(jnp.bfloat16)
        begin = (query_heads + value_heads) * HD
        raw_out[rows, begin:] = value_grad[rows, :].astype(jnp.bfloat16)

    loop_rows(count, 64, finish)


def attention_back(
    hidden_low, output_weight, queries, keys, values, totals, query_raw, key_raw,
    query_gain, key_gain, cosine, sine, segment_column, segment_row,
):
    count = hidden_low.shape[0]
    query_columns, key_columns = queries.shape[1], keys.shape[1]
    f32, b16 = jnp.float32, jnp.bfloat16
    shape = jax.ShapeDtypeStruct
    return pl.pallas_call(
        functools.partial(attention_back_kernel, 256),
        out_shape=[
            shape((count, query_columns + 2 * key_columns), b16),
            shape((8, HD), f32),
            shape((8, HD), f32),
        ],
        scratch_shapes=[
            pltpu.VMEM((count, query_columns), b16),
            pltpu.VMEM((count, query_columns), f32),
            pltpu.VMEM((count, key_columns), f32),
            pltpu.VMEM((count, key_columns), f32),
        ],
        compiler_params=pltpu.CompilerParams(vmem_limit_bytes=56 * 1024 * 1024),
        cost_estimate=pl.CostEstimate(
            flops=2 * count * hidden_low.shape[1] * query_columns + 10 * count * count * query_columns,
            bytes_accessed=24 * 1024 * 1024,
            transcendentals=count * count * query_columns // HD,
        ),
    )(
        hidden_low, output_weight, queries, keys, values, totals, query_raw, key_raw,
        query_gain[None], key_gain[None], cosine, sine, segment_column, segment_row,
    )


def finish_kernel(columns, number, *refs):
    inputs, gains = refs[:number], refs[number]
    outs, held = refs[number + 1 : -number - 2], refs[-number - 2 : -2]
    in_sems, out_sems = refs[-2:]
    rows = outs[number - 1].shape[0]
    fetches = [
        pltpu.make_async_copy(source, target, in_sems.at[index])
        for index, (source, target) in enumerate(zip(inputs, held))
    ]
    for copy in fetches:
        copy.start()
    stores = [[pltpu.make_async_copy(held[k], outs[k], out_sems.at[k])] for k in range(number - 1)]
    begin, last = 0, []
    for k, count in enumerate(columns):
        last.append(
            pltpu.make_async_copy(
                held[-1].at[pl.ds(0, rows), pl.ds(begin, count)],
                outs[number - 1 + k],
                out_sems.at[number - 1 + k],
            )
        )
        begin += count
    stores.append(last)
    for row, out in zip((0, 1, 8, 9), outs[number + 2 :]):
        out[...] = gains[row : row + 1, : out.shape[1]]
    for fetch, group in zip(fetches, stores):
        fetch.wait()
        for copy in group:
            copy.start()
    for group in stores:
        for copy in group:
            copy.wait()


def finish(columns, head_width, arrays, raw, gains):
    shape = jax.ShapeDtypeStruct
    any_space = pl.BlockSpec(memory_space=pl.ANY)
    in_vmem = pl.BlockSpec(memory_space=pltpu.VMEM)
    width = raw.shape[0] - 8
    number = len(arrays) + 1
    outs = [shape(value.shape, value.dtype) for value in arrays]
    outs += [shape((width, count), jnp.float32) for count in columns]
    outs += [shape((1, count), jnp.float32) for count in (width, width, head_width, head_width)]
    return pl.pallas_call(
        functools.partial(finish_kernel, columns, number),
        out_shape=outs,
        in_specs=[any_space] * number + [in_vmem],
        out_specs=[any_space] * (number + 2) + [in_vmem] * 4,
        scratch_shapes=[pltpu.VMEM(value.shape, value.dtype) for value in (*arrays, raw)]
        + [pltpu.SemaphoreType.DMA((number,)), pltpu.SemaphoreType.DMA((number + 2,))],
        compiler_params=pltpu.CompilerParams(vmem_limit_bytes=60 * 1024 * 1024),
    )(*arrays, raw, gains)


def plain_shards(
    tokens,
    attention_gain,
    query_weight,
    key_weight,
    value_weight,
    query_gain,
    key_gain,
    output_weight,
    feedforward_gain,
    gate_weight,
    up_weight,
    down_weight,
    segment_numbers,
    positions,
    cotangent,
):
    count = tokens.shape[0]
    batch = count // SEQ_LEN
    query_heads = query_weight.shape[1] // HD
    value_heads = key_weight.shape[1] // HD
    group = query_heads // value_heads
    inputs = tokens.astype(jnp.float32)
    first_inverse = rms_inverse(inputs)
    first_normed = inputs * first_inverse
    normed_low = (first_normed * attention_gain).astype(jnp.bfloat16)
    query_raw = jnp.dot(normed_low, query_weight, preferred_element_type=jnp.float32).reshape(
        count, query_heads, HD
    )
    key_raw = jnp.dot(normed_low, key_weight, preferred_element_type=jnp.float32).reshape(
        count, value_heads, HD
    )
    value_low = jnp.dot(normed_low, value_weight, preferred_element_type=jnp.float32).astype(
        jnp.bfloat16
    )
    cosine, sine = rotary_tables(positions)
    cosine = cosine[:, None]
    sine = sine[:, None]
    query_inverse = rms_inverse(query_raw)
    query_unit = query_raw * query_inverse
    query_low = rotate(query_unit * query_gain, cosine, sine).astype(jnp.bfloat16)
    key_inverse = rms_inverse(key_raw)
    key_unit = key_raw * key_inverse
    key_low = rotate(key_unit * key_gain, cosine, sine).astype(jnp.bfloat16)
    queries = query_low.reshape(batch, SEQ_LEN, value_heads, group, HD)
    keys = key_low.reshape(batch, SEQ_LEN, value_heads, HD)
    values = value_low.reshape(batch, SEQ_LEN, value_heads, HD)
    segments = segment_numbers.reshape(batch, SEQ_LEN)
    mixed, totals = lax.map(attend, (queries, keys, values, segments))
    mixed_low = mixed.reshape(count, query_heads * HD).astype(jnp.bfloat16)
    attention = lax.psum(
        jnp.dot(mixed_low, output_weight, preferred_element_type=jnp.float32), "tensor"
    )
    hidden = inputs + attention
    second_inverse = rms_inverse(hidden)
    second_normed = hidden * second_inverse
    second_low = (second_normed * feedforward_gain).astype(jnp.bfloat16)
    gate = jnp.dot(second_low, gate_weight, preferred_element_type=jnp.float32)
    upward = jnp.dot(second_low, up_weight, preferred_element_type=jnp.float32)
    sigmoid_gate = jax.nn.sigmoid(gate)
    activated = gate * sigmoid_gate
    product_low = (activated * upward).astype(jnp.bfloat16)
    feedforward = lax.psum(
        jnp.dot(product_low, down_weight, preferred_element_type=jnp.float32), "tensor"
    )
    layer_output = (hidden + feedforward).astype(jnp.bfloat16)
    down_grad = jnp.einsum("tf,td->fd", product_low, cotangent, preferred_element_type=jnp.float32)
    product_grad = jnp.einsum(
        "td,fd->tf", cotangent, down_weight, preferred_element_type=jnp.float32
    )
    gate_grad_low = (
        product_grad * upward * sigmoid_gate * (1.0 + gate * (1.0 - sigmoid_gate))
    ).astype(jnp.bfloat16)
    upward_grad_low = (product_grad * activated).astype(jnp.bfloat16)
    gate_weight_grad = jnp.einsum(
        "td,tf->df", second_low, gate_grad_low, preferred_element_type=jnp.float32
    )
    upward_weight_grad = jnp.einsum(
        "td,tf->df", second_low, upward_grad_low, preferred_element_type=jnp.float32
    )
    second_part = jnp.einsum(
        "tf,df->td", gate_grad_low, gate_weight, preferred_element_type=jnp.float32
    )
    second_part = second_part + jnp.einsum(
        "tf,df->td", upward_grad_low, up_weight, preferred_element_type=jnp.float32
    )
    second_grad = lax.psum(second_part, "tensor")
    second_gain_grad = jnp.sum(second_grad * second_normed, axis=0)
    hidden_grad = cotangent.astype(jnp.float32) + norm_back(
        second_grad, hidden, second_inverse, feedforward_gain
    )
    hidden_low = hidden_grad.astype(jnp.bfloat16)
    output_weight_grad = jnp.einsum(
        "tc,td->cd", mixed_low, hidden_low, preferred_element_type=jnp.float32
    )
    mixed_grad = jnp.einsum(
        "td,cd->tc", hidden_low, output_weight, preferred_element_type=jnp.float32
    ).astype(jnp.bfloat16)
    upstream = mixed_grad.reshape(batch, SEQ_LEN, value_heads, group, HD)
    query_back, key_back, value_back = lax.map(
        attend_back, (queries, keys, values, segments, totals, upstream)
    )
    query_unit_grad = rotate_back(query_back.reshape(count, query_heads, HD), cosine, sine)
    key_unit_grad = rotate_back(key_back.reshape(count, value_heads, HD), cosine, sine)
    query_gain_part = jnp.sum(query_unit_grad * query_unit, axis=(0, 1))
    key_gain_part = jnp.sum(key_unit_grad * key_unit, axis=(0, 1))
    query_raw_grad = (
        norm_back(query_unit_grad, query_raw, query_inverse, query_gain)
        .reshape(count, query_heads * HD)
        .astype(jnp.bfloat16)
    )
    key_raw_grad = (
        norm_back(key_unit_grad, key_raw, key_inverse, key_gain)
        .reshape(count, value_heads * HD)
        .astype(jnp.bfloat16)
    )
    value_raw_grad = value_back.reshape(count, value_heads * HD).astype(jnp.bfloat16)
    query_weight_grad = jnp.einsum(
        "td,tc->dc", normed_low, query_raw_grad, preferred_element_type=jnp.float32
    )
    key_weight_grad = jnp.einsum(
        "td,tc->dc", normed_low, key_raw_grad, preferred_element_type=jnp.float32
    )
    value_weight_grad = jnp.einsum(
        "td,tc->dc", normed_low, value_raw_grad, preferred_element_type=jnp.float32
    )
    first_part = jnp.einsum(
        "tc,dc->td", query_raw_grad, query_weight, preferred_element_type=jnp.float32
    )
    first_part = first_part + jnp.einsum(
        "tc,dc->td", key_raw_grad, key_weight, preferred_element_type=jnp.float32
    )
    first_part = first_part + jnp.einsum(
        "tc,dc->td", value_raw_grad, value_weight, preferred_element_type=jnp.float32
    )
    first_grad, query_gain_grad, key_gain_grad = lax.psum(
        (first_part, query_gain_part, key_gain_part), "tensor"
    )
    first_gain_grad = jnp.sum(first_grad * first_normed, axis=0)
    tokens_gradient = (
        hidden_grad + norm_back(first_grad, inputs, first_inverse, attention_gain)
    ).astype(jnp.bfloat16)
    summed = (
        lax.psum_scatter(first_gain_grad, "dp", scatter_dimension=0, tiled=True),
        lax.psum_scatter(query_weight_grad, "dp", scatter_dimension=0, tiled=True),
        lax.psum_scatter(key_weight_grad, "dp", scatter_dimension=0, tiled=True),
        lax.psum_scatter(value_weight_grad, "dp", scatter_dimension=0, tiled=True),
        lax.psum_scatter(query_gain_grad, "dp", scatter_dimension=0, tiled=True),
        lax.psum_scatter(key_gain_grad, "dp", scatter_dimension=0, tiled=True),
        lax.psum_scatter(output_weight_grad, "dp", scatter_dimension=1, tiled=True),
        lax.psum_scatter(second_gain_grad, "dp", scatter_dimension=0, tiled=True),
        lax.psum_scatter(gate_weight_grad, "dp", scatter_dimension=0, tiled=True),
        lax.psum_scatter(upward_weight_grad, "dp", scatter_dimension=0, tiled=True),
        lax.psum_scatter(down_grad, "dp", scatter_dimension=1, tiled=True),
    )
    return (
        layer_output,
        tokens_gradient,
        summed[0],
        summed[1],
        summed[2],
        summed[3],
        summed[4],
        summed[5],
        summed[6],
        summed[7],
        summed[8],
        summed[9],
        summed[10],
    )


def shards(
    dp,
    tokens,
    attention_gain,
    query_weight,
    key_weight,
    value_weight,
    query_gain,
    key_gain,
    output_weight,
    feedforward_gain,
    gate_weight,
    up_weight,
    down_weight,
    segment_numbers,
    positions,
    cotangent,
):
    count, depth = tokens.shape
    width = depth // dp
    high = dp // 2
    core = lax.axis_index("tensor") % 2
    upstream_first = lax.ppermute(
        lax.dynamic_slice_in_dim(cotangent, core * (count // 2), 3 * count // 16, 0).astype(jnp.float32),
        "dp",
        [(i, i ^ 2) for i in range(dp)],
    )

    cosine, sine = rotary_tables(positions)
    sine = jnp.concatenate([-sine[:, : HD // 2], sine[:, HD // 2 :]], axis=1)
    tables = (cosine, sine, segment_numbers[:, None], segment_numbers[None])
    normed_low, query_raw, key_raw, queries, keys, values, mixed_low, totals = attention(
        tokens,
        attention_gain,
        (query_weight, key_weight, value_weight),
        query_gain,
        key_gain,
        *tables,
    )
    (
        hidden,
        second_part,
        low_own,
        product_own,
        gate_own,
        upward_own,
        low_pair,
        product_pair,
        gate_pair,
        upward_pair,
        upstream_pair,
    ) = front(
        mixed_low,
        output_weight,
        tokens,
        cotangent,
        upstream_first,
        feedforward_gain,
        gate_weight,
        up_weight,
        down_weight,
    )[:11]
    hidden_grad, hidden_low, out_part, down_weight_grad, gate_ready, gate_given, gate_kept = middle(
        second_part,
        hidden,
        cotangent,
        upstream_pair,
        product_own,
        product_pair,
        gate_own,
        gate_pair,
        low_own,
        low_pair,
        feedforward_gain,
        down_weight,
    )
    gate_middle, gate_inward = (
        lax.ppermute(gate_ready, "dp", [(2 * a + k, 2 * b + k) for a, b in pairs for k in (0, 1)])
        for pairs in (((1, 2), (2, 1)), ((0, 1), (3, 2)))
    )
    gate_moved = lax.ppermute(gate_given, "dp", [(i, i ^ 1) for i in range(dp)])
    raw_grad, query_gain_part, key_gain_part = attention_back(
        hidden_low,
        output_weight,
        queries,
        keys,
        values,
        totals,
        query_raw,
        key_raw,
        query_gain,
        key_gain,
        *tables,
    )

    lines = [
        jnp.pad(value.reshape(dp, -1), ((0, 0), (0, raw_grad.shape[1] - value.size // dp)))
        for value in (jnp.sum(query_gain_part, axis=0), jnp.sum(key_gain_part, axis=0))
    ]
    gain_lines = jnp.pad(jnp.stack(lines, axis=1), ((0, 0), (0, 6), (0, 0)))

    (
        layer_output,
        tokens_gradient,
        gate_weight_grad,
        up_weight_grad,
        raw_whole,
        output_weight_grad,
        gains,
    ) = (
        rear(
            [line_order(high, p) for p in range(high)],
            [gate_middle, gate_inward, gate_kept + gate_moved]
            + [low_own, low_pair, upward_own, upward_pair]
            + [normed_low, raw_grad, hidden_low, mixed_low],
            gain_lines,
            [out_part, hidden, hidden_grad, tokens],
            [query_weight, key_weight, value_weight, gate_weight, up_weight],
            attention_gain,
            feedforward_gain,
        )[:7]
    )
    (
        layer_output,
        tokens_gradient,
        gate_weight_grad,
        up_weight_grad,
        output_weight_grad,
        down_weight_grad,
        query_weight_grad,
        key_weight_grad,
        value_weight_grad,
        attention_gain_grad,
        feedforward_gain_grad,
        query_gain_grad,
        key_gain_grad,
    ) = finish(
        (query_weight.shape[1], key_weight.shape[1], value_weight.shape[1]),
        HD // dp,
        [
            layer_output,
            tokens_gradient,
            gate_weight_grad,
            up_weight_grad,
            output_weight_grad,
            down_weight_grad,
        ],
        raw_whole,
        gains,
    )
    return (
        layer_output,
        tokens_gradient,
        attention_gain_grad[0],
        query_weight_grad,
        key_weight_grad,
        value_weight_grad,
        query_gain_grad[0],
        key_gain_grad[0],
        output_weight_grad,
        feedforward_gain_grad[0],
        gate_weight_grad,
        up_weight_grad,
        down_weight_grad,
    )


def solution(mesh):
    dp, tensor = mesh.shape["dp"], mesh.shape["tensor"]

    def program(*args):
        if dp == 8 and tensor == 4 and args[0].shape[0] == SEQ_LEN:
            return shards(dp, *args)
        return plain_shards(*args)

    return jax.shard_map(
        program,
        mesh=mesh,
        in_specs=(
            P("dp", None),
            P(),
            P(None, "tensor"),
            P(None, "tensor"),
            P(None, "tensor"),
            P(),
            P(),
            P("tensor", None),
            P(),
            P(None, "tensor"),
            P(None, "tensor"),
            P("tensor", None),
            P("dp"),
            P("dp"),
            P("dp", None),
        ),
        out_specs=(
            P("dp", None),
            P("dp", None),
            P("dp"),
            P("dp", "tensor"),
            P("dp", "tensor"),
            P("dp", "tensor"),
            P("dp"),
            P("dp"),
            P("tensor", "dp"),
            P("dp"),
            P("dp", "tensor"),
            P("dp", "tensor"),
            P("tensor", "dp"),
        ),
        check_vma=False,
    )
```

```python
import functools

import jax
import jax.numpy as jnp
from jax import lax
from jax.experimental import pallas as pl
from jax.experimental.pallas import tpu as pltpu
from jax.sharding import PartitionSpec as P

HD = 128
SEQ_LEN = 1024


epsilon = 1e-06
rope_base = 1000000.0
masked = -1e30


def rms_inverse(value):
    return lax.rsqrt(jnp.mean(value * value, axis=-1, keepdims=True) + epsilon)


def norm_back(upstream, value, inverse, gain):
    scaled = upstream * gain
    return inverse * scaled - value * inverse**3 * jnp.mean(scaled * value, axis=-1, keepdims=True)


def rotary_tables(positions):
    exponent = jnp.arange(0, HD, 2, dtype=jnp.float32) / HD
    frequency = rope_base ** (-exponent)
    phase = positions.astype(jnp.float32)[:, None] * frequency[None, :]
    phase = jnp.concatenate([phase, phase], axis=-1)
    return (jnp.cos(phase), jnp.sin(phase))


def rotate(value, cosine, sine):
    half = value.shape[-1] // 2
    turned = jnp.concatenate([-value[..., half:], value[..., :half]], axis=-1)
    return value * cosine + turned * sine


def rotate_back(upstream, cosine, sine):
    half = upstream.shape[-1] // 2
    moved = upstream * sine
    return upstream * cosine + jnp.concatenate([moved[..., half:], -moved[..., :half]], axis=-1)


def block_scores(query_rows, keys, row_segments, segments, begin):
    scores = jnp.einsum(
        "rkgd,tkd->kgrt", query_rows, keys, preferred_element_type=jnp.float32
    ) * HD ** (-0.5)
    rows = begin + lax.iota(jnp.int32, query_rows.shape[0])
    columns = lax.iota(jnp.int32, keys.shape[0])
    allowed = (row_segments[:, None] == segments[None, :]) & (rows[:, None] >= columns[None, :])
    return jnp.where(allowed[None, None], scores, masked)


def attend(item):
    queries, keys, values, segments = item
    length = queries.shape[0]
    width = min(512, length)
    outputs = []
    totals = []
    for begin in range(0, length, width):
        scores = block_scores(
            queries[begin : begin + width], keys, segments[begin : begin + width], segments, begin
        )
        peak = jnp.max(scores, axis=-1, keepdims=True)
        expons = jnp.exp(scores - peak)
        total = jnp.sum(expons, axis=-1, keepdims=True)
        chance_low = (expons / total).astype(jnp.bfloat16)
        outputs.append(
            jnp.einsum("kgrt,tkd->rkgd", chance_low, values, preferred_element_type=jnp.float32)
        )
        totals.append(peak + jnp.log(total))
    return (jnp.concatenate(outputs, axis=0), jnp.concatenate(totals, axis=2))


def attend_back(item):
    queries, keys, values, segments, totals, upstream = item
    length = queries.shape[0]
    width = min(512, length)
    query_parts = []
    key_grad = jnp.zeros(keys.shape, jnp.float32)
    value_grad = jnp.zeros(values.shape, jnp.float32)
    for begin in range(0, length, width):
        rows = queries[begin : begin + width]
        scores = block_scores(rows, keys, segments[begin : begin + width], segments, begin)
        chance = jnp.exp(scores - totals[:, :, begin : begin + width])
        chance_low = chance.astype(jnp.bfloat16)
        incoming = upstream[begin : begin + width]
        value_grad = value_grad + jnp.einsum(
            "kgrt,rkgd->tkd", chance_low, incoming, preferred_element_type=jnp.float32
        )
        along = jnp.einsum("rkgd,tkd->kgrt", incoming, values, preferred_element_type=jnp.float32)
        center = jnp.sum(along * chance, axis=-1, keepdims=True)
        score_grad = (chance * (along - center)).astype(jnp.bfloat16)
        query_parts.append(
            jnp.einsum("kgrt,tkd->rkgd", score_grad, keys, preferred_element_type=jnp.float32)
            * HD ** (-0.5)
        )
        key_grad = key_grad + jnp.einsum(
            "kgrt,rkgd->tkd", score_grad, rows, preferred_element_type=jnp.float32
        ) * HD ** (-0.5)
    return (jnp.concatenate(query_parts, axis=0), key_grad, value_grad)


def dot(left, right):
    return jnp.dot(left, right, preferred_element_type=jnp.float32)


def dot_back(left, right):
    return jnp.einsum("tc,dc->td", left, right, preferred_element_type=jnp.float32)


def dot_tokens(left, right):
    return jnp.einsum("tm,tn->mn", left, right, preferred_element_type=jnp.float32)


def line_order(high, place):
    steps = {}
    for block in range(high):
        if block > place:
            steps[block] = high - block + place
        elif block < place:
            steps[block] = high - place + block
    return sorted(steps, key=lambda block: (steps[block], block)) + [place]


MESH = pl.DeviceIdType.MESH


def neighbours():
    dp, tensor = lax.axis_index("dp"), lax.axis_index("tensor")
    core = lax.rem(tensor, 2)
    sibling = {"tensor": tensor + 1 - 2 * core}
    facing = {"tensor": lax.rem(tensor + 2, 4)}
    place = dp // 2
    pair = {"dp": dp + 2 * (1 - 2 * lax.rem(place, 2))}
    return core, sibling, facing, pair


def greet(devices):
    barrier = pltpu.get_barrier_semaphore()
    for device in devices:
        pl.semaphore_signal(barrier, inc=1, device_id=device, device_id_type=MESH)
    pl.semaphore_wait(barrier, len(devices))


def loop_rows(count, step, body):
    def run(index, carry):
        body(pl.ds(pl.multiple_of(index * step, step), step))
        return carry

    lax.fori_loop(0, count // step, run, 0)


def sequence_rows(size, core, which, k):
    side = core if which == 0 else 1 - core
    return pl.multiple_of(side * 4 * size + k * size, size)


def remote(source, target, sems, k, device):
    return pltpu.make_async_remote_copy(
        src_ref=source, dst_ref=target, send_sem=sems.at[0, k], recv_sem=sems.at[1, k],
        device_id=device, device_id_type=MESH,
    )


def front_kernel(
    size, first,
    mixed_hbm, output_weight_hbm, tokens_hbm, upstream_hbm, upstream_first,
    gain, gate_hbm, up_hbm, down_hbm,
    hidden_out, second_out, low_own, product_own, gate_own, upward_own,
    low_pair, product_pair, gate_pair, upward_pair, upstream_pair,
    c_landed, n_recv, n_side, u_recv, u_side,
    mixed, output_weight, gate_weight, up_weight, down_weight,
    x_send, x_recv, back_recv, tok, hid, z_send, low, rows16, pair16, tiles, stage, terms,
    load_sems, c_sems, x_sems, back_sems, n_sems, n_side_sems, u_sems, u_side_sems,
    tok_sems, hid_sems, low_sems, wave_sems, tile_sems, stage_sems, term_sems, join_sems,
):
    core, sibling, facing, pair = neighbours()
    depth = gain.shape[1]
    half = 4 * size
    units = gate_weight.shape[1]
    begin = functools.partial(sequence_rows, size, core)
    across_last = (((1,), (1,)), ((), ()))
    rest = half - first
    loads = [
        pltpu.make_async_copy(source, target, load_sems.at[index])
        for index, (source, target) in enumerate(
            [
                (
                    upstream_hbm.at[pl.ds(pl.multiple_of(core * half + first, 16), rest)],
                    rows16.at[pl.ds(0, rest)],
                ),
                (mixed_hbm, mixed),
                (output_weight_hbm, output_weight),
                (gate_hbm, gate_weight),
                (up_hbm, up_weight),
                (down_hbm, down_weight),
            ]
        )
    ]
    for load in loads:
        load.start()
    greet([sibling, facing, pair])

    c_copies = [
        remote(terms.at[pl.ds(k * size, size)], c_landed.at[k], c_sems, k, sibling) for k in range(4)
    ]
    x_copies = [remote(x_send.at[k], x_recv.at[k], x_sems, k, facing) for k in range(4)]
    back_copies = [remote(x_send.at[k], back_recv.at[k], back_sems, k, sibling) for k in range(4)]
    part = pl.ds(pl.multiple_of(lax.axis_index("tensor") // 2 * (size // 2), 16), size // 2)
    n_copies = [
        remote(z_send.at[k % 2], n_recv.at[k], n_sems, k, pair)
        if k < 2
        else remote(z_send.at[k % 2, part], n_recv.at[k, part], n_sems, k, pair)
        for k in range(4)
    ]
    n_joins = [
        remote(n_recv.at[k, part], n_recv.at[k, part], join_sems, k - 2, facing) for k in (2, 3)
    ]
    n_sides = [remote(n_recv.at[k], n_side.at[k], n_side_sems, k, sibling) for k in range(4)]
    u_rows = [(0, rest - 2 * size), (rest - 2 * size, size), (rest - size, size)]
    u_buffers = [hid.at[0, pl.ds(0, u_rows[0][1])], z_send.at[0], z_send.at[1]]
    u_copies = [
        remote(u_buffers[j], u_recv.at[pl.ds(start, number)], u_sems, j, pair)
        for j, (start, number) in enumerate(u_rows)
    ]
    u_sides = [remote(upstream_first, u_side.at[pl.ds(0, first)], u_side_sems, 0, sibling)] + [
        remote(
            u_recv.at[pl.ds(start, number)],
            u_side.at[pl.ds(first + start, number)],
            u_side_sems,
            1 + j,
            sibling,
        )
        for j, (start, number) in enumerate(u_rows)
    ]

    def stage_load(source, slot, number):
        return pltpu.make_async_copy(source, stage.at[slot, pl.ds(0, number)], stage_sems.at[slot])

    def upstream_send(j):
        start, number = u_rows[j]

        def run(row):
            u_buffers[j][row, :] = rows16[
                pl.ds(pl.multiple_of(start + row.start, 16), row.size), :
            ].astype(jnp.float32)

        loop_rows(number, 16, run)
        u_copies[j].start()

    def upstream_forward(j):
        u_copies[j].wait_recv()
        u_sides[1 + j].start()

    def attention_terms(k):
        rows = jnp.concatenate(
            [mixed[pl.ds(begin(which, k), size), :] for which in range(2)], axis=0
        )

        def run(column):
            both = jnp.dot(rows, output_weight[:, column], preferred_element_type=jnp.float32)
            x_send[k, :, column] = both[:size]
            terms[pl.ds(k * size, size), column] = both[size:]

        loop_rows(depth, 1024, run)
        c_copies[k].start()

    def attention_cores(k):
        c_copies[k].wait_recv()
        stage_load(c_landed.at[k], k % 2, size).start()
        stage_load(c_landed.at[k], k % 2, size).wait()

        def run(row):
            x_send[k, row, :] = x_send[k, row, :] + stage[k % 2, row, :]

        loop_rows(size, 16, run)
        x_copies[k].start()

    def attention_chips(k):
        x_copies[k].wait()

        def run(row):
            x_send[k, row, :] = x_send[k, row, :] + x_recv[k, row, :]

        loop_rows(size, 16, run)
        back_copies[k].start()

    def token_loads(k):
        return [
            pltpu.make_async_copy(
                tokens_hbm.at[pl.ds(begin(which, k), size)], tok.at[which], tok_sems.at[which]
            )
            for which in range(2)
        ]

    def hidden_stores(k):
        return [
            pltpu.make_async_copy(
                hid.at[which], hidden_out.at[pl.ds(begin(which, k), size)], hid_sems.at[which]
            )
            for which in range(2)
        ]

    def low_rows(which, k, row):
        side = core if which == 0 else 1 - core
        return pl.ds(pl.multiple_of((side + k % 2 * 2) * size + row.start, 16), row.size)

    def normed(k):
        for load in token_loads(k):
            load.wait()
        if k > 0:
            for store in hidden_stores(k - 1):
                store.wait()
        if k < 2:
            u_copies[1 + k].wait_send()
        else:
            n_copies[k - 2].wait_send()

        def run(which, source, row):
            value = tok[which, row, :].astype(jnp.float32) + source[k, row, :]
            hid[which, row, :] = value
            unit = value * lax.rsqrt(jnp.mean(value * value, axis=-1, keepdims=True) + epsilon)
            if which == 0:
                z_send[k % 2, row, :] = unit
            low[0, low_rows(which, k, row), :] = (unit * gain[...]).astype(jnp.bfloat16)

        loop_rows(size, 16, functools.partial(run, 0, x_send))
        n_copies[k].start()
        back_copies[k].wait_recv()
        loop_rows(size, 16, functools.partial(run, 1, back_recv))
        for store in hidden_stores(k):
            store.start()
        if k < 3:
            for load in token_loads(k + 1):
                load.start()

    def pipeline(pieces):
        def bring(index):
            before, source, number, _ = pieces[index]
            if before is not None:
                before.wait_recv()
            stage_load(source, index % 2, number).start()

        bring(0)
        for index, (_, source, number, consume) in enumerate(pieces):
            if index + 1 < len(pieces):
                bring(index + 1)
            stage_load(source, index % 2, number).wait()
            loop_rows(number, 16, functools.partial(consume, index % 2))

    def pair_join(k):
        n_copies[k].wait_recv()
        n_joins[k - 2].start()

    def pair_forward(k):
        if k < 2:
            n_copies[k].wait_recv()
        else:
            n_joins[k - 2].wait_recv()
        n_sides[k].start()

    def pair_rows(chunks):
        def consume(k, which, slot, row):
            low[1, low_rows(which, k, row), :] = (stage[slot, row, :] * gain[...]).astype(
                jnp.bfloat16
            )

        pipeline(
            [
                (
                    n_sides[k] if which else None,
                    (n_side if which else n_recv).at[k],
                    size,
                    functools.partial(consume, k, which),
                )
                for which in range(2)
                for k in chunks
            ]
        )

    def wave_copies(local, distant, sems, wave, inwards=False):
        copies = []
        for part in range(4):
            here = local.at[pl.ds(part * size, size)]
            there = distant.at[pl.ds(part % 2 * half + (2 * wave + part // 2) * size, size)]
            source, target = (there, here) if inwards else (here, there)
            copies.append(pltpu.make_async_copy(source, target, sems.at[part]))
        return copies

    def pair_stores(wave):
        return wave_copies(pair16, upstream_pair, wave_sems.at[1], wave)

    def upstream_wave(wave):
        def consume(which, start, slot, row):
            side = core if which == 0 else 1 - core
            chunk, within = start // size, start % size
            place = pl.multiple_of((2 * chunk + side) * size + within + row.start, 16)
            pair16[pl.ds(place, row.size), :] = stage[slot, row, :].astype(jnp.bfloat16)

        if wave == 0:
            own = [
                (upstream_first.at[pl.ds(0, size)], size, 0),
                (upstream_first.at[pl.ds(size, first - size)], first - size, size),
                (u_recv.at[pl.ds(0, u_rows[0][1])], u_rows[0][1], first),
            ]
            waits = [u_sides[0], u_sides[1]]
        else:
            own = [(u_recv.at[pl.ds(u_rows[j][0], size)], size, (j - 1) * size) for j in (1, 2)]
            waits = [u_sides[2], u_sides[3]]
        pieces = [
            (None, source, number, functools.partial(consume, 0, start))
            for source, number, start in own
        ]
        if wave == 0:
            waits[0].wait_recv()
            waits[1].wait_recv()
            waits = [None, None]
        pieces += [
            (
                waits[j],
                u_side.at[pl.ds((2 * wave + j) * size, size)],
                size,
                functools.partial(consume, 1, j * size),
            )
            for j in range(2)
        ]
        pipeline(pieces)
        for copy in pair_stores(wave):
            copy.start()

    def term_stores(wave):
        return wave_copies(terms, second_out, term_sems, wave)

    def low_stores(wave, index):
        return wave_copies(low.at[index], low_pair if index else low_own, low_sems.at[index], wave)

    def tile_stores(wave, index):
        outs = (
            (product_pair, gate_pair, upward_pair) if index else (product_own, gate_own, upward_own)
        )
        return [
            copy
            for which in range(3)
            for copy in wave_copies(tiles.at[which], outs[which], tile_sems.at[which], wave)
        ]

    feeds = [(0, 0), (1, 0), (0, 1), (1, 1)]

    def fetches(wave):
        return wave_copies(rows16, upstream_hbm, wave_sems.at[0], wave, True)

    def feed(wave, index, part=None):
        number = feeds.index((wave, index))
        rows = slice(None) if part is None else pl.ds(part * 2 * size, 2 * size)
        if not part:
            if number > 0:
                for copy in tile_stores(*feeds[number - 1]):
                    copy.wait()
        if index == 0 and not part:
            for copy in fetches(wave):
                copy.wait()

        def run(column):
            gate = jnp.dot(
                low[index, rows], gate_weight[:, column], preferred_element_type=jnp.float32
            )
            upward = jnp.dot(
                low[index, rows], up_weight[:, column], preferred_element_type=jnp.float32
            )
            grad = lax.dot_general(
                (pair16 if index else rows16)[rows],
                down_weight[column, :],
                across_last,
                preferred_element_type=jnp.float32,
            )
            sigmoid_gate = jax.nn.sigmoid(gate)
            activated = gate * sigmoid_gate
            tiles[0, rows, column] = (activated * upward).astype(jnp.bfloat16)
            tiles[1, rows, column] = (
                grad * upward * sigmoid_gate * (1.0 + gate * (1.0 - sigmoid_gate))
            ).astype(jnp.bfloat16)
            tiles[2, rows, column] = (grad * activated).astype(jnp.bfloat16)

        loop_rows(units, 512, run)
        copies = tile_stores(wave, index) + low_stores(wave, index)
        for number, copy in enumerate(copies):
            if part is None or number % 4 // 2 == part:
                copy.start()
        if index == 0:
            if wave > 0 and not part:
                for copy in term_stores(wave - 1):
                    copy.wait()

            def second(column):
                terms[rows, column] = lax.dot_general(
                    tiles[1, rows],
                    gate_weight[column, :],
                    across_last,
                    preferred_element_type=jnp.float32,
                ) + lax.dot_general(
                    tiles[2, rows],
                    up_weight[column, :],
                    across_last,
                    preferred_element_type=jnp.float32,
                )

            loop_rows(depth, 1024 if part is not None else 512, second)
            for number, copy in enumerate(term_stores(wave)):
                if part is None or number // 2 == part:
                    copy.start()

    for load in token_loads(0):
        load.start()
    loads[0].wait()
    for j in range(3):
        upstream_send(j)
    u_sides[0].start()
    loads[1].wait()
    loads[2].wait()
    attention_terms(0)
    attention_terms(1)
    attention_cores(0)
    attention_terms(2)
    attention_cores(1)
    attention_terms(3)
    attention_cores(2)
    attention_cores(3)
    for copy in fetches(0):
        copy.start()
    upstream_forward(0)
    upstream_wave(0)
    attention_chips(0)
    u_copies[0].wait_send()
    upstream_forward(1)
    normed(0)
    for load in loads[3:]:
        load.wait()
    for k in range(4):
        c_copies[k].wait_send()
    feed(0, 0, 0)
    attention_chips(1)
    normed(1)
    upstream_forward(2)
    feed(0, 0, 1)
    attention_chips(2)
    for copy in low_stores(0, 0):
        copy.wait()
    normed(2)
    pair_forward(0)
    for copy in fetches(1):
        copy.start()
    feed(1, 0, 0)
    attention_chips(3)
    normed(3)
    feed(1, 0, 1)
    pair_forward(1)
    pair_rows((0, 1))
    pair_join(2)
    feed(0, 1)
    for copy in pair_stores(0):
        copy.wait()
    pair_join(3)
    pair_forward(2)
    upstream_wave(1)
    for copy in low_stores(0, 1):
        copy.wait()
    pair_rows((2,))
    feed(1, 1, 0)
    pair_forward(3)
    pair_rows((3,))
    feed(1, 1, 1)

    for k in range(4):
        back_copies[k].wait_send()
        n_sides[k].wait_send()
        u_sides[k].wait_send()
        if k >= 2:
            n_copies[k].wait_send()
            n_joins[k - 2].wait_send()
    ends = hidden_stores(3) + term_stores(1) + low_stores(1, 0) + low_stores(1, 1)
    for copy in ends + pair_stores(1) + tile_stores(1, 1):
        copy.wait()


def front(mixed, output_weight, tokens, upstream, upstream_first, gain, gate_weight, up_weight, down_weight):
    rows, depth = tokens.shape
    inner, units = mixed.shape[1], gate_weight.shape[1]
    first = upstream_first.shape[0]
    size = rows // 8
    f32, b16 = jnp.float32, jnp.bfloat16
    any_space = pl.BlockSpec(memory_space=pl.ANY)
    shape = jax.ShapeDtypeStruct
    outs = [shape((rows, depth), f32)] * 2
    outs += ([shape((rows, depth), b16)] + [shape((rows, units), b16)] * 3) * 2
    outs += [shape((rows, depth), b16)] + [shape((4, size, depth), f32)] * 3
    outs += [shape((4 * size - first, depth), f32), shape((4 * size, depth), f32)]
    dma = pltpu.SemaphoreType.DMA
    vmem = pltpu.VMEM
    return pl.pallas_call(
        functools.partial(front_kernel, size, first),
        out_shape=outs,
        in_specs=[any_space] * 5 + [pl.BlockSpec(memory_space=pltpu.VMEM)] + [any_space] * 3,
        out_specs=[any_space] * len(outs),
        scratch_shapes=[
            vmem((rows, inner), b16),
            vmem((inner, depth), b16),
            vmem((depth, units), b16),
            vmem((depth, units), b16),
            vmem((units, depth), b16),
            vmem((4, size, depth), f32),
            vmem((4, size, depth), f32),
            vmem((4, size, depth), f32),
            vmem((2, size, depth), b16),
            vmem((2, size, depth), f32),
            vmem((2, size, depth), f32),
            vmem((2, 4 * size, depth), b16),
            vmem((4 * size, depth), b16),
            vmem((4 * size, depth), b16),
            vmem((3, 4 * size, units), b16),
            vmem((2, size, depth), f32),
            vmem((4 * size, depth), f32),
            dma((6,)),
            *[dma((2, 4))] * 5,
            dma((2, 3)),
            dma((2, 4)),
            dma((2,)),
            dma((2,)),
            dma((2, 4)),
            dma((2, 4)),
            dma((3, 4)),
            dma((2,)),
            dma((4,)),
            dma((2, 2)),
        ],
        compiler_params=pltpu.CompilerParams(
            collective_id=1, has_side_effects=True, vmem_limit_bytes=63 * 1024 * 1024
        ),
        cost_estimate=pl.CostEstimate(
            flops=12 * rows * depth * units, bytes_accessed=6 * depth * units, transcendentals=0
        ),
    )(mixed, output_weight, tokens, upstream, upstream_first, gain[None], gate_weight, up_weight, down_weight)


def grid_neighbours():
    dp = lax.axis_index("dp")
    place, lane = dp // 2, lax.rem(dp, 2)
    towards = 1 - 2 * (place // 2)
    across = {"dp": dp + 1 - 2 * lane}
    inward, outward = {"dp": dp + 2 * towards}, {"dp": dp - 2 * towards}
    team = place // 2
    side = lax.rem(place, 2)
    inner = lax.rem(team + side, 2)
    return place, lane, team, side, inner, across, inward, outward


def greet_grid(always, inner, outward):
    barrier = pltpu.get_barrier_semaphore()
    for device in always:
        pl.semaphore_signal(barrier, inc=1, device_id=device, device_id_type=MESH)

    @pl.when(inner == 1)
    def _():
        pl.semaphore_signal(barrier, inc=1, device_id=outward, device_id_type=MESH)

    pl.semaphore_wait(barrier, len(always) + inner)


def middle_kernel(
    size,
    second_hbm, hidden_hbm, upstream_hbm, upstream_pair, product_own, product_pair,
    gate_own, gate_pair, low_own, low_pair, gain, down_hbm,
    grad_out, grad_low_out, out_part, weight_out, gate_ready, gate_given, gate_own_block,
    products, down_weight, columns, c_recv, x_send, x_recv, back_recv,
    y_send, y_recv, kept, in_recv, mid_recv, out_recv,
    hid, tok, grad, grad_low, out_stage, gate_send, gate_kept, gate_stage,
    load_sems, gate_load_sems, gate_sems, c_sems, x_sems, back_sems, y_sems, z_sems, column_sems,
    x_load_sems, hid_sems, tok_sems, grad_sems, low_sems, out_sems, weight_sems,
):
    core, sibling, facing, _ = neighbours()
    place, lane, team, side, inner, across, inward, outward = grid_neighbours()
    depth = gain.shape[1]
    units = down_weight.shape[0]
    width = columns.shape[-1]
    begin = functools.partial(sequence_rows, size, core)
    rows_in = 8 * size
    down_first = (((0,), (0,)), ((), ()))
    loads = [
        pltpu.make_async_copy(source, target, load_sems.at[index])
        for index, (source, target) in enumerate(
            [
                (product_own, products.at[pl.ds(0, rows_in)]),
                (product_pair, products.at[pl.ds(rows_in, rows_in)]),
                (down_hbm, down_weight),
            ]
        )
    ]
    gate_loads = [
        pltpu.make_async_copy(
            source, products.at[pl.ds(index * rows_in, rows_in)], gate_load_sems.at[index]
        )
        for index, source in enumerate((gate_own, gate_pair))
    ]
    turns = [(0, 1), (1, 1), (0, 0), (1, 0)]
    turns += [(0, 1), (1, 1), (1, 0), (0, 0)]

    def column_loads(index):
        turn, other = turns[index]
        spot = lax.rem(1 - team + turn, 2)
        which = 1 - lane if other else lane
        start = pl.multiple_of((side * 4 + 2 * spot + which) * width, width)
        return [
            pltpu.make_async_copy(
                source.at[:, pl.ds(start, width)],
                columns.at[index % 2, pl.ds(part * rows_in, rows_in)],
                column_sems.at[index % 2, part],
            )
            for part, source in enumerate(
                (upstream_hbm, upstream_pair) if index < 4 else (low_own, low_pair)
            )
        ]

    x_loads = [
        pltpu.make_async_copy(
            second_hbm.at[pl.ds(begin(0, k), size)], x_send.at[k], x_load_sems.at[k]
        )
        for k in range(4)
    ]
    for copy in column_loads(0) + x_loads[:1] + loads[:2] + column_loads(1) + x_loads[1:] + loads[2:]:
        copy.start()
    greet_grid([sibling, facing, across, inward], inner, outward)
    c_copies = [
        remote(second_hbm.at[pl.ds(begin(1, k), size)], c_recv.at[k], c_sems, k, sibling)
        for k in range(4)
    ]
    x_copies = [remote(x_send.at[k], x_recv.at[k], x_sems, k, facing) for k in range(4)]
    back_copies = [remote(x_send.at[k], back_recv.at[k], back_sems, k, sibling) for k in range(4)]
    y_copies = [remote(y_send.at[k], y_recv.at[k], y_sems, k, across) for k in range(2)]
    in_copy = remote(kept.at[0], in_recv, z_sems, 0, inward)
    mid_copies = [remote(kept.at[k], mid_recv.at[k], z_sems, 1 + k, inward) for k in range(2)]
    out_copy = remote(mid_recv.at[0], out_recv, z_sems, 3, outward)
    for copy in c_copies:
        copy.start()

    def cores(k):
        x_loads[k].wait()
        c_copies[k].wait_recv()

        def run(row):
            x_send[k, row, :] = x_send[k, row, :] + c_recv[k, row, :]

        loop_rows(size, 16, run)
        x_copies[k].start()

    def chips(k):
        x_copies[k].wait()

        def run(row):
            x_send[k, row, :] = x_send[k, row, :] + x_recv[k, row, :]

        loop_rows(size, 16, run)
        back_copies[k].start()

    def block(index, target):
        for copy in column_loads(index):
            copy.wait()

        target[...] = lax.dot_general(
            products[...], columns[index % 2], down_first, preferred_element_type=jnp.float32
        )
        for copy in column_loads(index + 2):
            copy.start()

    gate_copy = remote(gate_send, gate_kept, gate_sems, 0, across)

    def gate_block(index, target):
        for copy in column_loads(index):
            copy.wait()
        target[...] = lax.dot_general(
            columns[index % 2], products[...], down_first, preferred_element_type=jnp.float32
        )
        if index + 2 < len(turns):
            for copy in column_loads(index + 2):
                copy.start()

    def gate_store(source, target, index):
        return pltpu.make_async_copy(source, target, gate_load_sems.at[2 + index])

    def chunk_loads(k):
        return [
            pltpu.make_async_copy(
                source.at[pl.ds(begin(which, k), size)], target.at[which], sems.at[which]
            )
            for which in range(2)
            for source, target, sems in ((hidden_hbm, hid, hid_sems), (upstream_hbm, tok, tok_sems))
        ]

    def grad_stores(k):
        return [
            pltpu.make_async_copy(
                source.at[which], target.at[pl.ds(begin(which, k), size)], sems.at[which]
            )
            for which in range(2)
            for source, target, sems in (
                (grad, grad_out, grad_sems),
                (grad_low, grad_low_out, low_sems),
            )
        ]

    def finish(k):
        for copy in chunk_loads(k):
            copy.wait()
        if k > 0:
            for copy in grad_stores(k - 1):
                copy.wait()
        back_copies[k].wait_recv()

        def run(which, source, row):
            value = hid[which, row, :]
            inverse = lax.rsqrt(jnp.mean(value * value, axis=-1, keepdims=True) + epsilon)
            total = tok[which, row, :].astype(jnp.float32) + norm_back(
                source[k, row, :], value, inverse, gain[...]
            )
            grad[which, row, :] = total
            grad_low[which, row, :] = total.astype(jnp.bfloat16)

        for which, source in enumerate((x_send, back_recv)):
            loop_rows(size, 16, functools.partial(run, which, source))
        for copy in grad_stores(k):
            copy.start()
        if k < 3:
            for copy in chunk_loads(k + 1):
                copy.start()

    def out_store(k):
        rows = 2 * size
        return pltpu.make_async_copy(
            out_stage, out_part.at[pl.ds(k * rows, rows)], out_sems.at[0]
        )

    def out_terms(k):
        if k > 0:
            out_store(k - 1).wait()
        rows = pl.ds(k * 2 * size, 2 * size)

        def run(column):
            out_stage[:, column] = jnp.dot(
                products[rows, :], down_weight[:, column], preferred_element_type=jnp.float32
            )

        loop_rows(depth, 1024, run)
        out_store(k).start()

    def take(k):
        y_copies[k].wait_recv()

        def run(row):
            kept[k, row, :] = kept[k, row, :] + y_recv[k, row, :]

        loop_rows(units, 64, run)

    for copy in loads[:2]:
        copy.wait()
    block(0, y_send.at[0])
    y_copies[0].start()
    cores(0)
    for copy in chunk_loads(0):
        copy.start()
    cores(1)
    cores(2)
    cores(3)
    block(1, y_send.at[1])
    y_copies[1].start()
    block(2, kept.at[0])
    loads[2].wait()
    out_terms(0)
    chips(0)
    out_terms(1)
    block(3, kept.at[1])
    finish(0)
    out_terms(2)
    take(0)

    @pl.when(inner == 1)
    def _():
        mid_copies[0].start()

    @pl.when(inner == 0)
    def _():
        in_copy.start()

    out_terms(3)
    for copy in gate_loads:
        copy.start()
    chips(1)
    for copy in gate_loads:
        copy.wait()
    gate_block(4, gate_send)
    gate_copy.start()
    finish(1)
    gate_block(5, gate_stage)
    gate_store(gate_stage, gate_given, 0).start()
    chips(2)
    take(1)

    @pl.when(inner == 1)
    def _():
        mid_copies[1].start()
        mid_copies[0].wait_recv()
        out_copy.start()

    finish(2)
    gate_store(gate_stage, gate_given, 0).wait()
    gate_block(6, gate_stage)
    gate_store(gate_stage, gate_own_block, 1).start()
    gate_store(gate_stage, gate_own_block, 1).wait()
    gate_block(7, gate_stage)
    chips(3)
    finish(3)
    gate_copy.wait()

    def run_gate(row):
        gate_kept[row, :] = gate_kept[row, :] + gate_stage[row, :]

    loop_rows(width, 16, run_gate)
    gate_store(gate_kept, gate_ready, 2).start()

    @pl.when(inner == 1)
    def _():
        in_copy.wait_recv()
        mid_copies[1].wait_recv()
        mid_copies[0].wait_send()
        mid_copies[1].wait_send()
        out_copy.wait_send()

        def run(row):
            kept[0, row, :] = in_recv[row, :] + mid_recv[1, row, :]

        loop_rows(units, 64, run)

    @pl.when(inner == 0)
    def _():
        in_copy.wait_send()
        out_copy.wait_recv()

        def run(row):
            kept[0, row, :] = kept[1, row, :] + out_recv[row, :]

        loop_rows(units, 64, run)

    store = pltpu.make_async_copy(kept.at[0], weight_out, weight_sems.at[0])
    store.start()
    for k in range(4):
        back_copies[k].wait_send()
        c_copies[k].wait_send()
    for k in range(2):
        y_copies[k].wait_send()
    for copy in grad_stores(3):
        copy.wait()
    gate_store(gate_kept, gate_ready, 2).wait()
    out_store(3).wait()
    store.wait()


def middle(
    second, hidden, upstream, upstream_pair, product_own, product_pair,
    gate_own, gate_pair, low_own, low_pair, gain, down_weight,
):
    rows, depth = hidden.shape
    units = down_weight.shape[0]
    size = rows // 8
    width = depth // 8
    f32, b16 = jnp.float32, jnp.bfloat16
    any_space = pl.BlockSpec(memory_space=pl.ANY)
    shape = jax.ShapeDtypeStruct
    dma = pltpu.SemaphoreType.DMA
    vmem = pltpu.VMEM
    return pl.pallas_call(
        functools.partial(middle_kernel, size),
        out_shape=[
            shape((rows, depth), f32),
            shape((rows, depth), b16),
            shape((rows, depth), f32),
            shape((units, width), f32),
        ]
        + [shape((width, units), f32)] * 3,
        in_specs=[any_space] * 10 + [pl.BlockSpec(memory_space=pltpu.VMEM), any_space],
        out_specs=[any_space] * 7,
        scratch_shapes=[
            vmem((2 * rows, units), b16),
            vmem((units, depth), b16),
            vmem((2, 2 * rows, width), b16),
            vmem((4, size, depth), f32),
            vmem((4, size, depth), f32),
            vmem((4, size, depth), f32),
            vmem((4, size, depth), f32),
            vmem((2, units, width), f32),
            vmem((2, units, width), f32),
            vmem((2, units, width), f32),
            vmem((units, width), f32),
            vmem((2, units, width), f32),
            vmem((units, width), f32),
            vmem((2, size, depth), f32),
            vmem((2, size, depth), b16),
            vmem((2, size, depth), f32),
            vmem((2, size, depth), b16),
            vmem((2 * size, depth), f32),
            vmem((width, units), f32),
            vmem((width, units), f32),
            vmem((width, units), f32),
            dma((3,)),
            dma((5,)),
            dma((2, 1)),
            dma((2, 4)),
            dma((2, 4)),
            dma((2, 4)),
            dma((2, 2)),
            dma((2, 4)),
            dma((2, 2)),
            dma((4,)),
            dma((2,)),
            dma((2,)),
            dma((2,)),
            dma((2,)),
            dma((1,)),
            dma((1,)),
        ],
        compiler_params=pltpu.CompilerParams(
            collective_id=2, has_side_effects=True, vmem_limit_bytes=62 * 1024 * 1024
        ),
        cost_estimate=pl.CostEstimate(
            flops=8 * rows * depth * units, bytes_accessed=6 * depth * units, transcendentals=0
        ),
    )(
        second, hidden, upstream, upstream_pair, product_own, product_pair,
        gate_own, gate_pair, low_own, low_pair, gain[None], down_weight,
    )


class TensorSum:
    def __init__(self, size, own, landed, stage, sems, stage_sems, devices):
        self.size, self.own, self.landed, self.stage = size, own, landed, stage
        self.stage_sems = stage_sems
        c_sems, x_sems, back_sems = sems
        self.sibling, facing = devices
        self.c_sems = c_sems
        self.x_copies = [remote(own.at[k], landed[1].at[k], x_sems, k, facing) for k in range(4)]
        self.back_copies = [
            remote(own.at[k], landed[2].at[k], back_sems, k, self.sibling) for k in range(4)
        ]
        self.c_copies = [None] * 4

    def give(self, k, source):
        self.c_copies[k] = remote(source, self.landed[0].at[k], self.c_sems, k, self.sibling)
        self.c_copies[k].start()

    def staged(self, which, k):
        copy = pltpu.make_async_copy(self.landed[which].at[k], self.stage.at[0], self.stage_sems.at[0])
        copy.start()
        copy.wait()

    def add_stage(self, k):
        def run(row):
            self.own[k, row, :] = self.own[k, row, :] + self.stage[0, row, :]

        loop_rows(self.size, 16, run)

    def cores(self, k):
        self.c_copies[k].wait_recv()
        self.staged(0, k)
        self.add_stage(k)
        self.x_copies[k].start()

    def chips(self, k):
        self.x_copies[k].wait()
        self.staged(1, k)
        self.add_stage(k)
        self.back_copies[k].start()

    def other(self, k):
        self.back_copies[k].wait_recv()
        self.staged(2, k)


def rear_kernel(
    size, turns,
    gate_middle, gate_inward, gate_ready, low_own, low_pair, upward_own, upward_pair,
    normed_hbm, raw_hbm, hidden_low_hbm, mixed_hbm, lines,
    out_hbm, hidden_hbm, grad_hbm, tokens_hbm,
    query_hbm, key_hbm, value_hbm, gate_hbm, up_hbm, gain, feed_gain,
    layer_out, tokens_out, gate_out, up_out, raw_out, head_out, gains_out,
    o_c, o_x, o_back, d_c, d_x, d_back, gate_landed, up_landed,
    upwards, raw, mixed, head_weights, feed_rows, gains, gain_rows, gains_in, gains_sum, columns,
    up_send, up_kept, raw_send, raw_kept, head_send, head_kept, raw_line, head_line,
    own, give, stage, wide, narrow, result,
    load_sems, column_sems, y_up_sems, y_raw_sems, y_head_sems, gate_sems, up_sems,
    raw_line_sems, head_line_sems,
    oc_sems, ox_sems, ob_sems, dc_sems, dx_sems, db_sems,
    own_sems, stage_sems, wide_sems, narrow_sems, result_sems, end_sems, gain_sems,
):
    core, sibling, facing, _ = neighbours()
    place, lane, team, side, inner, across, inward, outward = grid_neighbours()
    high = len(turns)
    depth = gain.shape[1]
    width = columns.shape[-1]
    units = upwards.shape[-1]
    begin = functools.partial(sequence_rows, size, core)
    rows_in = 8 * size
    down_first = (((0,), (0,)), ((), ()))
    cuts = (query_hbm.shape[1], key_hbm.shape[1])
    own_rows = pl.ds(pl.multiple_of(lax.axis_index("dp") * width, width), width)
    loads = [
        pltpu.make_async_copy(source, target, load_sems.at[index])
        for index, (source, target) in enumerate(
            [
                (raw_hbm, raw),
                (mixed_hbm, mixed),
                (upward_own, upwards.at[pl.ds(0, rows_in)]),
                (upward_pair, upwards.at[pl.ds(rows_in, rows_in)]),
                (query_hbm, head_weights.at[:, pl.ds(0, cuts[0])]),
                (key_hbm, head_weights.at[:, pl.ds(cuts[0], cuts[1])]),
                (value_hbm, head_weights.at[:, pl.ds(cuts[0] + cuts[1], cuts[1])]),
                (gate_hbm.at[own_rows], feed_rows.at[0]),
                (up_hbm.at[own_rows], feed_rows.at[1]),
            ]
        )
    ]
    blocks = [
        ("head", 0, 1), ("up", 0, 1), ("up", 1, 1), ("head", 1, 1), ("head", 2, 1), ("head", 3, 1),
        ("head", 0, 0), ("up", 0, 0), ("up", 1, 0), ("head", 1, 0), ("head", 2, 0), ("head", 3, 0),
    ]

    def spot_of(kind, turn):
        if kind == "up":
            return side * 2 + lax.rem(1 - team + turn, 2)
        spot = jnp.int32(turns[0][turn])
        for p in range(1, high):
            spot = jnp.where(place == p, jnp.int32(turns[p][turn]), spot)
        return spot

    def column_loads(index):
        kind, turn, other = blocks[index]
        which = 1 - lane if other else lane
        start = pl.multiple_of((2 * spot_of(kind, turn) + which) * width, width)
        sources = (low_own, low_pair) if kind == "up" else (normed_hbm, hidden_low_hbm)
        return [
            pltpu.make_async_copy(
                source.at[:, pl.ds(start, width)],
                columns.at[index % 2, pl.ds(part * rows_in, rows_in)],
                column_sems.at[index % 2, part],
            )
            for part, source in enumerate(sources)
        ]

    own_loads = [
        pltpu.make_async_copy(out_hbm.at[pl.ds(begin(0, k), size)], own.at[k], own_sems.at[k])
        for k in range(4)
    ]
    for copy in column_loads(0) + loads[:2] + column_loads(1) + own_loads + loads[2:]:
        copy.start()
    opposite = {"tensor": lax.rem(lax.axis_index("tensor") + 3 - 2 * core, 4)}
    greet_grid([sibling, facing, opposite, across, inward], inner, outward)
    devices = (sibling, facing)
    outs = TensorSum(
        size, own, (o_c, o_x, o_back), stage, (oc_sems, ox_sems, ob_sems), stage_sems, devices
    )
    heads = TensorSum(
        size, own, (d_c, d_x, d_back), stage, (dc_sems, dx_sems, db_sems), stage_sems, devices
    )
    for k in range(4):
        outs.give(k, out_hbm.at[pl.ds(begin(1, k), size)])

    def team_copies(values, landed, sems):
        return (
            remote(values[0], landed.at[0], sems, 0, inward),
            [remote(values[k], landed.at[1 + k], sems, 1 + k, inward) for k in range(2)],
            remote(landed.at[1], landed.at[3], sems, 3, outward),
        )

    gate_copies = (
        None,
        [None, remote(gate_ready, gate_landed.at[0], gate_sems, 0, inward)],
        remote(gate_middle, gate_landed.at[1], gate_sems, 1, outward),
    )
    up_copies = team_copies((up_kept.at[0], up_kept.at[1]), up_landed, up_sems)

    def team_send(copies, turn):
        @pl.when(inner == 1)
        def _():
            copies[1][turn].start()

        if turn == 0:

            @pl.when(inner == 0)
            def _():
                copies[0].start()

    def team_forward(copies):
        @pl.when(inner == 1)
        def _():
            copies[1][0].wait_recv()
            copies[2].start()

    def add_gain(lane_index, row, value, weight):
        total = jnp.sum(value * weight.astype(jnp.float32), axis=-1, keepdims=True)
        lanes = lax.broadcasted_iota(jnp.int32, (total.shape[0], gains.shape[1]), 1)
        gains[row, :] = gains[row, :] + jnp.where(lanes == lane_index, total, 0.0)

    def team_combine(copies, first, second, outward_landed, last, out, sem, which):
        def fetch(source, slot):
            copy = pltpu.make_async_copy(source, up_send.at[slot], end_sems.at[4 + slot])
            copy.start()
            copy.wait()

        @pl.when(inner == 1)
        def _():
            if copies[0] is not None:
                copies[0].wait_recv()
                copies[1][0].wait_send()
            copies[1][1].wait_recv()
            fetch(first, 0)
            fetch(second, 1)
            copies[1][1].wait_send()
            copies[2].wait_send()

        @pl.when(inner == 0)
        def _():
            if copies[0] is not None:
                copies[0].wait_send()
            copies[2].wait_recv()
            fetch(outward_landed, 0)
            fetch(last, 1)

        def run(row):
            total = up_send[0, row, :] + up_send[1, row, :]
            up_send[0, row, :] = total
            add_gain(1, row, total, feed_rows[which, row, :])

        loop_rows(width, 16, run)
        store = pltpu.make_async_copy(up_send.at[0], out, sem)
        store.start()
        store.wait()

    y_up = [remote(up_send.at[k], up_kept.at[k], y_up_sems, k, across) for k in range(2)]
    y_raw = [remote(raw_send.at[k], raw_kept.at[k], y_raw_sems, k, across) for k in range(high)]
    y_head = [
        remote(head_send.at[k], head_kept.at[k], y_head_sems, k, across) for k in range(high)
    ]

    def line_copy(p, turn, towards=None):
        block = turns[p][turn]
        ahead = block > p
        slot = block - 1 if ahead else high - 1 + block
        device = {"dp": lax.axis_index("dp") + (2 if ahead else -2)}
        return slot, [
            remote(kept.at[turn], line.at[slot], sems, slot, device)
            for kept, line, sems in (
                (raw_kept, raw_line, raw_line_sems),
                (head_kept, head_line, head_line_sems),
            )
        ]

    def line_arrived(slot, turn):
        for kept, line, sems in (
            (raw_kept, raw_line, raw_line_sems),
            (head_kept, head_line, head_line_sems),
        ):
            remote(kept.at[turn], line.at[slot], sems, slot, across).wait_recv()

            def run(row):
                kept[turn, row, :] = kept[turn, row, :] + line[slot, row, :]

            loop_rows(kept.shape[1], 8, run)

    def line_step(turn):
        for p in range(high):
            block = turns[p][turn]

            @pl.when(place == p)
            def _():
                slot, copies = line_copy(p, turn)
                if (block > p and p > 0) or (block < p and p < high - 1):
                    line_arrived(slot, turn)
                for copy in copies:
                    copy.start()

    def line_end():
        for p in range(high):

            @pl.when(place == p)
            def _():
                if p > 0:
                    line_arrived(p - 1, high - 1)
                if p < high - 1:
                    line_arrived(high - 1 + p, high - 1)
                for turn in range(high - 1):
                    for copy in line_copy(p, turn)[1]:
                        copy.wait_send()

    def up_block(index, target, added):
        for copy in column_loads(index):
            copy.wait()

        total = lax.dot_general(
            columns[index % 2], upwards[...], down_first, preferred_element_type=jnp.float32
        )
        target[...] = target[...] + total if added else total
        if index + 2 < len(blocks):
            for copy in column_loads(index + 2):
                copy.start()

    def head_block(index, raw_target, head_target, added):
        kind, turn, other = blocks[index]
        which = 1 - lane if other else lane
        for copy in column_loads(index):
            copy.wait()
        slot = index % 2
        total = lax.dot_general(
            columns[slot, :rows_in], raw[...], down_first, preferred_element_type=jnp.float32
        )
        line = lines[2 * spot_of(kind, turn) + which]
        raw_target[:width, :] = raw_target[:width, :] + total if added else total
        raw_target[width:, :] = raw_target[width:, :] + line if added else line
        total = lax.dot_general(
            mixed[...], columns[slot, rows_in:], down_first, preferred_element_type=jnp.float32
        )
        head_target[...] = head_target[...] + total if added else total
        if index + 2 < len(blocks):
            for copy in column_loads(index + 2):
                copy.start()

    def head_send_block(index):
        turn = blocks[index][1]
        head_block(index, raw_send.at[turn], head_send.at[turn], False)
        y_raw[turn].start()
        y_head[turn].start()

    def head_take(index):
        turn = blocks[index][1]
        y_raw[turn].wait_recv()
        y_head[turn].wait_recv()
        head_block(index, raw_kept.at[turn], head_kept.at[turn], True)

    def head_terms(k):
        outs.back_copies[k].wait_send()
        if k >= 2:
            heads.c_copies[k - 2].wait_send()
        rows = jnp.concatenate(
            [raw[pl.ds(begin(which, k), size), :] for which in range(2)], axis=0
        )

        def run(column):
            total = lax.dot_general(
                rows,
                head_weights[column, :],
                (((1,), (1,)), ((), ())),
                preferred_element_type=jnp.float32,
            )
            own[k, :, column] = total[:size]
            give[k % 2, :, column] = total[size:]

        loop_rows(depth, 1024, run)
        heads.give(k, give.at[k % 2])

    def fetches(what, k):
        pairs = ((hidden_hbm, wide, wide_sems),)
        if what == "tokens":
            pairs = ((grad_hbm, wide, wide_sems), (tokens_hbm, narrow, narrow_sems))
        return [
            pltpu.make_async_copy(
                source.at[pl.ds(begin(which, k), size)], target.at[which], sems.at[which]
            )
            for which in range(2)
            for source, target, sems in pairs
        ]

    def stores(what, k):
        return [
            pltpu.make_async_copy(
                result.at[which],
                (layer_out if what == "layer" else tokens_out).at[pl.ds(begin(which, k), size)],
                result_sems.at[which],
            )
            for which in range(2)
        ]

    sequence = [("layer", k) for k in range(4)] + [("tokens", k) for k in range(4)]

    def finish(what, k):
        number = sequence.index((what, k))
        for copy in fetches(what, k):
            copy.wait()
        if number > 0:
            for copy in stores(*sequence[number - 1]):
                copy.wait()
        (outs if what == "layer" else heads).other(k)

        def run(which, row):
            total = stage[0, row, :] if which else own[k, row, :]
            value = wide[which, row, :]
            if what == "layer":
                total = value + total
            else:
                inputs = narrow[which, row, :].astype(jnp.float32)
                inverse = lax.rsqrt(jnp.mean(inputs * inputs, axis=-1, keepdims=True) + epsilon)
                total = value + norm_back(total, inputs, inverse, gain[...])
            result[which, row, :] = total.astype(jnp.bfloat16)

        for which in range(2):
            loop_rows(size, 16, functools.partial(run, which))
        for copy in stores(what, k):
            copy.start()
        if number + 1 < len(sequence):
            for copy in fetches(*sequence[number + 1]):
                copy.start()

    team_send(gate_copies, 1)

    @pl.when(inner == 1)
    def _():
        gate_copies[2].start()

    gains[...] = jnp.zeros_like(gains)
    for copy in fetches("layer", 0):
        copy.start()
    for copy in loads[:2]:
        copy.wait()
    head_send_block(0)
    own_loads[0].wait()
    outs.cores(0)
    for copy in loads[2:]:
        copy.wait()
    up_block(1, up_send.at[0], False)
    y_up[0].start()
    for k in range(1, 4):
        own_loads[k].wait()
        outs.cores(k)
    up_block(2, up_send.at[1], False)
    y_up[1].start()
    for index in range(3, 6):
        head_send_block(index)
    outs.chips(0)
    finish("layer", 0)
    head_take(6)
    line_step(0)
    head_terms(0)
    outs.chips(1)
    finish("layer", 1)
    head_terms(1)
    heads.cores(0)
    y_up[0].wait_recv()
    up_block(7, up_kept.at[0], True)
    team_send(up_copies, 0)
    outs.chips(2)
    finish("layer", 2)
    head_terms(2)
    heads.cores(1)
    outs.chips(3)
    heads.cores(2)
    finish("layer", 3)
    head_terms(3)
    heads.cores(3)
    y_up[1].wait_recv()
    up_block(8, up_kept.at[1], True)
    team_send(up_copies, 1)
    team_forward(up_copies)
    heads.chips(0)
    finish("tokens", 0)
    for k in range(2):
        y_up[k].wait_send()
    team_combine(
        gate_copies, gate_inward, gate_landed.at[0], gate_landed.at[1], gate_ready,
        gate_out, end_sems.at[0], 0,
    )
    head_take(9)
    line_step(1)
    heads.chips(1)
    finish("tokens", 1)
    y_raw[0].wait_send()
    y_head[0].wait_send()
    heads.chips(2)
    finish("tokens", 2)
    head_take(10)
    line_step(2)
    head_block(11, raw_send.at[0], head_send.at[0], False)
    team_combine(
        up_copies, up_landed.at[0], up_landed.at[2], up_landed.at[3], up_kept.at[1],
        up_out, end_sems.at[1], 1,
    )
    heads.chips(3)
    finish("tokens", 3)
    y_raw[high - 1].wait_recv()
    y_head[high - 1].wait_recv()
    for kept, sent, step in ((raw_kept, raw_send, 8), (head_kept, head_send, 16)):

        def run_last(row):
            kept[high - 1, row, :] = kept[high - 1, row, :] + sent[0, row, :]

        loop_rows(kept.shape[1], step, run_last)
    line_end()
    ends = [
        pltpu.make_async_copy(raw_kept.at[high - 1], raw_out, end_sems.at[2]),
        pltpu.make_async_copy(head_kept.at[high - 1], head_out, end_sems.at[3]),
    ]
    for copy in ends:
        copy.start()

    def run_gain(row):
        place_row = pl.ds(pl.multiple_of(own_rows.start + row.start, 16), row.size)
        add_gain(0, row, raw_kept[high - 1, row, :], head_weights[place_row, :])

    loop_rows(width, 16, run_gain)
    own_columns = pl.ds(pl.multiple_of(own_rows.start, 128), width)
    turned = jnp.transpose(gains[...])[:8]
    scale = jnp.concatenate([gain[:, own_columns], feed_gain[:, own_columns]], axis=0)
    gain_rows[:8, :] = turned
    gain_rows[:2, :] = turned[:2] / scale
    gain_rows[8:, :] = raw_kept[high - 1, width:, :width]
    gain_copies = [
        remote(gain_rows, gains_in.at[k], gain_sems, k, device)
        for k, device in enumerate((sibling, facing, opposite))
    ]
    for copy in gain_copies:
        copy.start()
    for copy in gain_copies:
        copy.wait()
    gains_sum[...] = (gain_rows[...] + gains_in[0]) + (gains_in[1] + gains_in[2])
    gain_store = pltpu.make_async_copy(gains_sum, gains_out, own_sems.at[0])
    gain_store.start()
    gain_store.wait()
    for k in range(4):
        outs.c_copies[k].wait_send()
        heads.back_copies[k].wait_send()
    for k in range(2, 4):
        heads.c_copies[k].wait_send()
    for k in range(1, high):
        y_raw[k].wait_send()
        y_head[k].wait_send()
    for copy in stores(*sequence[-1]) + ends:
        copy.wait()


def rear(turns, arrays, lines, places, weights, gain, feed_gain):
    rows, depth = places[0].shape
    units = arrays[0].shape[1]
    heads, inner = arrays[8].shape[1], arrays[10].shape[1]
    size = rows // 8
    width = depth // 8
    high = len(turns)
    f32, b16 = jnp.float32, jnp.bfloat16
    any_space = pl.BlockSpec(memory_space=pl.ANY)
    in_vmem = pl.BlockSpec(memory_space=pltpu.VMEM)
    shape = jax.ShapeDtypeStruct
    dma = pltpu.SemaphoreType.DMA
    vmem = pltpu.VMEM
    slots = 2 * (high - 1)
    return pl.pallas_call(
        functools.partial(rear_kernel, size, turns),
        out_shape=[
            shape((rows, depth), b16),
            shape((rows, depth), b16),
            shape((width, units), f32),
            shape((width, units), f32),
            shape((width + 8, heads), f32),
            shape((inner, width), f32),
            shape((16, width), f32),
        ]
        + [shape((4, size, depth), f32)] * 6
        + [shape((2, width, units), f32), shape((4, width, units), f32)],
        in_specs=[any_space] * 11 + [in_vmem] + [any_space] * 9 + [in_vmem] * 2,
        out_specs=[any_space] * 15,
        scratch_shapes=[
            vmem((2 * rows, units), b16),
            vmem((rows, heads), b16),
            vmem((rows, inner), b16),
            vmem((depth, heads), b16),
            vmem((2, width, units), b16),
            vmem((width, HD), f32),
            vmem((16, width), f32),
            vmem((3, 16, width), f32),
            vmem((16, width), f32),
            vmem((2, 2 * rows, width), b16),
            vmem((2, width, units), f32),
            vmem((2, width, units), f32),
            vmem((high, width + 8, heads), f32),
            vmem((high, width + 8, heads), f32),
            vmem((high, inner, width), f32),
            vmem((high, inner, width), f32),
            vmem((slots, width + 8, heads), f32),
            vmem((slots, inner, width), f32),
            vmem((4, size, depth), f32),
            vmem((2, size, depth), f32),
            vmem((1, size, depth), f32),
            vmem((2, size, depth), f32),
            vmem((2, size, depth), b16),
            vmem((2, size, depth), b16),
            dma((9,)),
            dma((2, 2)),
            dma((2, 2)),
            dma((2, high)),
            dma((2, high)),
            dma((2, 4)),
            dma((2, 4)),
            dma((2, slots)),
            dma((2, slots)),
            *[dma((2, 4))] * 6,
            dma((4,)),
            dma((1,)),
            dma((2,)),
            dma((2,)),
            dma((2,)),
            dma((6,)),
            dma((2, 3)),
        ],
        compiler_params=pltpu.CompilerParams(
            collective_id=3, has_side_effects=True, vmem_limit_bytes=62 * 1024 * 1024
        ),
        cost_estimate=pl.CostEstimate(
            flops=8 * rows * depth * units, bytes_accessed=6 * depth * units, transcendentals=0
        ),
    )(*arrays, lines, *places, *weights, gain[None], feed_gain[None])


def block_mask(segment_column, segment_row, begin, rows, columns):
    row = begin + lax.broadcasted_iota(jnp.int32, (rows, columns), 0)
    column = lax.broadcasted_iota(jnp.int32, (rows, columns), 1)
    same = segment_column[pl.ds(begin, rows), :] == segment_row[:, :columns]
    return same & (row >= column)


def head_columns(index):
    return pl.ds(pl.multiple_of(index * HD, HD), HD)


def attention_kernel(
    step,
    tokens, gain, query_weight, key_weight, value_weight, query_gain, key_gain, cosine, sine,
    segment_column, segment_row,
    normed_out, query_raw, key_raw, query_out, key_out, value_out, mixed_out, total_out,
):
    count = tokens.shape[0]
    query_heads = query_weight.shape[1] // HD
    value_heads = key_weight.shape[1] // HD
    group = query_heads // value_heads

    def normalize(rows):
        value = tokens[rows, :].astype(jnp.float32)
        normed_out[rows, :] = (value * rms_inverse(value) * gain[...]).astype(jnp.bfloat16)

    loop_rows(count, 32, normalize)

    def project(rows):
        low = normed_out[rows, :]
        value_out[rows, :] = jnp.dot(
            low, value_weight[...], preferred_element_type=jnp.float32
        ).astype(jnp.bfloat16)
        for weight, raw, out, head_gain, heads in (
            (query_weight, query_raw, query_out, query_gain, query_heads),
            (key_weight, key_raw, key_out, key_gain, value_heads),
        ):
            product = jnp.dot(low, weight[...], preferred_element_type=jnp.float32)
            raw[rows, :] = product
            for head in range(heads):
                part = product[:, head * HD : (head + 1) * HD]
                unit = part * rms_inverse(part) * head_gain[...]
                turned = unit * cosine[rows, :] + pltpu.roll(unit, HD // 2, 1) * sine[rows, :]
                out[rows, head * HD : (head + 1) * HD] = turned.astype(jnp.bfloat16)

    loop_rows(count, step, project)

    def head_step(head, carry):
        own = head_columns(head)
        shared = head_columns(head // group)
        for begin in range(0, count, step):
            reach = begin + step
            scores = lax.dot_general(
                query_out[pl.ds(begin, step), own],
                key_out[pl.ds(0, reach), shared],
                (((1,), (1,)), ((), ())),
                preferred_element_type=jnp.float32,
            ) * HD ** (-0.5)
            allowed = block_mask(segment_column, segment_row, begin, step, reach)
            scores = jnp.where(allowed, scores, masked)
            peak = jnp.max(scores, axis=-1, keepdims=True)
            expons = jnp.exp(scores - peak)
            total = jnp.sum(expons, axis=-1, keepdims=True)
            chance = (expons * (1.0 / total)).astype(jnp.bfloat16)
            mixed_out[pl.ds(begin, step), own] = jnp.dot(
                chance, value_out[pl.ds(0, reach), shared], preferred_element_type=jnp.float32
            ).astype(jnp.bfloat16)
            total_out[head, pl.ds(begin, step), :] = jnp.broadcast_to(
                peak + jnp.log(total), (step, HD)
            )
        return carry

    lax.fori_loop(0, query_heads, head_step, 0)


def attention(tokens, gain, weights, query_gain, key_gain, cosine, sine, segment_column, segment_row):
    count, depth = tokens.shape
    queries, keys = weights[0].shape[1], weights[1].shape[1]
    f32, b16 = jnp.float32, jnp.bfloat16
    shape = jax.ShapeDtypeStruct
    return pl.pallas_call(
        functools.partial(attention_kernel, 256),
        out_shape=[
            shape((count, depth), b16),
            shape((count, queries), f32),
            shape((count, keys), f32),
            shape((count, queries), b16),
            shape((count, keys), b16),
            shape((count, keys), b16),
            shape((count, queries), b16),
            shape((queries // HD, count, HD), f32),
        ],
        compiler_params=pltpu.CompilerParams(vmem_limit_bytes=56 * 1024 * 1024),
        cost_estimate=pl.CostEstimate(
            flops=2 * count * depth * (queries + 2 * keys) + 4 * count * count * queries,
            bytes_accessed=32 * 1024 * 1024,
            transcendentals=count * count * queries // HD,
        ),
    )(tokens, gain[None], *weights, query_gain[None], key_gain[None], cosine, sine, segment_column, segment_row)


def attention_back_kernel(
    step,
    hidden_low, output_weight, queries, keys, values, totals, query_raw, key_raw,
    query_gain, key_gain, cosine, sine, segment_column, segment_row,
    raw_out, query_gain_out, key_gain_out,
    upstream, query_grad, key_grad, value_grad,
):
    count = hidden_low.shape[0]
    query_heads = queries.shape[1] // HD
    value_heads = keys.shape[1] // HD
    group = query_heads // value_heads
    across_last = (((1,), (1,)), ((), ()))
    down_first = (((0,), (0,)), ((), ()))

    def project(rows):
        upstream[rows, :] = lax.dot_general(
            hidden_low[rows, :],
            output_weight[...],
            across_last,
            preferred_element_type=jnp.float32,
        ).astype(jnp.bfloat16)

    loop_rows(count, step, project)
    key_grad[...] = jnp.zeros_like(key_grad)
    value_grad[...] = jnp.zeros_like(value_grad)

    def head_step(head, carry):
        own = head_columns(head)
        shared = head_columns(head // group)
        for begin in range(0, count, step):
            reach = begin + step
            rows, before = pl.ds(begin, step), pl.ds(0, reach)
            scores = lax.dot_general(
                queries[rows, own],
                keys[before, shared],
                across_last,
                preferred_element_type=jnp.float32,
            ) * HD ** (-0.5)
            allowed = block_mask(segment_column, segment_row, begin, step, reach)
            chance = jnp.exp(jnp.where(allowed, scores, masked) - totals[head, rows, :][:, :1])
            incoming = upstream[rows, own]
            value_grad[before, shared] += lax.dot_general(
                chance.astype(jnp.bfloat16),
                incoming,
                down_first,
                preferred_element_type=jnp.float32,
            )
            along = lax.dot_general(
                incoming, values[before, shared], across_last, preferred_element_type=jnp.float32
            )
            center = jnp.sum(along * chance, axis=-1, keepdims=True)
            score_grad = (chance * (along - center)).astype(jnp.bfloat16)
            query_grad[rows, own] = jnp.dot(
                score_grad, keys[before, shared], preferred_element_type=jnp.float32
            ) * HD ** (-0.5)
            key_grad[before, shared] += lax.dot_general(
                score_grad, queries[rows, own], down_first, preferred_element_type=jnp.float32
            ) * HD ** (-0.5)
        return carry

    lax.fori_loop(0, query_heads, head_step, 0)
    query_gain_out[...] = jnp.zeros_like(query_gain_out)
    key_gain_out[...] = jnp.zeros_like(key_gain_out)

    def finish(rows):
        for grad, raw, head_gain, gain_out, heads, place in (
            (query_grad, query_raw, query_gain, query_gain_out, query_heads, 0),
            (key_grad, key_raw, key_gain, key_gain_out, value_heads, query_heads),
        ):
            for head in range(heads):
                columns = slice(head * HD, (head + 1) * HD)
                upward = grad[rows, columns]
                unit_grad = upward * cosine[rows, :] - pltpu.roll(upward, HD // 2, 1) * sine[rows, :]
                value = raw[rows, columns]
                inverse = rms_inverse(value)
                product = unit_grad * (value * inverse)
                gain_out[...] += jnp.sum(product.reshape(-1, 8, HD), axis=0)
                begin = (place + head) * HD
                raw_out[rows, begin : begin + HD] = norm_back(
                    unit_grad, value, inverse, head_gain[...]
                ).astype(jnp.bfloat16)
        begin = (query_heads + value_heads) * HD
        raw_out[rows, begin:] = value_grad[rows, :].astype(jnp.bfloat16)

    loop_rows(count, 64, finish)


def attention_back(
    hidden_low, output_weight, queries, keys, values, totals, query_raw, key_raw,
    query_gain, key_gain, cosine, sine, segment_column, segment_row,
):
    count = hidden_low.shape[0]
    query_columns, key_columns = queries.shape[1], keys.shape[1]
    f32, b16 = jnp.float32, jnp.bfloat16
    shape = jax.ShapeDtypeStruct
    return pl.pallas_call(
        functools.partial(attention_back_kernel, 256),
        out_shape=[
            shape((count, query_columns + 2 * key_columns), b16),
            shape((8, HD), f32),
            shape((8, HD), f32),
        ],
        scratch_shapes=[
            pltpu.VMEM((count, query_columns), b16),
            pltpu.VMEM((count, query_columns), f32),
            pltpu.VMEM((count, key_columns), f32),
            pltpu.VMEM((count, key_columns), f32),
        ],
        compiler_params=pltpu.CompilerParams(vmem_limit_bytes=56 * 1024 * 1024),
        cost_estimate=pl.CostEstimate(
            flops=2 * count * hidden_low.shape[1] * query_columns + 10 * count * count * query_columns,
            bytes_accessed=24 * 1024 * 1024,
            transcendentals=count * count * query_columns // HD,
        ),
    )(
        hidden_low, output_weight, queries, keys, values, totals, query_raw, key_raw,
        query_gain[None], key_gain[None], cosine, sine, segment_column, segment_row,
    )


def finish_kernel(columns, number, *refs):
    inputs, gains = refs[:number], refs[number]
    outs, held = refs[number + 1 : -number - 2], refs[-number - 2 : -2]
    in_sems, out_sems = refs[-2:]
    rows = outs[number - 1].shape[0]
    fetches = [
        pltpu.make_async_copy(source, target, in_sems.at[index])
        for index, (source, target) in enumerate(zip(inputs, held))
    ]
    for copy in fetches:
        copy.start()
    stores = [[pltpu.make_async_copy(held[k], outs[k], out_sems.at[k])] for k in range(number - 1)]
    begin, last = 0, []
    for k, count in enumerate(columns):
        last.append(
            pltpu.make_async_copy(
                held[-1].at[pl.ds(0, rows), pl.ds(begin, count)],
                outs[number - 1 + k],
                out_sems.at[number - 1 + k],
            )
        )
        begin += count
    stores.append(last)
    for row, out in zip((0, 1, 8, 9), outs[number + 2 :]):
        out[...] = gains[row : row + 1, : out.shape[1]]
    for fetch, group in zip(fetches, stores):
        fetch.wait()
        for copy in group:
            copy.start()
    for group in stores:
        for copy in group:
            copy.wait()


def finish(columns, head_width, arrays, raw, gains):
    shape = jax.ShapeDtypeStruct
    any_space = pl.BlockSpec(memory_space=pl.ANY)
    in_vmem = pl.BlockSpec(memory_space=pltpu.VMEM)
    width = raw.shape[0] - 8
    number = len(arrays) + 1
    outs = [shape(value.shape, value.dtype) for value in arrays]
    outs += [shape((width, count), jnp.float32) for count in columns]
    outs += [shape((1, count), jnp.float32) for count in (width, width, head_width, head_width)]
    return pl.pallas_call(
        functools.partial(finish_kernel, columns, number),
        out_shape=outs,
        in_specs=[any_space] * number + [in_vmem],
        out_specs=[any_space] * (number + 2) + [in_vmem] * 4,
        scratch_shapes=[pltpu.VMEM(value.shape, value.dtype) for value in (*arrays, raw)]
        + [pltpu.SemaphoreType.DMA((number,)), pltpu.SemaphoreType.DMA((number + 2,))],
        compiler_params=pltpu.CompilerParams(vmem_limit_bytes=60 * 1024 * 1024),
    )(*arrays, raw, gains)


def plain_shards(
    tokens,
    attention_gain,
    query_weight,
    key_weight,
    value_weight,
    query_gain,
    key_gain,
    output_weight,
    feedforward_gain,
    gate_weight,
    up_weight,
    down_weight,
    segment_numbers,
    positions,
    cotangent,
):
    count = tokens.shape[0]
    batch = count // SEQ_LEN
    query_heads = query_weight.shape[1] // HD
    value_heads = key_weight.shape[1] // HD
    group = query_heads // value_heads
    inputs = tokens.astype(jnp.float32)
    first_inverse = rms_inverse(inputs)
    first_normed = inputs * first_inverse
    normed_low = (first_normed * attention_gain).astype(jnp.bfloat16)
    query_raw = jnp.dot(normed_low, query_weight, preferred_element_type=jnp.float32).reshape(
        count, query_heads, HD
    )
    key_raw = jnp.dot(normed_low, key_weight, preferred_element_type=jnp.float32).reshape(
        count, value_heads, HD
    )
    value_low = jnp.dot(normed_low, value_weight, preferred_element_type=jnp.float32).astype(
        jnp.bfloat16
    )
    cosine, sine = rotary_tables(positions)
    cosine = cosine[:, None]
    sine = sine[:, None]
    query_inverse = rms_inverse(query_raw)
    query_unit = query_raw * query_inverse
    query_low = rotate(query_unit * query_gain, cosine, sine).astype(jnp.bfloat16)
    key_inverse = rms_inverse(key_raw)
    key_unit = key_raw * key_inverse
    key_low = rotate(key_unit * key_gain, cosine, sine).astype(jnp.bfloat16)
    queries = query_low.reshape(batch, SEQ_LEN, value_heads, group, HD)
    keys = key_low.reshape(batch, SEQ_LEN, value_heads, HD)
    values = value_low.reshape(batch, SEQ_LEN, value_heads, HD)
    segments = segment_numbers.reshape(batch, SEQ_LEN)
    mixed, totals = lax.map(attend, (queries, keys, values, segments))
    mixed_low = mixed.reshape(count, query_heads * HD).astype(jnp.bfloat16)
    attention = lax.psum(
        jnp.dot(mixed_low, output_weight, preferred_element_type=jnp.float32), "tensor"
    )
    hidden = inputs + attention
    second_inverse = rms_inverse(hidden)
    second_normed = hidden * second_inverse
    second_low = (second_normed * feedforward_gain).astype(jnp.bfloat16)
    gate = jnp.dot(second_low, gate_weight, preferred_element_type=jnp.float32)
    upward = jnp.dot(second_low, up_weight, preferred_element_type=jnp.float32)
    sigmoid_gate = jax.nn.sigmoid(gate)
    activated = gate * sigmoid_gate
    product_low = (activated * upward).astype(jnp.bfloat16)
    feedforward = lax.psum(
        jnp.dot(product_low, down_weight, preferred_element_type=jnp.float32), "tensor"
    )
    layer_output = (hidden + feedforward).astype(jnp.bfloat16)
    down_grad = jnp.einsum("tf,td->fd", product_low, cotangent, preferred_element_type=jnp.float32)
    product_grad = jnp.einsum(
        "td,fd->tf", cotangent, down_weight, preferred_element_type=jnp.float32
    )
    gate_grad_low = (
        product_grad * upward * sigmoid_gate * (1.0 + gate * (1.0 - sigmoid_gate))
    ).astype(jnp.bfloat16)
    upward_grad_low = (product_grad * activated).astype(jnp.bfloat16)
    gate_weight_grad = jnp.einsum(
        "td,tf->df", second_low, gate_grad_low, preferred_element_type=jnp.float32
    )
    upward_weight_grad = jnp.einsum(
        "td,tf->df", second_low, upward_grad_low, preferred_element_type=jnp.float32
    )
    second_part = jnp.einsum(
        "tf,df->td", gate_grad_low, gate_weight, preferred_element_type=jnp.float32
    )
    second_part = second_part + jnp.einsum(
        "tf,df->td", upward_grad_low, up_weight, preferred_element_type=jnp.float32
    )
    second_grad = lax.psum(second_part, "tensor")
    second_gain_grad = jnp.sum(second_grad * second_normed, axis=0)
    hidden_grad = cotangent.astype(jnp.float32) + norm_back(
        second_grad, hidden, second_inverse, feedforward_gain
    )
    hidden_low = hidden_grad.astype(jnp.bfloat16)
    output_weight_grad = jnp.einsum(
        "tc,td->cd", mixed_low, hidden_low, preferred_element_type=jnp.float32
    )
    mixed_grad = jnp.einsum(
        "td,cd->tc", hidden_low, output_weight, preferred_element_type=jnp.float32
    ).astype(jnp.bfloat16)
    upstream = mixed_grad.reshape(batch, SEQ_LEN, value_heads, group, HD)
    query_back, key_back, value_back = lax.map(
        attend_back, (queries, keys, values, segments, totals, upstream)
    )
    query_unit_grad = rotate_back(query_back.reshape(count, query_heads, HD), cosine, sine)
    key_unit_grad = rotate_back(key_back.reshape(count, value_heads, HD), cosine, sine)
    query_gain_part = jnp.sum(query_unit_grad * query_unit, axis=(0, 1))
    key_gain_part = jnp.sum(key_unit_grad * key_unit, axis=(0, 1))
    query_raw_grad = (
        norm_back(query_unit_grad, query_raw, query_inverse, query_gain)
        .reshape(count, query_heads * HD)
        .astype(jnp.bfloat16)
    )
    key_raw_grad = (
        norm_back(key_unit_grad, key_raw, key_inverse, key_gain)
        .reshape(count, value_heads * HD)
        .astype(jnp.bfloat16)
    )
    value_raw_grad = value_back.reshape(count, value_heads * HD).astype(jnp.bfloat16)
    query_weight_grad = jnp.einsum(
        "td,tc->dc", normed_low, query_raw_grad, preferred_element_type=jnp.float32
    )
    key_weight_grad = jnp.einsum(
        "td,tc->dc", normed_low, key_raw_grad, preferred_element_type=jnp.float32
    )
    value_weight_grad = jnp.einsum(
        "td,tc->dc", normed_low, value_raw_grad, preferred_element_type=jnp.float32
    )
    first_part = jnp.einsum(
        "tc,dc->td", query_raw_grad, query_weight, preferred_element_type=jnp.float32
    )
    first_part = first_part + jnp.einsum(
        "tc,dc->td", key_raw_grad, key_weight, preferred_element_type=jnp.float32
    )
    first_part = first_part + jnp.einsum(
        "tc,dc->td", value_raw_grad, value_weight, preferred_element_type=jnp.float32
    )
    first_grad, query_gain_grad, key_gain_grad = lax.psum(
        (first_part, query_gain_part, key_gain_part), "tensor"
    )
    first_gain_grad = jnp.sum(first_grad * first_normed, axis=0)
    tokens_gradient = (
        hidden_grad + norm_back(first_grad, inputs, first_inverse, attention_gain)
    ).astype(jnp.bfloat16)
    summed = (
        lax.psum_scatter(first_gain_grad, "dp", scatter_dimension=0, tiled=True),
        lax.psum_scatter(query_weight_grad, "dp", scatter_dimension=0, tiled=True),
        lax.psum_scatter(key_weight_grad, "dp", scatter_dimension=0, tiled=True),
        lax.psum_scatter(value_weight_grad, "dp", scatter_dimension=0, tiled=True),
        lax.psum_scatter(query_gain_grad, "dp", scatter_dimension=0, tiled=True),
        lax.psum_scatter(key_gain_grad, "dp", scatter_dimension=0, tiled=True),
        lax.psum_scatter(output_weight_grad, "dp", scatter_dimension=1, tiled=True),
        lax.psum_scatter(second_gain_grad, "dp", scatter_dimension=0, tiled=True),
        lax.psum_scatter(gate_weight_grad, "dp", scatter_dimension=0, tiled=True),
        lax.psum_scatter(upward_weight_grad, "dp", scatter_dimension=0, tiled=True),
        lax.psum_scatter(down_grad, "dp", scatter_dimension=1, tiled=True),
    )
    return (
        layer_output,
        tokens_gradient,
        summed[0],
        summed[1],
        summed[2],
        summed[3],
        summed[4],
        summed[5],
        summed[6],
        summed[7],
        summed[8],
        summed[9],
        summed[10],
    )


def shards(
    dp,
    tokens,
    attention_gain,
    query_weight,
    key_weight,
    value_weight,
    query_gain,
    key_gain,
    output_weight,
    feedforward_gain,
    gate_weight,
    up_weight,
    down_weight,
    segment_numbers,
    positions,
    cotangent,
):
    count, depth = tokens.shape
    width = depth // dp
    high = dp // 2
    core = lax.axis_index("tensor") % 2
    upstream_first = lax.ppermute(
        lax.dynamic_slice_in_dim(cotangent, core * (count // 2), 11 * count // 64, 0).astype(jnp.float32),
        "dp",
        [(i, i ^ 2) for i in range(dp)],
    )

    cosine, sine = rotary_tables(positions)
    sine = jnp.concatenate([-sine[:, : HD // 2], sine[:, HD // 2 :]], axis=1)
    tables = (cosine, sine, segment_numbers[:, None], segment_numbers[None])
    normed_low, query_raw, key_raw, queries, keys, values, mixed_low, totals = attention(
        tokens,
        attention_gain,
        (query_weight, key_weight, value_weight),
        query_gain,
        key_gain,
        *tables,
    )
    (
        hidden,
        second_part,
        low_own,
        product_own,
        gate_own,
        upward_own,
        low_pair,
        product_pair,
        gate_pair,
        upward_pair,
        upstream_pair,
    ) = front(
        mixed_low,
        output_weight,
        tokens,
        cotangent,
        upstream_first,
        feedforward_gain,
        gate_weight,
        up_weight,
        down_weight,
    )[:11]
    hidden_grad, hidden_low, out_part, down_weight_grad, gate_ready, gate_given, gate_kept = middle(
        second_part,
        hidden,
        cotangent,
        upstream_pair,
        product_own,
        product_pair,
        gate_own,
        gate_pair,
        low_own,
        low_pair,
        feedforward_gain,
        down_weight,
    )
    gate_middle, gate_inward = (
        lax.ppermute(gate_ready, "dp", [(2 * a + k, 2 * b + k) for a, b in pairs for k in (0, 1)])
        for pairs in (((1, 2), (2, 1)), ((0, 1), (3, 2)))
    )
    gate_moved = lax.ppermute(gate_given, "dp", [(i, i ^ 1) for i in range(dp)])
    raw_grad, query_gain_part, key_gain_part = attention_back(
        hidden_low,
        output_weight,
        queries,
        keys,
        values,
        totals,
        query_raw,
        key_raw,
        query_gain,
        key_gain,
        *tables,
    )

    lines = [
        jnp.pad(value.reshape(dp, -1), ((0, 0), (0, raw_grad.shape[1] - value.size // dp)))
        for value in (jnp.sum(query_gain_part, axis=0), jnp.sum(key_gain_part, axis=0))
    ]
    gain_lines = jnp.pad(jnp.stack(lines, axis=1), ((0, 0), (0, 6), (0, 0)))

    (
        layer_output,
        tokens_gradient,
        gate_weight_grad,
        up_weight_grad,
        raw_whole,
        output_weight_grad,
        gains,
    ) = (
        rear(
            [line_order(high, p) for p in range(high)],
            [gate_middle, gate_inward, gate_kept + gate_moved]
            + [low_own, low_pair, upward_own, upward_pair]
            + [normed_low, raw_grad, hidden_low, mixed_low],
            gain_lines,
            [out_part, hidden, hidden_grad, tokens],
            [query_weight, key_weight, value_weight, gate_weight, up_weight],
            attention_gain,
            feedforward_gain,
        )[:7]
    )
    (
        layer_output,
        tokens_gradient,
        gate_weight_grad,
        up_weight_grad,
        output_weight_grad,
        down_weight_grad,
        query_weight_grad,
        key_weight_grad,
        value_weight_grad,
        attention_gain_grad,
        feedforward_gain_grad,
        query_gain_grad,
        key_gain_grad,
    ) = finish(
        (query_weight.shape[1], key_weight.shape[1], value_weight.shape[1]),
        HD // dp,
        [
            layer_output,
            tokens_gradient,
            gate_weight_grad,
            up_weight_grad,
            output_weight_grad,
            down_weight_grad,
        ],
        raw_whole,
        gains,
    )
    return (
        layer_output,
        tokens_gradient,
        attention_gain_grad[0],
        query_weight_grad,
        key_weight_grad,
        value_weight_grad,
        query_gain_grad[0],
        key_gain_grad[0],
        output_weight_grad,
        feedforward_gain_grad[0],
        gate_weight_grad,
        up_weight_grad,
        down_weight_grad,
    )


def solution(mesh):
    dp, tensor = mesh.shape["dp"], mesh.shape["tensor"]

    def program(*args):
        if dp == 8 and tensor == 4 and args[0].shape[0] == SEQ_LEN:
            return shards(dp, *args)
        return plain_shards(*args)

    return jax.shard_map(
        program,
        mesh=mesh,
        in_specs=(
            P("dp", None),
            P(),
            P(None, "tensor"),
            P(None, "tensor"),
            P(None, "tensor"),
            P(),
            P(),
            P("tensor", None),
            P(),
            P(None, "tensor"),
            P(None, "tensor"),
            P("tensor", None),
            P("dp"),
            P("dp"),
            P("dp", None),
        ),
        out_specs=(
            P("dp", None),
            P("dp", None),
            P("dp"),
            P("dp", "tensor"),
            P("dp", "tensor"),
            P("dp", "tensor"),
            P("dp"),
            P("dp"),
            P("tensor", "dp"),
            P("dp"),
            P("dp", "tensor"),
            P("dp", "tensor"),
            P("tensor", "dp"),
        ),
        check_vma=False,
    )
```
